128 devices in a mesh: section: 2 (over core), dp: 16 (over x, z), tensor: 4 (over y).
Axes of the slice: x: 4, y: 4, z: 4, core: 2. Of those that a mesh axis runs over, the one named last changes fastest.
Arguments:
- activations: float32 [2, 8192, 1024], P(None, ('dp', 'tensor')), may hold values from -6 to 6
- cotangent: float32 [2, 8192, 1024], P(None, ('dp', 'tensor')), may hold values from -6 to 6
- lengths: int32 [2, 16, 2], P(None, 'dp'), may hold values from 0 to 512, as said below
- norm_gain: float32 [2, 1024], P('section'), may hold values from 0.5 to 1.5
- in_weight: bfloat16 [2, 1024, 2, 2048], P('section', 'dp', None, 'tensor'), may hold values from -0.1875 to 0.1875
- bc_weight: bfloat16 [2, 1024, 256], P('section', 'dp'), may hold values from -0.1875 to 0.1875
- dt_weight: bfloat16 [2, 1024, 32], P('section', 'dp', 'tensor'), may hold values from -0.1875 to 0.1875
- conv_weight: float32 [2, 4, 2304], P('section'), may hold values from -3 to 3
- conv_bias: float32 [2, 2304], P('section'), may hold values from -3 to 3
- dt_bias: float32 [2, 32], P('section'), may hold values from -7 to -4
- a_log: float32 [2, 32], P('section'), may hold values from 0 to 3
- d_skip: float32 [2, 32], P('section'), may hold values from 0.5 to 1.5
- gated_gain: float32 [2, 2048], P('section'), may hold values from 0.5 to 1.5
- out_weight: bfloat16 [2, 2048, 1024], P('section', 'tensor', 'dp'), may hold values from -0.125 to 0.125
Outputs:
- layer_out: float32 [2, 2, 8192, 1024], P('section', None, ('dp', 'tensor'))
- layer_grad: float32 [2, 2, 8192, 1024], P('section', None, ('dp', 'tensor'))
- norm_gain_grad: float32 [2, 1024], P('section')
- in_weight_grad: float32 [2, 1024, 2, 2048], P('section', 'dp', None, 'tensor')
- bc_weight_grad: float32 [2, 1024, 256], P('section', ('dp', 'tensor'))
- dt_weight_grad: float32 [2, 1024, 32], P('section', 'dp', 'tensor')
- conv_weight_grad: float32 [2, 4, 2304], P('section')
- conv_bias_grad: float32 [2, 2304], P('section')
- dt_bias_grad: float32 [2, 32], P('section')
- a_log_grad: float32 [2, 32], P('section')
- d_skip_grad: float32 [2, 32], P('section')
- gated_gain_grad: float32 [2, 2048], P('section')
- out_weight_grad: float32 [2, 2048, 1024], P('section', 'tensor', 'dp')
The draws below stay inside these ranges and needn't reach their ends.
Inputs may be any that keep to these rules, and one draw needn't show every extreme that they name: lengths[m, g, 0] is over 384 and the two lengths of a group sum to at most 512; in every micro-batch one group has lengths[m, g, 0] = 512; slots past the two sequences are padding.
All inputs are finite; a program needn't handle non-finite values.
Results may differ from the reference program's by a relative error of at most 0.025.
Values may be sent and summed in bfloat16 or wider, within the bound.
A program may use at most 192 MiB of HBM per device.

```python
import jax
import jax.numpy as jnp
from jax import lax

D = 1024
DI = 2048
H = 32
P_SIZE = 64
N = 128
CONV = 4
BLOCK_LEN = 256
SEGS = 2
MICRO = 2
CAP = 512
TOKENS = 8192
N_DP = 16


def draw_lengths(key, part):
    key = jax.random.fold_in(key, 11)
    first_key, second_key, full_key = jax.random.split(key, 3)
    first_len = jax.random.randint(first_key, (MICRO, N_DP), 3 * CAP // 4 + 1, CAP + 1).astype(jnp.int32)
    room_left = CAP - first_len
    fraction = jax.random.randint(second_key, (MICRO, N_DP), 0, 1 << 20).astype(jnp.int32)
    second_len = room_left * fraction // (1 << 20)
    full_group = jax.random.randint(full_key, (MICRO,), 0, N_DP).astype(jnp.int32)
    marked = jnp.arange(N_DP).astype(jnp.int32)[None, :] == full_group[:, None]
    first_len = jnp.where(marked, CAP, first_len)
    second_len = jnp.where(marked, 0, second_len)
    return jnp.stack([first_len, second_len], axis=-1).astype(jnp.int32)


def level_of(key, shape, shards, smallest, largest):
    gain = 1.0
    for dim, parts in shards:
        steps = jax.random.uniform(jax.random.fold_in(jax.random.fold_in(key, 6), dim), (parts,), jnp.float32, smallest / len(shards), largest / len(shards))
        gain = gain * jnp.repeat(jnp.exp(steps), shape[dim] // parts).reshape((-1,) + (1,) * (len(shape) - 1 - dim))
    return gain


def centred(key, dims, scale, limit, shards=(), kind=jnp.bfloat16):
    level = level_of(key, dims, shards, -0.22, 0.18) if shards else 1.0
    entries = jax.random.normal(key, dims, jnp.float32) * scale * level
    return jnp.minimum(jnp.maximum(entries, -limit), limit).astype(kind)


def setup_inputs(seed: int = 0) -> dict:
    streams_of = jax.random.split(jax.random.key(seed), 15)
    activations = centred(streams_of[0], (MICRO, TOKENS, D), 1.0, 6.0, ((1, 64),), jnp.float32)
    cotangent = centred(streams_of[1], (MICRO, TOKENS, D), 1.0, 6.0, ((1, 64),), jnp.float32)
    lengths = draw_lengths(jax.random.fold_in(streams_of[14], 71), 0)
    norm_gain = jnp.clip(1.0 + 0.1 * jax.random.normal(streams_of[3], (2, D), jnp.float32), 0.5, 1.5)
    in_weight = centred(streams_of[4], (2, D, 2, DI), D ** -0.5, 0.1875, ((0, 2), (1, 16), (3, 4)))
    bc_weight = centred(streams_of[5], (2, D, 2 * N), D ** -0.5, 0.1875, ((0, 2), (1, 16)))
    dt_weight = centred(streams_of[6], (2, D, H), D ** -0.5, 0.1875, ((0, 2), (1, 16), (2, 4)))
    conv_weight = centred(streams_of[7], (2, CONV, DI + 2 * N), 0.5, 3.0, ((0, 2),), jnp.float32)
    conv_bias = centred(streams_of[8], (2, DI + 2 * N), 0.5, 3.0, ((0, 2),), jnp.float32)
    dt_bias = jnp.clip(-7.0 + 3.0 * jax.random.uniform(streams_of[9], (2, H), jnp.float32) ** level_of(streams_of[9], (2, H), ((0, 2),), -0.2, 0.2), -7.0, -4.0)
    a_log = jnp.clip(3.0 * jax.random.uniform(streams_of[10], (2, H), jnp.float32) ** level_of(streams_of[10], (2, H), ((0, 2),), -0.2, 0.2), 0.0, 3.0)
    d_skip = jnp.clip(0.5 + 1.0 * jax.random.uniform(streams_of[11], (2, H), jnp.float32) ** level_of(streams_of[11], (2, H), ((0, 2),), -0.2, 0.2), 0.5, 1.5)
    gated_gain = jnp.clip(1.0 + 0.1 * jax.random.normal(streams_of[12], (2, DI), jnp.float32), 0.5, 1.5)
    out_weight = centred(streams_of[13], (2, DI, D), DI ** -0.5, 0.125, ((0, 2), (1, 4), (2, 16)))
    return dict(activations=activations, cotangent=cotangent, lengths=lengths, norm_gain=norm_gain, in_weight=in_weight, bc_weight=bc_weight, dt_weight=dt_weight, conv_weight=conv_weight, conv_bias=conv_bias, dt_bias=dt_bias, a_log=a_log, d_skip=d_skip, gated_gain=gated_gain, out_weight=out_weight)


EPSILON = 1e-05
HIGHEST_MODE = lax.Precision.HIGHEST

@jax.custom_vjp
def low(v):
    return lax.optimization_barrier(v.astype(jnp.bfloat16)).astype(jnp.float32)

@jax.custom_vjp
def low_back(v):
    return v

def low_keep(v):
    return (low(v), None)

def low_pass(kept, grad):
    return (grad,)

def back_keep(v):
    return (v, None)

def back_low(kept, grad):
    return (low(grad),)
low.defvjp(low_keep, low_pass)
low_back.defvjp(back_keep, back_low)

def segment_ids(lengths, group_len):
    position = jnp.arange(group_len).astype(jnp.int32)
    seg_ends = jnp.cumsum(lengths, axis=-1).astype(jnp.int32)
    segment = lax.optimization_barrier(jnp.sum((position[:, None] >= seg_ends[..., None, :]).astype(jnp.int32), axis=-1)).astype(jnp.int32)
    valid = (position < seg_ends[..., -1:]).astype(jnp.float32)
    return (segment, valid)

def conv_silu(signal, segment, weight, offset):
    summed = offset[None, :] + weight[CONV - 1][None, :] * signal
    for back_step in range(1, CONV):
        earlier = jnp.pad(signal, ((back_step, 0), (0, 0)))[:-back_step]
        earlier_seg = jnp.pad(segment, (back_step, 0), constant_values=-1)[:-back_step]
        same_seg = (earlier_seg == segment).astype(jnp.float32)[:, None]
        summed = summed + weight[CONV - 1 - back_step][None, :] * earlier * same_seg
    return jax.nn.silu(summed)

def state_space(inner, step_size, in_proj, out_proj, segment, a_log, d_skip):
    length, head_count, head_width = inner.shape
    blocks = length // BLOCK_LEN
    decay_rate = -jnp.exp(a_log)
    inner_blocks = inner.reshape(blocks, BLOCK_LEN, head_count, head_width)
    step_blocks = step_size.reshape(blocks, BLOCK_LEN, head_count)
    in_blocks = in_proj.reshape(blocks, BLOCK_LEN, -1)
    out_blocks = out_proj.reshape(blocks, BLOCK_LEN, -1)
    seg_blocks = segment.reshape(blocks, BLOCK_LEN).astype(jnp.int32)
    cumulative = jnp.cumsum(step_blocks * decay_rate, axis=1)
    before = jnp.concatenate([jnp.full((1,), -1, jnp.int32), seg_blocks[:-1, -1]])
    offsets = jnp.arange(BLOCK_LEN)
    lower_tri = offsets[:, None] >= offsets[None, :]
    same_seg = (seg_blocks[:, :, None] == seg_blocks[:, None, :]) & lower_tri[None]
    same_float = same_seg.astype(jnp.float32)[..., None]
    spread = cumulative[:, :, None, :] - cumulative[:, None, :, :]
    decay_mask = jnp.exp(spread * same_float) * same_float
    scores = jnp.einsum('btn,bsn->bts', out_blocks, in_blocks, precision=HIGHEST_MODE)
    mixing = scores[..., None] * decay_mask * step_blocks[:, None, :, :]
    inside = jnp.einsum('btsh,bshp->bthp', mixing, inner_blocks, precision=HIGHEST_MODE)
    last_cum = cumulative[:, -1, :]
    tail_weight = jnp.exp(last_cum[:, None, :] - cumulative) * step_blocks * (seg_blocks == seg_blocks[:, -1:]).astype(jnp.float32)[..., None]
    states = jnp.einsum('bsh,bshp,bsn->bhpn', tail_weight, inner_blocks, in_blocks, precision=HIGHEST_MODE)
    keep_flag = (seg_blocks[:, -1] == before).astype(jnp.float32)

    def carry_step(running, block_item):
        block_state, block_keep, block_last = block_item
        return (block_keep * jnp.exp(block_last)[:, None, None] * running + block_state, running)
    start_state = jnp.zeros((head_count, head_width, in_blocks.shape[-1]), jnp.float32)
    _, starts = lax.scan(carry_step, start_state, (states, keep_flag, last_cum))
    entry_decay = jnp.exp(cumulative) * (seg_blocks == before[:, None]).astype(jnp.float32)[..., None]
    outside = jnp.einsum('btn,bhpn->bthp', out_blocks, starts, precision=HIGHEST_MODE) * entry_decay[..., None]
    result = (inside + outside).reshape(length, head_count, head_width)
    return result + d_skip[None, :, None] * inner

def layer_group(residual, segment, valid, norm_gain, in_weight, bc_weight, dt_weight, conv_weight, conv_bias, dt_bias, a_log, d_skip, gated_gain, out_weight):
    length = residual.shape[0]
    normed = residual * lax.rsqrt(lax.optimization_barrier(jnp.mean(residual * residual, axis=-1, keepdims=True)) + EPSILON) * norm_gain
    hidden = low(normed)
    projected = low_back(jnp.dot(hidden, in_weight.reshape(D, 2 * DI), precision=HIGHEST_MODE))
    bc_proj = jnp.dot(hidden, bc_weight, precision=HIGHEST_MODE)
    dt_proj = low_back(jnp.dot(hidden, dt_weight, precision=HIGHEST_MODE))
    gate_in = projected[:, :DI]
    inner = conv_silu(projected[:, DI:], segment, conv_weight[:, :DI], conv_bias[:DI])
    bc_conv = conv_silu(bc_proj, segment, conv_weight[:, DI:], conv_bias[DI:])
    step_size = jax.nn.softplus(dt_proj + dt_bias)
    mixed = state_space(inner.reshape(length, H, P_SIZE), step_size, bc_conv[:, :N], bc_conv[:, N:], segment, a_log, d_skip)
    gated = mixed.reshape(length, DI) * jax.nn.silu(gate_in)
    scaled = low(gated * lax.rsqrt(lax.optimization_barrier(jnp.sum(gated * gated, axis=-1, keepdims=True)) / DI + EPSILON) * gated_gain)
    branch = low_back(jnp.dot(scaled, out_weight, precision=HIGHEST_MODE))
    return residual + branch * valid[:, None]

def layer_all(residual, segment, valid, params):
    groups = residual.reshape(MICRO * N_DP, CAP, D)

    def one_group(group_item):
        return layer_group(group_item[0], group_item[1], group_item[2], *params)
    result = lax.map(jax.checkpoint(one_group), (groups, segment, valid))
    return result.reshape(MICRO, N_DP * CAP, D)

def reference(activations, cotangent, lengths, norm_gain, in_weight, bc_weight, dt_weight, conv_weight, conv_bias, dt_bias, a_log, d_skip, gated_gain, out_weight):
    segment, valid = segment_ids(lengths.reshape(MICRO * N_DP, SEGS), CAP)
    weights = [param.astype(jnp.float32) for param in (norm_gain, in_weight, bc_weight, dt_weight, conv_weight, conv_bias, dt_bias, a_log, d_skip, gated_gain, out_weight)]

    def section_layer(residual, *params):
        return layer_all(residual, segment, valid, params)
    first_out, first_back = jax.vjp(section_layer, activations.astype(jnp.float32), *[param[0] for param in weights])
    second_out, second_back = jax.vjp(section_layer, first_out, *[param[1] for param in weights])
    second_grads = second_back(cotangent.astype(jnp.float32))
    first_grads = first_back(second_grads[0])
    stacked = [jnp.stack([first_grads[index_num + 1], second_grads[index_num + 1]]) for index_num in range(11)]
    return (jnp.stack([first_out, second_out]), jnp.stack([first_grads[0], second_grads[0]]), stacked[0], stacked[1], stacked[2], stacked[3], stacked[4], stacked[5], stacked[6], stacked[7], stacked[8], stacked[9], stacked[10])
```

```python
import functools

import jax
import jax.numpy as jnp
from jax import lax
from jax.experimental import pallas as pl
from jax.experimental.pallas import tpu as pltpu
from jax.sharding import PartitionSpec as P

D = 1024
DI = 2048
H = 32
N = 128
CONV = 4
T = 512
ROWS = 128
CH = 512
HL = 8
WZX = 1024
WP = 1408
WALL = 1920
NDP = 16
EPSILON = 1e-05
LOG2E = 1.4426950408889634
NEG = -1e30
F32 = jnp.float32
BF16 = jnp.bfloat16
MESH = pl.DeviceIdType.MESH
VM = pltpu.VMEM


def dot_nn(a, b):
    return lax.dot_general(a, b, (((1,), (0,)), ((), ())), preferred_element_type=F32)


def dot_nt(a, b):
    return lax.dot_general(a, b, (((1,), (1,)), ((), ())), preferred_element_type=F32)


def dot_tn(a, b):
    return lax.dot_general(a, b, (((0,), (0,)), ((), ())), preferred_element_type=F32)


def pieces(v, count):
    parts = []
    for _ in range(count):
        part = v.astype(BF16)
        parts.append(part)
        v = v - part.astype(F32)
    return parts


def sum_rows_nt(selector, v, count):
    return sum(dot_nt(selector, part) for part in pieces(v, count))


def rows_times(v, matrix):
    a, b, c = pieces(v, 3)
    stacked = jnp.concatenate([a.astype(F32), b.astype(F32), c.astype(F32), jnp.zeros_like(v)], 0)
    out = dot_nn(stacked.astype(BF16), matrix)
    return out[0:8] + out[8:16] + out[16:24]


def iota(shape, dim):
    return lax.broadcasted_iota(jnp.int32, shape, dim)


def segment_of(position, e0, e1):
    return (position >= e0).astype(jnp.int32) + (position >= e1).astype(jnp.int32)


def conv_masks(e0, e1):
    p = iota((T, 128), 0)
    seg = segment_of(p, e0, e1)
    return [
        jnp.where((p >= k) & (segment_of(p - k, e0, e1) == seg), 1.0, 0.0).astype(F32)
        for k in range(1, CONV)
    ]


def conv_pre(v, masks, cw, lanes):
    pre = cw[CONV : CONV + 1, lanes] + cw[CONV - 1 : CONV, lanes] * v
    for k in range(1, CONV):
        pre = pre + cw[CONV - 1 - k : CONV - k, lanes] * (masks[k - 1] * pltpu.roll(v, k, 0))
    return pre


def sigmoid(v):
    return 1.0 / (1.0 + jnp.exp(-v))


def steps_of(dt_tile, hp_ref):
    raw = jnp.transpose(dt_tile)[0:HL] + hp_ref[:, 0:1]
    step = jnp.maximum(raw, 0.0) + jnp.log1p(jnp.exp(-jnp.abs(raw)))
    rate = hp_ref[:, 1:2]
    upper = jnp.where(iota((T, T), 0) <= iota((T, T), 1), 1.0, 0.0).astype(BF16)
    cum = rows_times(step * rate, upper) * LOG2E
    columns = jnp.transpose(
        jnp.concatenate([cum, step, jnp.zeros((112, T), F32)], axis=0)
    )
    return raw, step, cum, columns


def pair_columns(columns, first, j, rows=T):
    low = iota((rows, 128), 1) < 64
    return jnp.where(
        low,
        jnp.broadcast_to(columns[:, first + 2 * j : first + 2 * j + 1], (rows, 128)),
        jnp.broadcast_to(columns[:, first + 2 * j + 1 : first + 2 * j + 2], (rows, 128)),
    )


def tile(j):
    return slice(128 * j, 128 * j + 128)


def mixer_fwd_kernel(with_grad, lens, proj, cw, hp, rows, *rest):
    if with_grad:
        d_scaled, gg, yssd, st, inn, xb, bb, cb, cumr, colr = rest
    else:
        gg, yssd, st, inn, xb, bb, cb, cumr, colr = rest
    e0 = lens[0]
    e1 = e0 + lens[1]
    masks = conv_masks(e0, e1)
    _, _, cum, columns = steps_of(proj[:, 1280:1408], hp)
    cumr[...] = cum
    colr[...] = columns
    for j in range(4):
        v = proj[:, 512 + 128 * j : 640 + 128 * j]
        pre = conv_pre(v, masks, cw, tile(j))
        act = pre * sigmoid(pre)
        inn[:, tile(j)] = act
        xb[:, tile(j)] = (act * pair_columns(columns, HL, j)).astype(BF16)
    for j, ref in ((0, bb), (1, cb)):
        pre = conv_pre(proj[:, 1024 + 128 * j : 1152 + 128 * j], masks, cw, slice(512 + 128 * j, 640 + 128 * j))
        ref[...] = (pre * sigmoid(pre)).astype(BF16)
    low = iota((128, 128), 1) < 64
    for i in range(4):
        n = 128 * (i + 1)
        here = slice(128 * i, n)
        scores = dot_nt(cb[here, :], bb[0:n, :])
        p = iota((128, n), 0) + 128 * i
        q = iota((128, n), 1)
        bias = jnp.where((p >= q) & (segment_of(p, e0, e1) == segment_of(q, e0, e1)), 0.0, NEG).astype(F32)
        for j in range(4):
            halves = []
            for h in (2 * j, 2 * j + 1):
                decay = jnp.exp2(colr[here, h : h + 1] - cumr[h : h + 1, 0:n] + bias)
                halves.append(dot_nn((scores * decay).astype(BF16), xb[0:n, tile(j)]))
            yssd[here, tile(j)] = jnp.where(low, halves[0], halves[1])
    squares = jnp.zeros((8, T), F32)
    dots = jnp.zeros((8, T), F32)
    ones = jnp.ones((8, 128), BF16)
    for j in range(4):
        z = proj[:, tile(j)]
        gated = (yssd[:, tile(j)] + rows[1:2, tile(j)] * inn[:, tile(j)]) * (z * sigmoid(z))
        gained = gated * rows[0:1, tile(j)]
        gg[:, tile(j)] = gained.astype(BF16)
        squares = squares + sum_rows_nt(ones, gated * gated, 2)
        if with_grad:
            dots = dots + sum_rows_nt(ones, gained * d_scaled[:, tile(j)], 2)
    row = iota((8, T), 0)
    both = jnp.where(row == 0, squares, jnp.where(row == 1, dots, 0.0))
    for i in range(4):
        st[i] = both[:, tile(i)]


def vmem_specs(count):
    return [pl.BlockSpec(memory_space=VM)] * count


def mixer_fwd(lens, proj, cw, hp, rows, d_scaled=None):
    extra = () if d_scaled is None else (d_scaled,)
    return pl.pallas_call(
        functools.partial(mixer_fwd_kernel, d_scaled is not None),
        out_shape=(
            jax.ShapeDtypeStruct((T, CH), BF16),
            jax.ShapeDtypeStruct((T, CH), F32),
            jax.ShapeDtypeStruct((4, 8, 128), F32),
        ),
        in_specs=[pl.BlockSpec(memory_space=pltpu.SMEM)] + vmem_specs(4 + len(extra)),
        out_specs=tuple(vmem_specs(3)),
        scratch_shapes=[
            VM((T, CH), F32),
            VM((T, CH), BF16),
            VM((T, N), BF16),
            VM((T, N), BF16),
            VM((8, T), F32),
            VM((T, 128), F32),
        ],
        compiler_params=pltpu.CompilerParams(vmem_limit_bytes=40 << 20),
        name="mixer_fwd",
    )(lens, proj, cw, hp, rows, *extra)


def back_roll(v, k):
    return pltpu.roll(v, T - k, 0)


def conv_back(d_pre, v, masks, cw, lanes, sums, column0):
    d_v = cw[CONV - 1 : CONV, lanes] * d_pre
    out = slice(column0, column0 + 128)
    sums[CONV : CONV + 1, out] = jnp.sum(d_pre, axis=0, keepdims=True)
    sums[CONV - 1 : CONV, out] = jnp.sum(d_pre * v, axis=0, keepdims=True)
    for k in range(1, CONV):
        masked = masks[k - 1] * d_pre
        d_v = d_v + cw[CONV - 1 - k : CONV - k, lanes] * back_roll(masked, k)
        sums[CONV - 1 - k : CONV - k, out] = jnp.sum(masked * pltpu.roll(v, k, 0), axis=0, keepdims=True)
    return d_v


def mixer_bwd_kernel(
    lens, proj, cw, hp, rows, yssd, d_scaled, coef,
    d_proj, scaled, sums, heads,
    inn, xb, dyb, dyf, dx, bb, cb, d_c, cumr, colr,
):
    e0 = lens[0]
    e1 = e0 + lens[1]
    masks = conv_masks(e0, e1)
    raw, step, cum, columns = steps_of(proj[:, 1280:1408], hp)
    cumr[...] = cum
    colr[...] = columns
    norm_cols = jnp.transpose(jnp.concatenate(
        [jnp.concatenate([coef[i] for i in range(4)], axis=1), jnp.zeros((120, T), F32)], axis=0
    ))
    s_col = jnp.broadcast_to(norm_cols[:, 0:1], (T, 128))
    k_col = jnp.broadcast_to(norm_cols[:, 1:2], (T, 128))
    sums[...] = jnp.zeros_like(sums)
    for j in range(4):
        v = proj[:, 512 + 128 * j : 640 + 128 * j]
        pre = conv_pre(v, masks, cw, tile(j))
        act = pre * sigmoid(pre)
        inn[:, tile(j)] = act
        xb[:, tile(j)] = (act * pair_columns(columns, HL, j)).astype(BF16)
        z = proj[:, tile(j)]
        sig = sigmoid(z)
        gate = z * sig
        y = yssd[:, tile(j)] + rows[1:2, tile(j)] * act
        gated = y * gate
        gs = gated * s_col
        gain = rows[0:1, tile(j)]
        dsc = d_scaled[:, tile(j)]
        scaled[:, tile(j)] = (gs * gain).astype(BF16)
        sums[5:6, tile(j)] = jnp.sum(gs * dsc, axis=0, keepdims=True)
        d_gated = s_col * gain * dsc - gated * k_col
        d_proj[:, tile(j)] = (d_gated * y * (sig * (1.0 + z * (1.0 - sig)))).astype(BF16)
        dy = d_gated * gate
        dyf[:, tile(j)] = dy
        dyb[:, tile(j)] = dy.astype(BF16)
        sums[6:7, tile(j)] = jnp.sum(dy * act, axis=0, keepdims=True)
    for j, ref in ((0, bb), (1, cb)):
        pre = conv_pre(proj[:, 1024 + 128 * j : 1152 + 128 * j], masks, cw, slice(512 + 128 * j, 640 + 128 * j))
        ref[...] = (pre * sigmoid(pre)).astype(BF16)
    d_c[...] = jnp.zeros_like(d_c)
    low = iota((128, 128), 1) < 64
    zero = jnp.zeros((128, 128), BF16)
    d_b_blocks = []
    for i in range(4):
        first = 128 * i
        n = T - first
        here = slice(first, first + 128)
        scores = dot_nt(bb[here, :], cb[first:T, :])
        q = iota((128, n), 0) + first
        p = iota((128, n), 1) + first
        bias = jnp.where((p >= q) & (segment_of(p, e0, e1) == segment_of(q, e0, e1)), 0.0, NEG).astype(F32)
        d_scores = jnp.zeros((128, n), F32)
        for j in range(4):
            x_tile = xb[here, tile(j)]
            dy_tile = dyb[first:T, tile(j)]
            halves = []
            for h in (2 * j, 2 * j + 1):
                decay = jnp.exp2(cumr[h : h + 1, first:T] - colr[here, h : h + 1] + bias)
                halves.append(dot_nn((scores * decay).astype(BF16), dy_tile))
                x_head = jnp.where(low if h % 2 == 0 else jnp.logical_not(low), x_tile, zero)
                d_scores = d_scores + dot_nt(x_head, dy_tile) * decay
            dx[here, tile(j)] = jnp.where(low, halves[0], halves[1])
        d_scores = d_scores.astype(BF16)
        d_b_blocks.append(dot_nn(d_scores, cb[first:T, :]))
        d_c[first:T, :] = d_c[first:T, :] + dot_tn(d_scores, bb[here, :])
    d_cum = jnp.zeros((8, T), F32)
    d_step = jnp.zeros((8, T), F32)
    for j in range(4):
        selector = jnp.where(iota((8, 128), 0) == 2 * j + iota((8, 128), 1) // 64, 1.0, 0.0).astype(BF16)
        dxt = dx[:, tile(j)]
        act = inn[:, tile(j)]
        change = dyb[:, tile(j)].astype(F32) * yssd[:, tile(j)] - xb[:, tile(j)].astype(F32) * dxt
        d_cum = d_cum + sum_rows_nt(selector, change, 3)
        d_step = d_step + sum_rows_nt(selector, act * dxt, 2)
        d_act = pair_columns(columns, HL, j) * dxt + rows[1:2, tile(j)] * dyf[:, tile(j)]
        v = proj[:, 512 + 128 * j : 640 + 128 * j]
        pre = conv_pre(v, masks, cw, tile(j))
        sig = sigmoid(pre)
        d_pre = d_act * (sig * (1.0 + pre * (1.0 - sig)))
        d_proj[:, 512 + 128 * j : 640 + 128 * j] = conv_back(d_pre, v, masks, cw, tile(j), sums, 128 * j).astype(BF16)
    for j in (0, 1):
        lanes = slice(512 + 128 * j, 640 + 128 * j)
        at = slice(1024 + 128 * j, 1152 + 128 * j)
        v = proj[:, at]
        pre = conv_pre(v, masks, cw, lanes)
        sig = sigmoid(pre)
        d_act = jnp.concatenate(d_b_blocks, axis=0) if j == 0 else d_c[...]
        d_pre = d_act * (sig * (1.0 + pre * (1.0 - sig)))
        d_proj[:, at] = conv_back(d_pre, v, masks, cw, lanes, sums, 512 + 128 * j).astype(BF16)
    lower = jnp.where(iota((T, T), 0) >= iota((T, T), 1), 1.0, 0.0).astype(BF16)
    d_a = rows_times(d_cum, lower)
    rate = hp[:, 1:2]
    d_raw = (d_step + rate * d_a) * sigmoid(raw)
    d_proj[:, 1280:1408] = jnp.transpose(
        jnp.concatenate([d_raw, jnp.zeros((120, T), F32)], axis=0)
    ).astype(BF16)
    bias_grad = jnp.broadcast_to(jnp.sum(d_raw, axis=1, keepdims=True), (8, 128))
    rate_grad = jnp.broadcast_to(jnp.sum(d_a * step, axis=1, keepdims=True) * rate, (8, 128))
    lane = iota((8, 128), 1)
    heads[...] = jnp.where(lane == 0, bias_grad, jnp.where(lane == 1, rate_grad, 0.0))


def mixer_bwd(lens, proj, cw, hp, rows, yssd, d_scaled, coef):
    return pl.pallas_call(
        mixer_bwd_kernel,
        out_shape=(
            jax.ShapeDtypeStruct((T, WP), BF16),
            jax.ShapeDtypeStruct((T, CH), BF16),
            jax.ShapeDtypeStruct((8, 768), F32),
            jax.ShapeDtypeStruct((8, 128), F32),
        ),
        in_specs=[pl.BlockSpec(memory_space=pltpu.SMEM)] + vmem_specs(7),
        out_specs=tuple(vmem_specs(4)),
        scratch_shapes=[
            VM((T, CH), F32),
            VM((T, CH), BF16),
            VM((T, CH), BF16),
            VM((T, CH), F32),
            VM((T, CH), F32),
            VM((T, N), BF16),
            VM((T, N), BF16),
            VM((T, N), F32),
            VM((8, T), F32),
            VM((T, 128), F32),
        ],
        compiler_params=pltpu.CompilerParams(vmem_limit_bytes=48 << 20),
        name="mixer_bwd",
    )(lens, proj, cw, hp, rows, yssd, d_scaled, coef)


def wgrad_kernel(hid0, dp0, db0, sc0, hid1, dp1, db1, sc1, out):
    for layer, (hid, dp, db, sc) in enumerate(((hid0, dp0, db0, sc0), (hid1, dp1, db1, sc1))):
        for x in range(4):
            for half in range(2):
                at = 256 * x + 128 * half
                rows_in = dot_tn(hid[:, at : at + 128], dp[...]).astype(BF16)
                rows_out = dot_tn(db[:, at : at + 128], sc[...]).astype(BF16)
                for k in range(2):
                    out[layer, x, 2 * half + k, :, 0:WP] = rows_in[64 * k : 64 * k + 64]
                    out[layer, x, 2 * half + k, :, WP:WALL] = rows_out[64 * k : 64 * k + 64]


def wgrad(*arrays):
    return pl.pallas_call(
        wgrad_kernel,
        out_shape=jax.ShapeDtypeStruct((2, 4, 4, 64, WALL), BF16),
        in_specs=vmem_specs(8),
        out_specs=pl.BlockSpec(memory_space=VM),
        compiler_params=pltpu.CompilerParams(vmem_limit_bytes=40 << 20),
        name="weight_grads",
    )(*arrays)


def places():
    section = lax.axis_index("section")
    dp = lax.axis_index("dp")
    return section, dp // 4, dp % 4, lax.axis_index("tensor")


def x_peer(x, z, o):
    return {"dp": ((x + o) % 4) * 4 + z}


def z_peer(x, z, o):
    return {"dp": x * 4 + (z + o) % 4}


def t_peer(t, o):
    return {"tensor": (t + o) % 4}


def greet(peers):
    barrier = pltpu.get_barrier_semaphore()
    for peer in peers:
        pl.semaphore_signal(barrier, inc=1, device_id=peer, device_id_type=MESH)
    pl.semaphore_wait(barrier, len(peers))


def send(src, dst, send_sem, recv_sem, peer):
    copy = pltpu.make_async_remote_copy(
        src_ref=src, dst_ref=dst, send_sem=send_sem, recv_sem=recv_sem,
        device_id=peer, device_id_type=MESH,
    )
    copy.start()
    return copy


def input_norm(u, gain):
    return u * lax.rsqrt(jnp.mean(u * u, axis=-1, keepdims=True) + EPSILON) * gain


def dma_sems(*shape):
    return pltpu.SemaphoreType.DMA(shape)


def gather_kernel(
    wsh, par, u, db, w, par_all, hid, db_all,
    p_s, p_r, own_s, one_s, one_r, two_s, two_r, core_s, core_r, db_s, db_r, hid_s, hid_r,
):
    c, x, z, t = places()
    core = {"section": 1 - c}
    xs = [x_peer(x, z, o) for o in (1, 2, 3)]
    zs = [z_peer(x, z, o) for o in (1, 2, 3)]
    ts = [t_peer(t, o) for o in (1, 2, 3)]
    greet([core] + xs + zs + ts)
    par_copy = send(par, par_all.at[c], p_s.at[0], p_r.at[0], core)
    own = pltpu.make_async_copy(wsh, w.at[c, x, z], own_s.at[0])
    own.start()
    lo, hi = pl.ds(0, 32), pl.ds(32, 32)
    first_a, first_b, second_a, second_b = [], [], [], []
    for o in range(3):
        first_a.append(send(wsh.at[lo], w.at[c, x, z, lo], one_s.at[0, o], one_r.at[0, o], zs[o]))
        first_b.append(send(wsh.at[hi], w.at[c, x, z, hi], one_s.at[1, o], one_r.at[1, o], xs[o]))
    second_a.append([
        send(wsh.at[lo], w.at[c, x, z, lo], two_s.at[0, 0, o], two_r.at[0, 0, o], xs[o]) for o in range(3)
    ])
    second_b.append([
        send(wsh.at[hi], w.at[c, x, z, hi], two_s.at[1, 0, o], two_r.at[1, 0, o], zs[o]) for o in range(3)
    ])
    db_copies = [send(db, db_all.at[t], db_s.at[o], db_r.at[o], ts[o]) for o in range(3)]
    db_all[t] = db[...]
    par_all[c] = par[...]
    par_copy.wait_recv()
    hid[t] = input_norm(u[...], par_all[0, 0:1, :]).astype(BF16)
    hid_copies = [send(hid.at[t], hid.at[t], hid_s.at[o], hid_r.at[o], ts[o]) for o in range(3)]
    for k in range(3):
        first_a[k].wait_recv()
        from_z = (z + 3 - k) % 4
        block = w.at[c, x, from_z, lo]
        second_a.append([
            send(block, block, two_s.at[0, k + 1, o], two_r.at[0, k + 1, o], xs[o]) for o in range(3)
        ])
        first_b[k].wait_recv()
        from_x = (x + 3 - k) % 4
        block_b = w.at[c, from_x, z, hi]
        second_b.append([
            send(block_b, block_b, two_s.at[1, k + 1, o], two_r.at[1, k + 1, o], zs[o]) for o in range(3)
        ])
    own.wait()
    core_copies = []

    def to_core(block, slot):
        core_copies.append(send(block, block, core_s.at[slot], core_r.at[slot], core))

    to_core(w.at[c, x, :, lo], 0)
    to_core(w.at[c, :, z, hi], 1)
    for o in range(3):
        for k in range(4):
            second_a[k][o].wait_recv()
            second_b[k][o].wait_recv()
        to_core(w.at[c, (x + 3 - o) % 4, :, lo], 2 + 2 * o)
        to_core(w.at[c, :, (z + 3 - o) % 4, hi], 3 + 2 * o)
    for copy in db_copies + hid_copies:
        copy.wait()
    for copy in core_copies:
        copy.wait()
    par_copy.wait_send()
    for copy in first_a + first_b:
        copy.wait_send()
    for group in second_a + second_b:
        for copy in group:
            copy.wait_send()


def gather(wsh, par, u, db):
    return pl.pallas_call(
        gather_kernel,
        out_shape=(
            jax.ShapeDtypeStruct((2, 4, 4, 64, WALL), BF16),
            jax.ShapeDtypeStruct((2, 16, 1024), F32),
            jax.ShapeDtypeStruct((4, ROWS, D), BF16),
            jax.ShapeDtypeStruct((4, ROWS, D), BF16),
        ),
        in_specs=vmem_specs(4),
        out_specs=(pl.BlockSpec(memory_space=pl.ANY),) + tuple(vmem_specs(3)),
        scratch_shapes=[
            dma_sems(1), dma_sems(1), dma_sems(1),
            dma_sems(2, 3), dma_sems(2, 3), dma_sems(2, 4, 3), dma_sems(2, 4, 3),
            dma_sems(8), dma_sems(8), dma_sems(3), dma_sems(3), dma_sems(3), dma_sems(3),
        ],
        compiler_params=pltpu.CompilerParams(
            collective_id=0, has_side_effects=True, vmem_limit_bytes=24 << 20
        ),
        name="gather_weights",
    )(wsh, par, u, db)


def column_of(row):
    return jnp.transpose(jnp.broadcast_to(row, (128, 128)))


def middle_kernel(
    part, st, u, valid, gain, total, u_next, s_out, hid,
    rbuf, sbuf, a_s, a_r, b_s, b_r, h_s, h_r,
):
    _, _, _, t = places()
    ts = [t_peer(t, o) for o in (1, 2, 3)]
    greet(ts)
    copies = []
    for o in range(3):
        to = (t + o + 1) % 4
        copies.append(send(part.at[to], rbuf.at[o], a_s.at[o], a_r.at[o], ts[o]))
        copies.append(send(st.at[to], sbuf.at[o], b_s.at[o], b_r.at[o], ts[o]))
    acc = part[t].astype(F32)
    stats = st[t]
    for o in range(3):
        copies[2 * o].wait_recv()
        copies[2 * o + 1].wait_recv()
        acc = acc + rbuf[o].astype(F32)
        stats = stats + sbuf[o]
    total[...] = acc
    s_row = lax.rsqrt(stats / DI + EPSILON)
    s_out[...] = s_row
    scale = column_of(s_row[0:1]) * valid[...]
    for j in range(8):
        u_next[:, tile(j)] = u[:, tile(j)] + scale * total[:, tile(j)]
    hid[t] = input_norm(u_next[...], gain[...]).astype(BF16)
    for o in range(3):
        copies.append(send(hid.at[t], hid.at[t], h_s.at[o], h_r.at[o], ts[o]))
    for copy in copies[:6]:
        copy.wait_send()
    for copy in copies[6:]:
        copy.wait()


def middle(part, st, u, valid, gain):
    return pl.pallas_call(
        middle_kernel,
        out_shape=(
            jax.ShapeDtypeStruct((ROWS, D), F32),
            jax.ShapeDtypeStruct((ROWS, D), F32),
            jax.ShapeDtypeStruct((8, 128), F32),
            jax.ShapeDtypeStruct((4, ROWS, D), BF16),
        ),
        in_specs=vmem_specs(5),
        out_specs=tuple(vmem_specs(4)),
        scratch_shapes=[VM((3, ROWS, D), BF16), VM((3, 8, 128), F32)] + [dma_sems(3)] * 6,
        compiler_params=pltpu.CompilerParams(
            collective_id=1, has_side_effects=True, vmem_limit_bytes=24 << 20
        ),
        name="sum_and_gather_tokens",
    )(part, st, u, valid, gain)


def stats_kernel(st, coef, buf, a_s, a_r):
    _, _, _, t = places()
    ts = [t_peer(t, o) for o in (1, 2, 3)]
    greet(ts)
    copies = [send(st, buf.at[t], a_s.at[o], a_r.at[o], ts[o]) for o in range(3)]
    buf[t] = st[...]
    for copy in copies:
        copy.wait()
    for i in range(4):
        both = buf[0, i] + buf[1, i] + buf[2, i] + buf[3, i]
        s = lax.rsqrt(both[0:1] / DI + EPSILON)
        k = s * s * s * (both[1:2] / DI)
        row = iota((8, 128), 0)
        coef[i] = jnp.where(row == 0, s, jnp.where(row == 1, k, 0.0))


def stats(st):
    return pl.pallas_call(
        stats_kernel,
        out_shape=jax.ShapeDtypeStruct((4, 8, 128), F32),
        in_specs=vmem_specs(1),
        out_specs=pl.BlockSpec(memory_space=VM),
        scratch_shapes=[VM((4, 4, 8, 128), F32), dma_sems(3), dma_sems(3)],
        compiler_params=pltpu.CompilerParams(collective_id=2, has_side_effects=True),
        name="sum_stats",
    )(st)


def norm_back(u, gain, g, d_hidden):
    r = lax.rsqrt(jnp.mean(u * u, axis=-1, keepdims=True) + EPSILON)
    mean = jnp.mean(u * gain * d_hidden, axis=-1, keepdims=True)
    d_u = g + r * gain * d_hidden - u * (r * r * r) * mean
    return d_u, jnp.sum(u * r * d_hidden, axis=0, keepdims=True)


def back_middle_kernel(
    dh, part, u, g, valid, gain, coef, total0, s0, out1, g1, ng, db_all, coef_all,
    rdh, rpart, a_s, a_r, b_s, b_r, d_s, d_r, e_s, e_r,
):
    _, _, _, t = places()
    ts = [t_peer(t, o) for o in (1, 2, 3)]
    greet(ts)
    first, late = [], []
    for o in range(3):
        to = (t + o + 1) % 4
        first.append(send(dh.at[to], rdh.at[o], a_s.at[o], a_r.at[o], ts[o]))
    for o in range(3):
        to = (t + o + 1) % 4
        late.append(send(part.at[to], rpart.at[o], b_s.at[o], b_r.at[o], ts[o]))
    acc = dh[t].astype(F32)
    for o in range(3):
        first[o].wait_recv()
        acc = acc + rdh[o].astype(F32)
    d_u, gain_term = norm_back(u[...], gain[...], g[...], acc)
    g1[...] = d_u
    ng[...] = gain_term
    mean = jnp.zeros((ROWS, 128), F32)
    for j in range(8):
        d_branch = (g1[:, tile(j)] * valid[...]).astype(BF16)
        db_all[t, :, tile(j)] = d_branch
        mean = mean + d_branch.astype(F32) * total0[:, tile(j)]
    mean = jnp.broadcast_to(jnp.sum(mean, axis=-1, keepdims=True), (128, 128))
    mean_row = jnp.transpose(mean)[0:8] / DI
    s = s0[0:1, :]
    row = iota((8, 128), 0)
    coef_all[t] = jnp.where(row == 0, s, jnp.where(row == 1, s * s * s * mean_row, 0.0))
    sends = []
    for o in range(3):
        sends.append(send(coef_all.at[t], coef_all.at[t], e_s.at[o], e_r.at[o], ts[o]))
        sends.append(send(db_all.at[t], db_all.at[t], d_s.at[o], d_r.at[o], ts[o]))
    acc1 = part[t].astype(F32)
    for o in range(3):
        late[o].wait_recv()
        acc1 = acc1 + rpart[o].astype(F32)
    out1[...] = acc1
    scale = column_of(coef[t][0:1]) * valid[...]
    for j in range(8):
        out1[:, tile(j)] = u[:, tile(j)] + scale * out1[:, tile(j)]
    for copy in sends:
        copy.wait()
    for copy in first + late:
        copy.wait_send()


def back_middle(dh, part, u, g, valid, gain, coef, total0, s0):
    return pl.pallas_call(
        back_middle_kernel,
        out_shape=(
            jax.ShapeDtypeStruct((ROWS, D), F32),
            jax.ShapeDtypeStruct((ROWS, D), F32),
            jax.ShapeDtypeStruct((1, D), F32),
            jax.ShapeDtypeStruct((4, ROWS, D), BF16),
            jax.ShapeDtypeStruct((4, 8, 128), F32),
        ),
        in_specs=vmem_specs(9),
        out_specs=tuple(vmem_specs(5)),
        scratch_shapes=[VM((3, ROWS, D), BF16), VM((3, ROWS, D), BF16)] + [dma_sems(3)] * 8,
        compiler_params=pltpu.CompilerParams(
            collective_id=3, has_side_effects=True, vmem_limit_bytes=32 << 20
        ),
        name="back_sum_and_gather",
    )(dh, part, u, g, valid, gain, coef, total0, s0)


def finish_kernel(
    dh, u, g1, gain, out0, out1, ng1, sums0, heads0, sums1, heads1, grads,
    lo, lg, w_out, bc_out, small_out,
    rdh, los, lgs, sms, smr, smz, smx, rcore, acc, ra, rb, ra2, rb2, bcr,
    a_s, a_r, own_s, core_s, core_r, lo_s, lo_r, lg_s, lg_r, sm_s, sm_r,
    sz_s, sz_r, sx_s, sx_r, st_s, st_r, xa_s, xa_r, zb_s, zb_r, za_s, za_r, xb_s, xb_r, bc_s, bc_r,
):
    c, x, z, t = places()
    core = {"section": 1 - c}
    xs = [x_peer(x, z, o) for o in (1, 2, 3)]
    zs = [z_peer(x, z, o) for o in (1, 2, 3)]
    ts = [t_peer(t, o) for o in (1, 2, 3)]
    greet([core] + xs + zs + ts)
    sent = []

    def push(src, dst, send_sem, recv_sem, peer):
        copy = send(src, dst, send_sem, recv_sem, peer)
        sent.append(copy)
        return copy

    low, high = pl.ds(0, 32), pl.ds(32, 32)
    big = [
        push(grads.at[1 - c, :, :, part], rcore.at[:, :, part], core_s.at[k], core_r.at[k], core)
        for k, part in ((0, low), (1, high))
    ]
    own = pltpu.make_async_copy(grads.at[c], acc, own_s.at[0])
    own.start()
    dh_copies = [push(dh.at[(t + o + 1) % 4], rdh.at[o], a_s.at[o], a_r.at[o], ts[o]) for o in range(3)]
    los[0] = out0[...]
    los[1] = out1[...]
    lo_copy = push(los.at[1 - c], lo.at[c], lo_s.at[0], lo_r.at[0], core)
    lgs[1] = g1[...]
    lo[c] = los[c]
    total = dh[t].astype(F32)
    for o in range(3):
        dh_copies[o].wait_recv()
        total = total + rdh[o].astype(F32)
    d_u, gain_term = norm_back(u[...], gain[...], g1[...], total)
    lgs[0] = d_u
    lg_copy = push(lgs.at[1 - c], lg.at[c], lg_s.at[0], lg_r.at[0], core)
    lg[c] = lgs[c]
    sms[...] = jnp.zeros_like(sms)
    for layer, (sums, heads, term) in enumerate(((sums0, heads0, gain_term), (sums1, heads1, ng1[...]))):
        sms[layer, 0:8, :] = sums[:, 0:512]
        sms[layer, 8:16, 0:256] = sums[:, 512:768]
        sms[layer, 8:16, 256:384] = heads[...]
        sms[layer, 16:17, :] = term[:, 0:512]
        sms[layer, 17:18, :] = term[:, 512:1024]
    sm_copy = push(sms.at[1 - c], smr, sm_s.at[0], sm_r.at[0], core)
    own.wait()
    big[0].wait_recv()

    def add_core(part):
        def step(i, carry):
            xx, zz = i // 4, i % 4
            acc[xx, zz, part] = (
                acc[xx, zz, part].astype(F32) + rcore[xx, zz, part].astype(F32)
            ).astype(BF16)
            return carry

        lax.fori_loop(0, 16, step, 0)

    add_core(low)
    xa = [
        push(acc.at[(x + o + 1) % 4, :, low], ra.at[o], xa_s.at[o], xa_r.at[o], xs[o]) for o in range(3)
    ]
    big[1].wait_recv()
    add_core(high)
    zb = [
        push(acc.at[:, (z + o + 1) % 4, high], rb.at[o], zb_s.at[o], zb_r.at[o], zs[o]) for o in range(3)
    ]
    sm_copy.wait_recv()
    smz[z] = sms[c] + smr[...]
    sz = [push(smz.at[z], smz.at[z], sz_s.at[o], sz_r.at[o], zs[o]) for o in range(3)]
    for copy in sz:
        copy.wait_recv()
    smx[x] = smz[0] + smz[1] + smz[2] + smz[3]
    sx = [push(smx.at[x], smx.at[x], sx_s.at[o], sx_r.at[o], xs[o]) for o in range(3)]
    for copy in xa:
        copy.wait_recv()

    def add_a(zz, carry):
        acc[x, zz, low] = (
            acc[x, zz, low].astype(F32)
            + ra[0, zz].astype(F32) + ra[1, zz].astype(F32) + ra[2, zz].astype(F32)
        ).astype(BF16)
        return carry

    lax.fori_loop(0, 4, add_a, 0)
    za = [
        push(acc.at[x, (z + o + 1) % 4, low], ra2.at[o], za_s.at[o], za_r.at[o], zs[o]) for o in range(3)
    ]
    for copy in zb:
        copy.wait_recv()

    def add_b(xx, carry):
        acc[xx, z, high] = (
            acc[xx, z, high].astype(F32)
            + rb[0, xx].astype(F32) + rb[1, xx].astype(F32) + rb[2, xx].astype(F32)
        ).astype(BF16)
        return carry

    lax.fori_loop(0, 4, add_b, 0)
    xb = [
        push(acc.at[(x + o + 1) % 4, z, high], rb2.at[o], xb_s.at[o], xb_r.at[o], xs[o]) for o in range(3)
    ]
    for copy in sx:
        copy.wait_recv()
    small_out[t] = smx[0] + smx[1] + smx[2] + smx[3]
    st = [push(small_out.at[t], small_out.at[t], st_s.at[o], st_r.at[o], ts[o]) for o in range(3)]
    for copy in za:
        copy.wait_recv()
    w_out[0:32, :] = (
        acc[x, z, low].astype(F32)
        + ra2[0].astype(F32) + ra2[1].astype(F32) + ra2[2].astype(F32)
    )
    for copy in xb:
        copy.wait_recv()
    w_out[32:64, :] = (
        acc[x, z, high].astype(F32)
        + rb2[0].astype(F32) + rb2[1].astype(F32) + rb2[2].astype(F32)
    )
    bc = [
        push(
            w_out.at[pl.ds(pl.multiple_of(16 * ((t + o + 1) % 4), 16), 16), pl.ds(1024, 256)],
            bcr.at[o], bc_s.at[o], bc_r.at[o], ts[o],
        )
        for o in range(3)
    ]
    for copy in bc:
        copy.wait_recv()
    bc_out[...] = (
        w_out[pl.ds(pl.multiple_of(16 * t, 16), 16), 1024:1280] + bcr[0] + bcr[1] + bcr[2]
    )
    for copy in st + [lo_copy, lg_copy]:
        copy.wait_recv()
    for copy in sent:
        copy.wait_send()


def finish(*arrays):
    any_spec = pl.BlockSpec(memory_space=pl.ANY)
    return pl.pallas_call(
        finish_kernel,
        out_shape=(
            jax.ShapeDtypeStruct((2, ROWS, D), F32),
            jax.ShapeDtypeStruct((2, ROWS, D), F32),
            jax.ShapeDtypeStruct((64, WALL), F32),
            jax.ShapeDtypeStruct((16, 256), F32),
            jax.ShapeDtypeStruct((4, 24, 512), F32),
        ),
        in_specs=vmem_specs(11) + [any_spec],
        out_specs=tuple(vmem_specs(5)),
        scratch_shapes=[
            VM((3, ROWS, D), BF16), VM((2, ROWS, D), F32), VM((2, ROWS, D), F32),
            VM((2, 24, 512), F32), VM((24, 512), F32), VM((4, 24, 512), F32), VM((4, 24, 512), F32),
            VM((4, 4, 64, WALL), BF16), VM((4, 4, 64, WALL), BF16),
            VM((3, 4, 32, WALL), BF16), VM((3, 4, 32, WALL), BF16),
            VM((3, 32, WALL), BF16), VM((3, 32, WALL), BF16), VM((3, 16, 256), F32),
            dma_sems(3), dma_sems(3), dma_sems(1), dma_sems(2), dma_sems(2),
            dma_sems(1), dma_sems(1), dma_sems(1), dma_sems(1), dma_sems(1), dma_sems(1),
        ] + [dma_sems(3)] * 16,
        compiler_params=pltpu.CompilerParams(
            collective_id=4, has_side_effects=True, vmem_limit_bytes=48 << 20
        ),
        name="sum_gradients",
    )(*arrays)


def body(
    activations, cotangent, lengths, norm_gain, in_weight, bc_weight, dt_weight, conv_weight,
    conv_bias, dt_bias, a_log, d_skip, gated_gain, out_weight,
):
    section = lax.axis_index("section")
    t = lax.axis_index("tensor")
    lens = lax.dynamic_index_in_dim(lengths[:, 0], section, 0, keepdims=False)
    position = t * ROWS + jnp.arange(ROWS)
    valid = jnp.broadcast_to((position < lens[0] + lens[1]).astype(F32)[:, None], (ROWS, 128))
    u0 = lax.dynamic_index_in_dim(activations, section, 0, keepdims=False)
    cot = lax.dynamic_index_in_dim(cotangent, section, 0, keepdims=False)
    db1_own = (cot * valid[:, 0:1]).astype(BF16)
    wsh = jnp.concatenate(
        [
            in_weight[0].reshape(64, 1024),
            bc_weight[0],
            dt_weight[0],
            jnp.zeros((64, 120), BF16),
            out_weight[0].T,
        ],
        axis=1,
    )
    par = jnp.concatenate(
        [
            norm_gain[0], gated_gain[0], conv_weight[0].reshape(-1), conv_bias[0],
            dt_bias[0], a_log[0], d_skip[0], jnp.zeros((16384 - 14688,), F32),
        ]
    ).reshape(16, 1024)
    w, par_all, hid0, db1 = gather(wsh, par, u0, db1_own)
    w = w.reshape(2, D, WALL)
    flat = par_all.reshape(2, 16384)

    def unpack(layer):
        p = flat[layer]
        gain = p[0:1024].reshape(1, 1024)
        gated = lax.dynamic_slice_in_dim(p[1024:3072], t * CH, CH)
        taps = p[3072:12288].reshape(4, 2304)
        bias = p[12288:14592].reshape(1, 2304)
        both = jnp.concatenate([taps, bias, jnp.zeros((3, 2304), F32)], axis=0)
        cw = jnp.concatenate([lax.dynamic_slice_in_dim(both, t * CH, CH, 1), both[:, DI:]], axis=1)
        heads = lax.dynamic_slice_in_dim(p[14592:14688].reshape(3, H), t * HL, HL, 1)
        hp = jnp.concatenate(
            [heads[0][:, None], -jnp.exp(heads[1])[:, None], jnp.zeros((HL, 126), F32)], axis=1
        )
        rows = jnp.concatenate([gated[None], jnp.repeat(heads[2], 64)[None], jnp.zeros((6, CH), F32)], axis=0)
        return gain, cw, hp, rows

    gain0, cw0, hp0, rows0 = unpack(0)
    gain1, cw1, hp1, rows1 = unpack(1)
    proj_w = [w[0, :, :WP], w[1, :, :WP]]
    out_w = [w[0, :, WP:], w[1, :, WP:]]
    hid0 = hid0.reshape(T, D)
    db1 = db1.reshape(T, D)

    proj0 = dot_nn(hid0, proj_w[0])
    gg0, y0, st0 = mixer_fwd(lens, proj0, cw0, hp0, rows0)
    part0 = dot_nt(gg0, out_w[0]).astype(BF16).reshape(4, ROWS, D)
    total0, u1, s0, hid1 = middle(part0, st0, u0, valid, gain1)
    hid1 = hid1.reshape(T, D)
    d_scaled1 = dot_nn(db1, out_w[1])
    proj1 = dot_nn(hid1, proj_w[1])
    gg1, y1, st1 = mixer_fwd(lens, proj1, cw1, hp1, rows1, d_scaled1)
    coef1 = stats(st1)
    part1 = dot_nt(gg1, out_w[1]).astype(BF16).reshape(4, ROWS, D)
    dp1, sc1, sums1, heads1 = mixer_bwd(lens, proj1, cw1, hp1, rows1, y1, d_scaled1, coef1)
    dh1 = dot_nt(dp1, proj_w[1]).astype(BF16).reshape(4, ROWS, D)
    out1, g1, ng1, db0, coef0 = back_middle(dh1, part1, u1, cot, valid, gain1, coef1, total0, s0)
    db0 = db0.reshape(T, D)
    d_scaled0 = dot_nn(db0, out_w[0])
    dp0, sc0, sums0, heads0 = mixer_bwd(lens, proj0, cw0, hp0, rows0, y0, d_scaled0, coef0)
    dh0 = dot_nt(dp0, proj_w[0]).astype(BF16).reshape(4, ROWS, D)
    grads = wgrad(hid0, dp0, db0, sc0, hid1, dp1, db1, sc1)
    lo, lg, w_grad, bc_grad, small = finish(
        dh0, u0, g1, gain0, u1, out1, ng1, sums0, heads0, sums1, heads1, grads
    )
    local = small[:, 0:8]
    shared = small[0] + small[1] + small[2] + small[3]
    conv_w = jnp.concatenate(
        [jnp.moveaxis(local[:, 0:4], 0, 1).reshape(4, DI), shared[8:12, 0:256]], axis=1
    )
    conv_b = jnp.concatenate([local[:, 4].reshape(DI), shared[12, 0:256]])
    return (
        lo[None],
        lg[None],
        shared[16:18].reshape(1, D),
        w_grad[:, 0:1024].reshape(1, 64, 2, CH),
        bc_grad[None],
        w_grad[:, 1280:1288][None],
        conv_w[None],
        conv_b[None],
        small[:, 8:16, 256].reshape(1, H),
        small[:, 8:16, 257].reshape(1, H),
        jnp.sum(local[:, 6].reshape(H, 64), axis=1)[None],
        local[:, 5].reshape(1, DI),
        w_grad[:, WP:].T[None],
    )


def solution(mesh):
    return jax.shard_map(
        body,
        mesh=mesh,
        in_specs=(
            P(None, ("dp", "tensor"), None),
            P(None, ("dp", "tensor"), None),
            P(None, "dp", None),
            P("section", None),
            P("section", "dp", None, "tensor"),
            P("section", "dp", None),
            P("section", "dp", "tensor"),
            P("section", None, None),
            P("section", None),
            P("section", None),
            P("section", None),
            P("section", None),
            P("section", None),
            P("section", "tensor", "dp"),
        ),
        out_specs=(
            P("section", None, ("dp", "tensor"), None),
            P("section", None, ("dp", "tensor"), None),
            P("section", None),
            P("section", "dp", None, "tensor"),
            P("section", ("dp", "tensor"), None),
            P("section", "dp", "tensor"),
            P("section", None, None),
            P("section", None),
            P("section", None),
            P("section", None),
            P("section", None),
            P("section", None),
            P("section", "tensor", "dp"),
        ),
        check_vma=False,
    )
```

```python
import functools

import jax
import jax.numpy as jnp
from jax import lax
from jax.experimental import pallas as pl
from jax.experimental.pallas import tpu as pltpu
from jax.sharding import PartitionSpec as P

D = 1024
DI = 2048
H = 32
N = 128
CONV = 4
T = 512
ROWS = 128
CH = 512
HL = 8
WZX = 1024
WP = 1408
WALL = 1920
NDP = 16
EPSILON = 1e-05
LOG2E = 1.4426950408889634
NEG = -1e30
F32 = jnp.float32
BF16 = jnp.bfloat16
MESH = pl.DeviceIdType.MESH
VM = pltpu.VMEM


def dot_nn(a, b):
    return lax.dot_general(a, b, (((1,), (0,)), ((), ())), preferred_element_type=F32)


def dot_nt(a, b):
    return lax.dot_general(a, b, (((1,), (1,)), ((), ())), preferred_element_type=F32)


def dot_tn(a, b):
    return lax.dot_general(a, b, (((0,), (0,)), ((), ())), preferred_element_type=F32)


def pieces(v, count):
    parts = []
    for _ in range(count):
        part = v.astype(BF16)
        parts.append(part)
        v = v - part.astype(F32)
    return parts


def sum_rows_nt(selector, v, count):
    return sum(dot_nt(selector, part) for part in pieces(v, count))


def rows_times(v, matrix):
    a, b, c = pieces(v, 3)
    stacked = jnp.concatenate([a.astype(F32), b.astype(F32), c.astype(F32), jnp.zeros_like(v)], 0)
    out = dot_nn(stacked.astype(BF16), matrix)
    return out[0:8] + out[8:16] + out[16:24]


def iota(shape, dim):
    return lax.broadcasted_iota(jnp.int32, shape, dim)


def segment_of(position, e0, e1):
    return (position >= e0).astype(jnp.int32) + (position >= e1).astype(jnp.int32)


def conv_masks(e0, e1):
    p = iota((T, 128), 0)
    seg = segment_of(p, e0, e1)
    return [
        jnp.where((p >= k) & (segment_of(p - k, e0, e1) == seg), 1.0, 0.0).astype(F32)
        for k in range(1, CONV)
    ]


def conv_pre(v, masks, cw, lanes):
    pre = cw[CONV : CONV + 1, lanes] + cw[CONV - 1 : CONV, lanes] * v
    for k in range(1, CONV):
        pre = pre + cw[CONV - 1 - k : CONV - k, lanes] * (masks[k - 1] * pltpu.roll(v, k, 0))
    return pre


def sigmoid(v):
    return 1.0 / (1.0 + jnp.exp(-v))


def steps_of(dt_tile, hp_ref):
    raw = jnp.transpose(dt_tile)[0:HL] + hp_ref[:, 0:1]
    step = jnp.maximum(raw, 0.0) + jnp.log1p(jnp.exp(-jnp.abs(raw)))
    rate = hp_ref[:, 1:2]
    upper = jnp.where(iota((T, T), 0) <= iota((T, T), 1), 1.0, 0.0).astype(BF16)
    cum = rows_times(step * rate, upper) * LOG2E
    columns = jnp.transpose(
        jnp.concatenate([cum, step, jnp.zeros((112, T), F32)], axis=0)
    )
    return raw, step, cum, columns


def pair_columns(columns, first, j, rows=T):
    low = iota((rows, 128), 1) < 64
    return jnp.where(
        low,
        jnp.broadcast_to(columns[:, first + 2 * j : first + 2 * j + 1], (rows, 128)),
        jnp.broadcast_to(columns[:, first + 2 * j + 1 : first + 2 * j + 2], (rows, 128)),
    )


def tile(j):
    return slice(128 * j, 128 * j + 128)


def layer_params(par, layer):
    return (
        par.at[layer, :, pl.ds(0, 768)],
        par.at[layer, :, pl.ds(768, 128)],
        par.at[layer, :, pl.ds(896, 512)],
    )


def project(hid, w, proj):
    tokens = hid[...].reshape(T, D)
    for first, width in ((0, 512), (512, 512), (1024, 384)):
        at = slice(first, first + width)
        proj[:, at] = dot_nn(tokens, w[:, :, :, at].reshape(D, width))


def scale_back(db, w, d_scaled):
    d_scaled[...] = dot_nn(db[...].reshape(T, D), w[:, :, :, WP:WALL].reshape(D, CH))


def mixer_fwd_kernel(layer, lens, par, hid, w, *rest):
    with_grad = layer == 1
    if with_grad:
        db, proj, part, yssd, st, d_scaled, gg, inn, xb, bb, cb, cumr, colr = rest
        scale_back(db, w, d_scaled)
    else:
        proj, part, yssd, st, gg, inn, xb, bb, cb, cumr, colr = rest
    cw, hp, rows = layer_params(par, layer)
    project(hid, w, proj)
    e0 = lens[0]
    e1 = e0 + lens[1]
    masks = conv_masks(e0, e1)
    _, _, cum, columns = steps_of(proj[:, 1280:1408], hp)
    cumr[...] = cum
    colr[...] = columns
    for j in range(4):
        v = proj[:, 512 + 128 * j : 640 + 128 * j]
        pre = conv_pre(v, masks, cw, tile(j))
        act = pre * sigmoid(pre)
        inn[:, tile(j)] = act
        xb[:, tile(j)] = (act * pair_columns(columns, HL, j)).astype(BF16)
    for j, ref in ((0, bb), (1, cb)):
        pre = conv_pre(proj[:, 1024 + 128 * j : 1152 + 128 * j], masks, cw, slice(512 + 128 * j, 640 + 128 * j))
        ref[...] = (pre * sigmoid(pre)).astype(BF16)
    low = iota((128, 128), 1) < 64
    for i in range(4):
        n = 128 * (i + 1)
        here = slice(128 * i, n)
        scores = dot_nt(cb[here, :], bb[0:n, :])
        p = iota((128, n), 0) + 128 * i
        q = iota((128, n), 1)
        bias = jnp.where((p >= q) & (segment_of(p, e0, e1) == segment_of(q, e0, e1)), 0.0, NEG).astype(F32)
        for j in range(4):
            halves = []
            for h in (2 * j, 2 * j + 1):
                decay = jnp.exp2(colr[here, h : h + 1] - cumr[h : h + 1, 0:n] + bias)
                halves.append(dot_nn((scores * decay).astype(BF16), xb[0:n, tile(j)]))
            yssd[here, tile(j)] = jnp.where(low, halves[0], halves[1])
    squares = jnp.zeros((8, T), F32)
    dots = jnp.zeros((8, T), F32)
    ones = jnp.ones((8, 128), BF16)
    for j in range(4):
        z = proj[:, tile(j)]
        gated = (yssd[:, tile(j)] + rows[1:2, tile(j)] * inn[:, tile(j)]) * (z * sigmoid(z))
        gained = gated * rows[0:1, tile(j)]
        gg[:, tile(j)] = gained.astype(BF16)
        squares = squares + sum_rows_nt(ones, gated * gated, 2)
        if with_grad:
            dots = dots + sum_rows_nt(ones, gained * d_scaled[:, tile(j)], 2)
    row = iota((8, T), 0)
    both = jnp.where(row == 0, squares, jnp.where(row == 1, dots, 0.0))
    for i in range(4):
        st[i] = both[:, tile(i)]
    for x in range(4):
        columns_out = slice(256 * x, 256 * x + 256)
        branch = dot_nt(gg[...], w[x, :, :, WP:WALL].reshape(256, CH)).astype(BF16)
        part[:, :, columns_out] = branch.reshape(4, ROWS, 256)


def vmem_specs(count):
    return [pl.BlockSpec(memory_space=VM)] * count


def mixer_fwd(layer, lens, par, hid, w, *db):
    out_shape = [
        jax.ShapeDtypeStruct((T, WP), F32),
        jax.ShapeDtypeStruct((4, ROWS, D), BF16),
        jax.ShapeDtypeStruct((T, CH), F32),
        jax.ShapeDtypeStruct((4, 8, 128), F32),
    ] + [jax.ShapeDtypeStruct((T, CH), F32)] * layer
    return pl.pallas_call(
        functools.partial(mixer_fwd_kernel, layer),
        out_shape=tuple(out_shape),
        in_specs=[pl.BlockSpec(memory_space=pltpu.SMEM)] + vmem_specs(3 + len(db)),
        out_specs=tuple(vmem_specs(len(out_shape))),
        scratch_shapes=[
            VM((T, CH), BF16),
            VM((T, CH), F32),
            VM((T, CH), BF16),
            VM((T, N), BF16),
            VM((T, N), BF16),
            VM((8, T), F32),
            VM((T, 128), F32),
        ],
        compiler_params=pltpu.CompilerParams(vmem_limit_bytes=40 << 20),
        name="mixer_fwd",
    )(lens, par, hid, w, *db)


def head_selector(j):
    head = 2 * j + (iota((8, 128), 1) >= 64).astype(jnp.int32)
    return jnp.where(iota((8, 128), 0) == head, 1.0, 0.0).astype(BF16)


def back_roll(v, k):
    return pltpu.roll(v, T - k, 0)


def conv_back(d_pre, v, masks, cw, lanes, sums, column0):
    d_v = cw[CONV - 1 : CONV, lanes] * d_pre
    out = slice(column0, column0 + 128)
    sums[CONV : CONV + 1, out] = jnp.sum(d_pre, axis=0, keepdims=True)
    sums[CONV - 1 : CONV, out] = jnp.sum(d_pre * v, axis=0, keepdims=True)
    for k in range(1, CONV):
        masked = masks[k - 1] * d_pre
        d_v = d_v + cw[CONV - 1 - k : CONV - k, lanes] * back_roll(masked, k)
        sums[CONV - 1 - k : CONV - k, out] = jnp.sum(masked * pltpu.roll(v, k, 0), axis=0, keepdims=True)
    return d_v


def mixer_bwd_kernel(layer, lens, par, hid, w, db, proj, yssd, coef, *rest):
    if layer == 1:
        d_scaled, *rest = rest
    dh, grads, sums, heads, d_proj, scaled, inn, xb, dyb, dyf, dx, bb, cb, d_c, cumr, colr, *rest = rest
    if layer == 0:
        d_scaled = rest[0]
        scale_back(db, w, d_scaled)
    cw, hp, rows = layer_params(par, layer)
    e0 = lens[0]
    e1 = e0 + lens[1]
    masks = conv_masks(e0, e1)
    raw, step, cum, columns = steps_of(proj[:, 1280:1408], hp)
    cumr[...] = cum
    colr[...] = columns
    norm_cols = jnp.transpose(jnp.concatenate(
        [jnp.concatenate([coef[i] for i in range(4)], axis=1), jnp.zeros((120, T), F32)], axis=0
    ))
    s_col = jnp.broadcast_to(norm_cols[:, 0:1], (T, 128))
    k_col = jnp.broadcast_to(norm_cols[:, 1:2], (T, 128))
    sums[...] = jnp.zeros_like(sums)
    d_skip = jnp.zeros((8, T), F32)
    for j in range(4):
        selector = head_selector(j)
        v = proj[:, 512 + 128 * j : 640 + 128 * j]
        pre = conv_pre(v, masks, cw, tile(j))
        act = pre * sigmoid(pre)
        inn[:, tile(j)] = act
        xb[:, tile(j)] = (act * pair_columns(columns, HL, j)).astype(BF16)
        z = proj[:, tile(j)]
        sig = sigmoid(z)
        gate = z * sig
        y = yssd[:, tile(j)] + rows[1:2, tile(j)] * act
        gated = y * gate
        gs = gated * s_col
        gain = rows[0:1, tile(j)]
        dsc = d_scaled[:, tile(j)]
        scaled[:, tile(j)] = (gs * gain).astype(BF16)
        sums[5:6, tile(j)] = jnp.sum(gs * dsc, axis=0, keepdims=True)
        d_gated = s_col * gain * dsc - gated * k_col
        d_proj[:, tile(j)] = (d_gated * y * (sig * (1.0 + z * (1.0 - sig)))).astype(BF16)
        dy = d_gated * gate
        dyf[:, tile(j)] = dy
        dyb[:, tile(j)] = dy.astype(BF16)
        d_skip = d_skip + sum_rows_nt(selector, dy * act, 2)
    for j, ref in ((0, bb), (1, cb)):
        pre = conv_pre(proj[:, 1024 + 128 * j : 1152 + 128 * j], masks, cw, slice(512 + 128 * j, 640 + 128 * j))
        ref[...] = (pre * sigmoid(pre)).astype(BF16)
    d_c[...] = jnp.zeros_like(d_c)
    low = iota((128, 128), 1) < 64
    zero = jnp.zeros((128, 128), BF16)
    d_b_blocks = []
    for i in range(4):
        first = 128 * i
        n = T - first
        here = slice(first, first + 128)
        scores = dot_nt(bb[here, :], cb[first:T, :])
        q = iota((128, n), 0) + first
        p = iota((128, n), 1) + first
        bias = jnp.where((p >= q) & (segment_of(p, e0, e1) == segment_of(q, e0, e1)), 0.0, NEG).astype(F32)
        d_scores = jnp.zeros((128, n), F32)
        for j in range(4):
            x_tile = xb[here, tile(j)]
            dy_tile = dyb[first:T, tile(j)]
            halves = []
            for h in (2 * j, 2 * j + 1):
                decay = jnp.exp2(cumr[h : h + 1, first:T] - colr[here, h : h + 1] + bias)
                halves.append(dot_nn((scores * decay).astype(BF16), dy_tile))
                x_head = jnp.where(low if h % 2 == 0 else jnp.logical_not(low), x_tile, zero)
                d_scores = d_scores + dot_nt(x_head, dy_tile) * decay
            dx[here, tile(j)] = jnp.where(low, halves[0], halves[1])
        d_scores = d_scores.astype(BF16)
        d_b_blocks.append(dot_nn(d_scores, cb[first:T, :]))
        d_c[first:T, :] = d_c[first:T, :] + dot_tn(d_scores, bb[here, :])
    d_cum = jnp.zeros((8, T), F32)
    d_step = jnp.zeros((8, T), F32)
    for j in range(4):
        selector = head_selector(j)
        dxt = dx[:, tile(j)]
        act = inn[:, tile(j)]
        change = dyb[:, tile(j)].astype(F32) * yssd[:, tile(j)] - xb[:, tile(j)].astype(F32) * dxt
        d_cum = d_cum + sum_rows_nt(selector, change, 3)
        d_step = d_step + sum_rows_nt(selector, act * dxt, 2)
        d_act = pair_columns(columns, HL, j) * dxt + rows[1:2, tile(j)] * dyf[:, tile(j)]
        v = proj[:, 512 + 128 * j : 640 + 128 * j]
        pre = conv_pre(v, masks, cw, tile(j))
        sig = sigmoid(pre)
        d_pre = d_act * (sig * (1.0 + pre * (1.0 - sig)))
        d_proj[:, 512 + 128 * j : 640 + 128 * j] = conv_back(d_pre, v, masks, cw, tile(j), sums, 128 * j).astype(BF16)
    for j in (0, 1):
        lanes = slice(512 + 128 * j, 640 + 128 * j)
        at = slice(1024 + 128 * j, 1152 + 128 * j)
        v = proj[:, at]
        pre = conv_pre(v, masks, cw, lanes)
        sig = sigmoid(pre)
        d_act = jnp.concatenate(d_b_blocks, axis=0) if j == 0 else d_c[...]
        d_pre = d_act * (sig * (1.0 + pre * (1.0 - sig)))
        d_proj[:, at] = conv_back(d_pre, v, masks, cw, lanes, sums, 512 + 128 * j).astype(BF16)
    lower = jnp.where(iota((T, T), 0) >= iota((T, T), 1), 1.0, 0.0).astype(BF16)
    d_a = rows_times(d_cum, lower)
    rate = hp[:, 1:2]
    d_raw = (d_step + rate * d_a) * sigmoid(raw)
    d_proj[:, 1280:1408] = jnp.transpose(
        jnp.concatenate([d_raw, jnp.zeros((120, T), F32)], axis=0)
    ).astype(BF16)
    bias_grad = jnp.broadcast_to(jnp.sum(d_raw, axis=1, keepdims=True), (8, 128))
    rate_grad = jnp.broadcast_to(jnp.sum(d_a * step, axis=1, keepdims=True) * rate, (8, 128))
    skip_grad = jnp.broadcast_to(jnp.sum(d_skip, axis=1, keepdims=True), (8, 128))
    lane = iota((8, 128), 1)
    by_head = jnp.where(
        lane == 0, bias_grad, jnp.where(lane == 1, rate_grad, jnp.where(lane == 2, skip_grad, 0.0))
    )
    heads[...] = jnp.transpose(jnp.concatenate([by_head, jnp.zeros((120, 128), F32)], axis=0))[0:8]
    for x in range(4):
        back = dot_nt(d_proj[...], w[x, :, :, 0:WP].reshape(256, WP)).astype(BF16)
        dh[:, :, 256 * x : 256 * x + 256] = back.reshape(4, ROWS, 256)
    for x in range(4):
        for half in range(2):
            at = slice(256 * x + 128 * half, 256 * x + 128 * half + 128)
            rows_in = dot_tn(hid[:, :, at].reshape(T, 128), d_proj[...]).astype(BF16)
            rows_out = dot_tn(db[:, :, at].reshape(T, 128), scaled[...]).astype(BF16)
            for k in range(4):
                block = slice(32 * k, 32 * k + 32)
                grads[k % 2, x, 2 * half + k // 2, :, 0:WP] = rows_in[block]
                grads[k % 2, x, 2 * half + k // 2, :, WP:WALL] = rows_out[block]


def mixer_bwd(layer, lens, par, hid, w, db, proj, yssd, coef, *d_scaled):
    return pl.pallas_call(
        functools.partial(mixer_bwd_kernel, layer),
        out_shape=(
            jax.ShapeDtypeStruct((4, ROWS, D), BF16),
            jax.ShapeDtypeStruct((2, 4, 4, 32, WALL), BF16),
            jax.ShapeDtypeStruct((8, 768), F32),
            jax.ShapeDtypeStruct((8, 128), F32),
        ),
        in_specs=[pl.BlockSpec(memory_space=pltpu.SMEM)] + vmem_specs(7 + len(d_scaled)),
        out_specs=tuple(vmem_specs(4)),
        scratch_shapes=[
            VM((T, WP), BF16),
            VM((T, CH), BF16),
            VM((T, CH), F32),
            VM((T, CH), BF16),
            VM((T, CH), BF16),
            VM((T, CH), F32),
            VM((T, CH), F32),
            VM((T, N), BF16),
            VM((T, N), BF16),
            VM((T, N), F32),
            VM((8, T), F32),
            VM((T, 128), F32),
        ] + [VM((T, CH), F32)] * (1 - layer),
        compiler_params=pltpu.CompilerParams(vmem_limit_bytes=52 << 20),
        name="mixer_bwd",
    )(lens, par, hid, w, db, proj, yssd, coef, *d_scaled)


def places():
    section = lax.axis_index("section")
    dp = lax.axis_index("dp")
    return section, dp // 4, dp % 4, lax.axis_index("tensor")


class Peers:
    def __init__(self):
        self.c, self.x, self.z, self.t = places()
        self.core = {"section": 1 - self.c}
        self.xs = [{"dp": ((self.x + o) % 4) * 4 + self.z} for o in (1, 2, 3)]
        self.zs = [{"dp": self.x * 4 + (self.z + o) % 4} for o in (1, 2, 3)]
        self.ts = [{"tensor": (self.t + o) % 4} for o in (1, 2, 3)]


def greet(peers):
    barrier = pltpu.get_barrier_semaphore()
    for peer in peers:
        pl.semaphore_signal(barrier, inc=1, device_id=peer, device_id_type=MESH)
    pl.semaphore_wait(barrier, len(peers))


class Link:
    def __init__(self, send_sems, recv_sems):
        self.send_sems, self.recv_sems, self.sent = send_sems, recv_sems, []

    def send(self, src, dst, peer):
        k = len(self.sent)
        copy = pltpu.make_async_remote_copy(
            src_ref=src, dst_ref=dst, send_sem=self.send_sems.at[k], recv_sem=self.recv_sems.at[k],
            device_id=peer, device_id_type=MESH,
        )
        copy.start()
        self.sent.append(copy)
        return copy

    def drain(self):
        for copy in self.sent:
            copy.wait_send()


def spread(link, block, r, peers):
    plus, minus = peers[0], peers[2]

    def go(k, half, peer):
        return link.send(block(k, half), block(k, half), peer)

    from_left = [go(r, 0, plus)]
    from_right = [go(r, 1, minus)]
    from_left.append(go(r, 1, plus))
    from_right.append(go(r, 0, minus))
    yield
    from_left[0].wait_recv()
    far = [go((r + 3) % 4, 0, plus)]
    from_right[0].wait_recv()
    far.append(go((r + 1) % 4, 1, minus))
    yield
    for copy in (from_left[1], from_right[1]):
        copy.wait_recv()
    yield
    for copy in far:
        copy.wait_recv()
    yield


def collect(link, part, relay, sums, inbox, r, peers):
    plus, minus = peers[0], peers[2]
    left, right, far = (r + 3) % 4, (r + 1) % 4, (r + 2) % 4
    up = link.send(part(far, 0), relay.at[0], plus)
    down = link.send(part(far, 1), relay.at[1], minus)
    last = [
        link.send(part(right, 1), inbox(0, 1), plus),
        link.send(part(left, 0), inbox(1, 0), minus),
    ]
    yield
    up.wait_recv()
    sums[0] = (part(right, 0)[...].astype(F32) + relay[0].astype(F32)).astype(BF16)
    last.append(link.send(sums.at[0], inbox(0, 0), plus))
    down.wait_recv()
    sums[1] = (part(left, 1)[...].astype(F32) + relay[1].astype(F32)).astype(BF16)
    last.append(link.send(sums.at[1], inbox(1, 1), minus))
    yield
    for copy in last:
        copy.wait_recv()
    yield


def run(steps):
    for _ in steps:
        pass


def token_halves(ref):
    return lambda k, half: ref.at[k, pl.ds(64 * half, 64)]


def collect_tokens(link, ref, relay, sums, inbox, me):
    return collect(link, token_halves(ref), relay, sums, token_halves(inbox), me.t, me.ts)


def spread_tokens(link, ref, me):
    return spread(link, token_halves(ref), me.t, me.ts)


def core_rows(c):
    first = pl.multiple_of(32 * c, 32)
    return pl.ds(first, 32), pl.ds(first, 16), pl.ds(pl.multiple_of(32 * c + 16, 16), 16)


def gather_layer(link, own_sem, shard, w, me):
    c, x, z = me.c, me.x, me.z
    whole, a, b = core_rows(c)
    own = pltpu.make_async_copy(shard, w.at[x, z, whole], own_sem)
    own.start()
    first = []
    for o in range(3):
        first.append(link.send(shard.at[pl.ds(0, 16)], w.at[x, z, a], me.zs[o]))
        first.append(link.send(shard.at[pl.ds(16, 16)], w.at[x, z, b], me.xs[o]))
    yield
    own.wait()
    for copy in first:
        copy.wait_recv()
    along_x = spread(link, lambda k, half: w.at[k, pl.ds(2 * half, 2), a], x, me.xs)
    along_z = spread(link, lambda k, half: w.at[pl.ds(2 * half, 2), k, b], z, me.zs)
    next(along_x)
    next(along_z)
    core = []

    def to_core(o):
        block_a = w.at[(x + o) % 4, :, a]
        block_b = w.at[:, (z + o) % 4, b]
        core.append(link.send(block_a, block_a, me.core))
        core.append(link.send(block_b, block_b, me.core))

    to_core(0)
    yield
    next(along_x)
    next(along_z)
    yield
    next(along_x)
    next(along_z)
    to_core(1)
    to_core(3)
    yield
    next(along_x)
    next(along_z)
    to_core(2)
    yield
    for copy in core:
        copy.wait_recv()
    yield


GATHER_COPIES = 6 + 12 + 8


def reduce_layer(link, grads, out, core_in, acc, relay, sums, inbox, last_in, me):
    c, x, z = me.c, me.x, me.z
    a, b = pl.ds(0, 16), pl.ds(16, 16)
    arrive = [link.send(grads.at[1 - c, :, :, part], core_in.at[:, :, part], me.core) for part in (a, b)]
    yield

    def add_core(part):
        def step(xx, carry):
            acc[xx, :, part] = (
                grads[c, xx, :, part].astype(F32) + core_in[xx, :, part].astype(F32)
            ).astype(BF16)
            return carry

        lax.fori_loop(0, 4, step, 0)

    arrive[0].wait_recv()
    add_core(a)
    along_x = collect(
        link, lambda k, half: acc.at[k, pl.ds(2 * half, 2), a], relay.at[0], sums.at[0],
        lambda d, half: inbox.at[0, d, pl.ds(2 * half, 2)], x, me.xs,
    )
    next(along_x)
    arrive[1].wait_recv()
    add_core(b)
    along_z = collect(
        link, lambda k, half: acc.at[pl.ds(2 * half, 2), k, b], relay.at[1], sums.at[1],
        lambda d, half: inbox.at[1, d, pl.ds(2 * half, 2)], z, me.zs,
    )
    next(along_z)
    yield
    next(along_x)
    next(along_z)
    yield
    next(along_x)
    acc[x, :, a] = (
        acc[x, :, a].astype(F32) + inbox[0, 0].astype(F32) + inbox[0, 1].astype(F32)
    ).astype(BF16)
    last_a = [link.send(acc.at[x, (z + o + 1) % 4, a], last_in.at[0, o], me.zs[o]) for o in range(3)]
    next(along_z)
    acc[:, z, b] = (
        acc[:, z, b].astype(F32) + inbox[1, 0].astype(F32) + inbox[1, 1].astype(F32)
    ).astype(BF16)
    last_b = [link.send(acc.at[(x + o + 1) % 4, z, b], last_in.at[1, o], me.xs[o]) for o in range(3)]
    yield
    _, rows_a, rows_b = core_rows(c)
    rows = core_rows(c)[0]
    for k, (copies, at, part) in enumerate(((last_a, rows_a, a), (last_b, rows_b, b))):
        for copy in copies:
            copy.wait_recv()
        out[at, :] = (
            acc[x, z, part].astype(F32)
            + last_in[k, 0].astype(F32) + last_in[k, 1].astype(F32) + last_in[k, 2].astype(F32)
        )
    swap = link.send(out.at[rows], out.at[rows], me.core)
    yield
    swap.wait_recv()
    yield


REDUCE_COPIES = 2 + 12 + 6 + 1


def reduce_scratch():
    return [
        VM((4, 4, 32, WALL), BF16), VM((4, 4, 32, WALL), BF16),
        VM((2, 2, 2, 16, WALL), BF16), VM((2, 2, 2, 16, WALL), BF16),
        VM((2, 2, 4, 16, WALL), BF16), VM((2, 3, 16, WALL), BF16),
    ]


def token_scratch():
    return [VM((2, 64, D), BF16), VM((2, 64, D), BF16), VM((2, ROWS, D), BF16)]


def link_scratch(*counts):
    return [pltpu.SemaphoreType.DMA((n,)) for n in counts for _ in range(2)]


def input_norm(u, gain):
    return u * lax.rsqrt(jnp.mean(u * u, axis=-1, keepdims=True) + EPSILON) * gain


def gain_of(par, layer):
    return par[layer, 0:1, 1408:2432]


def gather_kernel(
    wsh, own_par, act, cot, valid, w0, shard1, par, hid, db,
    shards, own_sem, g_s, g_r, e_s, e_r, h_s, h_r, d_s, d_r,
):
    me = Peers()
    c, t = me.c, me.t
    greet([me.core] + me.xs + me.zs + me.ts)
    early, weights = Link(e_s, e_r), Link(g_s, g_r)
    shards[c] = wsh[core_rows(c)[0], :]
    theirs = early.send(wsh.at[core_rows(1 - c)[0]], shards.at[c], me.core)
    par[c] = own_par[...]
    par_copy = early.send(par.at[c], par.at[c], me.core)
    for j in range(8):
        db[t, :, tile(j)] = (cot[c, :, tile(j)] * valid[...]).astype(BF16)
    theirs.wait_recv()
    layer0 = gather_layer(weights, own_sem.at[0], shards.at[0], w0, me)
    next(layer0)
    par_copy.wait_recv()
    hid[t] = input_norm(act[c], gain_of(par, 0)).astype(BF16)
    tokens, branch = Link(h_s, h_r), Link(d_s, d_r)
    hid_steps = spread_tokens(tokens, hid, me)
    db_steps = spread_tokens(branch, db, me)
    next(hid_steps)
    next(layer0)
    next(db_steps)
    next(layer0)
    next(hid_steps)
    shard1[...] = shards[1]
    next(layer0)
    next(db_steps)
    run(layer0)
    run(hid_steps)
    run(db_steps)
    for link in (early, weights, tokens, branch):
        link.drain()


def gather(wsh, own_par, act, cot, valid):
    return pl.pallas_call(
        gather_kernel,
        out_shape=(
            jax.ShapeDtypeStruct((4, 4, 64, WALL), BF16),
            jax.ShapeDtypeStruct((32, WALL), BF16),
            jax.ShapeDtypeStruct((2, 8, 2432), F32),
            jax.ShapeDtypeStruct((4, ROWS, D), BF16),
            jax.ShapeDtypeStruct((4, ROWS, D), BF16),
        ),
        in_specs=vmem_specs(5),
        out_specs=(pl.BlockSpec(memory_space=pl.ANY),) + tuple(vmem_specs(4)),
        scratch_shapes=[VM((2, 32, WALL), BF16), pltpu.SemaphoreType.DMA((1,))]
        + link_scratch(GATHER_COPIES, 2, 6, 6),
        compiler_params=pltpu.CompilerParams(
            collective_id=0, has_side_effects=True, vmem_limit_bytes=24 << 20
        ),
        name="gather_weights",
    )(wsh, own_par, act, cot, valid)


def column_of(row):
    return jnp.transpose(jnp.broadcast_to(row, (128, 128)))


def middle_kernel(
    part, st, act, valid, par, shard1, total, u_next, s_out, hid, w1,
    relay, sums, inbox, sbuf, own_sem, g_s, g_r, p_s, p_r, b_s, b_r, h_s, h_r,
):
    me = Peers()
    c, t = me.c, me.t
    greet([me.core] + me.xs + me.zs + me.ts)
    weights, tokens, small, spreading = Link(g_s, g_r), Link(p_s, p_r), Link(b_s, b_r), Link(h_s, h_r)
    sum_steps = collect_tokens(tokens, part, relay, sums, inbox, me)
    next(sum_steps)
    stats = [small.send(st.at[(t + o + 1) % 4], sbuf.at[o], me.ts[o]) for o in range(3)]
    layer1 = gather_layer(weights, own_sem.at[0], shard1, w1, me)
    next(layer1)
    next(sum_steps)
    next(layer1)
    for copy in stats:
        copy.wait_recv()
    s_row = lax.rsqrt((st[t] + sbuf[0] + sbuf[1] + sbuf[2]) / DI + EPSILON)
    s_out[...] = s_row
    scale = column_of(s_row[0:1]) * valid[...]
    next(layer1)
    run(sum_steps)
    total[...] = part[t].astype(F32) + inbox[0].astype(F32) + inbox[1].astype(F32)
    for j in range(8):
        u_next[:, tile(j)] = act[c, :, tile(j)] + scale * total[:, tile(j)]
    hid[t] = input_norm(u_next[...], gain_of(par, 1)).astype(BF16)
    hid_steps = spread_tokens(spreading, hid, me)
    next(hid_steps)
    next(layer1)
    next(hid_steps)
    run(layer1)
    run(hid_steps)
    for link in (weights, tokens, small, spreading):
        link.drain()


def middle(part, st, act, valid, par, shard1):
    return pl.pallas_call(
        middle_kernel,
        out_shape=(
            jax.ShapeDtypeStruct((ROWS, D), F32),
            jax.ShapeDtypeStruct((ROWS, D), F32),
            jax.ShapeDtypeStruct((8, 128), F32),
            jax.ShapeDtypeStruct((4, ROWS, D), BF16),
            jax.ShapeDtypeStruct((4, 4, 64, WALL), BF16),
        ),
        in_specs=vmem_specs(6),
        out_specs=tuple(vmem_specs(4)) + (pl.BlockSpec(memory_space=pl.ANY),),
        scratch_shapes=token_scratch()
        + [VM((3, 8, 128), F32), pltpu.SemaphoreType.DMA((1,))]
        + link_scratch(GATHER_COPIES, 6, 3, 6),
        compiler_params=pltpu.CompilerParams(
            collective_id=1, has_side_effects=True, vmem_limit_bytes=24 << 20
        ),
        name="sum_and_gather_tokens",
    )(part, st, act, valid, par, shard1)


def stats_kernel(st, coef, buf, a_s, a_r):
    me = Peers()
    greet(me.ts)
    link = Link(a_s, a_r)
    copies = [link.send(st, buf.at[me.t], peer) for peer in me.ts]
    buf[me.t] = st[...]
    for copy in copies:
        copy.wait_recv()
    for i in range(4):
        both = buf[0, i] + buf[1, i] + buf[2, i] + buf[3, i]
        s = lax.rsqrt(both[0:1] / DI + EPSILON)
        k = s * s * s * (both[1:2] / DI)
        row = iota((8, 128), 0)
        coef[i] = jnp.where(row == 0, s, jnp.where(row == 1, k, 0.0))
    link.drain()


def stats(st):
    return pl.pallas_call(
        stats_kernel,
        out_shape=jax.ShapeDtypeStruct((4, 8, 128), F32),
        in_specs=vmem_specs(1),
        out_specs=pl.BlockSpec(memory_space=VM),
        scratch_shapes=[VM((4, 4, 8, 128), F32)] + link_scratch(3),
        compiler_params=pltpu.CompilerParams(collective_id=2, has_side_effects=True),
        name="sum_stats",
    )(st)


def norm_back(u, gain, g, d_hidden):
    r = lax.rsqrt(jnp.mean(u * u, axis=-1, keepdims=True) + EPSILON)
    mean = jnp.mean(u * gain * d_hidden, axis=-1, keepdims=True)
    d_u = g + r * gain * d_hidden - u * (r * r * r) * mean
    return d_u, jnp.sum(u * r * d_hidden, axis=0, keepdims=True)


def back_middle_kernel(
    dh, u, cot, valid, par, total0, s0, grads, g1, ng, db, coef, w_grad,
    relay, sums, inbox, core_in, acc, g_relay, g_sums, g_inbox, last_in,
    g_s, g_r, p_s, p_r, b_s, b_r, h_s, h_r,
):
    me = Peers()
    c, t = me.c, me.t
    greet([me.core] + me.xs + me.zs + me.ts)
    weights, tokens, small, spreading = Link(g_s, g_r), Link(p_s, p_r), Link(b_s, b_r), Link(h_s, h_r)
    sum_steps = collect_tokens(tokens, dh, relay, sums, inbox, me)
    next(sum_steps)
    layer1 = reduce_layer(
        weights, grads, w_grad, core_in, acc, g_relay, g_sums, g_inbox, last_in, me
    )
    next(layer1)
    next(sum_steps)
    next(layer1)
    run(sum_steps)
    total = dh[t].astype(F32) + inbox[0].astype(F32) + inbox[1].astype(F32)
    d_u, gain_term = norm_back(u[...], gain_of(par, 1), cot[c], total)
    g1[...] = d_u
    ng[...] = gain_term
    mean = jnp.zeros((ROWS, 128), F32)
    for j in range(8):
        d_branch = (g1[:, tile(j)] * valid[...]).astype(BF16)
        db[t, :, tile(j)] = d_branch
        mean = mean + d_branch.astype(F32) * total0[:, tile(j)]
    db_steps = spread_tokens(spreading, db, me)
    next(db_steps)
    mean = jnp.broadcast_to(jnp.sum(mean, axis=-1, keepdims=True), (128, 128))
    mean_row = jnp.transpose(mean)[0:8] / DI
    s = s0[0:1, :]
    row = iota((8, 128), 0)
    coef[t] = jnp.where(row == 0, s, jnp.where(row == 1, s * s * s * mean_row, 0.0))
    coef_copies = [small.send(coef.at[t], coef.at[t], peer) for peer in me.ts]
    next(layer1)
    next(db_steps)
    next(layer1)
    next(db_steps)
    next(layer1)
    run(db_steps)
    run(layer1)
    for copy in coef_copies:
        copy.wait_recv()
    for link in (weights, tokens, small, spreading):
        link.drain()


def back_middle(*arrays):
    return pl.pallas_call(
        back_middle_kernel,
        out_shape=(
            jax.ShapeDtypeStruct((ROWS, D), F32),
            jax.ShapeDtypeStruct((1, D), F32),
            jax.ShapeDtypeStruct((4, ROWS, D), BF16),
            jax.ShapeDtypeStruct((4, 8, 128), F32),
            jax.ShapeDtypeStruct((64, WALL), F32),
        ),
        in_specs=vmem_specs(8),
        out_specs=tuple(vmem_specs(5)),
        scratch_shapes=token_scratch() + reduce_scratch() + link_scratch(REDUCE_COPIES, 6, 3, 6),
        compiler_params=pltpu.CompilerParams(
            collective_id=3, has_side_effects=True, vmem_limit_bytes=40 << 20
        ),
        name="back_sum_and_gather",
    )(*arrays)


def finish_kernel(
    dh, part, act, u1, g1, valid, par, coef1, ng1, sums0, heads0, sums1, heads1, w_grad1, grads,
    lo, lg, o_norm, o_in, o_bc, o_dt, o_cw, o_cb, o_dtb, o_alog, o_skip, o_gain, o_out,
    relay, sums, inbox, relay2, sums2, inbox2, los, lgs, sms, smr, smz, smx, smt, w_grad, picked, bcr,
    core_in, acc, g_relay, g_sums, g_inbox, last_in,
    g_s, g_r, p_s, p_r, q_s, q_r, b_s, b_r,
):
    me = Peers()
    c, x, z, t = me.c, me.x, me.z, me.t
    greet([me.core] + me.xs + me.zs + me.ts)
    weights, tokens, tokens2, small = Link(g_s, g_r), Link(p_s, p_r), Link(q_s, q_r), Link(b_s, b_r)
    layer0 = reduce_layer(
        weights, grads, w_grad, core_in, acc, g_relay, g_sums, g_inbox, last_in, me
    )
    next(layer0)
    back_steps = collect_tokens(tokens, dh, relay, sums, inbox, me)
    next(back_steps)
    out_steps = collect_tokens(tokens2, part, relay2, sums2, inbox2, me)
    next(out_steps)
    los[0] = u1[...]
    lgs[1] = g1[...]
    next(layer0)
    next(back_steps)
    next(out_steps)
    next(layer0)
    run(back_steps)
    total = dh[t].astype(F32) + inbox[0].astype(F32) + inbox[1].astype(F32)
    d_u, gain_term = norm_back(act[c], gain_of(par, 0), g1[...], total)
    lgs[0] = d_u
    lg_copy = small.send(lgs.at[1 - c], lg.at[c], me.core)
    lg[c] = lgs[c]
    sms[...] = jnp.zeros_like(sms)
    for layer, (by_channel, heads, term) in enumerate(
        ((sums0, heads0, gain_term), (sums1, heads1, ng1[...]))
    ):
        sms[layer, 0:8, :] = by_channel[:, 0:512]
        sms[layer, 8:16, 0:256] = by_channel[:, 512:768]
        sms[layer, 8:16, 256:384] = heads[...]
        sms[layer, 16:17, :] = term[:, 0:512]
        sms[layer, 17:18, :] = term[:, 512:1024]
    sm_copy = small.send(sms.at[1 - c], smr, me.core)
    next(layer0)
    sm_copy.wait_recv()
    smz[z] = sms[c] + smr[...]
    sz = [small.send(smz.at[z], smz.at[z], peer) for peer in me.zs]
    run(out_steps)
    los[1] = part[t].astype(F32) + inbox2[0].astype(F32) + inbox2[1].astype(F32)
    scale = column_of(coef1[t][0:1]) * valid[...]
    for j in range(8):
        los[1, :, tile(j)] = u1[:, tile(j)] + scale * los[1, :, tile(j)]
    lo_copy = small.send(los.at[1 - c], lo.at[c], me.core)
    lo[c] = los[c]
    for copy in sz:
        copy.wait_recv()
    smx[x] = smz[0] + smz[1] + smz[2] + smz[3]
    sx = [small.send(smx.at[x], smx.at[x], peer) for peer in me.xs]
    next(layer0)
    for copy in sx:
        copy.wait_recv()
    smt[t] = smx[0] + smx[1] + smx[2] + smx[3]
    to_all = [small.send(smt.at[t], smt.at[t], peer) for peer in me.ts]
    run(layer0)
    picked[...] = jnp.where(c == 0, w_grad[...], w_grad1[...])
    bc = [
        small.send(
            picked.at[pl.ds(pl.multiple_of(16 * ((t + o + 1) % 4), 16), 16), pl.ds(1024, 256)],
            bcr.at[o], me.ts[o],
        )
        for o in range(3)
    ]
    o_in[:, 0, :] = picked[:, 0:512]
    o_in[:, 1, :] = picked[:, 512:1024]
    o_dt[...] = picked[:, 1280:1408][:, 0:HL]
    o_out[...] = jnp.transpose(picked[:, WP:WALL])
    for copy in to_all:
        copy.wait_recv()
    shared = smt[0, 8:24] + smt[1, 8:24] + smt[2, 8:24] + smt[3, 8:24]
    o_norm[:, 0:512] = shared[8:9]
    o_norm[:, 512:1024] = shared[9:10]
    o_cw[:, DI : DI + 2 * N] = shared[0:4, 0:256]
    o_cb[:, DI : DI + 2 * N] = shared[4:5, 0:256]
    for k in range(4):
        at = slice(512 * k, 512 * k + 512)
        o_cw[:, at] = smt[k, 0:4, :]
        o_cb[:, at] = smt[k, 4:5, :]
        o_gain[:, at] = smt[k, 5:6, :]
    heads = smt[0, 8:16, 256:384]
    for k in range(1, 4):
        heads = heads + pltpu.roll(smt[k, 8:16, 256:384], HL * k, 1)
    o_dtb[...] = heads[0:1, 0:H]
    o_alog[...] = heads[1:2, 0:H]
    o_skip[...] = heads[2:3, 0:H]
    for copy in bc:
        copy.wait_recv()
    o_bc[...] = (
        picked[pl.ds(pl.multiple_of(16 * t, 16), 16), 1024:1280] + bcr[0] + bcr[1] + bcr[2]
    )
    lo_copy.wait_recv()
    lg_copy.wait_recv()
    for link in (weights, tokens, tokens2, small):
        link.drain()


def finish(*arrays):
    return pl.pallas_call(
        finish_kernel,
        out_shape=(
            jax.ShapeDtypeStruct((2, ROWS, D), F32),
            jax.ShapeDtypeStruct((2, ROWS, D), F32),
            jax.ShapeDtypeStruct((1, D), F32),
            jax.ShapeDtypeStruct((64, 2, CH), F32),
            jax.ShapeDtypeStruct((16, 2 * N), F32),
            jax.ShapeDtypeStruct((64, HL), F32),
            jax.ShapeDtypeStruct((CONV, DI + 2 * N), F32),
            jax.ShapeDtypeStruct((1, DI + 2 * N), F32),
            jax.ShapeDtypeStruct((1, H), F32),
            jax.ShapeDtypeStruct((1, H), F32),
            jax.ShapeDtypeStruct((1, H), F32),
            jax.ShapeDtypeStruct((1, DI), F32),
            jax.ShapeDtypeStruct((CH, 64), F32),
        ),
        in_specs=vmem_specs(15),
        out_specs=tuple(vmem_specs(13)),
        scratch_shapes=token_scratch() + token_scratch()
        + [
            VM((2, ROWS, D), F32), VM((2, ROWS, D), F32),
            VM((2, 24, 512), F32), VM((24, 512), F32),
            VM((4, 24, 512), F32), VM((4, 24, 512), F32), VM((4, 24, 512), F32),
            VM((64, WALL), F32), VM((64, WALL), F32), VM((3, 16, 256), F32),
        ]
        + reduce_scratch() + link_scratch(REDUCE_COPIES, 6, 6, 15),
        compiler_params=pltpu.CompilerParams(
            collective_id=4, has_side_effects=True, vmem_limit_bytes=48 << 20
        ),
        name="sum_gradients",
    )(*arrays)


def body(
    activations, cotangent, lengths, norm_gain, in_weight, bc_weight, dt_weight, conv_weight,
    conv_bias, dt_bias, a_log, d_skip, gated_gain, out_weight,
):
    section = lax.axis_index("section")
    t = lax.axis_index("tensor")
    lens = lax.dynamic_index_in_dim(lengths[:, 0], section, 0, keepdims=False)
    position = t * ROWS + jnp.arange(ROWS)
    valid = jnp.broadcast_to((position < lens[0] + lens[1]).astype(F32)[:, None], (ROWS, 128))
    wsh = jnp.concatenate(
        [
            in_weight[0].reshape(64, 1024),
            bc_weight[0],
            dt_weight[0],
            jnp.zeros((64, 120), BF16),
            out_weight[0].T,
        ],
        axis=1,
    )

    def own(array, width):
        return lax.dynamic_slice_in_dim(array, t * width, width, array.ndim - 1)

    def rows8(*rows):
        stacked = jnp.concatenate(rows, axis=0)
        return jnp.pad(stacked, ((0, 8 - stacked.shape[0]), (0, 0)))

    taps = rows8(conv_weight[0], conv_bias)
    head_params = jnp.concatenate([own(dt_bias, HL), -jnp.exp(own(a_log, HL))], axis=0).T
    par_own = jnp.concatenate(
        [
            own(taps[:, :DI], CH),
            taps[:, DI:],
            jnp.pad(head_params, ((0, 0), (0, 126))),
            rows8(own(gated_gain, CH), jnp.repeat(own(d_skip, HL), 64, axis=1)),
            rows8(norm_gain),
        ],
        axis=1,
    )
    w0, shard1, par, hid0, db1 = gather(wsh, par_own, activations, cotangent, valid)
    proj0, part0, y0, st0 = mixer_fwd(0, lens, par, hid0, w0)
    total0, u1, s0, hid1, w1 = middle(part0, st0, activations, valid, par, shard1)
    proj1, part1, y1, st1, d_scaled1 = mixer_fwd(1, lens, par, hid1, w1, db1)
    coef1 = stats(st1)
    dh1, grads1, sums1, heads1 = mixer_bwd(1, lens, par, hid1, w1, db1, proj1, y1, coef1, d_scaled1)
    g1, ng1, db0, coef0, w_grad1 = back_middle(dh1, u1, cotangent, valid, par, total0, s0, grads1)
    dh0, grads0, sums0, heads0 = mixer_bwd(0, lens, par, hid0, w0, db0, proj0, y0, coef0)
    outs = finish(
        dh0, part1, activations, u1, g1, valid, par, coef1, ng1,
        sums0, heads0, sums1, heads1, w_grad1, grads0,
    )
    plain = (2, 8, 9, 10, 7, 11)
    return tuple(out if k in plain else out[None] for k, out in enumerate(outs))


def solution(mesh):
    return jax.shard_map(
        body,
        mesh=mesh,
        in_specs=(
            P(None, ("dp", "tensor"), None),
            P(None, ("dp", "tensor"), None),
            P(None, "dp", None),
            P("section", None),
            P("section", "dp", None, "tensor"),
            P("section", "dp", None),
            P("section", "dp", "tensor"),
            P("section", None, None),
            P("section", None),
            P("section", None),
            P("section", None),
            P("section", None),
            P("section", None),
            P("section", "tensor", "dp"),
        ),
        out_specs=(
            P("section", None, ("dp", "tensor"), None),
            P("section", None, ("dp", "tensor"), None),
            P("section", None),
            P("section", "dp", None, "tensor"),
            P("section", ("dp", "tensor"), None),
            P("section", "dp", "tensor"),
            P("section", None, None),
            P("section", None),
            P("section", None),
            P("section", None),
            P("section", None),
            P("section", None),
            P("section", "tensor", "dp"),
        ),
        check_vma=False,
    )
```

```python
import functools

import jax
import jax.numpy as jnp
from jax import lax
from jax.experimental import pallas as pl
from jax.experimental.pallas import tpu as pltpu
from jax.sharding import PartitionSpec as P

D = 1024
DI = 2048
H = 32
N = 128
CONV = 4
T = 512
ROWS = 128
CH = 512
HL = 8
WZX = 1024
WP = 1408
WALL = 1920
NDP = 16
EPSILON = 1e-05
LOG2E = 1.4426950408889634
NEG = -1e30
F32 = jnp.float32
BF16 = jnp.bfloat16
MESH = pl.DeviceIdType.MESH
VM = pltpu.VMEM
FWD_VMEM = 12 << 20
BWD_VMEM = 16 << 20


def dot_nn(a, b):
    return lax.dot_general(a, b, (((1,), (0,)), ((), ())), preferred_element_type=F32)


def dot_nt(a, b):
    return lax.dot_general(a, b, (((1,), (1,)), ((), ())), preferred_element_type=F32)


def dot_tn(a, b):
    return lax.dot_general(a, b, (((0,), (0,)), ((), ())), preferred_element_type=F32)


def pieces(v, count):
    parts = []
    for _ in range(count):
        part = v.astype(BF16)
        parts.append(part)
        v = v - part.astype(F32)
    return parts


def sum_rows_nt(selector, v, count):
    return sum(dot_nt(selector, part) for part in pieces(v, count))


def rows_times(v, matrix):
    a, b, c = pieces(v, 3)
    stacked = jnp.concatenate([a.astype(F32), b.astype(F32), c.astype(F32), jnp.zeros_like(v)], 0)
    out = dot_nn(stacked.astype(BF16), matrix)
    return out[0:8] + out[8:16] + out[16:24]


def iota(shape, dim):
    return lax.broadcasted_iota(jnp.int32, shape, dim)


def segment_of(position, e0, e1):
    return (position >= e0).astype(jnp.int32) + (position >= e1).astype(jnp.int32)


def conv_masks(e0, e1):
    p = iota((T, 128), 0)
    seg = segment_of(p, e0, e1)
    return [
        jnp.where((p >= k) & (segment_of(p - k, e0, e1) == seg), 1.0, 0.0).astype(F32)
        for k in range(1, CONV)
    ]


def conv_pre(v, masks, cw, lanes):
    pre = cw[CONV : CONV + 1, lanes] + cw[CONV - 1 : CONV, lanes] * v
    for k in range(1, CONV):
        pre = pre + cw[CONV - 1 - k : CONV - k, lanes] * (masks[k - 1] * pltpu.roll(v, k, 0))
    return pre


def sigmoid(v):
    return 0.5 * jnp.tanh(0.5 * v) + 0.5


def steps_of(dt_tile, hp_ref):
    raw = jnp.transpose(dt_tile)[0:HL] + hp_ref[:, 0:1]
    step = jnp.maximum(raw, 0.0) + jnp.log1p(jnp.exp(-jnp.abs(raw)))
    rate = hp_ref[:, 1:2]
    upper = jnp.where(iota((T, T), 0) <= iota((T, T), 1), 1.0, 0.0).astype(BF16)
    cum = rows_times(step * rate, upper) * LOG2E
    columns = jnp.transpose(
        jnp.concatenate([cum, step, jnp.zeros((112, T), F32)], axis=0)
    )
    return raw, step, cum, columns


def pair_columns(columns, first, j, rows=T):
    low = iota((rows, 128), 1) < 64
    return jnp.where(
        low,
        jnp.broadcast_to(columns[:, first + 2 * j : first + 2 * j + 1], (rows, 128)),
        jnp.broadcast_to(columns[:, first + 2 * j + 1 : first + 2 * j + 2], (rows, 128)),
    )


def tile(j):
    return slice(128 * j, 128 * j + 128)


def layer_params(par, layer):
    return (
        par.at[layer, :, pl.ds(0, 768)],
        par.at[layer, :, pl.ds(768, 128)],
        par.at[layer, :, pl.ds(896, 512)],
    )


def skip_row(hp, j):
    low = iota((1, 128), 1) < 64
    first = jnp.broadcast_to(hp[2 * j : 2 * j + 1, 2:3], (1, 128))
    second = jnp.broadcast_to(hp[2 * j + 1 : 2 * j + 2, 2:3], (1, 128))
    return jnp.where(low, first, second)


def segment_ends(lengths):
    c = lax.axis_index("section")
    first = lengths[c, 0, 0]
    return first, first + lengths[c, 0, 1]


def project(hid, w, proj):
    tokens = hid[...].reshape(T, D)
    for first, width in ((0, 512), (512, 512), (1024, 384)):
        at = slice(first, first + width)
        proj[:, at] = dot_nn(tokens, w[:, :, :, at].reshape(D, width))


def scale_back(db, w, d_scaled):
    d_scaled[...] = dot_nn(db[...].reshape(T, D), w[:, :, :, WP:WALL].reshape(D, CH))


def mixer_fwd_kernel(layer, lens, par, hid, w, *rest):
    with_grad = layer == 1
    if with_grad:
        db, proj, kept, part, yssd, st, d_scaled, gg, inn, xb, bb, cb, cumr, colr = rest
        scale_back(db, w, d_scaled)
    else:
        proj, kept, part, yssd, st, gg, inn, xb, bb, cb, cumr, colr = rest
    cw, hp, rows = layer_params(par, layer)
    project(hid, w, proj)
    e0, e1 = segment_ends(lens)
    masks = conv_masks(e0, e1)
    _, _, cum, columns = steps_of(proj[:, 1280:1408], hp)
    cumr[...] = cum
    colr[...] = columns
    for j in range(4):
        v = proj[:, 512 + 128 * j : 640 + 128 * j]
        pre = conv_pre(v, masks, cw, tile(j))
        kept[:, tile(j)] = pre
        act = pre * sigmoid(pre)
        inn[:, tile(j)] = act
        xb[:, tile(j)] = (act * pair_columns(columns, HL, j)).astype(BF16)
    for j, ref in ((0, bb), (1, cb)):
        lanes = slice(512 + 128 * j, 640 + 128 * j)
        pre = conv_pre(proj[:, 1024 + 128 * j : 1152 + 128 * j], masks, cw, lanes)
        kept[:, lanes] = pre
        ref[...] = (pre * sigmoid(pre)).astype(BF16)
    low = iota((128, 128), 1) < 64
    for i in range(4):
        n = 128 * (i + 1)
        here = slice(128 * i, n)
        scores = dot_nt(cb[here, :], bb[0:n, :])
        p = iota((128, n), 0) + 128 * i
        q = iota((128, n), 1)
        bias = jnp.where((p >= q) & (segment_of(p, e0, e1) == segment_of(q, e0, e1)), 0.0, NEG).astype(F32)
        for j in range(4):
            halves = []
            for h in (2 * j, 2 * j + 1):
                decay = jnp.exp2(colr[here, h : h + 1] - cumr[h : h + 1, 0:n] + bias)
                halves.append(dot_nn((scores * decay).astype(BF16), xb[0:n, tile(j)]))
            yssd[here, tile(j)] = jnp.where(low, halves[0], halves[1])
    squares = jnp.zeros((8, T), F32)
    dots = jnp.zeros((8, T), F32)
    ones = jnp.ones((8, 128), BF16)
    for j in range(4):
        z = proj[:, tile(j)]
        gated = (yssd[:, tile(j)] + skip_row(hp, j) * inn[:, tile(j)]) * (z * sigmoid(z))
        gained = gated * rows[0:1, tile(j)]
        gg[:, tile(j)] = gained.astype(BF16)
        squares = squares + sum_rows_nt(ones, gated * gated, 1)
        if with_grad:
            dots = dots + sum_rows_nt(ones, gained * d_scaled[:, tile(j)], 2)
    row = iota((8, T), 0)
    both = jnp.where(row == 0, squares, jnp.where(row == 1, dots, 0.0))
    for i in range(4):
        st[i] = both[:, tile(i)]
    for x in range(4):
        columns_out = slice(256 * x, 256 * x + 256)
        branch = dot_nt(gg[...], w[x, :, :, WP:WALL].reshape(256, CH)).astype(BF16)
        part[:, :, columns_out] = branch.reshape(4, ROWS, 256)


def vmem_specs(count):
    return [pl.BlockSpec(memory_space=VM)] * count


def mixer_fwd(layer, lens, par, hid, w, *db):
    out_shape = [
        jax.ShapeDtypeStruct((T, WP), F32),
        jax.ShapeDtypeStruct((T, 768), F32),
        jax.ShapeDtypeStruct((4, ROWS, D), BF16),
        jax.ShapeDtypeStruct((T, CH), F32),
        jax.ShapeDtypeStruct((4, 8, 128), F32),
    ] + [jax.ShapeDtypeStruct((T, CH), F32)] * layer
    return pl.pallas_call(
        functools.partial(mixer_fwd_kernel, layer),
        out_shape=tuple(out_shape),
        in_specs=[pl.BlockSpec(memory_space=pltpu.SMEM)] + vmem_specs(3 + len(db)),
        out_specs=tuple(vmem_specs(len(out_shape))),
        scratch_shapes=[
            VM((T, CH), BF16),
            VM((T, CH), F32),
            VM((T, CH), BF16),
            VM((T, N), BF16),
            VM((T, N), BF16),
            VM((8, T), F32),
            VM((T, 128), F32),
        ],
        compiler_params=pltpu.CompilerParams(vmem_limit_bytes=FWD_VMEM),
        name="mixer_fwd",
    )(lens, par, hid, w, *db)


def head_selector(j):
    head = 2 * j + (iota((8, 128), 1) >= 64).astype(jnp.int32)
    return jnp.where(iota((8, 128), 0) == head, 1.0, 0.0).astype(BF16)


def back_roll(v, k):
    return pltpu.roll(v, T - k, 0)


def conv_back(d_pre, v, masks, cw, lanes, sums, column0):
    d_v = cw[CONV - 1 : CONV, lanes] * d_pre
    out = slice(column0, column0 + 128)
    sums[CONV : CONV + 1, out] = jnp.sum(d_pre, axis=0, keepdims=True)
    sums[CONV - 1 : CONV, out] = jnp.sum(d_pre * v, axis=0, keepdims=True)
    for k in range(1, CONV):
        masked = masks[k - 1] * d_pre
        d_v = d_v + cw[CONV - 1 - k : CONV - k, lanes] * back_roll(masked, k)
        sums[CONV - 1 - k : CONV - k, out] = jnp.sum(masked * pltpu.roll(v, k, 0), axis=0, keepdims=True)
    return d_v


def mixer_bwd_kernel(layer, lens, par, w, proj, kept, yssd, coef, *rest):
    given, *rest = rest
    dh, d_proj, scaled, sums, heads, inn, xb, dyb, dyf, dx, bb, cb, d_c, cumr, colr, *rest = rest
    if layer == 1:
        d_scaled = given
    else:
        db, d_scaled = given, rest[0]
        scale_back(db, w, d_scaled)
    cw, hp, rows = layer_params(par, layer)
    e0, e1 = segment_ends(lens)
    masks = conv_masks(e0, e1)
    raw, step, cum, columns = steps_of(proj[:, 1280:1408], hp)
    cumr[...] = cum
    colr[...] = columns
    norm_cols = jnp.transpose(jnp.concatenate(
        [jnp.concatenate([coef[i] for i in range(4)], axis=1), jnp.zeros((120, T), F32)], axis=0
    ))
    s_col = jnp.broadcast_to(norm_cols[:, 0:1], (T, 128))
    k_col = jnp.broadcast_to(norm_cols[:, 1:2], (T, 128))
    sums[...] = jnp.zeros_like(sums)
    d_skip = jnp.zeros((8, T), F32)
    for j in range(4):
        selector = head_selector(j)
        pre = kept[:, tile(j)]
        act = pre * sigmoid(pre)
        inn[:, tile(j)] = act
        xb[:, tile(j)] = (act * pair_columns(columns, HL, j)).astype(BF16)
        z = proj[:, tile(j)]
        sig = sigmoid(z)
        gate = z * sig
        y = yssd[:, tile(j)] + skip_row(hp, j) * act
        gated = y * gate
        gs = gated * s_col
        gain = rows[0:1, tile(j)]
        dsc = d_scaled[:, tile(j)]
        scaled[:, tile(j)] = (gs * gain).astype(BF16)
        sums[5:6, tile(j)] = jnp.sum(gs * dsc, axis=0, keepdims=True)
        d_gated = s_col * gain * dsc - gated * k_col
        d_proj[:, tile(j)] = (d_gated * y * (sig * (1.0 + z * (1.0 - sig)))).astype(BF16)
        dy = d_gated * gate
        dyf[:, tile(j)] = dy
        dyb[:, tile(j)] = dy.astype(BF16)
        d_skip = d_skip + sum_rows_nt(selector, dy * act, 2)
    for j, ref in ((0, bb), (1, cb)):
        pre = kept[:, 512 + 128 * j : 640 + 128 * j]
        ref[...] = (pre * sigmoid(pre)).astype(BF16)
    d_c[...] = jnp.zeros_like(d_c)
    low = iota((128, 128), 1) < 64
    zero = jnp.zeros((128, 128), BF16)
    d_b_blocks = []
    for i in range(4):
        first = 128 * i
        n = T - first
        here = slice(first, first + 128)
        scores = dot_nt(bb[here, :], cb[first:T, :])
        q = iota((128, n), 0) + first
        p = iota((128, n), 1) + first
        bias = jnp.where((p >= q) & (segment_of(p, e0, e1) == segment_of(q, e0, e1)), 0.0, NEG).astype(F32)
        d_scores = jnp.zeros((128, n), F32)
        for j in range(4):
            x_tile = xb[here, tile(j)]
            dy_tile = dyb[first:T, tile(j)]
            halves = []
            for h in (2 * j, 2 * j + 1):
                decay = jnp.exp2(cumr[h : h + 1, first:T] - colr[here, h : h + 1] + bias)
                halves.append(dot_nn((scores * decay).astype(BF16), dy_tile))
                x_head = jnp.where(low if h % 2 == 0 else jnp.logical_not(low), x_tile, zero)
                d_scores = d_scores + dot_nt(x_head, dy_tile) * decay
            dx[here, tile(j)] = jnp.where(low, halves[0], halves[1])
        d_scores = d_scores.astype(BF16)
        d_b_blocks.append(dot_nn(d_scores, cb[first:T, :]))
        d_c[first:T, :] = d_c[first:T, :] + dot_tn(d_scores, bb[here, :])
    d_cum = jnp.zeros((8, T), F32)
    d_step = jnp.zeros((8, T), F32)
    for j in range(4):
        selector = head_selector(j)
        dxt = dx[:, tile(j)]
        act = inn[:, tile(j)]
        change = dyb[:, tile(j)].astype(F32) * yssd[:, tile(j)] - xb[:, tile(j)].astype(F32) * dxt
        d_cum = d_cum + sum_rows_nt(selector, change, 3)
        d_step = d_step + sum_rows_nt(selector, act * dxt, 2)
        d_act = pair_columns(columns, HL, j) * dxt + skip_row(hp, j) * dyf[:, tile(j)]
        v = proj[:, 512 + 128 * j : 640 + 128 * j]
        pre = kept[:, tile(j)]
        sig = sigmoid(pre)
        d_pre = d_act * (sig * (1.0 + pre * (1.0 - sig)))
        d_proj[:, 512 + 128 * j : 640 + 128 * j] = conv_back(d_pre, v, masks, cw, tile(j), sums, 128 * j).astype(BF16)
    for j in (0, 1):
        lanes = slice(512 + 128 * j, 640 + 128 * j)
        at = slice(1024 + 128 * j, 1152 + 128 * j)
        v = proj[:, at]
        pre = kept[:, lanes]
        sig = sigmoid(pre)
        d_act = jnp.concatenate(d_b_blocks, axis=0) if j == 0 else d_c[...]
        d_pre = d_act * (sig * (1.0 + pre * (1.0 - sig)))
        d_proj[:, at] = conv_back(d_pre, v, masks, cw, lanes, sums, 512 + 128 * j).astype(BF16)
    lower = jnp.where(iota((T, T), 0) >= iota((T, T), 1), 1.0, 0.0).astype(BF16)
    d_a = rows_times(d_cum, lower)
    rate = hp[:, 1:2]
    d_raw = (d_step + rate * d_a) * sigmoid(raw)
    d_proj[:, 1280:1408] = jnp.transpose(
        jnp.concatenate([d_raw, jnp.zeros((120, T), F32)], axis=0)
    ).astype(BF16)
    bias_grad = jnp.broadcast_to(jnp.sum(d_raw, axis=1, keepdims=True), (8, 128))
    rate_grad = jnp.broadcast_to(jnp.sum(d_a * step, axis=1, keepdims=True) * rate, (8, 128))
    skip_grad = jnp.broadcast_to(jnp.sum(d_skip, axis=1, keepdims=True), (8, 128))
    lane = iota((8, 128), 1)
    by_head = jnp.where(
        lane == 0, bias_grad, jnp.where(lane == 1, rate_grad, jnp.where(lane == 2, skip_grad, 0.0))
    )
    heads[...] = jnp.transpose(jnp.concatenate([by_head, jnp.zeros((120, 128), F32)], axis=0))[0:8]
    for x in range(4):
        back = dot_nt(d_proj[...], w[x, :, :, 0:WP].reshape(256, WP)).astype(BF16)
        dh[:, :, 256 * x : 256 * x + 256] = back.reshape(4, ROWS, 256)


def mixer_bwd(layer, lens, par, w, proj, kept, yssd, coef, given):
    return pl.pallas_call(
        functools.partial(mixer_bwd_kernel, layer),
        out_shape=(
            jax.ShapeDtypeStruct((4, ROWS, D), BF16),
            jax.ShapeDtypeStruct((T, WP), BF16),
            jax.ShapeDtypeStruct((T, CH), BF16),
            jax.ShapeDtypeStruct((8, 768), F32),
            jax.ShapeDtypeStruct((8, 128), F32),
        ),
        in_specs=[pl.BlockSpec(memory_space=pltpu.SMEM)] + vmem_specs(7),
        out_specs=tuple(vmem_specs(5)),
        scratch_shapes=[
            VM((T, CH), F32),
            VM((T, CH), BF16),
            VM((T, CH), BF16),
            VM((T, CH), F32),
            VM((T, CH), F32),
            VM((T, N), BF16),
            VM((T, N), BF16),
            VM((T, N), F32),
            VM((8, T), F32),
            VM((T, 128), F32),
        ] + [VM((T, CH), F32)] * (1 - layer),
        compiler_params=pltpu.CompilerParams(vmem_limit_bytes=BWD_VMEM),
        name="mixer_bwd",
    )(lens, par, w, proj, kept, yssd, coef, given)


def places():
    section = lax.axis_index("section")
    dp = lax.axis_index("dp")
    return section, dp // 4, dp % 4, lax.axis_index("tensor")


class Peers:
    def __init__(self):
        self.c, self.x, self.z, self.t = places()
        self.core = {"section": 1 - self.c}
        self.xs = [{"dp": ((self.x + o) % 4) * 4 + self.z} for o in (1, 2, 3)]
        self.zs = [{"dp": self.x * 4 + (self.z + o) % 4} for o in (1, 2, 3)]
        self.ts = [{"tensor": (self.t + o) % 4} for o in (1, 2, 3)]
        self.far_ts = [{"section": 1 - self.c, "tensor": (self.t + o) % 4} for o in (1, 2, 3)]

    def near_dp(self):
        return [self.core] + self.xs + self.zs + self.ts

    def everyone(self):
        return [self.core] + self.xs + self.zs + self.ts + self.far_ts


def barrier_start(peers):
    barrier = pltpu.get_barrier_semaphore()
    for peer in peers:
        pl.semaphore_signal(barrier, inc=1, device_id=peer, device_id_type=MESH)


def barrier_end(peers):
    pl.semaphore_wait(pltpu.get_barrier_semaphore(), len(peers))


def greet(peers):
    barrier_start(peers)
    barrier_end(peers)


class Link:
    def __init__(self, send_sems, recv_sems):
        self.send_sems, self.recv_sems, self.sent = send_sems, recv_sems, []

    def send(self, src, dst, peer):
        k = len(self.sent)
        copy = pltpu.make_async_remote_copy(
            src_ref=src, dst_ref=dst, send_sem=self.send_sems.at[k], recv_sem=self.recv_sems.at[k],
            device_id=peer, device_id_type=MESH,
        )
        copy.start()
        self.sent.append(copy)
        return copy

    def drain(self):
        for copy in self.sent:
            copy.wait_send()


def spread(link, block, r, peers):
    plus, minus = peers[0], peers[2]

    def go(k, half, peer):
        return link.send(block(k, half), block(k, half), peer)

    from_left = [go(r, 0, plus)]
    from_right = [go(r, 1, minus)]
    from_left.append(go(r, 1, plus))
    from_right.append(go(r, 0, minus))
    yield
    from_left[0].wait_recv()
    far = [go((r + 3) % 4, 0, plus)]
    from_right[0].wait_recv()
    far.append(go((r + 1) % 4, 1, minus))
    yield
    for copy in (from_left[1], from_right[1]):
        copy.wait_recv()
    yield
    for copy in far:
        copy.wait_recv()
    yield


def collect(link, part, relay, sums, inbox, r, peers):
    plus, minus = peers[0], peers[2]
    left, right, far = (r + 3) % 4, (r + 1) % 4, (r + 2) % 4
    up = link.send(part(far, 0), relay.at[0], plus)
    down = link.send(part(far, 1), relay.at[1], minus)
    last = [
        link.send(part(right, 1), inbox(0, 1), plus),
        link.send(part(left, 0), inbox(1, 0), minus),
    ]
    yield
    up.wait_recv()
    sums[0] = (part(right, 0)[...].astype(F32) + relay[0].astype(F32)).astype(BF16)
    last.append(link.send(sums.at[0], inbox(0, 0), plus))
    down.wait_recv()
    sums[1] = (part(left, 1)[...].astype(F32) + relay[1].astype(F32)).astype(BF16)
    last.append(link.send(sums.at[1], inbox(1, 1), minus))
    yield
    for copy in last:
        copy.wait_recv()
    yield


def run(steps):
    for _ in steps:
        pass


def token_halves(ref):
    return lambda k, half: ref.at[k, pl.ds(64 * half, 64)]


def collect_tokens(link, ref, relay, sums, inbox, me):
    return collect(link, token_halves(ref), relay, sums, token_halves(inbox), me.t, me.ts)


def spread_tokens(link, ref, me):
    return spread(link, token_halves(ref), me.t, me.ts)


def core_rows(c):
    first = pl.multiple_of(32 * c, 32)
    return pl.ds(first, 32), pl.ds(first, 16), pl.ds(pl.multiple_of(32 * c + 16, 16), 16)


def gather_layer(link, own_sem, shard, w, me):
    c, x, z = me.c, me.x, me.z
    whole, a, b = core_rows(c)
    own = pltpu.make_async_copy(shard, w.at[x, z, whole], own_sem)
    own.start()
    first = []
    for o in range(3):
        first.append(link.send(shard.at[pl.ds(0, 16)], w.at[x, z, a], me.zs[o]))
        first.append(link.send(shard.at[pl.ds(16, 16)], w.at[x, z, b], me.xs[o]))
    yield
    own.wait()
    for copy in first:
        copy.wait_recv()
    along_x = spread(link, lambda k, half: w.at[k, pl.ds(2 * half, 2), a], x, me.xs)
    along_z = spread(link, lambda k, half: w.at[pl.ds(2 * half, 2), k, b], z, me.zs)
    next(along_x)
    next(along_z)
    core = []

    def to_core(o):
        block_a = w.at[(x + o) % 4, :, a]
        block_b = w.at[:, (z + o) % 4, b]
        core.append(link.send(block_a, block_a, me.core))
        core.append(link.send(block_b, block_b, me.core))

    to_core(0)
    yield
    next(along_x)
    next(along_z)
    yield
    next(along_x)
    next(along_z)
    to_core(1)
    to_core(3)
    yield
    next(along_x)
    next(along_z)
    to_core(2)
    yield
    for copy in core:
        copy.wait_recv()
    yield


GATHER_COPIES = 6 + 12 + 8


def reduce_layer(link, factors, grads, out, bc_all, core_in, acc, relay, sums, inbox, last_in, me):
    c, x, z = me.c, me.x, me.z
    hid, d_proj, db, scaled = factors
    a, b = pl.ds(0, 16), pl.ds(16, 16)
    arrive = []
    for xx in range(4):
        for half in range(2):
            at = slice(256 * xx + 128 * half, 256 * xx + 128 * half + 128)
            rows_in = dot_tn(hid[:, :, at].reshape(T, 128), d_proj[...]).astype(BF16)
            rows_out = dot_tn(db[:, :, at].reshape(T, 128), scaled[...]).astype(BF16)
            for k in range(4):
                block = slice(32 * k, 32 * k + 32)
                grads[k % 2, xx, 2 * half + k // 2, :, 0:WP] = rows_in[block]
                grads[k % 2, xx, 2 * half + k // 2, :, WP:WALL] = rows_out[block]
        arrive.append(link.send(grads.at[1 - c, xx], core_in.at[xx], me.core))
        if xx % 2 == 1:
            yield
    for xx in range(4):
        arrive[xx].wait_recv()
        acc[xx] = (grads[c, xx].astype(F32) + core_in[xx].astype(F32)).astype(BF16)
    along_x = collect(
        link, lambda k, half: acc.at[k, pl.ds(2 * half, 2), a], relay.at[0], sums.at[0],
        lambda d, half: inbox.at[0, d, pl.ds(2 * half, 2)], x, me.xs,
    )
    next(along_x)
    along_z = collect(
        link, lambda k, half: acc.at[pl.ds(2 * half, 2), k, b], relay.at[1], sums.at[1],
        lambda d, half: inbox.at[1, d, pl.ds(2 * half, 2)], z, me.zs,
    )
    next(along_z)
    yield
    next(along_x)
    next(along_z)
    yield
    next(along_x)
    acc[x, :, a] = (
        acc[x, :, a].astype(F32) + inbox[0, 0].astype(F32) + inbox[0, 1].astype(F32)
    ).astype(BF16)
    last_a = [link.send(acc.at[x, (z + o + 1) % 4, a], last_in.at[0, o], me.zs[o]) for o in range(3)]
    next(along_z)
    acc[:, z, b] = (
        acc[:, z, b].astype(F32) + inbox[1, 0].astype(F32) + inbox[1, 1].astype(F32)
    ).astype(BF16)
    last_b = [link.send(acc.at[(x + o + 1) % 4, z, b], last_in.at[1, o], me.xs[o]) for o in range(3)]
    yield
    _, rows_a, rows_b = core_rows(c)
    rows = core_rows(c)[0]
    for k, (copies, at, part) in enumerate(((last_a, rows_a, a), (last_b, rows_b, b))):
        for copy in copies:
            copy.wait_recv()
        out[at, :] = (
            acc[x, z, part].astype(F32)
            + last_in[k, 0].astype(F32) + last_in[k, 1].astype(F32) + last_in[k, 2].astype(F32)
        )
    bc_all[me.t, rows, :] = out[rows, 1024:1280]
    swap = [link.send(out.at[rows], out.at[rows], me.core)]
    for peer in [me.core] + me.ts + me.far_ts:
        mine = bc_all.at[me.t, rows]
        swap.append(link.send(mine, mine, peer))
    yield
    for copy in swap:
        copy.wait_recv()
    yield


REDUCE_COPIES = 4 + 12 + 6 + 8


def reduce_scratch():
    return [
        VM((2, 4, 4, 32, WALL), BF16),
        VM((4, 4, 32, WALL), BF16), VM((4, 4, 32, WALL), BF16),
        VM((2, 2, 2, 16, WALL), BF16), VM((2, 2, 2, 16, WALL), BF16),
        VM((2, 2, 4, 16, WALL), BF16), VM((2, 3, 16, WALL), BF16),
    ]


def token_scratch():
    return [VM((2, 64, D), BF16), VM((2, 64, D), BF16), VM((2, ROWS, D), BF16)]


def dma_sems(n):
    return pltpu.SemaphoreType.DMA((n,))


def link_scratch(*counts):
    return [pltpu.SemaphoreType.DMA((n,)) for n in counts for _ in range(2)]


def input_norm(u, gain):
    return u * lax.rsqrt(jnp.mean(u * u, axis=-1, keepdims=True) + EPSILON) * gain


def gain_of(par, layer):
    return par[layer, 0:1, 1408:2432]


def gather_kernel(
    lengths, w_in, *rest,
):
    in_hbm, (act, cot), rest = rest[:10], rest[10:12], rest[12:]
    (w0, shard1, par, hid, db, u0, cot_own, valid), rest = rest[:8], rest[8:]
    near, rest = rest[:10], rest[10:]
    wsh, shards, turned, own_sem, act_sem, g_s, g_r, e_s, e_r, h_s, h_r, d_s, d_r = rest
    w_bc, w_dt, w_out, conv_w, conv_b, dt_bias, a_log, d_skip, gated, norm = near
    me = Peers()
    c, t = me.c, me.t
    fetch = [
        pltpu.make_async_copy(act.at[c], u0, act_sem.at[0]),
        pltpu.make_async_copy(cot.at[c], cot_own, act_sem.at[1]),
    ]
    loads = [
        pltpu.make_async_copy(src, dst, act_sem.at[2 + k])
        for k, (src, dst) in enumerate(zip(in_hbm, near))
    ]
    for copy in loads + fetch:
        copy.start()
    barrier_start(me.near_dp())
    wsh[:, 0:WZX] = w_in[...]
    for copy in loads:
        copy.wait()
    wsh[:, 1024:1280] = w_bc[...]
    dt_rows = jnp.concatenate([w_dt[...].astype(F32), jnp.zeros((HL, 64), F32)], axis=1)
    dt_rows = jnp.concatenate([dt_rows, jnp.zeros((120, 128), F32)], axis=0)
    wsh[:, 1280:1408] = jnp.transpose(dt_rows)[0:64].astype(BF16)
    wsh[:, WP:WALL] = w_out[...]
    shards[c] = wsh[core_rows(c)[0], :]
    own = pl.ds(pl.multiple_of(CH * t, CH), CH)
    par[c] = jnp.zeros((8, 2432), F32)
    par[c, 0:4, 0:512] = conv_w[:, own]
    par[c, 0:4, 512:768] = conv_w[:, DI : DI + 2 * N]
    par[c, 4:5, 0:512] = conv_b[:, own]
    par[c, 4:5, 512:768] = conv_b[:, DI : DI + 2 * N]
    heads = jnp.concatenate([dt_bias[...], a_log[...], d_skip[...], jnp.zeros((5, H), F32)], axis=0)
    heads = jnp.concatenate([heads, jnp.zeros((8, 128 - H), F32)], axis=1)
    turned[...] = jnp.transpose(jnp.concatenate([heads, jnp.zeros((120, 128), F32)], axis=0))
    heads = turned[pl.ds(pl.multiple_of(HL * t, HL), HL), :]
    par[c, :, 768:896] = jnp.where(iota((8, 128), 1) == 1, -jnp.exp(heads), heads)
    par[c, 0:1, 896:1408] = gated[:, own]
    par[c, 0:1, 1408:2432] = norm[...]
    end = lengths[c, 0, 0] + lengths[c, 0, 1]
    valid[...] = jnp.where(iota((ROWS, 128), 0) + ROWS * t < end, 1.0, 0.0).astype(F32)
    barrier_end(me.near_dp())
    early, weights = Link(e_s, e_r), Link(g_s, g_r)
    theirs = early.send(wsh.at[core_rows(1 - c)[0]], shards.at[c], me.core)
    par_copy = early.send(par.at[c], par.at[c], me.core)
    fetch[1].wait()
    for j in range(8):
        db[t, :, tile(j)] = (cot_own[:, tile(j)] * valid[...]).astype(BF16)
    theirs.wait_recv()
    layer0 = gather_layer(weights, own_sem.at[0], shards.at[0], w0, me)
    next(layer0)
    par_copy.wait_recv()
    fetch[0].wait()
    hid[t] = input_norm(u0[...], gain_of(par, 0)).astype(BF16)
    tokens, branch = Link(h_s, h_r), Link(d_s, d_r)
    hid_steps = spread_tokens(tokens, hid, me)
    db_steps = spread_tokens(branch, db, me)
    next(hid_steps)
    next(layer0)
    next(db_steps)
    next(layer0)
    next(hid_steps)
    shard1[...] = shards[1]
    next(layer0)
    next(db_steps)
    run(layer0)
    run(hid_steps)
    run(db_steps)
    for link in (early, weights, tokens, branch):
        link.drain()


def gather(*arrays):
    hbm_spec = pl.BlockSpec(memory_space=pltpu.HBM)
    near = [VM(array.shape, array.dtype) for array in arrays[2:12]]
    return pl.pallas_call(
        gather_kernel,
        out_shape=(
            jax.ShapeDtypeStruct((4, 4, 64, WALL), BF16),
            jax.ShapeDtypeStruct((32, WALL), BF16),
            jax.ShapeDtypeStruct((2, 8, 2432), F32),
            jax.ShapeDtypeStruct((4, ROWS, D), BF16),
            jax.ShapeDtypeStruct((4, ROWS, D), BF16),
            jax.ShapeDtypeStruct((ROWS, D), F32),
            jax.ShapeDtypeStruct((ROWS, D), F32),
            jax.ShapeDtypeStruct((ROWS, 128), F32),
        ),
        in_specs=[pl.BlockSpec(memory_space=pltpu.SMEM)] + vmem_specs(1) + [hbm_spec] * 12,
        out_specs=tuple(vmem_specs(8)),
        scratch_shapes=near
        + [
            VM((64, WALL), BF16), VM((2, 32, WALL), BF16), VM((128, 128), F32),
            dma_sems(1), dma_sems(12),
        ]
        + link_scratch(GATHER_COPIES, 2, 6, 6),
        compiler_params=pltpu.CompilerParams(
            collective_id=0, has_side_effects=True, vmem_limit_bytes=6 << 20
        ),
        name="gather_weights",
    )(*arrays)


def column_of(row):
    return jnp.transpose(jnp.broadcast_to(row, (128, 128)))


def middle_kernel(
    part, st, u0, valid, par, shard1, total, u_next, s_out, hid, w1,
    relay, sums, inbox, sbuf, own_sem, g_s, g_r, p_s, p_r, b_s, b_r, h_s, h_r,
):
    me = Peers()
    c, t = me.c, me.t
    greet([me.core] + me.xs + me.zs + me.ts)
    weights, tokens, small, spreading = Link(g_s, g_r), Link(p_s, p_r), Link(b_s, b_r), Link(h_s, h_r)
    sum_steps = collect_tokens(tokens, part, relay, sums, inbox, me)
    next(sum_steps)
    stats = [small.send(st.at[(t + o + 1) % 4], sbuf.at[o], me.ts[o]) for o in range(3)]
    layer1 = gather_layer(weights, own_sem.at[0], shard1, w1, me)
    next(layer1)
    next(sum_steps)
    next(layer1)
    for copy in stats:
        copy.wait_recv()
    s_row = lax.rsqrt((st[t] + sbuf[0] + sbuf[1] + sbuf[2]) / DI + EPSILON)
    s_out[...] = s_row
    scale = column_of(s_row[0:1]) * valid[...]
    next(layer1)
    run(sum_steps)
    total[...] = part[t].astype(F32) + inbox[0].astype(F32) + inbox[1].astype(F32)
    for j in range(8):
        u_next[:, tile(j)] = u0[:, tile(j)] + scale * total[:, tile(j)]
    hid[t] = input_norm(u_next[...], gain_of(par, 1)).astype(BF16)
    hid_steps = spread_tokens(spreading, hid, me)
    next(hid_steps)
    next(layer1)
    next(hid_steps)
    run(layer1)
    run(hid_steps)
    for link in (weights, tokens, small, spreading):
        link.drain()


def middle(*arrays):
    return pl.pallas_call(
        middle_kernel,
        out_shape=(
            jax.ShapeDtypeStruct((ROWS, D), F32),
            jax.ShapeDtypeStruct((ROWS, D), F32),
            jax.ShapeDtypeStruct((8, 128), F32),
            jax.ShapeDtypeStruct((4, ROWS, D), BF16),
            jax.ShapeDtypeStruct((4, 4, 64, WALL), BF16),
        ),
        in_specs=vmem_specs(6),
        out_specs=tuple(vmem_specs(5)),
        scratch_shapes=token_scratch()
        + [VM((3, 8, 128), F32), pltpu.SemaphoreType.DMA((1,))]
        + link_scratch(GATHER_COPIES, 6, 3, 6),
        compiler_params=pltpu.CompilerParams(
            collective_id=1, has_side_effects=True, vmem_limit_bytes=6 << 20
        ),
        name="sum_and_gather_tokens",
    )(*arrays)


def stats_kernel(st, coef, buf, a_s, a_r):
    me = Peers()
    greet(me.ts)
    link = Link(a_s, a_r)
    copies = [link.send(st, buf.at[me.t], peer) for peer in me.ts]
    buf[me.t] = st[...]
    for copy in copies:
        copy.wait_recv()
    for i in range(4):
        both = buf[0, i] + buf[1, i] + buf[2, i] + buf[3, i]
        s = lax.rsqrt(both[0:1] / DI + EPSILON)
        k = s * s * s * (both[1:2] / DI)
        row = iota((8, 128), 0)
        coef[i] = jnp.where(row == 0, s, jnp.where(row == 1, k, 0.0))
    link.drain()


def stats(st):
    return pl.pallas_call(
        stats_kernel,
        out_shape=jax.ShapeDtypeStruct((4, 8, 128), F32),
        in_specs=vmem_specs(1),
        out_specs=pl.BlockSpec(memory_space=VM),
        scratch_shapes=[VM((4, 4, 8, 128), F32)] + link_scratch(3),
        compiler_params=pltpu.CompilerParams(
            collective_id=2, has_side_effects=True, vmem_limit_bytes=1 << 20
        ),
        name="sum_stats",
    )(st)


def norm_back(u, gain, g, d_hidden):
    r = lax.rsqrt(jnp.mean(u * u, axis=-1, keepdims=True) + EPSILON)
    mean = jnp.mean(u * gain * d_hidden, axis=-1, keepdims=True)
    d_u = g + r * gain * d_hidden - u * (r * r * r) * mean
    return d_u, jnp.sum(u * r * d_hidden, axis=0, keepdims=True)


def back_middle_kernel(
    dh, u, cot, valid, par, total0, s0, hid1, d_proj1, db1, scaled1, g1, ng, db, coef, w_grad, bc_all,
    relay, sums, inbox, grads, core_in, acc, g_relay, g_sums, g_inbox, last_in,
    g_s, g_r, p_s, p_r, b_s, b_r, h_s, h_r,
):
    me = Peers()
    c, t = me.c, me.t
    greet(me.everyone())
    weights, tokens, small, spreading = Link(g_s, g_r), Link(p_s, p_r), Link(b_s, b_r), Link(h_s, h_r)
    sum_steps = collect_tokens(tokens, dh, relay, sums, inbox, me)
    next(sum_steps)
    layer1 = reduce_layer(
        weights, (hid1, d_proj1, db1, scaled1), grads, w_grad, bc_all, core_in, acc,
        g_relay, g_sums, g_inbox, last_in, me,
    )
    next(layer1)
    next(sum_steps)
    next(layer1)
    next(layer1)
    run(sum_steps)
    total = dh[t].astype(F32) + inbox[0].astype(F32) + inbox[1].astype(F32)
    d_u, gain_term = norm_back(u[...], gain_of(par, 1), cot[...], total)
    g1[...] = d_u
    ng[...] = gain_term
    mean = jnp.zeros((ROWS, 128), F32)
    for j in range(8):
        d_branch = (g1[:, tile(j)] * valid[...]).astype(BF16)
        db[t, :, tile(j)] = d_branch
        mean = mean + d_branch.astype(F32) * total0[:, tile(j)]
    db_steps = spread_tokens(spreading, db, me)
    next(db_steps)
    mean = jnp.broadcast_to(jnp.sum(mean, axis=-1, keepdims=True), (128, 128))
    mean_row = jnp.transpose(mean)[0:8] / DI
    s = s0[0:1, :]
    row = iota((8, 128), 0)
    coef[t] = jnp.where(row == 0, s, jnp.where(row == 1, s * s * s * mean_row, 0.0))
    coef_copies = [small.send(coef.at[t], coef.at[t], peer) for peer in me.ts]
    next(layer1)
    next(db_steps)
    next(layer1)
    next(db_steps)
    next(layer1)
    run(db_steps)
    run(layer1)
    for copy in coef_copies:
        copy.wait_recv()
    for link in (weights, tokens, small, spreading):
        link.drain()


def back_middle(*arrays):
    return pl.pallas_call(
        back_middle_kernel,
        out_shape=(
            jax.ShapeDtypeStruct((ROWS, D), F32),
            jax.ShapeDtypeStruct((1, D), F32),
            jax.ShapeDtypeStruct((4, ROWS, D), BF16),
            jax.ShapeDtypeStruct((4, 8, 128), F32),
            jax.ShapeDtypeStruct((64, WALL), F32),
            jax.ShapeDtypeStruct((4, 64, 2 * N), F32),
        ),
        in_specs=vmem_specs(11),
        out_specs=tuple(vmem_specs(6)),
        scratch_shapes=token_scratch() + reduce_scratch() + link_scratch(REDUCE_COPIES, 6, 3, 6),
        compiler_params=pltpu.CompilerParams(
            collective_id=3, has_side_effects=True, vmem_limit_bytes=14 << 20
        ),
        name="back_sum_and_gather",
    )(*arrays)


def finish_kernel(
    dh, part, u0, u1, g1, valid, par, coef1, ng1, sums0, heads0, sums1, heads1, w_grad1, bc_all1,
    hid0, d_proj0, db0, scaled0,
    lo, lg, smt, picked, o_bc,
    relay, sums, inbox, relay2, sums2, inbox2, los, lgs, sms, smr, smz, smx, w_grad, bc_all,
    grads, core_in, acc, g_relay, g_sums, g_inbox, last_in,
    g_s, g_r, p_s, p_r, q_s, q_r, b_s, b_r,
):
    me = Peers()
    c, x, z, t = me.c, me.x, me.z, me.t
    greet(me.everyone())
    weights, tokens, tokens2, small = Link(g_s, g_r), Link(p_s, p_r), Link(q_s, q_r), Link(b_s, b_r)
    back_steps = collect_tokens(tokens, dh, relay, sums, inbox, me)
    next(back_steps)
    layer0 = reduce_layer(
        weights, (hid0, d_proj0, db0, scaled0), grads, w_grad, bc_all, core_in, acc,
        g_relay, g_sums, g_inbox, last_in, me,
    )
    next(layer0)
    next(back_steps)
    next(layer0)
    next(layer0)
    out_steps = collect_tokens(tokens2, part, relay2, sums2, inbox2, me)
    next(out_steps)
    los[0] = u1[...]
    lgs[1] = g1[...]
    run(back_steps)
    total = dh[t].astype(F32) + inbox[0].astype(F32) + inbox[1].astype(F32)
    d_u, gain_term = norm_back(u0[...], gain_of(par, 0), g1[...], total)
    lgs[0] = d_u
    lg_copy = small.send(lgs.at[1 - c], lg.at[c], me.core)
    lg[c] = lgs[c]
    next(out_steps)
    next(layer0)
    sms[...] = jnp.zeros_like(sms)
    for layer, (by_channel, heads, term) in enumerate(
        ((sums0, heads0, gain_term), (sums1, heads1, ng1[...]))
    ):
        sms[layer, 0:8, :] = by_channel[:, 0:512]
        sms[layer, 8:16, 0:256] = by_channel[:, 512:768]
        sms[layer, 8:16, 256:384] = heads[...]
        sms[layer, 16:17, :] = term[:, 0:512]
        sms[layer, 17:18, :] = term[:, 512:1024]
    sm_copy = small.send(sms.at[1 - c], smr, me.core)
    sm_copy.wait_recv()
    smz[z] = sms[c] + smr[...]
    sz = [small.send(smz.at[z], smz.at[z], peer) for peer in me.zs]
    next(layer0)
    run(out_steps)
    los[1] = part[t].astype(F32) + inbox2[0].astype(F32) + inbox2[1].astype(F32)
    scale = column_of(coef1[t][0:1]) * valid[...]
    for j in range(8):
        los[1, :, tile(j)] = u1[:, tile(j)] + scale * los[1, :, tile(j)]
    lo_copy = small.send(los.at[1 - c], lo.at[c], me.core)
    lo[c] = los[c]
    for copy in sz:
        copy.wait_recv()
    smx[x] = smz[0] + smz[1] + smz[2] + smz[3]
    sx = [small.send(smx.at[x], smx.at[x], peer) for peer in me.xs]
    next(layer0)
    for copy in sx:
        copy.wait_recv()
    smt[t] = smx[0] + smx[1] + smx[2] + smx[3]
    to_all = [small.send(smt.at[t], smt.at[t], peer) for peer in me.ts]
    run(layer0)
    picked[...] = jnp.where(c == 0, w_grad[...], w_grad1[...])
    rows = pl.ds(pl.multiple_of(16 * t, 16), 16)
    bc0 = bc_all[0, rows, :] + bc_all[1, rows, :] + bc_all[2, rows, :] + bc_all[3, rows, :]
    bc1 = bc_all1[0, rows, :] + bc_all1[1, rows, :] + bc_all1[2, rows, :] + bc_all1[3, rows, :]
    o_bc[...] = jnp.where(c == 0, bc0, bc1)
    for copy in to_all + [lo_copy, lg_copy]:
        copy.wait_recv()
    for link in (weights, tokens, tokens2, small):
        link.drain()


def finish(*arrays):
    return pl.pallas_call(
        finish_kernel,
        out_shape=(
            jax.ShapeDtypeStruct((2, ROWS, D), F32),
            jax.ShapeDtypeStruct((2, ROWS, D), F32),
            jax.ShapeDtypeStruct((4, 24, 512), F32),
            jax.ShapeDtypeStruct((64, WALL), F32),
            jax.ShapeDtypeStruct((16, 2 * N), F32),
        ),
        in_specs=vmem_specs(19),
        out_specs=tuple(vmem_specs(5)),
        scratch_shapes=token_scratch() + token_scratch()
        + [
            VM((2, ROWS, D), F32), VM((2, ROWS, D), F32),
            VM((2, 24, 512), F32), VM((24, 512), F32),
            VM((4, 24, 512), F32), VM((4, 24, 512), F32),
            VM((64, WALL), F32), VM((4, 64, 2 * N), F32),
        ]
        + reduce_scratch() + link_scratch(REDUCE_COPIES, 6, 6, 12),
        compiler_params=pltpu.CompilerParams(
            collective_id=4, has_side_effects=True, vmem_limit_bytes=20 << 20
        ),
        name="sum_gradients",
    )(*arrays)


def write_kernel(lo, lg, smt, picked, bc, *rest):
    outs, (in_part, dt, conv_w, conv_b, gain, norm, heads, sem) = rest[:13], rest[13:]
    (o_lo, o_lg, o_norm, o_in, o_bc, o_dt, o_cw, o_cb, o_dtb, o_alog, o_skip, o_gain, o_out) = outs
    copies = []

    def write(src, dst):
        copy = pltpu.make_async_copy(src, dst, sem.at[len(copies)])
        copy.start()
        copies.append(copy)

    write(lo, o_lo)
    write(lg, o_lg)
    write(bc, o_bc)
    in_part[:, 0, :] = picked[:, 0:512]
    in_part[:, 1, :] = picked[:, 512:1024]
    write(in_part, o_in)
    write(picked.at[:, pl.ds(WP, CH)], o_out)
    dt_rows = jnp.concatenate([picked[:, 1280:1408], jnp.zeros((64, 128), F32)], axis=0)
    dt[...] = jnp.transpose(dt_rows)[0:HL, 0:64]
    write(dt, o_dt)
    shared = smt[0, 8:24] + smt[1, 8:24] + smt[2, 8:24] + smt[3, 8:24]
    norm[:, 0:512] = shared[8:9]
    norm[:, 512:1024] = shared[9:10]
    write(norm, o_norm)
    conv_w[:, DI : DI + 2 * N] = shared[0:4, 0:256]
    conv_b[:, DI : DI + 2 * N] = shared[4:5, 0:256]
    for k in range(4):
        at = slice(512 * k, 512 * k + 512)
        conv_w[:, at] = smt[k, 0:4, :]
        conv_b[:, at] = smt[k, 4:5, :]
        gain[:, at] = smt[k, 5:6, :]
    write(conv_w, o_cw)
    write(conv_b, o_cb)
    write(gain, o_gain)
    all_heads = smt[0, 8:16, 256:384]
    for k in range(1, 4):
        all_heads = all_heads + pltpu.roll(smt[k, 8:16, 256:384], HL * k, 1)
    for k, out in ((0, o_dtb), (1, o_alog), (2, o_skip)):
        heads[k] = all_heads[k : k + 1, 0:H]
        write(heads.at[k], out)
    for copy in copies:
        copy.wait()


def write_outputs(*arrays):
    hbm_spec = pl.BlockSpec(memory_space=pltpu.HBM)
    shapes = [
        (2, ROWS, D), (2, ROWS, D), (1, D), (64, 2, CH), (16, 2 * N), (HL, 64), (CONV, DI + 2 * N),
        (1, DI + 2 * N), (1, H), (1, H), (1, H), (1, DI), (64, CH),
    ]
    return pl.pallas_call(
        write_kernel,
        out_shape=tuple(jax.ShapeDtypeStruct(shape, F32) for shape in shapes),
        in_specs=vmem_specs(5),
        out_specs=(hbm_spec,) * 13,
        scratch_shapes=[
            VM((64, 2, CH), F32), VM((HL, 64), F32), VM((CONV, DI + 2 * N), F32),
            VM((1, DI + 2 * N), F32), VM((1, DI), F32), VM((1, D), F32), VM((3, 1, H), F32),
            pltpu.SemaphoreType.DMA((13,)),
        ],
        compiler_params=pltpu.CompilerParams(vmem_limit_bytes=6 << 20),
        name="write_outputs",
    )(*arrays)


def body(
    activations, cotangent, lengths, norm_gain, in_weight, bc_weight, dt_weight, conv_weight,
    conv_bias, dt_bias, a_log, d_skip, gated_gain, out_weight,
):
    w0, shard1, par, hid0, db1, u0, cot, valid = gather(
        lengths, in_weight[0].reshape(64, WZX), bc_weight[0], dt_weight[0].T, out_weight[0].T,
        conv_weight[0], conv_bias, dt_bias, a_log, d_skip, gated_gain, norm_gain,
        activations, cotangent,
    )
    proj0, kept0, part0, y0, st0 = mixer_fwd(0, lengths, par, hid0, w0)
    total0, u1, s0, hid1, w1 = middle(part0, st0, u0, valid, par, shard1)
    proj1, kept1, part1, y1, st1, d_scaled1 = mixer_fwd(1, lengths, par, hid1, w1, db1)
    coef1 = stats(st1)
    dh1, dp1, sc1, sums1, heads1 = mixer_bwd(1, lengths, par, w1, proj1, kept1, y1, coef1, d_scaled1)
    g1, ng1, db0, coef0, w_grad1, bc_all1 = back_middle(
        dh1, u1, cot, valid, par, total0, s0, hid1, dp1, db1, sc1
    )
    dh0, dp0, sc0, sums0, heads0 = mixer_bwd(0, lengths, par, w0, proj0, kept0, y0, coef0, db0)
    outs = write_outputs(
        *finish(
            dh0, part1, u0, u1, g1, valid, par, coef1, ng1,
            sums0, heads0, sums1, heads1, w_grad1, bc_all1, hid0, dp0, db0, sc0,
        )
    )
    outs = [out.T if k in (5, 12) else out for k, out in enumerate(outs)]
    plain = (2, 8, 9, 10, 7, 11)
    return tuple(out if k in plain else out[None] for k, out in enumerate(outs))


def solution(mesh):
    return jax.shard_map(
        body,
        mesh=mesh,
        in_specs=(
            P(None, ("dp", "tensor"), None),
            P(None, ("dp", "tensor"), None),
            P(None, "dp", None),
            P("section", None),
            P("section", "dp", None, "tensor"),
            P("section", "dp", None),
            P("section", "dp", "tensor"),
            P("section", None, None),
            P("section", None),
            P("section", None),
            P("section", None),
            P("section", None),
            P("section", None),
            P("section", "tensor", "dp"),
        ),
        out_specs=(
            P("section", None, ("dp", "tensor"), None),
            P("section", None, ("dp", "tensor"), None),
            P("section", None),
            P("section", "dp", None, "tensor"),
            P("section", ("dp", "tensor"), None),
            P("section", "dp", "tensor"),
            P("section", None, None),
            P("section", None),
            P("section", None),
            P("section", None),
            P("section", None),
            P("section", None),
            P("section", "tensor", "dp"),
        ),
        check_vma=False,
    )
```

```python
import functools

import jax
import jax.numpy as jnp
from jax import lax
from jax.experimental import pallas as pl
from jax.experimental.pallas import tpu as pltpu
from jax.sharding import PartitionSpec as P

D = 1024
DI = 2048
H = 32
N = 128
CONV = 4
T = 512
ROWS = 128
CH = 512
HL = 8
WZX = 1024
WP = 1408
WALL = 1920
NDP = 16
EPSILON = 1e-05
LOG2E = 1.4426950408889634
NEG = -1e30
F32 = jnp.float32
BF16 = jnp.bfloat16
MESH = pl.DeviceIdType.MESH
VM = pltpu.VMEM
FWD_VMEM = 12 << 20
BWD_VMEM = 16 << 20


def dot_nn(a, b):
    return lax.dot_general(a, b, (((1,), (0,)), ((), ())), preferred_element_type=F32)


def dot_nt(a, b):
    return lax.dot_general(a, b, (((1,), (1,)), ((), ())), preferred_element_type=F32)


def dot_tn(a, b):
    return lax.dot_general(a, b, (((0,), (0,)), ((), ())), preferred_element_type=F32)


def pieces(v, count):
    parts = []
    for _ in range(count):
        part = v.astype(BF16)
        parts.append(part)
        v = v - part.astype(F32)
    return parts


def sum_rows_nt(selector, v, count):
    return sum(dot_nt(selector, part) for part in pieces(v, count))


def rows_times(v, matrix):
    a, b, c = pieces(v, 3)
    stacked = jnp.concatenate([a.astype(F32), b.astype(F32), c.astype(F32), jnp.zeros_like(v)], 0)
    out = dot_nn(stacked.astype(BF16), matrix)
    return out[0:8] + out[8:16] + out[16:24]


def iota(shape, dim):
    return lax.broadcasted_iota(jnp.int32, shape, dim)


def segment_of(position, e0, e1):
    return (position >= e0).astype(jnp.int32) + (position >= e1).astype(jnp.int32)


def conv_masks(e0, e1):
    p = iota((T, 128), 0)
    seg = segment_of(p, e0, e1)
    return [
        jnp.where((p >= k) & (segment_of(p - k, e0, e1) == seg), 1.0, 0.0).astype(F32)
        for k in range(1, CONV)
    ]


def conv_pre(v, masks, cw, lanes):
    pre = cw[CONV : CONV + 1, lanes] + cw[CONV - 1 : CONV, lanes] * v
    for k in range(1, CONV):
        pre = pre + cw[CONV - 1 - k : CONV - k, lanes] * (masks[k - 1] * pltpu.roll(v, k, 0))
    return pre


def sigmoid(v):
    return 0.5 * jnp.tanh(0.5 * v) + 0.5


def steps_of(dt_tile, hp_ref):
    raw = jnp.transpose(dt_tile)[0:HL] + hp_ref[:, 0:1]
    step = jnp.maximum(raw, 0.0) + jnp.log1p(jnp.exp(-jnp.abs(raw)))
    rate = hp_ref[:, 1:2]
    upper = jnp.where(iota((T, T), 0) <= iota((T, T), 1), 1.0, 0.0).astype(BF16)
    cum = rows_times(step * rate, upper) * LOG2E
    columns = jnp.transpose(
        jnp.concatenate([cum, step, jnp.zeros((112, T), F32)], axis=0)
    )
    return raw, step, cum, columns


def pair_columns(columns, first, j, rows=T):
    low = iota((rows, 128), 1) < 64
    return jnp.where(
        low,
        jnp.broadcast_to(columns[:, first + 2 * j : first + 2 * j + 1], (rows, 128)),
        jnp.broadcast_to(columns[:, first + 2 * j + 1 : first + 2 * j + 2], (rows, 128)),
    )


def tile(j):
    return slice(128 * j, 128 * j + 128)


def layer_params(par, layer):
    return (
        par.at[layer, :, pl.ds(0, 768)],
        par.at[layer, :, pl.ds(768, 128)],
        par.at[layer, :, pl.ds(896, 512)],
    )


def skip_row(hp, j):
    low = iota((1, 128), 1) < 64
    first = jnp.broadcast_to(hp[2 * j : 2 * j + 1, 2:3], (1, 128))
    second = jnp.broadcast_to(hp[2 * j + 1 : 2 * j + 2, 2:3], (1, 128))
    return jnp.where(low, first, second)


def segment_ends(lengths):
    c = lax.axis_index("section")
    first = lengths[c, 0, 0]
    return first, first + lengths[c, 0, 1]


def project(hid, w, proj):
    tokens = hid[...].reshape(T, D)
    for first, width in ((0, 512), (512, 512), (1024, 384)):
        at = slice(first, first + width)
        proj[:, at] = dot_nn(tokens, w[:, :, :, at].reshape(D, width))


def scale_back(db, w, d_scaled):
    d_scaled[...] = dot_nn(db[...].reshape(T, D), w[:, :, :, WP:WALL].reshape(D, CH))


def mixer_fwd_kernel(layer, lens, par, hid, w, *rest):
    with_grad = layer == 1
    if with_grad:
        db, proj, kept, part, yssd, st, d_scaled, gg, inn, xb, bb, cb, cumr, colr = rest
        scale_back(db, w, d_scaled)
    else:
        proj, kept, part, yssd, st, gg, inn, xb, bb, cb, cumr, colr = rest
    cw, hp, rows = layer_params(par, layer)
    project(hid, w, proj)
    e0, e1 = segment_ends(lens)
    masks = conv_masks(e0, e1)
    _, _, cum, columns = steps_of(proj[:, 1280:1408], hp)
    cumr[...] = cum
    colr[...] = columns
    for j in range(4):
        v = proj[:, 512 + 128 * j : 640 + 128 * j]
        pre = conv_pre(v, masks, cw, tile(j))
        kept[:, tile(j)] = pre
        act = pre * sigmoid(pre)
        inn[:, tile(j)] = act
        xb[:, tile(j)] = (act * pair_columns(columns, HL, j)).astype(BF16)
    for j, ref in ((0, bb), (1, cb)):
        lanes = slice(512 + 128 * j, 640 + 128 * j)
        pre = conv_pre(proj[:, 1024 + 128 * j : 1152 + 128 * j], masks, cw, lanes)
        kept[:, lanes] = pre
        ref[...] = (pre * sigmoid(pre)).astype(BF16)
    low = iota((128, 128), 1) < 64
    for i in range(4):
        n = 128 * (i + 1)
        here = slice(128 * i, n)
        scores = dot_nt(cb[here, :], bb[0:n, :])
        p = iota((128, n), 0) + 128 * i
        q = iota((128, n), 1)
        bias = jnp.where((p >= q) & (segment_of(p, e0, e1) == segment_of(q, e0, e1)), 0.0, NEG).astype(F32)
        for j in range(4):
            mixing = []
            for h in (2 * j, 2 * j + 1):
                decay = jnp.exp2(colr[here, h : h + 1] - cumr[h : h + 1, 0:n] + bias)
                mixing.append((scores * decay).astype(BF16))
            both = dot_nn(jnp.concatenate(mixing, axis=0), xb[0:n, tile(j)])
            yssd[here, tile(j)] = jnp.where(low, both[0:128], both[128:256])
    squares = jnp.zeros((8, T), F32)
    dots = jnp.zeros((8, T), F32)
    ones = jnp.ones((8, 128), BF16)
    for j in range(4):
        z = proj[:, tile(j)]
        gated = (yssd[:, tile(j)] + skip_row(hp, j) * inn[:, tile(j)]) * (z * sigmoid(z))
        gained = gated * rows[0:1, tile(j)]
        gg[:, tile(j)] = gained.astype(BF16)
        squares = squares + sum_rows_nt(ones, gated * gated, 1)
        if with_grad:
            dots = dots + sum_rows_nt(ones, gained * d_scaled[:, tile(j)], 2)
    row = iota((8, T), 0)
    both = jnp.where(row == 0, squares, jnp.where(row == 1, dots, 0.0))
    for i in range(4):
        st[i] = both[:, tile(i)]
    for x in range(4):
        columns_out = slice(256 * x, 256 * x + 256)
        branch = dot_nt(gg[...], w[x, :, :, WP:WALL].reshape(256, CH)).astype(BF16)
        part[:, :, columns_out] = branch.reshape(4, ROWS, 256)


def vmem_specs(count):
    return [pl.BlockSpec(memory_space=VM)] * count


def mixer_fwd(layer, lens, par, hid, w, *db):
    out_shape = [
        jax.ShapeDtypeStruct((T, WP), F32),
        jax.ShapeDtypeStruct((T, 768), F32),
        jax.ShapeDtypeStruct((4, ROWS, D), BF16),
        jax.ShapeDtypeStruct((T, CH), F32),
        jax.ShapeDtypeStruct((4, 8, 128), F32),
    ] + [jax.ShapeDtypeStruct((T, CH), F32)] * layer
    return pl.pallas_call(
        functools.partial(mixer_fwd_kernel, layer),
        out_shape=tuple(out_shape),
        in_specs=[pl.BlockSpec(memory_space=pltpu.SMEM)] + vmem_specs(3 + len(db)),
        out_specs=tuple(vmem_specs(len(out_shape))),
        scratch_shapes=[
            VM((T, CH), BF16),
            VM((T, CH), F32),
            VM((T, CH), BF16),
            VM((T, N), BF16),
            VM((T, N), BF16),
            VM((8, T), F32),
            VM((T, 128), F32),
        ],
        compiler_params=pltpu.CompilerParams(vmem_limit_bytes=FWD_VMEM),
        name="mixer_fwd",
    )(lens, par, hid, w, *db)


def head_selector(j):
    head = 2 * j + (iota((8, 128), 1) >= 64).astype(jnp.int32)
    return jnp.where(iota((8, 128), 0) == head, 1.0, 0.0).astype(BF16)


def back_roll(v, k):
    return pltpu.roll(v, T - k, 0)


def conv_back(d_pre, v, masks, cw, lanes, sums, column0):
    d_v = cw[CONV - 1 : CONV, lanes] * d_pre
    out = slice(column0, column0 + 128)
    sums[CONV : CONV + 1, out] = jnp.sum(d_pre, axis=0, keepdims=True)
    sums[CONV - 1 : CONV, out] = jnp.sum(d_pre * v, axis=0, keepdims=True)
    for k in range(1, CONV):
        masked = masks[k - 1] * d_pre
        d_v = d_v + cw[CONV - 1 - k : CONV - k, lanes] * back_roll(masked, k)
        sums[CONV - 1 - k : CONV - k, out] = jnp.sum(masked * pltpu.roll(v, k, 0), axis=0, keepdims=True)
    return d_v


def mixer_bwd_kernel(layer, lens, par, w, proj, kept, yssd, coef, *rest):
    given, *rest = rest
    dh, d_proj, scaled, sums, heads, inn, xb, dyb, dyf, dx, bb, cb, d_c, cumr, colr, *rest = rest
    if layer == 1:
        d_scaled = given
    else:
        db, d_scaled = given, rest[0]
        scale_back(db, w, d_scaled)
    cw, hp, rows = layer_params(par, layer)
    e0, e1 = segment_ends(lens)
    masks = conv_masks(e0, e1)
    raw, step, cum, columns = steps_of(proj[:, 1280:1408], hp)
    cumr[...] = cum
    colr[...] = columns
    norm_cols = jnp.transpose(jnp.concatenate(
        [jnp.concatenate([coef[i] for i in range(4)], axis=1), jnp.zeros((120, T), F32)], axis=0
    ))
    s_col = jnp.broadcast_to(norm_cols[:, 0:1], (T, 128))
    k_col = jnp.broadcast_to(norm_cols[:, 1:2], (T, 128))
    sums[...] = jnp.zeros_like(sums)
    d_skip = jnp.zeros((8, T), F32)
    for j in range(4):
        selector = head_selector(j)
        pre = kept[:, tile(j)]
        act = pre * sigmoid(pre)
        inn[:, tile(j)] = act
        xb[:, tile(j)] = (act * pair_columns(columns, HL, j)).astype(BF16)
        z = proj[:, tile(j)]
        sig = sigmoid(z)
        gate = z * sig
        y = yssd[:, tile(j)] + skip_row(hp, j) * act
        gated = y * gate
        gs = gated * s_col
        gain = rows[0:1, tile(j)]
        dsc = d_scaled[:, tile(j)]
        scaled[:, tile(j)] = (gs * gain).astype(BF16)
        sums[5:6, tile(j)] = jnp.sum(gs * dsc, axis=0, keepdims=True)
        d_gated = s_col * gain * dsc - gated * k_col
        d_proj[:, tile(j)] = (d_gated * y * (sig * (1.0 + z * (1.0 - sig)))).astype(BF16)
        dy = d_gated * gate
        dyf[:, tile(j)] = dy
        dyb[:, tile(j)] = dy.astype(BF16)
        d_skip = d_skip + sum_rows_nt(selector, dy * act, 2)
    for j, ref in ((0, bb), (1, cb)):
        pre = kept[:, 512 + 128 * j : 640 + 128 * j]
        ref[...] = (pre * sigmoid(pre)).astype(BF16)
    d_c[...] = jnp.zeros_like(d_c)
    low = iota((128, 128), 1) < 64
    zero = jnp.zeros((128, 128), BF16)
    d_b_blocks = []
    for i in range(4):
        first = 128 * i
        n = T - first
        here = slice(first, first + 128)
        scores = dot_nt(bb[here, :], cb[first:T, :])
        q = iota((128, n), 0) + first
        p = iota((128, n), 1) + first
        bias = jnp.where((p >= q) & (segment_of(p, e0, e1) == segment_of(q, e0, e1)), 0.0, NEG).astype(F32)
        d_scores = jnp.zeros((128, n), F32)
        for j in range(4):
            x_tile = xb[here, tile(j)]
            dy_tile = dyb[first:T, tile(j)]
            heads_of = jnp.concatenate([jnp.where(low, x_tile, zero), jnp.where(low, zero, x_tile)], axis=0)
            d_mixing = dot_nt(heads_of, dy_tile)
            mixing = []
            for k in (0, 1):
                h = 2 * j + k
                decay = jnp.exp2(cumr[h : h + 1, first:T] - colr[here, h : h + 1] + bias)
                mixing.append((scores * decay).astype(BF16))
                d_scores = d_scores + d_mixing[128 * k : 128 * k + 128] * decay
            both = dot_nn(jnp.concatenate(mixing, axis=0), dy_tile)
            dx[here, tile(j)] = jnp.where(low, both[0:128], both[128:256])
        d_scores = d_scores.astype(BF16)
        d_b_blocks.append(dot_nn(d_scores, cb[first:T, :]))
        d_c[first:T, :] = d_c[first:T, :] + dot_tn(d_scores, bb[here, :])
    d_cum = jnp.zeros((8, T), F32)
    d_step = jnp.zeros((8, T), F32)
    for j in range(4):
        selector = head_selector(j)
        dxt = dx[:, tile(j)]
        act = inn[:, tile(j)]
        change = dyb[:, tile(j)].astype(F32) * yssd[:, tile(j)] - xb[:, tile(j)].astype(F32) * dxt
        d_cum = d_cum + sum_rows_nt(selector, change, 3)
        d_step = d_step + sum_rows_nt(selector, act * dxt, 2)
        d_act = pair_columns(columns, HL, j) * dxt + skip_row(hp, j) * dyf[:, tile(j)]
        v = proj[:, 512 + 128 * j : 640 + 128 * j]
        pre = kept[:, tile(j)]
        sig = sigmoid(pre)
        d_pre = d_act * (sig * (1.0 + pre * (1.0 - sig)))
        d_proj[:, 512 + 128 * j : 640 + 128 * j] = conv_back(d_pre, v, masks, cw, tile(j), sums, 128 * j).astype(BF16)
    for j in (0, 1):
        lanes = slice(512 + 128 * j, 640 + 128 * j)
        at = slice(1024 + 128 * j, 1152 + 128 * j)
        v = proj[:, at]
        pre = kept[:, lanes]
        sig = sigmoid(pre)
        d_act = jnp.concatenate(d_b_blocks, axis=0) if j == 0 else d_c[...]
        d_pre = d_act * (sig * (1.0 + pre * (1.0 - sig)))
        d_proj[:, at] = conv_back(d_pre, v, masks, cw, lanes, sums, 512 + 128 * j).astype(BF16)
    lower = jnp.where(iota((T, T), 0) >= iota((T, T), 1), 1.0, 0.0).astype(BF16)
    d_a = rows_times(d_cum, lower)
    rate = hp[:, 1:2]
    d_raw = (d_step + rate * d_a) * sigmoid(raw)
    d_proj[:, 1280:1408] = jnp.transpose(
        jnp.concatenate([d_raw, jnp.zeros((120, T), F32)], axis=0)
    ).astype(BF16)
    bias_grad = jnp.broadcast_to(jnp.sum(d_raw, axis=1, keepdims=True), (8, 128))
    rate_grad = jnp.broadcast_to(jnp.sum(d_a * step, axis=1, keepdims=True) * rate, (8, 128))
    skip_grad = jnp.broadcast_to(jnp.sum(d_skip, axis=1, keepdims=True), (8, 128))
    lane = iota((8, 128), 1)
    by_head = jnp.where(
        lane == 0, bias_grad, jnp.where(lane == 1, rate_grad, jnp.where(lane == 2, skip_grad, 0.0))
    )
    heads[...] = jnp.transpose(jnp.concatenate([by_head, jnp.zeros((120, 128), F32)], axis=0))[0:8]
    for x in range(4):
        back = dot_nt(d_proj[...], w[x, :, :, 0:WP].reshape(256, WP)).astype(BF16)
        dh[:, :, 256 * x : 256 * x + 256] = back.reshape(4, ROWS, 256)


def mixer_bwd(layer, lens, par, w, proj, kept, yssd, coef, given):
    return pl.pallas_call(
        functools.partial(mixer_bwd_kernel, layer),
        out_shape=(
            jax.ShapeDtypeStruct((4, ROWS, D), BF16),
            jax.ShapeDtypeStruct((T, WP), BF16),
            jax.ShapeDtypeStruct((T, CH), BF16),
            jax.ShapeDtypeStruct((8, 768), F32),
            jax.ShapeDtypeStruct((8, 128), F32),
        ),
        in_specs=[pl.BlockSpec(memory_space=pltpu.SMEM)] + vmem_specs(7),
        out_specs=tuple(vmem_specs(5)),
        scratch_shapes=[
            VM((T, CH), F32),
            VM((T, CH), BF16),
            VM((T, CH), BF16),
            VM((T, CH), F32),
            VM((T, CH), F32),
            VM((T, N), BF16),
            VM((T, N), BF16),
            VM((T, N), F32),
            VM((8, T), F32),
            VM((T, 128), F32),
        ] + [VM((T, CH), F32)] * (1 - layer),
        compiler_params=pltpu.CompilerParams(vmem_limit_bytes=BWD_VMEM),
        name="mixer_bwd",
    )(lens, par, w, proj, kept, yssd, coef, given)


def places():
    section = lax.axis_index("section")
    dp = lax.axis_index("dp")
    return section, dp // 4, dp % 4, lax.axis_index("tensor")


class Peers:
    def __init__(self):
        self.c, self.x, self.z, self.t = places()
        self.core = {"section": 1 - self.c}
        self.xs = [{"dp": ((self.x + o) % 4) * 4 + self.z} for o in (1, 2, 3)]
        self.zs = [{"dp": self.x * 4 + (self.z + o) % 4} for o in (1, 2, 3)]
        self.ts = [{"tensor": (self.t + o) % 4} for o in (1, 2, 3)]
        self.far_ts = [{"section": 1 - self.c, "tensor": (self.t + o) % 4} for o in (1, 2, 3)]

    def near_dp(self):
        return [self.core] + self.xs + self.zs + self.ts

    def everyone(self):
        return [self.core] + self.xs + self.zs + self.ts + self.far_ts


def barrier_start(peers):
    barrier = pltpu.get_barrier_semaphore()
    for peer in peers:
        pl.semaphore_signal(barrier, inc=1, device_id=peer, device_id_type=MESH)


def barrier_end(peers):
    pl.semaphore_wait(pltpu.get_barrier_semaphore(), len(peers))


def greet(peers):
    barrier_start(peers)
    barrier_end(peers)


class Link:
    def __init__(self, send_sems, recv_sems):
        self.send_sems, self.recv_sems, self.sent = send_sems, recv_sems, []

    def send(self, src, dst, peer):
        k = len(self.sent)
        copy = pltpu.make_async_remote_copy(
            src_ref=src, dst_ref=dst, send_sem=self.send_sems.at[k], recv_sem=self.recv_sems.at[k],
            device_id=peer, device_id_type=MESH,
        )
        copy.start()
        self.sent.append(copy)
        return copy

    def drain(self):
        for copy in self.sent:
            copy.wait_send()


def spread(link, block, r, peers):
    plus, minus = peers[0], peers[2]

    def go(k, half, peer):
        return link.send(block(k, half), block(k, half), peer)

    from_left = [go(r, 0, plus)]
    from_right = [go(r, 1, minus)]
    from_left.append(go(r, 1, plus))
    from_right.append(go(r, 0, minus))
    yield
    from_left[0].wait_recv()
    far = [go((r + 3) % 4, 0, plus)]
    from_right[0].wait_recv()
    far.append(go((r + 1) % 4, 1, minus))
    yield
    for copy in (from_left[1], from_right[1]):
        copy.wait_recv()
    yield
    for copy in far:
        copy.wait_recv()
    yield


def collect(link, part, relay, sums, inbox, r, peers):
    plus, minus = peers[0], peers[2]
    left, right, far = (r + 3) % 4, (r + 1) % 4, (r + 2) % 4
    up = link.send(part(far, 0), relay.at[0], plus)
    down = link.send(part(far, 1), relay.at[1], minus)
    last = [
        link.send(part(right, 1), inbox(0, 1), plus),
        link.send(part(left, 0), inbox(1, 0), minus),
    ]
    yield
    up.wait_recv()
    sums[0] = (part(right, 0)[...].astype(F32) + relay[0].astype(F32)).astype(BF16)
    last.append(link.send(sums.at[0], inbox(0, 0), plus))
    down.wait_recv()
    sums[1] = (part(left, 1)[...].astype(F32) + relay[1].astype(F32)).astype(BF16)
    last.append(link.send(sums.at[1], inbox(1, 1), minus))
    yield
    for copy in last:
        copy.wait_recv()
    yield


def run(steps):
    for _ in steps:
        pass


def token_halves(ref):
    return lambda k, half: ref.at[k, pl.ds(64 * half, 64)]


def collect_tokens(link, ref, relay, sums, inbox, me):
    return collect(link, token_halves(ref), relay, sums, token_halves(inbox), me.t, me.ts)


def spread_tokens(link, ref, me):
    return spread(link, token_halves(ref), me.t, me.ts)


def core_rows(c):
    first = pl.multiple_of(32 * c, 32)
    return pl.ds(first, 32), pl.ds(first, 16), pl.ds(pl.multiple_of(32 * c + 16, 16), 16)


def gather_layer(link, own_sem, shard, w, me):
    c, x, z = me.c, me.x, me.z
    whole, a, b = core_rows(c)
    own = pltpu.make_async_copy(shard, w.at[x, z, whole], own_sem)
    own.start()
    first = []
    for o in range(3):
        first.append(link.send(shard.at[pl.ds(0, 16)], w.at[x, z, a], me.zs[o]))
        first.append(link.send(shard.at[pl.ds(16, 16)], w.at[x, z, b], me.xs[o]))
    yield
    own.wait()
    for copy in first:
        copy.wait_recv()
    along_x = spread(link, lambda k, half: w.at[k, pl.ds(2 * half, 2), a], x, me.xs)
    along_z = spread(link, lambda k, half: w.at[pl.ds(2 * half, 2), k, b], z, me.zs)
    next(along_x)
    next(along_z)
    core = []

    def to_core(o):
        block_a = w.at[(x + o) % 4, :, a]
        block_b = w.at[:, (z + o) % 4, b]
        core.append(link.send(block_a, block_a, me.core))
        core.append(link.send(block_b, block_b, me.core))

    to_core(0)
    yield
    next(along_x)
    next(along_z)
    yield
    next(along_x)
    next(along_z)
    to_core(1)
    to_core(3)
    yield
    next(along_x)
    next(along_z)
    to_core(2)
    yield
    for copy in core:
        copy.wait_recv()
    yield


GATHER_COPIES = 6 + 12 + 8


def reduce_rings(link, factors, grads, out_a, out_b, core_in, acc, relay, sums, inbox, me):
    c, x, z = me.c, me.x, me.z
    hid, d_proj, db, scaled = factors
    a, b = pl.ds(0, 16), pl.ds(16, 16)
    arrive = []
    for xx in range(4):
        at = slice(256 * xx, 256 * xx + 256)
        rows_in = dot_tn(hid[:, :, at].reshape(T, 256), d_proj[...]).astype(BF16)
        rows_out = dot_tn(db[:, :, at].reshape(T, 256), scaled[...]).astype(BF16)
        for k in range(8):
            block = slice(32 * k, 32 * k + 32)
            grads[k % 2, xx, k // 2, :, 0:WP] = rows_in[block]
            grads[k % 2, xx, k // 2, :, WP:WALL] = rows_out[block]
        arrive.append(link.send(grads.at[1 - c, xx], core_in.at[xx], me.core))
        if xx % 2 == 1:
            yield
    for xx in range(4):
        arrive[xx].wait_recv()
        acc[xx] = grads[c, xx] + core_in[xx]
    along_x = collect(
        link, lambda k, half: acc.at[k, pl.ds(2 * half, 2), a], relay.at[0], sums.at[0],
        lambda d, half: inbox.at[0, d, pl.ds(2 * half, 2)], x, me.xs,
    )
    next(along_x)
    along_z = collect(
        link, lambda k, half: acc.at[pl.ds(2 * half, 2), k, b], relay.at[1], sums.at[1],
        lambda d, half: inbox.at[1, d, pl.ds(2 * half, 2)], z, me.zs,
    )
    next(along_z)
    yield
    next(along_x)
    next(along_z)
    yield
    next(along_x)
    out_a[...] = (
        acc[x, :, a].astype(F32) + inbox[0, 0].astype(F32) + inbox[0, 1].astype(F32)
    ).astype(BF16)
    next(along_z)
    out_b[...] = (
        acc[:, z, b].astype(F32) + inbox[1, 0].astype(F32) + inbox[1, 1].astype(F32)
    ).astype(BF16)
    yield


RING_COPIES = 4 + 12


def reduce_last(link, sum_a, sum_b, out, bc_all, last_in, me):
    c, x, z = me.c, me.x, me.z
    last_a = [link.send(sum_a.at[(z + o + 1) % 4], last_in.at[0, o], me.zs[o]) for o in range(3)]
    last_b = [link.send(sum_b.at[(x + o + 1) % 4], last_in.at[1, o], me.xs[o]) for o in range(3)]
    yield
    rows, rows_a, rows_b = core_rows(c)
    for k, (copies, at, mine) in enumerate(((last_a, rows_a, sum_a.at[z]), (last_b, rows_b, sum_b.at[x]))):
        for copy in copies:
            copy.wait_recv()
        out[at, :] = (
            mine[...].astype(F32)
            + last_in[k, 0].astype(F32) + last_in[k, 1].astype(F32) + last_in[k, 2].astype(F32)
        )
    bc_all[me.t, rows, :] = out[rows, 1024:1280]
    swap = [link.send(out.at[rows], out.at[rows], me.core)]
    for peer in [me.core] + me.ts + me.far_ts:
        mine = bc_all.at[me.t, rows]
        swap.append(link.send(mine, mine, peer))
    yield
    for copy in swap:
        copy.wait_recv()
    yield


LAST_COPIES = 6 + 8


def ring_scratch():
    return [
        VM((2, 4, 4, 32, WALL), BF16),
        VM((4, 4, 32, WALL), BF16), VM((4, 4, 32, WALL), BF16),
        VM((2, 2, 2, 16, WALL), BF16), VM((2, 2, 2, 16, WALL), BF16),
        VM((2, 2, 4, 16, WALL), BF16),
    ]


def last_scratch():
    return [VM((64, WALL), F32), VM((4, 64, 2 * N), F32), VM((2, 3, 16, WALL), BF16)]


def token_scratch():
    return [VM((2, 64, D), BF16), VM((2, 64, D), BF16), VM((2, ROWS, D), BF16)]


def dma_sems(n):
    return pltpu.SemaphoreType.DMA((n,))


def link_scratch(*counts):
    return [pltpu.SemaphoreType.DMA((n,)) for n in counts for _ in range(2)]


def input_norm(u, gain):
    return u * lax.rsqrt(jnp.mean(u * u, axis=-1, keepdims=True) + EPSILON) * gain


def gain_of(par, layer):
    return par[layer, 0:1, 1408:2432]


def gather_kernel(
    lengths, w_in, w_bc, w_dt, w_out, conv_w, flat, u0, cot,
    w0, shard1, par, hid, db, valid,
    wsh, shards, turned, own_sem, g_s, g_r, e_s, e_r, h_s, h_r, d_s, d_r,
):
    me = Peers()
    c, t = me.c, me.t
    barrier_start(me.near_dp())
    wsh[:, 0:WZX] = w_in[...]
    wsh[:, 1024:1280] = w_bc[...]
    dt_rows = jnp.concatenate([w_dt[...].astype(F32), jnp.zeros((HL, 64), F32)], axis=1)
    dt_rows = jnp.concatenate([dt_rows, jnp.zeros((120, 128), F32)], axis=0)
    wsh[:, 1280:1408] = jnp.transpose(dt_rows)[0:64].astype(BF16)
    wsh[:, WP:WALL] = w_out[...]
    shards[c] = wsh[core_rows(c)[0], :]
    own = pl.ds(pl.multiple_of(CH * t, CH), CH)
    par[c] = jnp.zeros((8, 2432), F32)
    par[c, 0:4, 0:512] = conv_w[:, own]
    par[c, 0:4, 512:768] = conv_w[:, DI : DI + 2 * N]
    par[c, 4:5, 0:512] = flat[:, own]
    par[c, 4:5, 512:768] = flat[:, DI : DI + 2 * N]
    by_row = jnp.broadcast_to(flat[:, 5376:5504], (8, 128))
    row = iota((8, 128), 0)
    by_row = jnp.where(
        row == 0, by_row,
        jnp.where(row == 1, pltpu.roll(by_row, 128 - H, 1), pltpu.roll(by_row, 128 - 2 * H, 1)),
    )
    turned[...] = jnp.transpose(jnp.concatenate([by_row, jnp.zeros((120, 128), F32)], axis=0))
    heads = turned[pl.ds(pl.multiple_of(HL * t, HL), HL), :]
    par[c, :, 768:896] = jnp.where(iota((8, 128), 1) == 1, -jnp.exp(heads), heads)
    par[c, 0:1, 896:1408] = flat[:, pl.ds(pl.multiple_of(2304 + CH * t, 256), CH)]
    par[c, 0:1, 1408:2432] = flat[:, 4352:5376]
    end = lengths[c, 0, 0] + lengths[c, 0, 1]
    valid[...] = jnp.where(iota((ROWS, 128), 0) + ROWS * t < end, 1.0, 0.0).astype(F32)
    barrier_end(me.near_dp())
    early, weights = Link(e_s, e_r), Link(g_s, g_r)
    theirs = early.send(wsh.at[core_rows(1 - c)[0]], shards.at[c], me.core)
    par_copy = early.send(par.at[c], par.at[c], me.core)
    for j in range(8):
        db[t, :, tile(j)] = (cot[:, tile(j)] * valid[...]).astype(BF16)
    theirs.wait_recv()
    layer0 = gather_layer(weights, own_sem.at[0], shards.at[0], w0, me)
    next(layer0)
    par_copy.wait_recv()
    hid[t] = input_norm(u0[...], gain_of(par, 0)).astype(BF16)
    tokens, branch = Link(h_s, h_r), Link(d_s, d_r)
    hid_steps = spread_tokens(tokens, hid, me)
    db_steps = spread_tokens(branch, db, me)
    next(hid_steps)
    next(layer0)
    next(db_steps)
    next(layer0)
    next(hid_steps)
    shard1[...] = shards[1]
    next(layer0)
    next(db_steps)
    run(layer0)
    run(hid_steps)
    run(db_steps)
    for link in (early, weights, tokens, branch):
        link.drain()


def gather(*arrays):
    return pl.pallas_call(
        gather_kernel,
        out_shape=(
            jax.ShapeDtypeStruct((4, 4, 64, WALL), BF16),
            jax.ShapeDtypeStruct((32, WALL), BF16),
            jax.ShapeDtypeStruct((2, 8, 2432), F32),
            jax.ShapeDtypeStruct((4, ROWS, D), BF16),
            jax.ShapeDtypeStruct((4, ROWS, D), BF16),
            jax.ShapeDtypeStruct((ROWS, 128), F32),
        ),
        in_specs=[pl.BlockSpec(memory_space=pltpu.SMEM)] + vmem_specs(8),
        out_specs=tuple(vmem_specs(6)),
        scratch_shapes=[
            VM((64, WALL), BF16), VM((2, 32, WALL), BF16), VM((128, 128), F32),
            dma_sems(1),
        ]
        + link_scratch(GATHER_COPIES, 2, 6, 6),
        compiler_params=pltpu.CompilerParams(
            collective_id=0, has_side_effects=True, vmem_limit_bytes=6 << 20
        ),
        name="gather_weights",
    )(*arrays)


def column_of(row):
    return jnp.transpose(jnp.broadcast_to(row, (128, 128)))


def middle_kernel(
    part, st, u0, valid, par, shard1, total, u_next, s_out, hid, w1,
    relay, sums, inbox, sbuf, own_sem, g_s, g_r, p_s, p_r, b_s, b_r, h_s, h_r,
):
    me = Peers()
    c, t = me.c, me.t
    greet([me.core] + me.xs + me.zs + me.ts)
    weights, tokens, small, spreading = Link(g_s, g_r), Link(p_s, p_r), Link(b_s, b_r), Link(h_s, h_r)
    sum_steps = collect_tokens(tokens, part, relay, sums, inbox, me)
    next(sum_steps)
    stats = [small.send(st.at[(t + o + 1) % 4], sbuf.at[o], me.ts[o]) for o in range(3)]
    layer1 = gather_layer(weights, own_sem.at[0], shard1, w1, me)
    next(layer1)
    next(sum_steps)
    next(layer1)
    for copy in stats:
        copy.wait_recv()
    s_row = lax.rsqrt((st[t] + sbuf[0] + sbuf[1] + sbuf[2]) / DI + EPSILON)
    s_out[...] = s_row
    scale = column_of(s_row[0:1]) * valid[...]
    next(layer1)
    run(sum_steps)
    total[...] = part[t].astype(F32) + inbox[0].astype(F32) + inbox[1].astype(F32)
    for j in range(8):
        u_next[:, tile(j)] = u0[:, tile(j)] + scale * total[:, tile(j)]
    hid[t] = input_norm(u_next[...], gain_of(par, 1)).astype(BF16)
    hid_steps = spread_tokens(spreading, hid, me)
    next(hid_steps)
    next(layer1)
    next(hid_steps)
    run(layer1)
    run(hid_steps)
    for link in (weights, tokens, small, spreading):
        link.drain()


def middle(*arrays):
    return pl.pallas_call(
        middle_kernel,
        out_shape=(
            jax.ShapeDtypeStruct((ROWS, D), F32),
            jax.ShapeDtypeStruct((ROWS, D), F32),
            jax.ShapeDtypeStruct((8, 128), F32),
            jax.ShapeDtypeStruct((4, ROWS, D), BF16),
            jax.ShapeDtypeStruct((4, 4, 64, WALL), BF16),
        ),
        in_specs=vmem_specs(6),
        out_specs=tuple(vmem_specs(5)),
        scratch_shapes=token_scratch()
        + [VM((3, 8, 128), F32), pltpu.SemaphoreType.DMA((1,))]
        + link_scratch(GATHER_COPIES, 6, 3, 6),
        compiler_params=pltpu.CompilerParams(
            collective_id=1, has_side_effects=True, vmem_limit_bytes=6 << 20
        ),
        name="sum_and_gather_tokens",
    )(*arrays)


def stats_kernel(st, coef, buf, a_s, a_r):
    me = Peers()
    greet(me.ts)
    link = Link(a_s, a_r)
    copies = [link.send(st, buf.at[me.t], peer) for peer in me.ts]
    buf[me.t] = st[...]
    for copy in copies:
        copy.wait_recv()
    for i in range(4):
        both = buf[0, i] + buf[1, i] + buf[2, i] + buf[3, i]
        s = lax.rsqrt(both[0:1] / DI + EPSILON)
        k = s * s * s * (both[1:2] / DI)
        row = iota((8, 128), 0)
        coef[i] = jnp.where(row == 0, s, jnp.where(row == 1, k, 0.0))
    link.drain()


def stats(st):
    return pl.pallas_call(
        stats_kernel,
        out_shape=jax.ShapeDtypeStruct((4, 8, 128), F32),
        in_specs=vmem_specs(1),
        out_specs=pl.BlockSpec(memory_space=VM),
        scratch_shapes=[VM((4, 4, 8, 128), F32)] + link_scratch(3),
        compiler_params=pltpu.CompilerParams(
            collective_id=2, has_side_effects=True, vmem_limit_bytes=1 << 20
        ),
        name="sum_stats",
    )(st)


def norm_back(u, gain, g, d_hidden):
    r = lax.rsqrt(jnp.mean(u * u, axis=-1, keepdims=True) + EPSILON)
    mean = jnp.mean(u * gain * d_hidden, axis=-1, keepdims=True)
    d_u = g + r * gain * d_hidden - u * (r * r * r) * mean
    return d_u, jnp.sum(u * r * d_hidden, axis=0, keepdims=True)


def back_middle_kernel(
    dh, u, cot, valid, par, total0, s0, hid1, d_proj1, db1, scaled1, g1, ng, db, coef, sum_a, sum_b,
    relay, sums, inbox, grads, core_in, acc, g_relay, g_sums, g_inbox,
    g_s, g_r, p_s, p_r, b_s, b_r, h_s, h_r,
):
    me = Peers()
    c, t = me.c, me.t
    greet(me.near_dp())
    weights, tokens, small, spreading = Link(g_s, g_r), Link(p_s, p_r), Link(b_s, b_r), Link(h_s, h_r)
    sum_steps = collect_tokens(tokens, dh, relay, sums, inbox, me)
    next(sum_steps)
    layer1 = reduce_rings(
        weights, (hid1, d_proj1, db1, scaled1), grads, sum_a, sum_b, core_in, acc,
        g_relay, g_sums, g_inbox, me,
    )
    next(layer1)
    next(sum_steps)
    next(layer1)
    next(layer1)
    run(sum_steps)
    total = dh[t].astype(F32) + inbox[0].astype(F32) + inbox[1].astype(F32)
    d_u, gain_term = norm_back(u[...], gain_of(par, 1), cot[...], total)
    g1[...] = d_u
    ng[...] = gain_term
    mean = jnp.zeros((ROWS, 128), F32)
    for j in range(8):
        d_branch = (g1[:, tile(j)] * valid[...]).astype(BF16)
        db[t, :, tile(j)] = d_branch
        mean = mean + d_branch.astype(F32) * total0[:, tile(j)]
    db_steps = spread_tokens(spreading, db, me)
    next(db_steps)
    mean = jnp.broadcast_to(jnp.sum(mean, axis=-1, keepdims=True), (128, 128))
    mean_row = jnp.transpose(mean)[0:8] / DI
    s = s0[0:1, :]
    row = iota((8, 128), 0)
    coef[t] = jnp.where(row == 0, s, jnp.where(row == 1, s * s * s * mean_row, 0.0))
    coef_copies = [small.send(coef.at[t], coef.at[t], peer) for peer in me.ts]
    next(layer1)
    next(db_steps)
    next(layer1)
    run(db_steps)
    for copy in coef_copies:
        copy.wait_recv()
    for link in (weights, tokens, small, spreading):
        link.drain()


def back_middle(*arrays):
    return pl.pallas_call(
        back_middle_kernel,
        out_shape=(
            jax.ShapeDtypeStruct((ROWS, D), F32),
            jax.ShapeDtypeStruct((1, D), F32),
            jax.ShapeDtypeStruct((4, ROWS, D), BF16),
            jax.ShapeDtypeStruct((4, 8, 128), F32),
            jax.ShapeDtypeStruct((4, 16, WALL), BF16),
            jax.ShapeDtypeStruct((4, 16, WALL), BF16),
        ),
        in_specs=vmem_specs(11),
        out_specs=tuple(vmem_specs(6)),
        scratch_shapes=token_scratch() + ring_scratch() + link_scratch(RING_COPIES, 6, 3, 6),
        compiler_params=pltpu.CompilerParams(
            collective_id=3, has_side_effects=True, vmem_limit_bytes=14 << 20
        ),
        name="back_sum_and_gather",
    )(*arrays)


def finish_kernel(
    dh, part, u0, u1, g1, valid, par, coef1, ng1, sums0, heads0, sums1, heads1, sum_a1, sum_b1,
    hid0, d_proj0, db0, scaled0,
    lo, lg, smt, picked, o_bc,
    relay, sums, inbox, relay2, sums2, inbox2, los, lgs, sms, smr, smz, smx, sum_a0, sum_b0,
    grads, core_in, acc, g_relay, g_sums, g_inbox, w_grad0, bc_all0, last_in0, w_grad1, bc_all1, last_in1,
    g_s, g_r, f_s, f_r, l_s, l_r, p_s, p_r, q_s, q_r, b_s, b_r,
):
    me = Peers()
    c, x, z, t = me.c, me.x, me.z, me.t
    greet(me.everyone())
    weights, final0, final1 = Link(g_s, g_r), Link(f_s, f_r), Link(l_s, l_r)
    tokens, tokens2, small = Link(p_s, p_r), Link(q_s, q_r), Link(b_s, b_r)
    back_steps = collect_tokens(tokens, dh, relay, sums, inbox, me)
    next(back_steps)
    last1 = reduce_last(final1, sum_a1, sum_b1, w_grad1, bc_all1, last_in1, me)
    next(last1)
    layer0 = reduce_rings(
        weights, (hid0, d_proj0, db0, scaled0), grads, sum_a0, sum_b0, core_in, acc,
        g_relay, g_sums, g_inbox, me,
    )
    next(layer0)
    next(back_steps)
    next(layer0)
    next(layer0)
    next(last1)
    out_steps = collect_tokens(tokens2, part, relay2, sums2, inbox2, me)
    next(out_steps)
    los[0] = u1[...]
    lgs[1] = g1[...]
    run(back_steps)
    total = dh[t].astype(F32) + inbox[0].astype(F32) + inbox[1].astype(F32)
    d_u, gain_term = norm_back(u0[...], gain_of(par, 0), g1[...], total)
    lgs[0] = d_u
    lg_copy = small.send(lgs.at[1 - c], lg.at[c], me.core)
    lg[c] = lgs[c]
    next(layer0)
    next(out_steps)
    sms[...] = jnp.zeros_like(sms)
    for layer, (by_channel, heads, term) in enumerate(
        ((sums0, heads0, gain_term), (sums1, heads1, ng1[...]))
    ):
        sms[layer, 0:8, :] = by_channel[:, 0:512]
        sms[layer, 8:16, 0:256] = by_channel[:, 512:768]
        sms[layer, 8:16, 256:384] = heads[...]
        sms[layer, 16:17, :] = term[:, 0:512]
        sms[layer, 17:18, :] = term[:, 512:1024]
    sm_copy = small.send(sms.at[1 - c], smr, me.core)
    run(last1)
    sm_copy.wait_recv()
    smz[z] = sms[c] + smr[...]
    sz = [small.send(smz.at[z], smz.at[z], peer) for peer in me.zs]
    next(layer0)
    last0 = reduce_last(final0, sum_a0, sum_b0, w_grad0, bc_all0, last_in0, me)
    next(last0)
    for copy in sz:
        copy.wait_recv()
    smx[x] = smz[0] + smz[1] + smz[2] + smz[3]
    sx = [small.send(smx.at[x], smx.at[x], peer) for peer in me.xs]
    run(out_steps)
    los[1] = part[t].astype(F32) + inbox2[0].astype(F32) + inbox2[1].astype(F32)
    scale = column_of(coef1[t][0:1]) * valid[...]
    for j in range(8):
        los[1, :, tile(j)] = u1[:, tile(j)] + scale * los[1, :, tile(j)]
    lo_copy = small.send(los.at[1 - c], lo.at[c], me.core)
    lo[c] = los[c]
    for copy in sx:
        copy.wait_recv()
    smt[t] = smx[0] + smx[1] + smx[2] + smx[3]
    to_all = [small.send(smt.at[t], smt.at[t], peer) for peer in me.ts]
    next(last0)
    run(last0)
    picked[...] = jnp.where(c == 0, w_grad0[...], w_grad1[...])
    rows = pl.ds(pl.multiple_of(16 * t, 16), 16)
    bc0 = bc_all0[0, rows, :] + bc_all0[1, rows, :] + bc_all0[2, rows, :] + bc_all0[3, rows, :]
    bc1 = bc_all1[0, rows, :] + bc_all1[1, rows, :] + bc_all1[2, rows, :] + bc_all1[3, rows, :]
    o_bc[...] = jnp.where(c == 0, bc0, bc1)
    for copy in to_all + [lo_copy, lg_copy]:
        copy.wait_recv()
    for link in (weights, final0, final1, tokens, tokens2, small):
        link.drain()


def finish(*arrays):
    return pl.pallas_call(
        finish_kernel,
        out_shape=(
            jax.ShapeDtypeStruct((2, ROWS, D), F32),
            jax.ShapeDtypeStruct((2, ROWS, D), F32),
            jax.ShapeDtypeStruct((4, 24, 512), F32),
            jax.ShapeDtypeStruct((64, WALL), F32),
            jax.ShapeDtypeStruct((16, 2 * N), F32),
        ),
        in_specs=vmem_specs(19),
        out_specs=tuple(vmem_specs(5)),
        scratch_shapes=token_scratch() + token_scratch()
        + [
            VM((2, ROWS, D), F32), VM((2, ROWS, D), F32),
            VM((2, 24, 512), F32), VM((24, 512), F32),
            VM((4, 24, 512), F32), VM((4, 24, 512), F32),
            VM((4, 16, WALL), BF16), VM((4, 16, WALL), BF16),
        ]
        + ring_scratch() + last_scratch() + last_scratch()
        + link_scratch(RING_COPIES, LAST_COPIES, LAST_COPIES, 6, 6, 12),
        compiler_params=pltpu.CompilerParams(
            collective_id=4, has_side_effects=True, vmem_limit_bytes=22 << 20
        ),
        name="sum_gradients",
    )(*arrays)


def write_kernel(lo, lg, smt, picked, bc, *rest):
    outs, (in_part, dt, conv_w, conv_b, gain, norm, heads, sem) = rest[:13], rest[13:]
    (o_lo, o_lg, o_norm, o_in, o_bc, o_dt, o_cw, o_cb, o_dtb, o_alog, o_skip, o_gain, o_out) = outs
    copies = []

    def write(src, dst):
        copy = pltpu.make_async_copy(src, dst, sem.at[len(copies)])
        copy.start()
        copies.append(copy)

    write(lo, o_lo)
    write(lg, o_lg)
    write(bc, o_bc)
    in_part[:, 0, :] = picked[:, 0:512]
    in_part[:, 1, :] = picked[:, 512:1024]
    write(in_part, o_in)
    write(picked.at[:, pl.ds(WP, CH)], o_out)
    dt_rows = jnp.concatenate([picked[:, 1280:1408], jnp.zeros((64, 128), F32)], axis=0)
    dt[...] = jnp.transpose(dt_rows)[0:HL, 0:64]
    write(dt, o_dt)
    shared = smt[0, 8:24] + smt[1, 8:24] + smt[2, 8:24] + smt[3, 8:24]
    norm[:, 0:512] = shared[8:9]
    norm[:, 512:1024] = shared[9:10]
    write(norm, o_norm)
    conv_w[:, DI : DI + 2 * N] = shared[0:4, 0:256]
    conv_b[:, DI : DI + 2 * N] = shared[4:5, 0:256]
    for k in range(4):
        at = slice(512 * k, 512 * k + 512)
        conv_w[:, at] = smt[k, 0:4, :]
        conv_b[:, at] = smt[k, 4:5, :]
        gain[:, at] = smt[k, 5:6, :]
    write(conv_w, o_cw)
    write(conv_b, o_cb)
    write(gain, o_gain)
    all_heads = smt[0, 8:16, 256:384]
    for k in range(1, 4):
        all_heads = all_heads + pltpu.roll(smt[k, 8:16, 256:384], HL * k, 1)
    for k, out in ((0, o_dtb), (1, o_alog), (2, o_skip)):
        heads[k] = all_heads[k : k + 1, 0:H]
        write(heads.at[k], out)
    for copy in copies:
        copy.wait()


def write_outputs(*arrays):
    hbm_spec = pl.BlockSpec(memory_space=pltpu.HBM)
    shapes = [
        (2, ROWS, D), (2, ROWS, D), (1, D), (64, 2, CH), (16, 2 * N), (HL, 64), (CONV, DI + 2 * N),
        (1, DI + 2 * N), (1, H), (1, H), (1, H), (1, DI), (64, CH),
    ]
    return pl.pallas_call(
        write_kernel,
        out_shape=tuple(jax.ShapeDtypeStruct(shape, F32) for shape in shapes),
        in_specs=vmem_specs(5),
        out_specs=(hbm_spec,) * 13,
        scratch_shapes=[
            VM((64, 2, CH), F32), VM((HL, 64), F32), VM((CONV, DI + 2 * N), F32),
            VM((1, DI + 2 * N), F32), VM((1, DI), F32), VM((1, D), F32), VM((3, 1, H), F32),
            pltpu.SemaphoreType.DMA((13,)),
        ],
        compiler_params=pltpu.CompilerParams(vmem_limit_bytes=6 << 20),
        name="write_outputs",
    )(*arrays)


def body(
    activations, cotangent, lengths, norm_gain, in_weight, bc_weight, dt_weight, conv_weight,
    conv_bias, dt_bias, a_log, d_skip, gated_gain, out_weight,
):
    section = lax.axis_index("section")
    u0 = lax.dynamic_index_in_dim(activations, section, 0, keepdims=False)
    cot = lax.dynamic_index_in_dim(cotangent, section, 0, keepdims=False)
    flat = jnp.concatenate(
        [conv_bias, gated_gain, norm_gain, dt_bias, a_log, d_skip, jnp.zeros((1, 32), F32)], axis=1
    )
    w0, shard1, par, hid0, db1, valid = gather(
        lengths, in_weight[0].reshape(64, WZX), bc_weight[0], dt_weight[0].T, out_weight[0].T,
        conv_weight[0], flat, u0, cot,
    )
    proj0, kept0, part0, y0, st0 = mixer_fwd(0, lengths, par, hid0, w0)
    total0, u1, s0, hid1, w1 = middle(part0, st0, u0, valid, par, shard1)
    proj1, kept1, part1, y1, st1, d_scaled1 = mixer_fwd(1, lengths, par, hid1, w1, db1)
    coef1 = stats(st1)
    dh1, dp1, sc1, sums1, heads1 = mixer_bwd(1, lengths, par, w1, proj1, kept1, y1, coef1, d_scaled1)
    g1, ng1, db0, coef0, sum_a1, sum_b1 = back_middle(
        dh1, u1, cot, valid, par, total0, s0, hid1, dp1, db1, sc1
    )
    dh0, dp0, sc0, sums0, heads0 = mixer_bwd(0, lengths, par, w0, proj0, kept0, y0, coef0, db0)
    outs = write_outputs(
        *finish(
            dh0, part1, u0, u1, g1, valid, par, coef1, ng1,
            sums0, heads0, sums1, heads1, sum_a1, sum_b1, hid0, dp0, db0, sc0,
        )
    )
    outs = [out.T if k in (5, 12) else out for k, out in enumerate(outs)]
    plain = (2, 8, 9, 10, 7, 11)
    return tuple(out if k in plain else out[None] for k, out in enumerate(outs))


def solution(mesh):
    return jax.shard_map(
        body,
        mesh=mesh,
        in_specs=(
            P(None, ("dp", "tensor"), None),
            P(None, ("dp", "tensor"), None),
            P(None, "dp", None),
            P("section", None),
            P("section", "dp", None, "tensor"),
            P("section", "dp", None),
            P("section", "dp", "tensor"),
            P("section", None, None),
            P("section", None),
            P("section", None),
            P("section", None),
            P("section", None),
            P("section", None),
            P("section", "tensor", "dp"),
        ),
        out_specs=(
            P("section", None, ("dp", "tensor"), None),
            P("section", None, ("dp", "tensor"), None),
            P("section", None),
            P("section", "dp", None, "tensor"),
            P("section", ("dp", "tensor"), None),
            P("section", "dp", "tensor"),
            P("section", None, None),
            P("section", None),
            P("section", None),
            P("section", None),
            P("section", None),
            P("section", None),
            P("section", "tensor", "dp"),
        ),
        check_vma=False,
    )
```

```python
import functools

import jax
import jax.numpy as jnp
from jax import lax
from jax.experimental import pallas as pl
from jax.experimental.pallas import tpu as pltpu
from jax.sharding import PartitionSpec as P

D = 1024
DI = 2048
H = 32
N = 128
CONV = 4
T = 512
ROWS = 128
CH = 512
HL = 8
WZX = 1024
WP = 1408
WALL = 1920
NDP = 16
EPSILON = 1e-05
LOG2E = 1.4426950408889634
NEG = -1e30
F32 = jnp.float32
BF16 = jnp.bfloat16
MESH = pl.DeviceIdType.MESH
VM = pltpu.VMEM
FWD_VMEM = 12 << 20
BWD_VMEM = 16 << 20


def dot_nn(a, b):
    return lax.dot_general(a, b, (((1,), (0,)), ((), ())), preferred_element_type=F32)


def dot_nt(a, b):
    return lax.dot_general(a, b, (((1,), (1,)), ((), ())), preferred_element_type=F32)


def dot_tn(a, b):
    return lax.dot_general(a, b, (((0,), (0,)), ((), ())), preferred_element_type=F32)


def pieces(v, count):
    parts = []
    for _ in range(count):
        part = v.astype(BF16)
        parts.append(part)
        v = v - part.astype(F32)
    return parts


def sum_rows_nt(selector, v, count):
    return sum(dot_nt(selector, part) for part in pieces(v, count))


def rows_times(v, matrix):
    a, b, c = pieces(v, 3)
    stacked = jnp.concatenate([a.astype(F32), b.astype(F32), c.astype(F32), jnp.zeros_like(v)], 0)
    out = dot_nn(stacked.astype(BF16), matrix)
    return out[0:8] + out[8:16] + out[16:24]


def iota(shape, dim):
    return lax.broadcasted_iota(jnp.int32, shape, dim)


def segment_of(position, e0, e1):
    return (position >= e0).astype(jnp.int32) + (position >= e1).astype(jnp.int32)


def conv_masks(e0, e1):
    p = iota((T, 128), 0)
    seg = segment_of(p, e0, e1)
    return [
        jnp.where((p >= k) & (segment_of(p - k, e0, e1) == seg), 1.0, 0.0).astype(F32)
        for k in range(1, CONV)
    ]


def conv_pre(v, masks, cw, lanes):
    pre = cw[CONV : CONV + 1, lanes] + cw[CONV - 1 : CONV, lanes] * v
    for k in range(1, CONV):
        pre = pre + cw[CONV - 1 - k : CONV - k, lanes] * (masks[k - 1] * pltpu.roll(v, k, 0))
    return pre


def sigmoid(v):
    return 0.5 * jnp.tanh(0.5 * v) + 0.5


def steps_of(dt_tile, hp_ref):
    raw = jnp.transpose(dt_tile)[0:HL] + hp_ref[:, 0:1]
    step = jnp.maximum(raw, 0.0) + jnp.log1p(jnp.exp(-jnp.abs(raw)))
    rate = hp_ref[:, 1:2]
    upper = jnp.where(iota((T, T), 0) <= iota((T, T), 1), 1.0, 0.0).astype(BF16)
    cum = rows_times(step * rate, upper) * LOG2E
    columns = jnp.transpose(
        jnp.concatenate([cum, step, jnp.zeros((112, T), F32)], axis=0)
    )
    return raw, step, cum, columns


def pair_columns(columns, first, j, rows=T):
    low = iota((rows, 128), 1) < 64
    return jnp.where(
        low,
        jnp.broadcast_to(columns[:, first + 2 * j : first + 2 * j + 1], (rows, 128)),
        jnp.broadcast_to(columns[:, first + 2 * j + 1 : first + 2 * j + 2], (rows, 128)),
    )


def tile(j):
    return slice(128 * j, 128 * j + 128)


def layer_params(par, layer):
    return (
        par.at[layer, :, pl.ds(0, 768)],
        par.at[layer, :, pl.ds(768, 128)],
        par.at[layer, :, pl.ds(896, 512)],
    )


def skip_row(hp, j):
    low = iota((1, 128), 1) < 64
    first = jnp.broadcast_to(hp[2 * j : 2 * j + 1, 2:3], (1, 128))
    second = jnp.broadcast_to(hp[2 * j + 1 : 2 * j + 2, 2:3], (1, 128))
    return jnp.where(low, first, second)


def segment_ends(lengths):
    c = lax.axis_index("section")
    first = lengths[c, 0, 0]
    return first, first + lengths[c, 0, 1]


def project(hid, w, proj):
    tokens = hid[...].reshape(T, D)
    for first, width in ((0, 512), (512, 512), (1024, 384)):
        at = slice(first, first + width)
        proj[:, at] = dot_nn(tokens, w[:, :, :, at].reshape(D, width))


def scale_back(db, w, d_scaled):
    d_scaled[...] = dot_nn(db[...].reshape(T, D), w[:, :, :, WP:WALL].reshape(D, CH))


def mixer_fwd_kernel(layer, lens, par, hid, w, *rest):
    with_grad = layer == 1
    if with_grad:
        db, proj, kept, part, yssd, coef, d_scaled, gg, inn, xb, bb, cb, cumr, colr, *rest = rest
        st, buf, send_sems, recv_sems = rest
        me = Peers()
        barrier_start(me.ts)
        scale_back(db, w, d_scaled)
    else:
        proj, kept, part, yssd, st, gg, inn, xb, bb, cb, cumr, colr = rest
    cw, hp, rows = layer_params(par, layer)
    project(hid, w, proj)
    e0, e1 = segment_ends(lens)
    masks = conv_masks(e0, e1)
    _, _, cum, columns = steps_of(proj[:, 1280:1408], hp)
    cumr[...] = cum
    colr[...] = columns
    for j in range(4):
        v = proj[:, 512 + 128 * j : 640 + 128 * j]
        pre = conv_pre(v, masks, cw, tile(j))
        kept[:, tile(j)] = pre
        act = pre * sigmoid(pre)
        inn[:, tile(j)] = act
        xb[:, tile(j)] = (act * pair_columns(columns, HL, j)).astype(BF16)
    for j, ref in ((0, bb), (1, cb)):
        lanes = slice(512 + 128 * j, 640 + 128 * j)
        pre = conv_pre(proj[:, 1024 + 128 * j : 1152 + 128 * j], masks, cw, lanes)
        kept[:, lanes] = pre
        ref[...] = (pre * sigmoid(pre)).astype(BF16)
    low = iota((128, 128), 1) < 64
    for i in range(4):
        n = 128 * (i + 1)
        here = slice(128 * i, n)
        scores = dot_nt(cb[here, :], bb[0:n, :])
        p = iota((128, n), 0) + 128 * i
        q = iota((128, n), 1)
        bias = jnp.where((p >= q) & (segment_of(p, e0, e1) == segment_of(q, e0, e1)), 0.0, NEG).astype(F32)
        for j in range(4):
            mixing = []
            for h in (2 * j, 2 * j + 1):
                decay = jnp.exp2(colr[here, h : h + 1] - cumr[h : h + 1, 0:n] + bias)
                mixing.append((scores * decay).astype(BF16))
            both = dot_nn(jnp.concatenate(mixing, axis=0), xb[0:n, tile(j)])
            yssd[here, tile(j)] = jnp.where(low, both[0:128], both[128:256])
    squares = jnp.zeros((8, T), F32)
    dots = jnp.zeros((8, T), F32)
    ones = jnp.ones((8, 128), BF16)
    for j in range(4):
        z = proj[:, tile(j)]
        gated = (yssd[:, tile(j)] + skip_row(hp, j) * inn[:, tile(j)]) * (z * sigmoid(z))
        gained = gated * rows[0:1, tile(j)]
        gg[:, tile(j)] = gained.astype(BF16)
        squares = squares + sum_rows_nt(ones, gated * gated, 1)
        if with_grad:
            dots = dots + sum_rows_nt(ones, gained * d_scaled[:, tile(j)], 2)
    row = iota((8, T), 0)
    both = jnp.where(row == 0, squares, jnp.where(row == 1, dots, 0.0))
    for i in range(4):
        st[i] = both[:, tile(i)]
    if with_grad:
        exchange = stats_exchange(Link(send_sems, recv_sems), st, buf, coef, me)
        next(exchange)
    for x in range(4):
        columns_out = slice(256 * x, 256 * x + 256)
        branch = dot_nt(gg[...], w[x, :, :, WP:WALL].reshape(256, CH)).astype(BF16)
        part[:, :, columns_out] = branch.reshape(4, ROWS, 256)
    if with_grad:
        run(exchange)


def vmem_specs(count):
    return [pl.BlockSpec(memory_space=VM)] * count


def mixer_fwd(layer, lens, par, hid, w, *db):
    out_shape = [
        jax.ShapeDtypeStruct((T, WP), F32),
        jax.ShapeDtypeStruct((T, 768), F32),
        jax.ShapeDtypeStruct((4, ROWS, D), BF16),
        jax.ShapeDtypeStruct((T, CH), F32),
        jax.ShapeDtypeStruct((4, 8, 128), F32),
    ] + [jax.ShapeDtypeStruct((T, CH), F32)] * layer
    shared = {"collective_id": 2, "has_side_effects": True} if layer else {}
    return pl.pallas_call(
        functools.partial(mixer_fwd_kernel, layer),
        out_shape=tuple(out_shape),
        in_specs=[pl.BlockSpec(memory_space=pltpu.SMEM)] + vmem_specs(3 + len(db)),
        out_specs=tuple(vmem_specs(len(out_shape))),
        scratch_shapes=[
            VM((T, CH), BF16),
            VM((T, CH), F32),
            VM((T, CH), BF16),
            VM((T, N), BF16),
            VM((T, N), BF16),
            VM((8, T), F32),
            VM((T, 128), F32),
        ] + ([VM((4, 8, 128), F32), VM((4, 4, 8, 128), F32)] + link_scratch(3)) * layer,
        compiler_params=pltpu.CompilerParams(vmem_limit_bytes=FWD_VMEM, **shared),
        name="mixer_fwd",
    )(lens, par, hid, w, *db)


def head_selector(j):
    head = 2 * j + (iota((8, 128), 1) >= 64).astype(jnp.int32)
    return jnp.where(iota((8, 128), 0) == head, 1.0, 0.0).astype(BF16)


def back_roll(v, k):
    return pltpu.roll(v, T - k, 0)


def conv_back(d_pre, v, masks, cw, lanes, sums, column0):
    d_v = cw[CONV - 1 : CONV, lanes] * d_pre
    out = slice(column0, column0 + 128)
    sums[CONV : CONV + 1, out] = jnp.sum(d_pre, axis=0, keepdims=True)
    sums[CONV - 1 : CONV, out] = jnp.sum(d_pre * v, axis=0, keepdims=True)
    for k in range(1, CONV):
        masked = masks[k - 1] * d_pre
        d_v = d_v + cw[CONV - 1 - k : CONV - k, lanes] * back_roll(masked, k)
        sums[CONV - 1 - k : CONV - k, out] = jnp.sum(masked * pltpu.roll(v, k, 0), axis=0, keepdims=True)
    return d_v


def mixer_bwd_kernel(layer, lens, par, w, proj, kept, yssd, coef, *rest):
    given, *rest = rest
    dh, d_proj, scaled, sums, heads, inn, xb, dyb, dyf, dx, bb, cb, d_c, cumr, colr, *rest = rest
    if layer == 1:
        d_scaled = given
    else:
        db, d_scaled = given, rest[0]
        scale_back(db, w, d_scaled)
    cw, hp, rows = layer_params(par, layer)
    e0, e1 = segment_ends(lens)
    masks = conv_masks(e0, e1)
    raw, step, cum, columns = steps_of(proj[:, 1280:1408], hp)
    cumr[...] = cum
    colr[...] = columns
    norm_cols = jnp.transpose(jnp.concatenate(
        [jnp.concatenate([coef[i] for i in range(4)], axis=1), jnp.zeros((120, T), F32)], axis=0
    ))
    s_col = jnp.broadcast_to(norm_cols[:, 0:1], (T, 128))
    k_col = jnp.broadcast_to(norm_cols[:, 1:2], (T, 128))
    sums[...] = jnp.zeros_like(sums)
    d_skip = jnp.zeros((8, T), F32)
    for j in range(4):
        selector = head_selector(j)
        pre = kept[:, tile(j)]
        act = pre * sigmoid(pre)
        inn[:, tile(j)] = act
        xb[:, tile(j)] = (act * pair_columns(columns, HL, j)).astype(BF16)
        z = proj[:, tile(j)]
        sig = sigmoid(z)
        gate = z * sig
        y = yssd[:, tile(j)] + skip_row(hp, j) * act
        gated = y * gate
        gs = gated * s_col
        gain = rows[0:1, tile(j)]
        dsc = d_scaled[:, tile(j)]
        scaled[:, tile(j)] = (gs * gain).astype(BF16)
        sums[5:6, tile(j)] = jnp.sum(gs * dsc, axis=0, keepdims=True)
        d_gated = s_col * gain * dsc - gated * k_col
        d_proj[:, tile(j)] = (d_gated * y * (sig * (1.0 + z * (1.0 - sig)))).astype(BF16)
        dy = d_gated * gate
        dyf[:, tile(j)] = dy
        dyb[:, tile(j)] = dy.astype(BF16)
        d_skip = d_skip + sum_rows_nt(selector, dy * act, 2)
    for j, ref in ((0, bb), (1, cb)):
        pre = kept[:, 512 + 128 * j : 640 + 128 * j]
        ref[...] = (pre * sigmoid(pre)).astype(BF16)
    d_c[...] = jnp.zeros_like(d_c)
    low = iota((128, 128), 1) < 64
    zero = jnp.zeros((128, 128), BF16)
    d_b_blocks = []
    for i in range(4):
        first = 128 * i
        n = T - first
        here = slice(first, first + 128)
        scores = dot_nt(bb[here, :], cb[first:T, :])
        q = iota((128, n), 0) + first
        p = iota((128, n), 1) + first
        bias = jnp.where((p >= q) & (segment_of(p, e0, e1) == segment_of(q, e0, e1)), 0.0, NEG).astype(F32)
        d_scores = jnp.zeros((128, n), F32)
        for j in range(4):
            x_tile = xb[here, tile(j)]
            dy_tile = dyb[first:T, tile(j)]
            heads_of = jnp.concatenate([jnp.where(low, x_tile, zero), jnp.where(low, zero, x_tile)], axis=0)
            d_mixing = dot_nt(heads_of, dy_tile)
            mixing = []
            for k in (0, 1):
                h = 2 * j + k
                decay = jnp.exp2(cumr[h : h + 1, first:T] - colr[here, h : h + 1] + bias)
                mixing.append((scores * decay).astype(BF16))
                d_scores = d_scores + d_mixing[128 * k : 128 * k + 128] * decay
            both = dot_nn(jnp.concatenate(mixing, axis=0), dy_tile)
            dx[here, tile(j)] = jnp.where(low, both[0:128], both[128:256])
        d_scores = d_scores.astype(BF16)
        d_b_blocks.append(dot_nn(d_scores, cb[first:T, :]))
        d_c[first:T, :] = d_c[first:T, :] + dot_tn(d_scores, bb[here, :])
    d_cum = jnp.zeros((8, T), F32)
    d_step = jnp.zeros((8, T), F32)
    for j in range(4):
        selector = head_selector(j)
        dxt = dx[:, tile(j)]
        act = inn[:, tile(j)]
        change = dyb[:, tile(j)].astype(F32) * yssd[:, tile(j)] - xb[:, tile(j)].astype(F32) * dxt
        d_cum = d_cum + sum_rows_nt(selector, change, 3)
        d_step = d_step + sum_rows_nt(selector, act * dxt, 2)
        d_act = pair_columns(columns, HL, j) * dxt + skip_row(hp, j) * dyf[:, tile(j)]
        v = proj[:, 512 + 128 * j : 640 + 128 * j]
        pre = kept[:, tile(j)]
        sig = sigmoid(pre)
        d_pre = d_act * (sig * (1.0 + pre * (1.0 - sig)))
        d_proj[:, 512 + 128 * j : 640 + 128 * j] = conv_back(d_pre, v, masks, cw, tile(j), sums, 128 * j).astype(BF16)
    for j in (0, 1):
        lanes = slice(512 + 128 * j, 640 + 128 * j)
        at = slice(1024 + 128 * j, 1152 + 128 * j)
        v = proj[:, at]
        pre = kept[:, lanes]
        sig = sigmoid(pre)
        d_act = jnp.concatenate(d_b_blocks, axis=0) if j == 0 else d_c[...]
        d_pre = d_act * (sig * (1.0 + pre * (1.0 - sig)))
        d_proj[:, at] = conv_back(d_pre, v, masks, cw, lanes, sums, 512 + 128 * j).astype(BF16)
    lower = jnp.where(iota((T, T), 0) >= iota((T, T), 1), 1.0, 0.0).astype(BF16)
    d_a = rows_times(d_cum, lower)
    rate = hp[:, 1:2]
    d_raw = (d_step + rate * d_a) * sigmoid(raw)
    d_proj[:, 1280:1408] = jnp.transpose(
        jnp.concatenate([d_raw, jnp.zeros((120, T), F32)], axis=0)
    ).astype(BF16)
    bias_grad = jnp.broadcast_to(jnp.sum(d_raw, axis=1, keepdims=True), (8, 128))
    rate_grad = jnp.broadcast_to(jnp.sum(d_a * step, axis=1, keepdims=True) * rate, (8, 128))
    skip_grad = jnp.broadcast_to(jnp.sum(d_skip, axis=1, keepdims=True), (8, 128))
    lane = iota((8, 128), 1)
    by_head = jnp.where(
        lane == 0, bias_grad, jnp.where(lane == 1, rate_grad, jnp.where(lane == 2, skip_grad, 0.0))
    )
    heads[...] = jnp.transpose(jnp.concatenate([by_head, jnp.zeros((120, 128), F32)], axis=0))[0:8]
    for x in range(4):
        back = dot_nt(d_proj[...], w[x, :, :, 0:WP].reshape(256, WP)).astype(BF16)
        dh[:, :, 256 * x : 256 * x + 256] = back.reshape(4, ROWS, 256)


def mixer_bwd(layer, lens, par, w, proj, kept, yssd, coef, given):
    return pl.pallas_call(
        functools.partial(mixer_bwd_kernel, layer),
        out_shape=(
            jax.ShapeDtypeStruct((4, ROWS, D), BF16),
            jax.ShapeDtypeStruct((T, WP), BF16),
            jax.ShapeDtypeStruct((T, CH), BF16),
            jax.ShapeDtypeStruct((8, 768), F32),
            jax.ShapeDtypeStruct((8, 128), F32),
        ),
        in_specs=[pl.BlockSpec(memory_space=pltpu.SMEM)] + vmem_specs(7),
        out_specs=tuple(vmem_specs(5)),
        scratch_shapes=[
            VM((T, CH), F32),
            VM((T, CH), BF16),
            VM((T, CH), BF16),
            VM((T, CH), F32),
            VM((T, CH), F32),
            VM((T, N), BF16),
            VM((T, N), BF16),
            VM((T, N), F32),
            VM((8, T), F32),
            VM((T, 128), F32),
        ] + [VM((T, CH), F32)] * (1 - layer),
        compiler_params=pltpu.CompilerParams(vmem_limit_bytes=BWD_VMEM),
        name="mixer_bwd",
    )(lens, par, w, proj, kept, yssd, coef, given)


def places():
    section = lax.axis_index("section")
    dp = lax.axis_index("dp")
    return section, dp // 4, dp % 4, lax.axis_index("tensor")


class Peers:
    def __init__(self):
        self.c, self.x, self.z, self.t = places()
        self.core = {"section": 1 - self.c}
        self.xs = [{"dp": ((self.x + o) % 4) * 4 + self.z} for o in (1, 2, 3)]
        self.zs = [{"dp": self.x * 4 + (self.z + o) % 4} for o in (1, 2, 3)]
        self.ts = [{"tensor": (self.t + o) % 4} for o in (1, 2, 3)]
        self.far_ts = [{"section": 1 - self.c, "tensor": (self.t + o) % 4} for o in (1, 2, 3)]

    def near_dp(self):
        return [self.core] + self.xs + self.zs + self.ts

    def everyone(self):
        return [self.core] + self.xs + self.zs + self.ts + self.far_ts


def barrier_start(peers):
    barrier = pltpu.get_barrier_semaphore()
    for peer in peers:
        pl.semaphore_signal(barrier, inc=1, device_id=peer, device_id_type=MESH)


def barrier_end(peers):
    pl.semaphore_wait(pltpu.get_barrier_semaphore(), len(peers))


def greet(peers):
    barrier_start(peers)
    barrier_end(peers)


class Link:
    def __init__(self, send_sems, recv_sems):
        self.send_sems, self.recv_sems, self.sent = send_sems, recv_sems, []

    def send(self, src, dst, peer):
        k = len(self.sent)
        copy = pltpu.make_async_remote_copy(
            src_ref=src, dst_ref=dst, send_sem=self.send_sems.at[k], recv_sem=self.recv_sems.at[k],
            device_id=peer, device_id_type=MESH,
        )
        copy.start()
        self.sent.append(copy)
        return copy

    def drain(self):
        for copy in self.sent:
            copy.wait_send()


def spread(link, block, r, peers):
    plus, minus = peers[0], peers[2]

    def go(k, half, peer):
        return link.send(block(k, half), block(k, half), peer)

    from_left = [go(r, 0, plus)]
    from_right = [go(r, 1, minus)]
    from_left.append(go(r, 1, plus))
    from_right.append(go(r, 0, minus))
    yield
    from_left[0].wait_recv()
    far = [go((r + 3) % 4, 0, plus)]
    from_right[0].wait_recv()
    far.append(go((r + 1) % 4, 1, minus))
    yield
    for copy in (from_left[1], from_right[1]):
        copy.wait_recv()
    yield
    for copy in far:
        copy.wait_recv()
    yield


def collect(link, part, relay, sums, inbox, r, peers):
    plus, minus = peers[0], peers[2]
    left, right, far = (r + 3) % 4, (r + 1) % 4, (r + 2) % 4
    up = link.send(part(far, 0), relay.at[0], plus)
    down = link.send(part(far, 1), relay.at[1], minus)
    last = [
        link.send(part(right, 1), inbox(0, 1), plus),
        link.send(part(left, 0), inbox(1, 0), minus),
    ]
    yield
    up.wait_recv()
    sums[0] = (part(right, 0)[...].astype(F32) + relay[0].astype(F32)).astype(BF16)
    last.append(link.send(sums.at[0], inbox(0, 0), plus))
    down.wait_recv()
    sums[1] = (part(left, 1)[...].astype(F32) + relay[1].astype(F32)).astype(BF16)
    last.append(link.send(sums.at[1], inbox(1, 1), minus))
    yield
    for copy in last:
        copy.wait_recv()
    yield


def run(steps):
    for _ in steps:
        pass


def token_halves(ref):
    return lambda k, half: ref.at[k, pl.ds(64 * half, 64)]


def collect_tokens(link, ref, relay, sums, inbox, me):
    return collect(link, token_halves(ref), relay, sums, token_halves(inbox), me.t, me.ts)


def spread_tokens(link, ref, me):
    return spread(link, token_halves(ref), me.t, me.ts)


def core_rows(c):
    first = pl.multiple_of(32 * c, 32)
    return pl.ds(first, 32), pl.ds(first, 16), pl.ds(pl.multiple_of(32 * c + 16, 16), 16)


def gather_layer(link, own_sem, shard, w, me):
    c, x, z = me.c, me.x, me.z
    whole, a, b = core_rows(c)
    own = pltpu.make_async_copy(shard, w.at[x, z, whole], own_sem)
    own.start()
    first = []
    for o in range(3):
        first.append(link.send(shard.at[pl.ds(0, 16)], w.at[x, z, a], me.zs[o]))
        first.append(link.send(shard.at[pl.ds(16, 16)], w.at[x, z, b], me.xs[o]))
    yield
    own.wait()
    for copy in first:
        copy.wait_recv()
    along_x = spread(link, lambda k, half: w.at[k, pl.ds(2 * half, 2), a], x, me.xs)
    along_z = spread(link, lambda k, half: w.at[pl.ds(2 * half, 2), k, b], z, me.zs)
    next(along_x)
    next(along_z)
    core = []

    def to_core(o):
        block_a = w.at[(x + o) % 4, :, a]
        block_b = w.at[:, (z + o) % 4, b]
        core.append(link.send(block_a, block_a, me.core))
        core.append(link.send(block_b, block_b, me.core))

    to_core(0)
    yield
    next(along_x)
    next(along_z)
    yield
    next(along_x)
    next(along_z)
    to_core(1)
    to_core(3)
    yield
    next(along_x)
    next(along_z)
    to_core(2)
    yield
    for copy in core:
        copy.wait_recv()
    yield


GATHER_COPIES = 6 + 12 + 8


def reduce_rings(link, factors, grads, out_a, out_b, core_in, acc, relay, sums, inbox, me):
    c, x, z = me.c, me.x, me.z
    hid, d_proj, db, scaled = factors
    a, b = pl.ds(0, 16), pl.ds(16, 16)
    arrive = []
    for xx in range(4):
        at = slice(256 * xx, 256 * xx + 256)
        rows_in = dot_tn(hid[:, :, at].reshape(T, 256), d_proj[...]).astype(BF16)
        rows_out = dot_tn(db[:, :, at].reshape(T, 256), scaled[...]).astype(BF16)
        for k in range(8):
            block = slice(32 * k, 32 * k + 32)
            grads[k % 2, xx, k // 2, :, 0:WP] = rows_in[block]
            grads[k % 2, xx, k // 2, :, WP:WALL] = rows_out[block]
        arrive.append(link.send(grads.at[1 - c, xx], core_in.at[xx], me.core))
        if xx % 2 == 1:
            yield
    for xx in range(4):
        arrive[xx].wait_recv()
        acc[xx] = grads[c, xx] + core_in[xx]
    along_x = collect(
        link, lambda k, half: acc.at[k, pl.ds(2 * half, 2), a], relay.at[0], sums.at[0],
        lambda d, half: inbox.at[0, d, pl.ds(2 * half, 2)], x, me.xs,
    )
    next(along_x)
    along_z = collect(
        link, lambda k, half: acc.at[pl.ds(2 * half, 2), k, b], relay.at[1], sums.at[1],
        lambda d, half: inbox.at[1, d, pl.ds(2 * half, 2)], z, me.zs,
    )
    next(along_z)
    yield
    next(along_x)
    next(along_z)
    yield
    next(along_x)
    out_a[...] = (
        acc[x, :, a].astype(F32) + inbox[0, 0].astype(F32) + inbox[0, 1].astype(F32)
    ).astype(BF16)
    next(along_z)
    out_b[...] = (
        acc[:, z, b].astype(F32) + inbox[1, 0].astype(F32) + inbox[1, 1].astype(F32)
    ).astype(BF16)
    yield


RING_COPIES = 4 + 12


def reduce_last(link, sum_a, sum_b, out, bc_all, last_in, me):
    c, x, z = me.c, me.x, me.z
    last_a = [link.send(sum_a.at[(z + o + 1) % 4], last_in.at[0, o], me.zs[o]) for o in range(3)]
    last_b = [link.send(sum_b.at[(x + o + 1) % 4], last_in.at[1, o], me.xs[o]) for o in range(3)]
    yield
    rows, rows_a, rows_b = core_rows(c)
    for k, (copies, at, mine) in enumerate(((last_a, rows_a, sum_a.at[z]), (last_b, rows_b, sum_b.at[x]))):
        for copy in copies:
            copy.wait_recv()
        out[at, :] = (
            mine[...].astype(F32)
            + last_in[k, 0].astype(F32) + last_in[k, 1].astype(F32) + last_in[k, 2].astype(F32)
        )
    swap = [link.send(out.at[rows], out.at[rows], me.core)]

    def wanted(t):
        return pl.ds(pl.multiple_of(32 * c + 16 * (t % 2), 16), 16)

    bc_all[me.t, c] = out[wanted(me.t), 1024:1280]
    slot = bc_all.at[me.t, c]
    swap.append(link.send(slot, slot, me.core))
    for o in range(3):
        block = out.at[wanted(me.t + o + 1), pl.ds(1024, 256)]
        swap.append(link.send(block, slot, me.ts[o]))
        swap.append(link.send(block, slot, me.far_ts[o]))
    yield
    for copy in swap:
        copy.wait_recv()
    yield


LAST_COPIES = 6 + 8


def ring_scratch():
    return [
        VM((2, 4, 4, 32, WALL), BF16),
        VM((4, 4, 32, WALL), BF16), VM((4, 4, 32, WALL), BF16),
        VM((2, 2, 2, 16, WALL), BF16), VM((2, 2, 2, 16, WALL), BF16),
        VM((2, 2, 4, 16, WALL), BF16),
    ]


def last_scratch():
    return [VM((64, WALL), F32), VM((4, 2, 16, 2 * N), F32), VM((2, 3, 16, WALL), BF16)]


def token_scratch():
    return [VM((2, 64, D), BF16), VM((2, 64, D), BF16), VM((2, ROWS, D), BF16)]


def dma_sems(n):
    return pltpu.SemaphoreType.DMA((n,))


def link_scratch(*counts):
    return [pltpu.SemaphoreType.DMA((n,)) for n in counts for _ in range(2)]


def input_norm(u, gain):
    return u * lax.rsqrt(jnp.mean(u * u, axis=-1, keepdims=True) + EPSILON) * gain


def gain_of(par, layer):
    return par[layer, 0:1, 1408:2432]


def gather_kernel(
    lengths, w_in, w_bc, w_dt, w_out, conv_w, flat, u0, cot,
    w0, shard1, par, hid, db, valid,
    wsh, shards, turned, own_sem, g_s, g_r, e_s, e_r, h_s, h_r, d_s, d_r,
):
    me = Peers()
    c, t = me.c, me.t
    barrier_start(me.near_dp())
    wsh[:, 0:WZX] = w_in[...]
    wsh[:, 1024:1280] = w_bc[...]
    dt_rows = jnp.concatenate([w_dt[...].astype(F32), jnp.zeros((HL, 64), F32)], axis=1)
    dt_rows = jnp.concatenate([dt_rows, jnp.zeros((120, 128), F32)], axis=0)
    wsh[:, 1280:1408] = jnp.transpose(dt_rows)[0:64].astype(BF16)
    wsh[:, WP:WALL] = w_out[...]
    shards[c] = wsh[core_rows(c)[0], :]
    own = pl.ds(pl.multiple_of(CH * t, CH), CH)
    par[c] = jnp.zeros((8, 2432), F32)
    par[c, 0:4, 0:512] = conv_w[:, own]
    par[c, 0:4, 512:768] = conv_w[:, DI : DI + 2 * N]
    par[c, 4:5, 0:512] = flat[:, own]
    par[c, 4:5, 512:768] = flat[:, DI : DI + 2 * N]
    by_row = jnp.broadcast_to(flat[:, 5376:5504], (8, 128))
    row = iota((8, 128), 0)
    by_row = jnp.where(
        row == 0, by_row,
        jnp.where(row == 1, pltpu.roll(by_row, 128 - H, 1), pltpu.roll(by_row, 128 - 2 * H, 1)),
    )
    turned[...] = jnp.transpose(jnp.concatenate([by_row, jnp.zeros((120, 128), F32)], axis=0))
    heads = turned[pl.ds(pl.multiple_of(HL * t, HL), HL), :]
    par[c, :, 768:896] = jnp.where(iota((8, 128), 1) == 1, -jnp.exp(heads), heads)
    par[c, 0:1, 896:1408] = flat[:, pl.ds(pl.multiple_of(2304 + CH * t, 256), CH)]
    par[c, 0:1, 1408:2432] = flat[:, 4352:5376]
    end = lengths[c, 0, 0] + lengths[c, 0, 1]
    valid[...] = jnp.where(iota((ROWS, 128), 0) + ROWS * t < end, 1.0, 0.0).astype(F32)
    barrier_end(me.near_dp())
    early, weights = Link(e_s, e_r), Link(g_s, g_r)
    theirs = early.send(wsh.at[core_rows(1 - c)[0]], shards.at[c], me.core)
    par_copy = early.send(par.at[c], par.at[c], me.core)
    for j in range(8):
        db[t, :, tile(j)] = (cot[:, tile(j)] * valid[...]).astype(BF16)
    theirs.wait_recv()
    layer0 = gather_layer(weights, own_sem.at[0], shards.at[0], w0, me)
    next(layer0)
    par_copy.wait_recv()
    hid[t] = input_norm(u0[...], gain_of(par, 0)).astype(BF16)
    tokens, branch = Link(h_s, h_r), Link(d_s, d_r)
    hid_steps = spread_tokens(tokens, hid, me)
    db_steps = spread_tokens(branch, db, me)
    next(hid_steps)
    next(layer0)
    next(db_steps)
    next(layer0)
    next(hid_steps)
    shard1[...] = shards[1]
    next(layer0)
    next(db_steps)
    run(layer0)
    run(hid_steps)
    run(db_steps)
    for link in (early, weights, tokens, branch):
        link.drain()


def gather(*arrays):
    return pl.pallas_call(
        gather_kernel,
        out_shape=(
            jax.ShapeDtypeStruct((4, 4, 64, WALL), BF16),
            jax.ShapeDtypeStruct((32, WALL), BF16),
            jax.ShapeDtypeStruct((2, 8, 2432), F32),
            jax.ShapeDtypeStruct((4, ROWS, D), BF16),
            jax.ShapeDtypeStruct((4, ROWS, D), BF16),
            jax.ShapeDtypeStruct((ROWS, 128), F32),
        ),
        in_specs=[pl.BlockSpec(memory_space=pltpu.SMEM)] + vmem_specs(8),
        out_specs=tuple(vmem_specs(6)),
        scratch_shapes=[
            VM((64, WALL), BF16), VM((2, 32, WALL), BF16), VM((128, 128), F32),
            dma_sems(1),
        ]
        + link_scratch(GATHER_COPIES, 2, 6, 6),
        compiler_params=pltpu.CompilerParams(
            collective_id=0, has_side_effects=True, vmem_limit_bytes=6 << 20
        ),
        name="gather_weights",
    )(*arrays)


def column_of(row):
    return jnp.transpose(jnp.broadcast_to(row, (128, 128)))


def middle_kernel(
    part, st, u0, valid, par, shard1, total, u_next, s_out, hid, w1,
    relay, sums, inbox, sbuf, own_sem, g_s, g_r, p_s, p_r, b_s, b_r, h_s, h_r,
):
    me = Peers()
    c, t = me.c, me.t
    greet([me.core] + me.xs + me.zs + me.ts)
    weights, tokens, small, spreading = Link(g_s, g_r), Link(p_s, p_r), Link(b_s, b_r), Link(h_s, h_r)
    sum_steps = collect_tokens(tokens, part, relay, sums, inbox, me)
    next(sum_steps)
    stats = [small.send(st.at[(t + o + 1) % 4], sbuf.at[o], me.ts[o]) for o in range(3)]
    layer1 = gather_layer(weights, own_sem.at[0], shard1, w1, me)
    next(layer1)
    next(sum_steps)
    next(layer1)
    for copy in stats:
        copy.wait_recv()
    s_row = lax.rsqrt((st[t] + sbuf[0] + sbuf[1] + sbuf[2]) / DI + EPSILON)
    s_out[...] = s_row
    scale = column_of(s_row[0:1]) * valid[...]
    next(layer1)
    run(sum_steps)
    total[...] = part[t].astype(F32) + inbox[0].astype(F32) + inbox[1].astype(F32)
    for j in range(8):
        u_next[:, tile(j)] = u0[:, tile(j)] + scale * total[:, tile(j)]
    hid[t] = input_norm(u_next[...], gain_of(par, 1)).astype(BF16)
    hid_steps = spread_tokens(spreading, hid, me)
    next(hid_steps)
    next(layer1)
    next(hid_steps)
    run(layer1)
    run(hid_steps)
    for link in (weights, tokens, small, spreading):
        link.drain()


def middle(*arrays):
    return pl.pallas_call(
        middle_kernel,
        out_shape=(
            jax.ShapeDtypeStruct((ROWS, D), F32),
            jax.ShapeDtypeStruct((ROWS, D), F32),
            jax.ShapeDtypeStruct((8, 128), F32),
            jax.ShapeDtypeStruct((4, ROWS, D), BF16),
            jax.ShapeDtypeStruct((4, 4, 64, WALL), BF16),
        ),
        in_specs=vmem_specs(6),
        out_specs=tuple(vmem_specs(5)),
        scratch_shapes=token_scratch()
        + [VM((3, 8, 128), F32), pltpu.SemaphoreType.DMA((1,))]
        + link_scratch(GATHER_COPIES, 6, 3, 6),
        compiler_params=pltpu.CompilerParams(
            collective_id=1, has_side_effects=True, vmem_limit_bytes=6 << 20
        ),
        name="sum_and_gather_tokens",
    )(*arrays)


def stats_exchange(link, st, buf, coef, me):
    barrier_end(me.ts)
    copies = [link.send(st, buf.at[me.t], peer) for peer in me.ts]
    buf[me.t] = st[...]
    yield
    for copy in copies:
        copy.wait_recv()
    for i in range(4):
        both = buf[0, i] + buf[1, i] + buf[2, i] + buf[3, i]
        s = lax.rsqrt(both[0:1] / DI + EPSILON)
        k = s * s * s * (both[1:2] / DI)
        row = iota((8, 128), 0)
        coef[i] = jnp.where(row == 0, s, jnp.where(row == 1, k, 0.0))
    link.drain()
    yield


def norm_back(u, gain, g, d_hidden):
    r = lax.rsqrt(jnp.mean(u * u, axis=-1, keepdims=True) + EPSILON)
    mean = jnp.mean(u * gain * d_hidden, axis=-1, keepdims=True)
    d_u = g + r * gain * d_hidden - u * (r * r * r) * mean
    return d_u, jnp.sum(u * r * d_hidden, axis=0, keepdims=True)


def back_middle_kernel(
    dh, u, cot, valid, par, total0, s0, hid1, d_proj1, db1, scaled1, g1, ng, db, coef, sum_a, sum_b,
    relay, sums, inbox, grads, core_in, acc, g_relay, g_sums, g_inbox,
    g_s, g_r, p_s, p_r, b_s, b_r, h_s, h_r,
):
    me = Peers()
    c, t = me.c, me.t
    greet(me.near_dp())
    weights, tokens, small, spreading = Link(g_s, g_r), Link(p_s, p_r), Link(b_s, b_r), Link(h_s, h_r)
    sum_steps = collect_tokens(tokens, dh, relay, sums, inbox, me)
    next(sum_steps)
    layer1 = reduce_rings(
        weights, (hid1, d_proj1, db1, scaled1), grads, sum_a, sum_b, core_in, acc,
        g_relay, g_sums, g_inbox, me,
    )
    next(layer1)
    next(sum_steps)
    next(layer1)
    next(layer1)
    run(sum_steps)
    total = dh[t].astype(F32) + inbox[0].astype(F32) + inbox[1].astype(F32)
    d_u, gain_term = norm_back(u[...], gain_of(par, 1), cot[...], total)
    g1[...] = d_u
    ng[...] = gain_term
    mean = jnp.zeros((ROWS, 128), F32)
    for j in range(8):
        d_branch = (g1[:, tile(j)] * valid[...]).astype(BF16)
        db[t, :, tile(j)] = d_branch
        mean = mean + d_branch.astype(F32) * total0[:, tile(j)]
    db_steps = spread_tokens(spreading, db, me)
    next(db_steps)
    mean = jnp.broadcast_to(jnp.sum(mean, axis=-1, keepdims=True), (128, 128))
    mean_row = jnp.transpose(mean)[0:8] / DI
    s = s0[0:1, :]
    row = iota((8, 128), 0)
    coef[t] = jnp.where(row == 0, s, jnp.where(row == 1, s * s * s * mean_row, 0.0))
    coef_copies = [small.send(coef.at[t], coef.at[t], peer) for peer in me.ts]
    next(layer1)
    next(db_steps)
    next(layer1)
    run(db_steps)
    for copy in coef_copies:
        copy.wait_recv()
    for link in (weights, tokens, small, spreading):
        link.drain()


def back_middle(*arrays):
    return pl.pallas_call(
        back_middle_kernel,
        out_shape=(
            jax.ShapeDtypeStruct((ROWS, D), F32),
            jax.ShapeDtypeStruct((1, D), F32),
            jax.ShapeDtypeStruct((4, ROWS, D), BF16),
            jax.ShapeDtypeStruct((4, 8, 128), F32),
            jax.ShapeDtypeStruct((4, 16, WALL), BF16),
            jax.ShapeDtypeStruct((4, 16, WALL), BF16),
        ),
        in_specs=vmem_specs(11),
        out_specs=tuple(vmem_specs(6)),
        scratch_shapes=token_scratch() + ring_scratch() + link_scratch(RING_COPIES, 6, 3, 6),
        compiler_params=pltpu.CompilerParams(
            collective_id=3, has_side_effects=True, vmem_limit_bytes=14 << 20
        ),
        name="back_sum_and_gather",
    )(*arrays)


def small_sum(link, own, arrived, by_z, by_x, by_t, me):
    c, x, z, t = me.c, me.x, me.z, me.t
    swap = link.send(own.at[1 - c], arrived, me.core)
    yield
    swap.wait_recv()
    by_z[z] = own[c] + arrived[...]
    copies = [link.send(by_z.at[z], by_z.at[z], peer) for peer in me.zs]
    yield
    for copy in copies:
        copy.wait_recv()
    by_x[x] = by_z[0] + by_z[1] + by_z[2] + by_z[3]
    copies = [link.send(by_x.at[x], by_x.at[x], peer) for peer in me.xs]
    yield
    for copy in copies:
        copy.wait_recv()
    by_t[t] = by_x[0] + by_x[1] + by_x[2] + by_x[3]
    copies = [link.send(by_t.at[t], by_t.at[t], peer) for peer in me.ts]
    yield
    for copy in copies:
        copy.wait_recv()
    yield


def finish_kernel(
    dh, part, u0, u1, g1, valid, par, coef1, ng1, sums0, heads0, sums1, heads1, sum_a1, sum_b1,
    hid0, d_proj0, db0, scaled0,
    lo, lg, smt, nmt, picked, o_bc,
    relay, sums, inbox, relay2, sums2, inbox2, los, lgs, sms, smr, smz, smx, nms, nmr, nmz, nmx, sum_a0, sum_b0,
    grads, core_in, acc, g_relay, g_sums, g_inbox, w_grad0, bc_all0, last_in0, w_grad1, bc_all1, last_in1,
    g_s, g_r, f_s, f_r, l_s, l_r, p_s, p_r, q_s, q_r, b_s, b_r,
):
    me = Peers()
    c, x, z, t = me.c, me.x, me.z, me.t
    greet(me.everyone())
    weights, final0, final1 = Link(g_s, g_r), Link(f_s, f_r), Link(l_s, l_r)
    tokens, tokens2, small = Link(p_s, p_r), Link(q_s, q_r), Link(b_s, b_r)
    for layer, (by_channel, heads) in enumerate(((sums0, heads0), (sums1, heads1))):
        sms[layer, 0:8, :] = by_channel[:, 0:512]
        sms[layer, 8:16, 0:256] = by_channel[:, 512:768]
        sms[layer, 8:16, 256:384] = heads[...]
        sms[layer, 8:16, 384:512] = jnp.zeros((8, 128), F32)
    chain = small_sum(small, sms, smr, smz, smx, smt, me)
    next(chain)
    back_steps = collect_tokens(tokens, dh, relay, sums, inbox, me)
    next(back_steps)
    last1 = reduce_last(final1, sum_a1, sum_b1, w_grad1, bc_all1, last_in1, me)
    next(last1)
    layer0 = reduce_rings(
        weights, (hid0, d_proj0, db0, scaled0), grads, sum_a0, sum_b0, core_in, acc,
        g_relay, g_sums, g_inbox, me,
    )
    next(layer0)
    next(chain)
    next(back_steps)
    next(layer0)
    next(layer0)
    next(last1)
    next(chain)
    out_steps = collect_tokens(tokens2, part, relay2, sums2, inbox2, me)
    next(out_steps)
    los[0] = u1[...]
    lgs[1] = g1[...]
    run(back_steps)
    total = dh[t].astype(F32) + inbox[0].astype(F32) + inbox[1].astype(F32)
    d_u, gain_term = norm_back(u0[...], gain_of(par, 0), g1[...], total)
    lgs[0] = d_u
    lg_copy = small.send(lgs.at[1 - c], lg.at[c], me.core)
    lg[c] = lgs[c]
    next(layer0)
    next(out_steps)
    for layer, term in enumerate((gain_term, ng1[...])):
        for j in range(8):
            nms[layer, j : j + 1, :] = term[:, tile(j)]
    norm_chain = small_sum(small, nms, nmr, nmz, nmx, nmt, me)
    next(norm_chain)
    next(chain)
    run(last1)
    next(norm_chain)
    next(layer0)
    last0 = reduce_last(final0, sum_a0, sum_b0, w_grad0, bc_all0, last_in0, me)
    next(last0)
    next(norm_chain)
    run(out_steps)
    los[1] = part[t].astype(F32) + inbox2[0].astype(F32) + inbox2[1].astype(F32)
    scale = column_of(coef1[t][0:1]) * valid[...]
    for j in range(8):
        los[1, :, tile(j)] = u1[:, tile(j)] + scale * los[1, :, tile(j)]
    lo_copy = small.send(los.at[1 - c], lo.at[c], me.core)
    lo[c] = los[c]
    next(norm_chain)
    next(last0)
    run(last0)
    picked[...] = jnp.where(c == 0, w_grad0[...], w_grad1[...])
    half = t // 2
    bc0 = bc_all0[0, half] + bc_all0[1, half] + bc_all0[2, half] + bc_all0[3, half]
    bc1 = bc_all1[0, half] + bc_all1[1, half] + bc_all1[2, half] + bc_all1[3, half]
    o_bc[...] = jnp.where(c == 0, bc0, bc1)
    run(chain)
    run(norm_chain)
    lo_copy.wait_recv()
    lg_copy.wait_recv()
    for link in (weights, final0, final1, tokens, tokens2, small):
        link.drain()


def finish(*arrays):
    return pl.pallas_call(
        finish_kernel,
        out_shape=(
            jax.ShapeDtypeStruct((2, ROWS, D), F32),
            jax.ShapeDtypeStruct((2, ROWS, D), F32),
            jax.ShapeDtypeStruct((4, 16, 512), F32),
            jax.ShapeDtypeStruct((4, 8, 128), F32),
            jax.ShapeDtypeStruct((64, WALL), F32),
            jax.ShapeDtypeStruct((16, 2 * N), F32),
        ),
        in_specs=vmem_specs(19),
        out_specs=tuple(vmem_specs(6)),
        scratch_shapes=token_scratch() + token_scratch()
        + [
            VM((2, ROWS, D), F32), VM((2, ROWS, D), F32),
            VM((2, 16, 512), F32), VM((16, 512), F32), VM((4, 16, 512), F32), VM((4, 16, 512), F32),
            VM((2, 8, 128), F32), VM((8, 128), F32), VM((4, 8, 128), F32), VM((4, 8, 128), F32),
            VM((4, 16, WALL), BF16), VM((4, 16, WALL), BF16),
        ]
        + ring_scratch() + last_scratch() + last_scratch()
        + link_scratch(RING_COPIES, LAST_COPIES, LAST_COPIES, 6, 6, 22),
        compiler_params=pltpu.CompilerParams(
            collective_id=4, has_side_effects=True, vmem_limit_bytes=22 << 20
        ),
        name="sum_gradients",
    )(*arrays)


def write_kernel(lo, lg, smt, nmt, picked, bc, *rest):
    outs, (in_part, dt, conv_w, conv_b, gain, norm, heads, sem) = rest[:13], rest[13:]
    (o_lo, o_lg, o_norm, o_in, o_bc, o_dt, o_cw, o_cb, o_dtb, o_alog, o_skip, o_gain, o_out) = outs
    copies = []

    def write(src, dst):
        copy = pltpu.make_async_copy(src, dst, sem.at[len(copies)])
        copy.start()
        copies.append(copy)

    write(lo, o_lo)
    write(lg, o_lg)
    write(bc, o_bc)
    in_part[:, 0, :] = picked[:, 0:512]
    in_part[:, 1, :] = picked[:, 512:1024]
    write(in_part, o_in)
    write(picked.at[:, pl.ds(WP, CH)], o_out)
    dt_rows = jnp.concatenate([picked[:, 1280:1408], jnp.zeros((64, 128), F32)], axis=0)
    dt[...] = jnp.transpose(dt_rows)[0:HL, 0:64]
    write(dt, o_dt)
    shared = smt[0, 8:16] + smt[1, 8:16] + smt[2, 8:16] + smt[3, 8:16]
    norms = nmt[0] + nmt[1] + nmt[2] + nmt[3]
    for j in range(8):
        norm[:, tile(j)] = norms[j : j + 1]
    write(norm, o_norm)
    conv_w[:, DI : DI + 2 * N] = shared[0:4, 0:256]
    conv_b[:, DI : DI + 2 * N] = shared[4:5, 0:256]
    for k in range(4):
        at = slice(512 * k, 512 * k + 512)
        conv_w[:, at] = smt[k, 0:4, :]
        conv_b[:, at] = smt[k, 4:5, :]
        gain[:, at] = smt[k, 5:6, :]
    write(conv_w, o_cw)
    write(conv_b, o_cb)
    write(gain, o_gain)
    all_heads = smt[0, 8:16, 256:384]
    for k in range(1, 4):
        all_heads = all_heads + pltpu.roll(smt[k, 8:16, 256:384], HL * k, 1)
    for k, out in ((0, o_dtb), (1, o_alog), (2, o_skip)):
        heads[k] = all_heads[k : k + 1, 0:H]
        write(heads.at[k], out)
    for copy in copies:
        copy.wait()


def write_outputs(*arrays):
    hbm_spec = pl.BlockSpec(memory_space=pltpu.HBM)
    shapes = [
        (2, ROWS, D), (2, ROWS, D), (1, D), (64, 2, CH), (16, 2 * N), (HL, 64), (CONV, DI + 2 * N),
        (1, DI + 2 * N), (1, H), (1, H), (1, H), (1, DI), (64, CH),
    ]
    return pl.pallas_call(
        write_kernel,
        out_shape=tuple(jax.ShapeDtypeStruct(shape, F32) for shape in shapes),
        in_specs=vmem_specs(6),
        out_specs=(hbm_spec,) * 13,
        scratch_shapes=[
            VM((64, 2, CH), F32), VM((HL, 64), F32), VM((CONV, DI + 2 * N), F32),
            VM((1, DI + 2 * N), F32), VM((1, DI), F32), VM((1, D), F32), VM((3, 1, H), F32),
            pltpu.SemaphoreType.DMA((13,)),
        ],
        compiler_params=pltpu.CompilerParams(vmem_limit_bytes=6 << 20),
        name="write_outputs",
    )(*arrays)


def body(
    activations, cotangent, lengths, norm_gain, in_weight, bc_weight, dt_weight, conv_weight,
    conv_bias, dt_bias, a_log, d_skip, gated_gain, out_weight,
):
    section = lax.axis_index("section")
    u0 = lax.dynamic_index_in_dim(activations, section, 0, keepdims=False)
    cot = lax.dynamic_index_in_dim(cotangent, section, 0, keepdims=False)
    flat = jnp.concatenate(
        [conv_bias, gated_gain, norm_gain, dt_bias, a_log, d_skip, jnp.zeros((1, 32), F32)], axis=1
    )
    w0, shard1, par, hid0, db1, valid = gather(
        lengths, in_weight[0].reshape(64, WZX), bc_weight[0], dt_weight[0].T, out_weight[0].T,
        conv_weight[0], flat, u0, cot,
    )
    proj0, kept0, part0, y0, st0 = mixer_fwd(0, lengths, par, hid0, w0)
    total0, u1, s0, hid1, w1 = middle(part0, st0, u0, valid, par, shard1)
    proj1, kept1, part1, y1, coef1, d_scaled1 = mixer_fwd(1, lengths, par, hid1, w1, db1)
    dh1, dp1, sc1, sums1, heads1 = mixer_bwd(1, lengths, par, w1, proj1, kept1, y1, coef1, d_scaled1)
    g1, ng1, db0, coef0, sum_a1, sum_b1 = back_middle(
        dh1, u1, cot, valid, par, total0, s0, hid1, dp1, db1, sc1
    )
    dh0, dp0, sc0, sums0, heads0 = mixer_bwd(0, lengths, par, w0, proj0, kept0, y0, coef0, db0)
    outs = write_outputs(
        *finish(
            dh0, part1, u0, u1, g1, valid, par, coef1, ng1,
            sums0, heads0, sums1, heads1, sum_a1, sum_b1, hid0, dp0, db0, sc0,
        )
    )
    outs = [out.T if k in (5, 12) else out for k, out in enumerate(outs)]
    plain = (2, 8, 9, 10, 7, 11)
    return tuple(out if k in plain else out[None] for k, out in enumerate(outs))


def solution(mesh):
    return jax.shard_map(
        body,
        mesh=mesh,
        in_specs=(
            P(None, ("dp", "tensor"), None),
            P(None, ("dp", "tensor"), None),
            P(None, "dp", None),
            P("section", None),
            P("section", "dp", None, "tensor"),
            P("section", "dp", None),
            P("section", "dp", "tensor"),
            P("section", None, None),
            P("section", None),
            P("section", None),
            P("section", None),
            P("section", None),
            P("section", None),
            P("section", "tensor", "dp"),
        ),
        out_specs=(
            P("section", None, ("dp", "tensor"), None),
            P("section", None, ("dp", "tensor"), None),
            P("section", None),
            P("section", "dp", None, "tensor"),
            P("section", ("dp", "tensor"), None),
            P("section", "dp", "tensor"),
            P("section", None, None),
            P("section", None),
            P("section", None),
            P("section", None),
            P("section", None),
            P("section", None),
            P("section", "tensor", "dp"),
        ),
        check_vma=False,
    )
```

```python
import functools

import jax
import jax.numpy as jnp
from jax import lax
from jax.experimental import pallas as pl
from jax.experimental.pallas import tpu as pltpu
from jax.sharding import PartitionSpec as P

D = 1024
DI = 2048
H = 32
N = 128
CONV = 4
T = 512
ROWS = 128
CH = 512
HL = 8
WZX = 1024
WP = 1408
WALL = 1920
NDP = 16
EPSILON = 1e-05
LOG2E = 1.4426950408889634
NEG = -1e30
F32 = jnp.float32
BF16 = jnp.bfloat16
MESH = pl.DeviceIdType.MESH
VM = pltpu.VMEM
FWD_VMEM = 12 << 20
BWD_VMEM = 16 << 20


def dot_nn(a, b):
    return lax.dot_general(a, b, (((1,), (0,)), ((), ())), preferred_element_type=F32)


def dot_nt(a, b):
    return lax.dot_general(a, b, (((1,), (1,)), ((), ())), preferred_element_type=F32)


def dot_tn(a, b):
    return lax.dot_general(a, b, (((0,), (0,)), ((), ())), preferred_element_type=F32)


def pieces(v, count):
    parts = []
    for _ in range(count):
        part = v.astype(BF16)
        parts.append(part)
        v = v - part.astype(F32)
    return parts


def sum_rows_nt(selector, v, count):
    return sum(dot_nt(selector, part) for part in pieces(v, count))


def rows_times(v, matrix):
    a, b, c = pieces(v, 3)
    stacked = jnp.concatenate([a.astype(F32), b.astype(F32), c.astype(F32), jnp.zeros_like(v)], 0)
    out = dot_nn(stacked.astype(BF16), matrix)
    return out[0:8] + out[8:16] + out[16:24]


def iota(shape, dim):
    return lax.broadcasted_iota(jnp.int32, shape, dim)


def segment_of(position, e0, e1):
    return (position >= e0).astype(jnp.int32) + (position >= e1).astype(jnp.int32)


def conv_masks(e0, e1):
    p = iota((T, 128), 0)
    seg = segment_of(p, e0, e1)
    return [
        jnp.where((p >= k) & (segment_of(p - k, e0, e1) == seg), 1.0, 0.0).astype(F32)
        for k in range(1, CONV)
    ]


def conv_pre(v, masks, cw, lanes):
    pre = cw[CONV : CONV + 1, lanes] + cw[CONV - 1 : CONV, lanes] * v
    for k in range(1, CONV):
        pre = pre + cw[CONV - 1 - k : CONV - k, lanes] * (masks[k - 1] * pltpu.roll(v, k, 0))
    return pre


def sigmoid(v):
    return 0.5 * jnp.tanh(0.5 * v) + 0.5


def steps_of(dt_tile, hp_ref):
    raw = jnp.transpose(dt_tile)[0:HL] + hp_ref[:, 0:1]
    step = jnp.maximum(raw, 0.0) + jnp.log1p(jnp.exp(-jnp.abs(raw)))
    rate = hp_ref[:, 1:2]
    upper = jnp.where(iota((T, T), 0) <= iota((T, T), 1), 1.0, 0.0).astype(BF16)
    cum = rows_times(step * rate, upper) * LOG2E
    columns = jnp.transpose(
        jnp.concatenate([cum, step, jnp.zeros((112, T), F32)], axis=0)
    )
    return raw, step, cum, columns


def pair_columns(columns, first, j, rows=T):
    low = iota((rows, 128), 1) < 64
    return jnp.where(
        low,
        jnp.broadcast_to(columns[:, first + 2 * j : first + 2 * j + 1], (rows, 128)),
        jnp.broadcast_to(columns[:, first + 2 * j + 1 : first + 2 * j + 2], (rows, 128)),
    )


def tile(j):
    return slice(128 * j, 128 * j + 128)


def layer_params(par, layer):
    return (
        par.at[layer, :, pl.ds(0, 768)],
        par.at[layer, :, pl.ds(768, 128)],
        par.at[layer, :, pl.ds(896, 512)],
    )


def skip_row(hp, j):
    low = iota((1, 128), 1) < 64
    first = jnp.broadcast_to(hp[2 * j : 2 * j + 1, 2:3], (1, 128))
    second = jnp.broadcast_to(hp[2 * j + 1 : 2 * j + 2, 2:3], (1, 128))
    return jnp.where(low, first, second)


def segment_ends(lengths):
    c = lax.axis_index("section")
    first = lengths[c, 0, 0]
    return first, first + lengths[c, 0, 1]


def project(hid, w, proj):
    tokens = hid[...].reshape(T, D)
    for first, width in ((0, 512), (512, 512), (1024, 384)):
        at = slice(first, first + width)
        proj[:, at] = dot_nn(tokens, w[:, :, :, at].reshape(D, width))


def scale_back(db, w, d_scaled):
    d_scaled[...] = dot_nn(db[...].reshape(T, D), w[:, :, :, WP:WALL].reshape(D, CH))


def mixer_fwd_kernel(layer, lens, par, hid, w, *rest, early=None):
    with_grad = layer == 1
    if with_grad:
        db, proj, kept, part, yssd, coef, d_scaled, gg, inn, xb, bb, cb, cumr, colr, *rest = rest
        st, buf, send_sems, recv_sems = rest
        me = Peers()
        barrier_start(me.ts)
        scale_back(db, w, d_scaled)
    else:
        proj, kept, part, yssd, st, gg, inn, xb, bb, cb, cumr, colr = rest
    cw, hp, rows = layer_params(par, layer)
    project(hid, w, proj)
    if early is not None:
        early()
    e0, e1 = segment_ends(lens)
    masks = conv_masks(e0, e1)
    _, _, cum, columns = steps_of(proj[:, 1280:1408], hp)
    cumr[...] = cum
    colr[...] = columns
    for j in range(4):
        v = proj[:, 512 + 128 * j : 640 + 128 * j]
        pre = conv_pre(v, masks, cw, tile(j))
        kept[:, tile(j)] = pre
        act = pre * sigmoid(pre)
        inn[:, tile(j)] = act
        xb[:, tile(j)] = (act * pair_columns(columns, HL, j)).astype(BF16)
    for j, ref in ((0, bb), (1, cb)):
        lanes = slice(512 + 128 * j, 640 + 128 * j)
        pre = conv_pre(proj[:, 1024 + 128 * j : 1152 + 128 * j], masks, cw, lanes)
        kept[:, lanes] = pre
        ref[...] = (pre * sigmoid(pre)).astype(BF16)
    low = iota((128, 128), 1) < 64
    for i in range(4):
        n = 128 * (i + 1)
        here = slice(128 * i, n)
        scores = dot_nt(cb[here, :], bb[0:n, :])
        p = iota((128, n), 0) + 128 * i
        q = iota((128, n), 1)
        bias = jnp.where((p >= q) & (segment_of(p, e0, e1) == segment_of(q, e0, e1)), 0.0, NEG).astype(F32)
        for j in range(4):
            mixing = []
            for h in (2 * j, 2 * j + 1):
                decay = jnp.exp2(colr[here, h : h + 1] - cumr[h : h + 1, 0:n] + bias)
                mixing.append((scores * decay).astype(BF16))
            both = dot_nn(jnp.concatenate(mixing, axis=0), xb[0:n, tile(j)])
            yssd[here, tile(j)] = jnp.where(low, both[0:128], both[128:256])
    squares = jnp.zeros((8, T), F32)
    dots = jnp.zeros((8, T), F32)
    ones = jnp.ones((8, 128), BF16)
    for j in range(4):
        z = proj[:, tile(j)]
        gated = (yssd[:, tile(j)] + skip_row(hp, j) * inn[:, tile(j)]) * (z * sigmoid(z))
        gained = gated * rows[0:1, tile(j)]
        gg[:, tile(j)] = gained.astype(BF16)
        squares = squares + sum_rows_nt(ones, gated * gated, 1)
        if with_grad:
            dots = dots + sum_rows_nt(ones, gained * d_scaled[:, tile(j)], 2)
    row = iota((8, T), 0)
    both = jnp.where(row == 0, squares, jnp.where(row == 1, dots, 0.0))
    for i in range(4):
        st[i] = both[:, tile(i)]
    if with_grad:
        exchange = stats_exchange(Link(send_sems, recv_sems), st, buf, coef, me)
        next(exchange)
    for x in range(4):
        columns_out = slice(256 * x, 256 * x + 256)
        branch = dot_nt(gg[...], w[x, :, :, WP:WALL].reshape(256, CH)).astype(BF16)
        part[:, :, columns_out] = branch.reshape(4, ROWS, 256)
    if with_grad:
        run(exchange)


def vmem_specs(count):
    return [pl.BlockSpec(memory_space=VM)] * count


def fwd_scratch():
    return [
        VM((T, CH), BF16),
        VM((T, CH), F32),
        VM((T, CH), BF16),
        VM((T, N), BF16),
        VM((T, N), BF16),
        VM((8, T), F32),
        VM((T, 128), F32),
    ]


def mixer_fwd(layer, lens, par, hid, w, *db):
    out_shape = [
        jax.ShapeDtypeStruct((T, WP), F32),
        jax.ShapeDtypeStruct((T, 768), F32),
        jax.ShapeDtypeStruct((4, ROWS, D), BF16),
        jax.ShapeDtypeStruct((T, CH), F32),
        jax.ShapeDtypeStruct((4, 8, 128), F32),
    ] + [jax.ShapeDtypeStruct((T, CH), F32)] * layer
    shared = {"collective_id": 2, "has_side_effects": True} if layer else {}
    return pl.pallas_call(
        functools.partial(mixer_fwd_kernel, layer),
        out_shape=tuple(out_shape),
        in_specs=[pl.BlockSpec(memory_space=pltpu.SMEM)] + vmem_specs(3 + len(db)),
        out_specs=tuple(vmem_specs(len(out_shape))),
        scratch_shapes=fwd_scratch() + ([VM((4, 8, 128), F32), VM((4, 4, 8, 128), F32)] + link_scratch(3)) * layer,
        compiler_params=pltpu.CompilerParams(vmem_limit_bytes=FWD_VMEM, **shared),
        name="mixer_fwd",
    )(lens, par, hid, w, *db)


def head_selector(j):
    head = 2 * j + (iota((8, 128), 1) >= 64).astype(jnp.int32)
    return jnp.where(iota((8, 128), 0) == head, 1.0, 0.0).astype(BF16)


def back_roll(v, k):
    return pltpu.roll(v, T - k, 0)


def conv_back(d_pre, v, masks, cw, lanes, sums, column0):
    d_v = cw[CONV - 1 : CONV, lanes] * d_pre
    out = slice(column0, column0 + 128)
    sums[CONV : CONV + 1, out] = jnp.sum(d_pre, axis=0, keepdims=True)
    sums[CONV - 1 : CONV, out] = jnp.sum(d_pre * v, axis=0, keepdims=True)
    for k in range(1, CONV):
        masked = masks[k - 1] * d_pre
        d_v = d_v + cw[CONV - 1 - k : CONV - k, lanes] * back_roll(masked, k)
        sums[CONV - 1 - k : CONV - k, out] = jnp.sum(masked * pltpu.roll(v, k, 0), axis=0, keepdims=True)
    return d_v


def mixer_bwd_kernel(layer, lens, par, w, proj, kept, yssd, coef, *rest, early=None, later=None):
    given, *rest = rest
    dh, d_proj, scaled, sums, heads, inn, xb, dyb, dyf, dx, bb, cb, d_c, cumr, colr, *rest = rest
    if layer == 1:
        d_scaled = given
    else:
        db, d_scaled = given, rest[0]
        scale_back(db, w, d_scaled)
    cw, hp, rows = layer_params(par, layer)
    e0, e1 = segment_ends(lens)
    masks = conv_masks(e0, e1)
    raw, step, cum, columns = steps_of(proj[:, 1280:1408], hp)
    cumr[...] = cum
    colr[...] = columns
    norm_cols = jnp.transpose(jnp.concatenate(
        [jnp.concatenate([coef[i] for i in range(4)], axis=1), jnp.zeros((120, T), F32)], axis=0
    ))
    s_col = jnp.broadcast_to(norm_cols[:, 0:1], (T, 128))
    k_col = jnp.broadcast_to(norm_cols[:, 1:2], (T, 128))
    sums[...] = jnp.zeros_like(sums)
    d_skip = jnp.zeros((8, T), F32)
    for j in range(4):
        selector = head_selector(j)
        pre = kept[:, tile(j)]
        act = pre * sigmoid(pre)
        inn[:, tile(j)] = act
        xb[:, tile(j)] = (act * pair_columns(columns, HL, j)).astype(BF16)
        z = proj[:, tile(j)]
        sig = sigmoid(z)
        gate = z * sig
        y = yssd[:, tile(j)] + skip_row(hp, j) * act
        gated = y * gate
        gs = gated * s_col
        gain = rows[0:1, tile(j)]
        dsc = d_scaled[:, tile(j)]
        scaled[:, tile(j)] = (gs * gain).astype(BF16)
        sums[5:6, tile(j)] = jnp.sum(gs * dsc, axis=0, keepdims=True)
        d_gated = s_col * gain * dsc - gated * k_col
        d_proj[:, tile(j)] = (d_gated * y * (sig * (1.0 + z * (1.0 - sig)))).astype(BF16)
        dy = d_gated * gate
        dyf[:, tile(j)] = dy
        dyb[:, tile(j)] = dy.astype(BF16)
        d_skip = d_skip + sum_rows_nt(selector, dy * act, 2)
    for j, ref in ((0, bb), (1, cb)):
        pre = kept[:, 512 + 128 * j : 640 + 128 * j]
        ref[...] = (pre * sigmoid(pre)).astype(BF16)
    if early is not None:
        early()
    d_c[...] = jnp.zeros_like(d_c)
    low = iota((128, 128), 1) < 64
    zero = jnp.zeros((128, 128), BF16)
    d_b_blocks = []
    for i in range(4):
        first = 128 * i
        n = T - first
        here = slice(first, first + 128)
        scores = dot_nt(bb[here, :], cb[first:T, :])
        q = iota((128, n), 0) + first
        p = iota((128, n), 1) + first
        bias = jnp.where((p >= q) & (segment_of(p, e0, e1) == segment_of(q, e0, e1)), 0.0, NEG).astype(F32)
        d_scores = jnp.zeros((128, n), F32)
        for j in range(4):
            x_tile = xb[here, tile(j)]
            dy_tile = dyb[first:T, tile(j)]
            heads_of = jnp.concatenate([jnp.where(low, x_tile, zero), jnp.where(low, zero, x_tile)], axis=0)
            d_mixing = dot_nt(heads_of, dy_tile)
            mixing = []
            for k in (0, 1):
                h = 2 * j + k
                decay = jnp.exp2(cumr[h : h + 1, first:T] - colr[here, h : h + 1] + bias)
                mixing.append((scores * decay).astype(BF16))
                d_scores = d_scores + d_mixing[128 * k : 128 * k + 128] * decay
            both = dot_nn(jnp.concatenate(mixing, axis=0), dy_tile)
            dx[here, tile(j)] = jnp.where(low, both[0:128], both[128:256])
        d_scores = d_scores.astype(BF16)
        d_b_blocks.append(dot_nn(d_scores, cb[first:T, :]))
        d_c[first:T, :] = d_c[first:T, :] + dot_tn(d_scores, bb[here, :])
    if later is not None:
        later()
    d_cum = jnp.zeros((8, T), F32)
    d_step = jnp.zeros((8, T), F32)
    for j in range(4):
        selector = head_selector(j)
        dxt = dx[:, tile(j)]
        act = inn[:, tile(j)]
        change = dyb[:, tile(j)].astype(F32) * yssd[:, tile(j)] - xb[:, tile(j)].astype(F32) * dxt
        d_cum = d_cum + sum_rows_nt(selector, change, 3)
        d_step = d_step + sum_rows_nt(selector, act * dxt, 2)
        d_act = pair_columns(columns, HL, j) * dxt + skip_row(hp, j) * dyf[:, tile(j)]
        v = proj[:, 512 + 128 * j : 640 + 128 * j]
        pre = kept[:, tile(j)]
        sig = sigmoid(pre)
        d_pre = d_act * (sig * (1.0 + pre * (1.0 - sig)))
        d_proj[:, 512 + 128 * j : 640 + 128 * j] = conv_back(d_pre, v, masks, cw, tile(j), sums, 128 * j).astype(BF16)
    for j in (0, 1):
        lanes = slice(512 + 128 * j, 640 + 128 * j)
        at = slice(1024 + 128 * j, 1152 + 128 * j)
        v = proj[:, at]
        pre = kept[:, lanes]
        sig = sigmoid(pre)
        d_act = jnp.concatenate(d_b_blocks, axis=0) if j == 0 else d_c[...]
        d_pre = d_act * (sig * (1.0 + pre * (1.0 - sig)))
        d_proj[:, at] = conv_back(d_pre, v, masks, cw, lanes, sums, 512 + 128 * j).astype(BF16)
    lower = jnp.where(iota((T, T), 0) >= iota((T, T), 1), 1.0, 0.0).astype(BF16)
    d_a = rows_times(d_cum, lower)
    rate = hp[:, 1:2]
    d_raw = (d_step + rate * d_a) * sigmoid(raw)
    d_proj[:, 1280:1408] = jnp.transpose(
        jnp.concatenate([d_raw, jnp.zeros((120, T), F32)], axis=0)
    ).astype(BF16)
    bias_grad = jnp.broadcast_to(jnp.sum(d_raw, axis=1, keepdims=True), (8, 128))
    rate_grad = jnp.broadcast_to(jnp.sum(d_a * step, axis=1, keepdims=True) * rate, (8, 128))
    skip_grad = jnp.broadcast_to(jnp.sum(d_skip, axis=1, keepdims=True), (8, 128))
    lane = iota((8, 128), 1)
    by_head = jnp.where(
        lane == 0, bias_grad, jnp.where(lane == 1, rate_grad, jnp.where(lane == 2, skip_grad, 0.0))
    )
    heads[...] = jnp.transpose(jnp.concatenate([by_head, jnp.zeros((120, 128), F32)], axis=0))[0:8]
    for x in range(4):
        back = dot_nt(d_proj[...], w[x, :, :, 0:WP].reshape(256, WP)).astype(BF16)
        dh[:, :, 256 * x : 256 * x + 256] = back.reshape(4, ROWS, 256)


def bwd_scratch():
    return [
        VM((4, ROWS, D), BF16),
        VM((T, WP), BF16),
        VM((T, CH), BF16),
    ], [
        VM((T, CH), F32),
        VM((T, CH), BF16),
        VM((T, CH), BF16),
        VM((T, CH), F32),
        VM((T, CH), F32),
        VM((T, N), BF16),
        VM((T, N), BF16),
        VM((T, N), F32),
        VM((8, T), F32),
        VM((T, 128), F32),
    ]


def places():
    section = lax.axis_index("section")
    dp = lax.axis_index("dp")
    return section, dp // 4, dp % 4, lax.axis_index("tensor")


class Peers:
    def __init__(self):
        self.c, self.x, self.z, self.t = places()
        self.core = {"section": 1 - self.c}
        self.xs = [{"dp": ((self.x + o) % 4) * 4 + self.z} for o in (1, 2, 3)]
        self.zs = [{"dp": self.x * 4 + (self.z + o) % 4} for o in (1, 2, 3)]
        self.ts = [{"tensor": (self.t + o) % 4} for o in (1, 2, 3)]
        self.far_ts = [{"section": 1 - self.c, "tensor": (self.t + o) % 4} for o in (1, 2, 3)]

    def near_dp(self):
        return [self.core] + self.xs + self.zs + self.ts

    def everyone(self):
        return [self.core] + self.xs + self.zs + self.ts + self.far_ts


def barrier_start(peers):
    barrier = pltpu.get_barrier_semaphore()
    for peer in peers:
        pl.semaphore_signal(barrier, inc=1, device_id=peer, device_id_type=MESH)


def barrier_end(peers):
    pl.semaphore_wait(pltpu.get_barrier_semaphore(), len(peers))


def greet(peers):
    barrier_start(peers)
    barrier_end(peers)


class Link:
    def __init__(self, send_sems, recv_sems):
        self.send_sems, self.recv_sems, self.sent = send_sems, recv_sems, []

    def send(self, src, dst, peer):
        k = len(self.sent)
        copy = pltpu.make_async_remote_copy(
            src_ref=src, dst_ref=dst, send_sem=self.send_sems.at[k], recv_sem=self.recv_sems.at[k],
            device_id=peer, device_id_type=MESH,
        )
        copy.start()
        self.sent.append(copy)
        return copy

    def drain(self):
        for copy in self.sent:
            copy.wait_send()


def spread(link, block, r, peers):
    plus, minus = peers[0], peers[2]

    def go(k, half, peer):
        return link.send(block(k, half), block(k, half), peer)

    from_left = [go(r, 0, plus)]
    from_right = [go(r, 1, minus)]
    from_left.append(go(r, 1, plus))
    from_right.append(go(r, 0, minus))
    yield
    from_left[0].wait_recv()
    far = [go((r + 3) % 4, 0, plus)]
    from_right[0].wait_recv()
    far.append(go((r + 1) % 4, 1, minus))
    yield
    for copy in (from_left[1], from_right[1]):
        copy.wait_recv()
    yield
    for copy in far:
        copy.wait_recv()
    yield


def collect(link, part, relay, sums, inbox, r, peers):
    plus, minus = peers[0], peers[2]
    left, right, far = (r + 3) % 4, (r + 1) % 4, (r + 2) % 4
    up = link.send(part(far, 0), relay.at[0], plus)
    down = link.send(part(far, 1), relay.at[1], minus)
    last = [
        link.send(part(right, 1), inbox(0, 1), plus),
        link.send(part(left, 0), inbox(1, 0), minus),
    ]
    yield
    up.wait_recv()
    sums[0] = (part(right, 0)[...].astype(F32) + relay[0].astype(F32)).astype(BF16)
    last.append(link.send(sums.at[0], inbox(0, 0), plus))
    down.wait_recv()
    sums[1] = (part(left, 1)[...].astype(F32) + relay[1].astype(F32)).astype(BF16)
    last.append(link.send(sums.at[1], inbox(1, 1), minus))
    yield
    for copy in last:
        copy.wait_recv()
    yield


def run(steps):
    for _ in steps:
        pass


def token_halves(ref):
    return lambda k, half: ref.at[k, pl.ds(64 * half, 64)]


def collect_tokens(link, ref, relay, sums, inbox, me):
    return collect(link, token_halves(ref), relay, sums, token_halves(inbox), me.t, me.ts)


def spread_tokens(link, ref, me):
    return spread(link, token_halves(ref), me.t, me.ts)


def core_rows(c):
    first = pl.multiple_of(32 * c, 32)
    return pl.ds(first, 32), pl.ds(first, 16), pl.ds(pl.multiple_of(32 * c + 16, 16), 16)


def gather_layer(link, own_sem, shard, w, me):
    c, x, z = me.c, me.x, me.z
    whole, a, b = core_rows(c)
    own = pltpu.make_async_copy(shard, w.at[x, z, whole], own_sem)
    own.start()
    first = []
    for o in range(3):
        first.append(link.send(shard.at[pl.ds(0, 16)], w.at[x, z, a], me.zs[o]))
        first.append(link.send(shard.at[pl.ds(16, 16)], w.at[x, z, b], me.xs[o]))
    yield
    own.wait()
    for copy in first:
        copy.wait_recv()
    along_x = spread(link, lambda k, half: w.at[k, pl.ds(2 * half, 2), a], x, me.xs)
    along_z = spread(link, lambda k, half: w.at[pl.ds(2 * half, 2), k, b], z, me.zs)
    next(along_x)
    next(along_z)
    core = []

    def to_core(o):
        block_a = w.at[(x + o) % 4, :, a]
        block_b = w.at[:, (z + o) % 4, b]
        core.append(link.send(block_a, block_a, me.core))
        core.append(link.send(block_b, block_b, me.core))

    to_core(0)
    yield
    next(along_x)
    next(along_z)
    yield
    next(along_x)
    next(along_z)
    to_core(1)
    to_core(3)
    yield
    next(along_x)
    next(along_z)
    to_core(2)
    yield
    for copy in core:
        copy.wait_recv()
    yield


GATHER_COPIES = 6 + 12 + 8


def reduce_rings(link, factors, grads, out_a, out_b, core_in, acc, relay, sums, inbox, me):
    c, x, z = me.c, me.x, me.z
    hid, d_proj, db, scaled = factors
    a, b = pl.ds(0, 16), pl.ds(16, 16)
    arrive = []
    for xx in range(4):
        at = slice(256 * xx, 256 * xx + 256)
        rows_in = dot_tn(hid[:, :, at].reshape(T, 256), d_proj[...]).astype(BF16)
        rows_out = dot_tn(db[:, :, at].reshape(T, 256), scaled[...]).astype(BF16)
        for k in range(8):
            block = slice(32 * k, 32 * k + 32)
            grads[k % 2, xx, k // 2, :, 0:WP] = rows_in[block]
            grads[k % 2, xx, k // 2, :, WP:WALL] = rows_out[block]
        arrive.append(link.send(grads.at[1 - c, xx], core_in.at[xx], me.core))
        if xx % 2 == 1:
            yield
    for xx in range(4):
        arrive[xx].wait_recv()
        acc[xx] = grads[c, xx] + core_in[xx]
    along_x = collect(
        link, lambda k, half: acc.at[k, pl.ds(2 * half, 2), a], relay.at[0], sums.at[0],
        lambda d, half: inbox.at[0, d, pl.ds(2 * half, 2)], x, me.xs,
    )
    next(along_x)
    along_z = collect(
        link, lambda k, half: acc.at[pl.ds(2 * half, 2), k, b], relay.at[1], sums.at[1],
        lambda d, half: inbox.at[1, d, pl.ds(2 * half, 2)], z, me.zs,
    )
    next(along_z)
    yield
    next(along_x)
    next(along_z)
    yield
    next(along_x)
    out_a[...] = (
        acc[x, :, a].astype(F32) + inbox[0, 0].astype(F32) + inbox[0, 1].astype(F32)
    ).astype(BF16)
    next(along_z)
    out_b[...] = (
        acc[:, z, b].astype(F32) + inbox[1, 0].astype(F32) + inbox[1, 1].astype(F32)
    ).astype(BF16)
    yield


RING_COPIES = 4 + 12


def reduce_last(link, sum_a, sum_b, out, bc_all, last_in, me):
    c, x, z = me.c, me.x, me.z
    last_a = [link.send(sum_a.at[(z + o + 1) % 4], last_in.at[0, o], me.zs[o]) for o in range(3)]
    last_b = [link.send(sum_b.at[(x + o + 1) % 4], last_in.at[1, o], me.xs[o]) for o in range(3)]
    yield
    rows, rows_a, rows_b = core_rows(c)
    for k, (copies, at, mine) in enumerate(((last_a, rows_a, sum_a.at[z]), (last_b, rows_b, sum_b.at[x]))):
        for copy in copies:
            copy.wait_recv()
        out[at, :] = (
            mine[...].astype(F32)
            + last_in[k, 0].astype(F32) + last_in[k, 1].astype(F32) + last_in[k, 2].astype(F32)
        )
    swap = [link.send(out.at[rows], out.at[rows], me.core)]

    def wanted(t):
        return pl.ds(pl.multiple_of(32 * c + 16 * (t % 2), 16), 16)

    bc_all[me.t, c] = out[wanted(me.t), 1024:1280]
    slot = bc_all.at[me.t, c]
    swap.append(link.send(slot, slot, me.core))
    for o in range(3):
        block = out.at[wanted(me.t + o + 1), pl.ds(1024, 256)]
        swap.append(link.send(block, slot, me.ts[o]))
        swap.append(link.send(block, slot, me.far_ts[o]))
    yield
    for copy in swap:
        copy.wait_recv()
    yield


LAST_COPIES = 6 + 8


def ring_scratch():
    return [
        VM((2, 4, 4, 32, WALL), BF16),
        VM((4, 4, 32, WALL), BF16), VM((4, 4, 32, WALL), BF16),
        VM((2, 2, 2, 16, WALL), BF16), VM((2, 2, 2, 16, WALL), BF16),
        VM((2, 2, 4, 16, WALL), BF16),
    ]


def last_scratch():
    return [VM((64, WALL), F32), VM((4, 2, 16, 2 * N), F32), VM((2, 3, 16, WALL), BF16)]


def token_scratch():
    return [VM((2, 64, D), BF16), VM((2, 64, D), BF16), VM((2, ROWS, D), BF16)]


def dma_sems(n):
    return pltpu.SemaphoreType.DMA((n,))


def link_scratch(*counts):
    return [pltpu.SemaphoreType.DMA((n,)) for n in counts for _ in range(2)]


def input_norm(u, gain):
    return u * lax.rsqrt(jnp.mean(u * u, axis=-1, keepdims=True) + EPSILON) * gain


def gain_of(par, layer):
    return par[layer, 0:1, 1408:2432]


def gather_kernel(
    lengths, w_in, w_bc, w_dt, w_out, conv_w, flat, u0, cot,
    w0, shard1, par, hid, db, valid,
    wsh, shards, turned, own_sem, g_s, g_r, e_s, e_r, h_s, h_r, d_s, d_r,
):
    me = Peers()
    c, t = me.c, me.t
    barrier_start(me.near_dp())
    wsh[:, 0:WZX] = w_in[...]
    wsh[:, 1024:1280] = w_bc[...]
    dt_rows = jnp.concatenate([w_dt[...].astype(F32), jnp.zeros((HL, 64), F32)], axis=1)
    dt_rows = jnp.concatenate([dt_rows, jnp.zeros((120, 128), F32)], axis=0)
    wsh[:, 1280:1408] = jnp.transpose(dt_rows)[0:64].astype(BF16)
    wsh[:, WP:WALL] = w_out[...]
    shards[c] = wsh[core_rows(c)[0], :]
    own = pl.ds(pl.multiple_of(CH * t, CH), CH)
    par[c] = jnp.zeros((8, 2432), F32)
    par[c, 0:4, 0:512] = conv_w[:, own]
    par[c, 0:4, 512:768] = conv_w[:, DI : DI + 2 * N]
    par[c, 4:5, 0:512] = flat[:, own]
    par[c, 4:5, 512:768] = flat[:, DI : DI + 2 * N]
    by_row = jnp.broadcast_to(flat[:, 5376:5504], (8, 128))
    row = iota((8, 128), 0)
    by_row = jnp.where(
        row == 0, by_row,
        jnp.where(row == 1, pltpu.roll(by_row, 128 - H, 1), pltpu.roll(by_row, 128 - 2 * H, 1)),
    )
    turned[...] = jnp.transpose(jnp.concatenate([by_row, jnp.zeros((120, 128), F32)], axis=0))
    heads = turned[pl.ds(pl.multiple_of(HL * t, HL), HL), :]
    par[c, :, 768:896] = jnp.where(iota((8, 128), 1) == 1, -jnp.exp(heads), heads)
    par[c, 0:1, 896:1408] = flat[:, pl.ds(pl.multiple_of(2304 + CH * t, 256), CH)]
    par[c, 0:1, 1408:2432] = flat[:, 4352:5376]
    end = lengths[c, 0, 0] + lengths[c, 0, 1]
    valid[...] = jnp.where(iota((ROWS, 128), 0) + ROWS * t < end, 1.0, 0.0).astype(F32)
    barrier_end(me.near_dp())
    early, weights = Link(e_s, e_r), Link(g_s, g_r)
    theirs = early.send(wsh.at[core_rows(1 - c)[0]], shards.at[c], me.core)
    par_copy = early.send(par.at[c], par.at[c], me.core)
    for j in range(8):
        db[t, :, tile(j)] = (cot[:, tile(j)] * valid[...]).astype(BF16)
    theirs.wait_recv()
    layer0 = gather_layer(weights, own_sem.at[0], shards.at[0], w0, me)
    next(layer0)
    par_copy.wait_recv()
    hid[t] = input_norm(u0[...], gain_of(par, 0)).astype(BF16)
    tokens, branch = Link(h_s, h_r), Link(d_s, d_r)
    hid_steps = spread_tokens(tokens, hid, me)
    db_steps = spread_tokens(branch, db, me)
    next(hid_steps)
    next(layer0)
    next(db_steps)
    next(layer0)
    next(hid_steps)
    shard1[...] = shards[1]
    next(layer0)
    next(db_steps)
    run(layer0)
    run(hid_steps)
    run(db_steps)
    for link in (early, weights, tokens, branch):
        link.drain()


def gather(*arrays):
    return pl.pallas_call(
        gather_kernel,
        out_shape=(
            jax.ShapeDtypeStruct((4, 4, 64, WALL), BF16),
            jax.ShapeDtypeStruct((32, WALL), BF16),
            jax.ShapeDtypeStruct((2, 8, 2432), F32),
            jax.ShapeDtypeStruct((4, ROWS, D), BF16),
            jax.ShapeDtypeStruct((4, ROWS, D), BF16),
            jax.ShapeDtypeStruct((ROWS, 128), F32),
        ),
        in_specs=[pl.BlockSpec(memory_space=pltpu.SMEM)] + vmem_specs(8),
        out_specs=tuple(vmem_specs(6)),
        scratch_shapes=[
            VM((64, WALL), BF16), VM((2, 32, WALL), BF16), VM((128, 128), F32),
            dma_sems(1),
        ]
        + link_scratch(GATHER_COPIES, 2, 6, 6),
        compiler_params=pltpu.CompilerParams(
            collective_id=0, has_side_effects=True, vmem_limit_bytes=6 << 20
        ),
        name="gather_weights",
    )(*arrays)


def column_of(row):
    return jnp.transpose(jnp.broadcast_to(row, (128, 128)))


def middle_kernel(
    lens, par, hid0, w0, u0, valid, shard1,
    proj, kept, yssd, total, u_next, s_out, hid, w1,
    part, st, gg, inn, xb, bb, cb, cumr, colr,
    relay, sums, inbox, sbuf, own_sem, g_s, g_r, p_s, p_r, b_s, b_r, h_s, h_r,
):
    me = Peers()
    t = me.t
    barrier_start(me.near_dp())
    weights, tokens, small, spreading = Link(g_s, g_r), Link(p_s, p_r), Link(b_s, b_r), Link(h_s, h_r)
    started = []

    def early():
        barrier_end(me.near_dp())
        started.append(gather_layer(weights, own_sem.at[0], shard1, w1, me))
        next(started[0])

    mixer_fwd_kernel(
        0, lens, par, hid0, w0, proj, kept, part, yssd, st, gg, inn, xb, bb, cb, cumr, colr, early=early
    )
    layer1 = started[0]
    sum_steps = collect_tokens(tokens, part, relay, sums, inbox, me)
    next(sum_steps)
    stats = [small.send(st.at[(t + o + 1) % 4], sbuf.at[o], me.ts[o]) for o in range(3)]
    next(layer1)
    next(sum_steps)
    for copy in stats:
        copy.wait_recv()
    s_row = lax.rsqrt((st[t] + sbuf[0] + sbuf[1] + sbuf[2]) / DI + EPSILON)
    s_out[...] = s_row
    scale = column_of(s_row[0:1]) * valid[...]
    next(layer1)
    run(sum_steps)
    total[...] = part[t].astype(F32) + inbox[0].astype(F32) + inbox[1].astype(F32)
    for j in range(8):
        u_next[:, tile(j)] = u0[:, tile(j)] + scale * total[:, tile(j)]
    hid[t] = input_norm(u_next[...], gain_of(par, 1)).astype(BF16)
    hid_steps = spread_tokens(spreading, hid, me)
    next(hid_steps)
    next(layer1)
    next(hid_steps)
    run(layer1)
    run(hid_steps)
    for link in (weights, tokens, small, spreading):
        link.drain()


def middle(*arrays):
    return pl.pallas_call(
        middle_kernel,
        out_shape=(
            jax.ShapeDtypeStruct((T, WP), F32),
            jax.ShapeDtypeStruct((T, 768), F32),
            jax.ShapeDtypeStruct((T, CH), F32),
            jax.ShapeDtypeStruct((ROWS, D), F32),
            jax.ShapeDtypeStruct((ROWS, D), F32),
            jax.ShapeDtypeStruct((8, 128), F32),
            jax.ShapeDtypeStruct((4, ROWS, D), BF16),
            jax.ShapeDtypeStruct((4, 4, 64, WALL), BF16),
        ),
        in_specs=[pl.BlockSpec(memory_space=pltpu.SMEM)] + vmem_specs(6),
        out_specs=tuple(vmem_specs(8)),
        scratch_shapes=[VM((4, ROWS, D), BF16), VM((4, 8, 128), F32)] + fwd_scratch() + token_scratch()
        + [VM((3, 8, 128), F32), pltpu.SemaphoreType.DMA((1,))]
        + link_scratch(GATHER_COPIES, 6, 3, 6),
        compiler_params=pltpu.CompilerParams(
            collective_id=1, has_side_effects=True, vmem_limit_bytes=16 << 20
        ),
        name="forward_0_and_tokens",
    )(*arrays)


def stats_exchange(link, st, buf, coef, me):
    barrier_end(me.ts)
    copies = [link.send(st, buf.at[me.t], peer) for peer in me.ts]
    buf[me.t] = st[...]
    yield
    for copy in copies:
        copy.wait_recv()
    for i in range(4):
        both = buf[0, i] + buf[1, i] + buf[2, i] + buf[3, i]
        s = lax.rsqrt(both[0:1] / DI + EPSILON)
        k = s * s * s * (both[1:2] / DI)
        row = iota((8, 128), 0)
        coef[i] = jnp.where(row == 0, s, jnp.where(row == 1, k, 0.0))
    link.drain()
    yield


def norm_back(u, gain, g, d_hidden):
    r = lax.rsqrt(jnp.mean(u * u, axis=-1, keepdims=True) + EPSILON)
    mean = jnp.mean(u * gain * d_hidden, axis=-1, keepdims=True)
    d_u = g + r * gain * d_hidden - u * (r * r * r) * mean
    return d_u, jnp.sum(u * r * d_hidden, axis=0, keepdims=True)


def back_middle_kernel(
    lens, par, w1, proj1, kept1, yssd1, coef1, d_scaled1, u, cot, valid, total0, s0, hid1, db1,
    sums1, heads1, g1, ng, db, coef, sum_a, sum_b,
    dh, d_proj1, scaled1, inn, xb, dyb, dyf, dx, bb, cb, d_c, cumr, colr,
    relay, sums, inbox, grads, core_in, acc, g_relay, g_sums, g_inbox,
    g_s, g_r, p_s, p_r, b_s, b_r, h_s, h_r,
):
    me = Peers()
    t = me.t
    barrier_start(me.near_dp())
    mixer_bwd_kernel(
        1, lens, par, w1, proj1, kept1, yssd1, coef1, d_scaled1, dh, d_proj1, scaled1, sums1, heads1,
        inn, xb, dyb, dyf, dx, bb, cb, d_c, cumr, colr,
        early=lambda: barrier_end(me.near_dp()),
    )
    weights, tokens, small, spreading = Link(g_s, g_r), Link(p_s, p_r), Link(b_s, b_r), Link(h_s, h_r)
    sum_steps = collect_tokens(tokens, dh, relay, sums, inbox, me)
    next(sum_steps)
    layer1 = reduce_rings(
        weights, (hid1, d_proj1, db1, scaled1), grads, sum_a, sum_b, core_in, acc,
        g_relay, g_sums, g_inbox, me,
    )
    next(layer1)
    next(sum_steps)
    next(layer1)
    next(layer1)
    run(sum_steps)
    total = dh[t].astype(F32) + inbox[0].astype(F32) + inbox[1].astype(F32)
    d_u, gain_term = norm_back(u[...], gain_of(par, 1), cot[...], total)
    g1[...] = d_u
    ng[...] = gain_term
    mean = jnp.zeros((ROWS, 128), F32)
    for j in range(8):
        d_branch = (g1[:, tile(j)] * valid[...]).astype(BF16)
        db[t, :, tile(j)] = d_branch
        mean = mean + d_branch.astype(F32) * total0[:, tile(j)]
    db_steps = spread_tokens(spreading, db, me)
    next(db_steps)
    mean = jnp.broadcast_to(jnp.sum(mean, axis=-1, keepdims=True), (128, 128))
    mean_row = jnp.transpose(mean)[0:8] / DI
    s = s0[0:1, :]
    row = iota((8, 128), 0)
    coef[t] = jnp.where(row == 0, s, jnp.where(row == 1, s * s * s * mean_row, 0.0))
    coef_copies = [small.send(coef.at[t], coef.at[t], peer) for peer in me.ts]
    next(layer1)
    next(db_steps)
    next(layer1)
    run(db_steps)
    for copy in coef_copies:
        copy.wait_recv()
    for link in (weights, tokens, small, spreading):
        link.drain()


def back_middle(*arrays):
    return pl.pallas_call(
        back_middle_kernel,
        out_shape=(
            jax.ShapeDtypeStruct((8, 768), F32),
            jax.ShapeDtypeStruct((8, 128), F32),
            jax.ShapeDtypeStruct((ROWS, D), F32),
            jax.ShapeDtypeStruct((1, D), F32),
            jax.ShapeDtypeStruct((4, ROWS, D), BF16),
            jax.ShapeDtypeStruct((4, 8, 128), F32),
            jax.ShapeDtypeStruct((4, 16, WALL), BF16),
            jax.ShapeDtypeStruct((4, 16, WALL), BF16),
        ),
        in_specs=[pl.BlockSpec(memory_space=pltpu.SMEM)] + vmem_specs(14),
        out_specs=tuple(vmem_specs(8)),
        scratch_shapes=bwd_scratch()[0] + bwd_scratch()[1] + token_scratch() + ring_scratch() + link_scratch(RING_COPIES, 6, 3, 6),
        compiler_params=pltpu.CompilerParams(
            collective_id=3, has_side_effects=True, vmem_limit_bytes=26 << 20
        ),
        name="backward_1_and_tokens",
    )(*arrays)


def small_sum(link, own, arrived, by_z, by_x, by_t, me):
    c, x, z, t = me.c, me.x, me.z, me.t
    swap = link.send(own.at[1 - c], arrived, me.core)
    yield
    swap.wait_recv()
    by_z[z] = own[c] + arrived[...]
    copies = [link.send(by_z.at[z], by_z.at[z], peer) for peer in me.zs]
    yield
    for copy in copies:
        copy.wait_recv()
    by_x[x] = by_z[0] + by_z[1] + by_z[2] + by_z[3]
    copies = [link.send(by_x.at[x], by_x.at[x], peer) for peer in me.xs]
    yield
    for copy in copies:
        copy.wait_recv()
    by_t[t] = by_x[0] + by_x[1] + by_x[2] + by_x[3]
    copies = [link.send(by_t.at[t], by_t.at[t], peer) for peer in me.ts]
    yield
    for copy in copies:
        copy.wait_recv()
    yield


def finish_kernel(
    lens, w0, proj0, kept0, yssd0, coef0, db0,
    part, u0, u1, g1, valid, par, coef1, ng1, sums1, heads1, sum_a1, sum_b1, hid0,
    lo, lg, smt, nmt, picked, o_bc,
    dh, d_proj0, scaled0, inn, xb, dyb, dyf, dx, bb, cb, d_c, cumr, colr, d_scaled0, sums0, heads0,
    relay, sums, inbox, relay2, sums2, inbox2, los, lgs, sms, smr, smz, smx, nms, nmr, nmz, nmx, sum_a0, sum_b0,
    grads, core_in, acc, g_relay, g_sums, g_inbox, w_grad0, bc_all0, last_in0, w_grad1, bc_all1, last_in1,
    g_s, g_r, f_s, f_r, l_s, l_r, p_s, p_r, q_s, q_r, b_s, b_r,
):
    me = Peers()
    c, x, z, t = me.c, me.x, me.z, me.t
    barrier_start(me.everyone())
    weights, final0, final1 = Link(g_s, g_r), Link(f_s, f_r), Link(l_s, l_r)
    tokens, tokens2, small = Link(p_s, p_r), Link(q_s, q_r), Link(b_s, b_r)
    last1 = reduce_last(final1, sum_a1, sum_b1, w_grad1, bc_all1, last_in1, me)
    out_steps = collect_tokens(tokens2, part, relay2, sums2, inbox2, me)

    def early():
        barrier_end(me.everyone())
        next(last1)
        next(out_steps)

    def later():
        next(last1)
        next(out_steps)

    mixer_bwd_kernel(
        0, lens, par, w0, proj0, kept0, yssd0, coef0, db0, dh, d_proj0, scaled0, sums0, heads0,
        inn, xb, dyb, dyf, dx, bb, cb, d_c, cumr, colr, d_scaled0, early=early, later=later,
    )
    for layer, (by_channel, heads) in enumerate(((sums0, heads0), (sums1, heads1))):
        sms[layer, 0:8, :] = by_channel[:, 0:512]
        sms[layer, 8:16, 0:256] = by_channel[:, 512:768]
        sms[layer, 8:16, 256:384] = heads[...]
        sms[layer, 8:16, 384:512] = jnp.zeros((8, 128), F32)
    chain = small_sum(small, sms, smr, smz, smx, smt, me)
    next(chain)
    back_steps = collect_tokens(tokens, dh, relay, sums, inbox, me)
    next(back_steps)
    layer0 = reduce_rings(
        weights, (hid0, d_proj0, db0, scaled0), grads, sum_a0, sum_b0, core_in, acc,
        g_relay, g_sums, g_inbox, me,
    )
    next(layer0)
    next(chain)
    next(back_steps)
    next(layer0)
    next(layer0)
    next(chain)
    los[0] = u1[...]
    lgs[1] = g1[...]
    run(back_steps)
    total = dh[t].astype(F32) + inbox[0].astype(F32) + inbox[1].astype(F32)
    d_u, gain_term = norm_back(u0[...], gain_of(par, 0), g1[...], total)
    lgs[0] = d_u
    lg_copy = small.send(lgs.at[1 - c], lg.at[c], me.core)
    lg[c] = lgs[c]
    next(layer0)
    for layer, term in enumerate((gain_term, ng1[...])):
        for j in range(8):
            nms[layer, j : j + 1, :] = term[:, tile(j)]
    norm_chain = small_sum(small, nms, nmr, nmz, nmx, nmt, me)
    next(norm_chain)
    next(chain)
    run(last1)
    next(norm_chain)
    next(layer0)
    last0 = reduce_last(final0, sum_a0, sum_b0, w_grad0, bc_all0, last_in0, me)
    next(last0)
    next(norm_chain)
    run(out_steps)
    los[1] = part[t].astype(F32) + inbox2[0].astype(F32) + inbox2[1].astype(F32)
    scale = column_of(coef1[t][0:1]) * valid[...]
    for j in range(8):
        los[1, :, tile(j)] = u1[:, tile(j)] + scale * los[1, :, tile(j)]
    lo_copy = small.send(los.at[1 - c], lo.at[c], me.core)
    lo[c] = los[c]
    next(norm_chain)
    next(last0)
    run(last0)
    picked[...] = jnp.where(c == 0, w_grad0[...], w_grad1[...])
    half = t // 2
    bc0 = bc_all0[0, half] + bc_all0[1, half] + bc_all0[2, half] + bc_all0[3, half]
    bc1 = bc_all1[0, half] + bc_all1[1, half] + bc_all1[2, half] + bc_all1[3, half]
    o_bc[...] = jnp.where(c == 0, bc0, bc1)
    run(chain)
    run(norm_chain)
    lo_copy.wait_recv()
    lg_copy.wait_recv()
    for link in (weights, final0, final1, tokens, tokens2, small):
        link.drain()


def finish(*arrays):
    return pl.pallas_call(
        finish_kernel,
        out_shape=(
            jax.ShapeDtypeStruct((2, ROWS, D), F32),
            jax.ShapeDtypeStruct((2, ROWS, D), F32),
            jax.ShapeDtypeStruct((4, 16, 512), F32),
            jax.ShapeDtypeStruct((4, 8, 128), F32),
            jax.ShapeDtypeStruct((64, WALL), F32),
            jax.ShapeDtypeStruct((16, 2 * N), F32),
        ),
        in_specs=[pl.BlockSpec(memory_space=pltpu.SMEM)] + vmem_specs(19),
        out_specs=tuple(vmem_specs(6)),
        scratch_shapes=bwd_scratch()[0] + bwd_scratch()[1]
        + [VM((T, CH), F32), VM((8, 768), F32), VM((8, 128), F32)]
        + token_scratch() + token_scratch()
        + [
            VM((2, ROWS, D), F32), VM((2, ROWS, D), F32),
            VM((2, 16, 512), F32), VM((16, 512), F32), VM((4, 16, 512), F32), VM((4, 16, 512), F32),
            VM((2, 8, 128), F32), VM((8, 128), F32), VM((4, 8, 128), F32), VM((4, 8, 128), F32),
            VM((4, 16, WALL), BF16), VM((4, 16, WALL), BF16),
        ]
        + ring_scratch() + last_scratch() + last_scratch()
        + link_scratch(RING_COPIES, LAST_COPIES, LAST_COPIES, 6, 6, 22),
        compiler_params=pltpu.CompilerParams(
            collective_id=4, has_side_effects=True, vmem_limit_bytes=34 << 20
        ),
        name="backward_0_and_gradients",
    )(*arrays)


def write_kernel(lo, lg, smt, nmt, picked, bc, *rest):
    outs, (in_part, dt, conv_w, conv_b, gain, norm, heads, sem) = rest[:13], rest[13:]
    (o_lo, o_lg, o_norm, o_in, o_bc, o_dt, o_cw, o_cb, o_dtb, o_alog, o_skip, o_gain, o_out) = outs
    copies = []

    def write(src, dst):
        copy = pltpu.make_async_copy(src, dst, sem.at[len(copies)])
        copy.start()
        copies.append(copy)

    write(lo, o_lo)
    write(lg, o_lg)
    write(bc, o_bc)
    in_part[:, 0, :] = picked[:, 0:512]
    in_part[:, 1, :] = picked[:, 512:1024]
    write(in_part, o_in)
    write(picked.at[:, pl.ds(WP, CH)], o_out)
    dt_rows = jnp.concatenate([picked[:, 1280:1408], jnp.zeros((64, 128), F32)], axis=0)
    dt[...] = jnp.transpose(dt_rows)[0:HL, 0:64]
    write(dt, o_dt)
    shared = smt[0, 8:16] + smt[1, 8:16] + smt[2, 8:16] + smt[3, 8:16]
    norms = nmt[0] + nmt[1] + nmt[2] + nmt[3]
    for j in range(8):
        norm[:, tile(j)] = norms[j : j + 1]
    write(norm, o_norm)
    conv_w[:, DI : DI + 2 * N] = shared[0:4, 0:256]
    conv_b[:, DI : DI + 2 * N] = shared[4:5, 0:256]
    for k in range(4):
        at = slice(512 * k, 512 * k + 512)
        conv_w[:, at] = smt[k, 0:4, :]
        conv_b[:, at] = smt[k, 4:5, :]
        gain[:, at] = smt[k, 5:6, :]
    write(conv_w, o_cw)
    write(conv_b, o_cb)
    write(gain, o_gain)
    all_heads = smt[0, 8:16, 256:384]
    for k in range(1, 4):
        all_heads = all_heads + pltpu.roll(smt[k, 8:16, 256:384], HL * k, 1)
    for k, out in ((0, o_dtb), (1, o_alog), (2, o_skip)):
        heads[k] = all_heads[k : k + 1, 0:H]
        write(heads.at[k], out)
    for copy in copies:
        copy.wait()


def write_outputs(*arrays):
    hbm_spec = pl.BlockSpec(memory_space=pltpu.HBM)
    shapes = [
        (2, ROWS, D), (2, ROWS, D), (1, D), (64, 2, CH), (16, 2 * N), (HL, 64), (CONV, DI + 2 * N),
        (1, DI + 2 * N), (1, H), (1, H), (1, H), (1, DI), (64, CH),
    ]
    return pl.pallas_call(
        write_kernel,
        out_shape=tuple(jax.ShapeDtypeStruct(shape, F32) for shape in shapes),
        in_specs=vmem_specs(6),
        out_specs=(hbm_spec,) * 13,
        scratch_shapes=[
            VM((64, 2, CH), F32), VM((HL, 64), F32), VM((CONV, DI + 2 * N), F32),
            VM((1, DI + 2 * N), F32), VM((1, DI), F32), VM((1, D), F32), VM((3, 1, H), F32),
            pltpu.SemaphoreType.DMA((13,)),
        ],
        compiler_params=pltpu.CompilerParams(vmem_limit_bytes=6 << 20),
        name="write_outputs",
    )(*arrays)


def body(
    activations, cotangent, lengths, norm_gain, in_weight, bc_weight, dt_weight, conv_weight,
    conv_bias, dt_bias, a_log, d_skip, gated_gain, out_weight,
):
    section = lax.axis_index("section")
    u0 = lax.dynamic_index_in_dim(activations, section, 0, keepdims=False)
    cot = lax.dynamic_index_in_dim(cotangent, section, 0, keepdims=False)
    flat = jnp.concatenate(
        [conv_bias, gated_gain, norm_gain, dt_bias, a_log, d_skip, jnp.zeros((1, 32), F32)], axis=1
    )
    w0, shard1, par, hid0, db1, valid = gather(
        lengths, in_weight[0].reshape(64, WZX), bc_weight[0], dt_weight[0].T, out_weight[0].T,
        conv_weight[0], flat, u0, cot,
    )
    proj0, kept0, y0, total0, u1, s0, hid1, w1 = middle(lengths, par, hid0, w0, u0, valid, shard1)
    proj1, kept1, part1, y1, coef1, d_scaled1 = mixer_fwd(1, lengths, par, hid1, w1, db1)
    sums1, heads1, g1, ng1, db0, coef0, sum_a1, sum_b1 = back_middle(
        lengths, par, w1, proj1, kept1, y1, coef1, d_scaled1, u1, cot, valid, total0, s0, hid1, db1
    )
    outs = write_outputs(
        *finish(
            lengths, w0, proj0, kept0, y0, coef0, db0, part1, u0, u1, g1, valid, par, coef1, ng1,
            sums1, heads1, sum_a1, sum_b1, hid0,
        )
    )
    outs = [out.T if k in (5, 12) else out for k, out in enumerate(outs)]
    plain = (2, 8, 9, 10, 7, 11)
    return tuple(out if k in plain else out[None] for k, out in enumerate(outs))


def solution(mesh):
    return jax.shard_map(
        body,
        mesh=mesh,
        in_specs=(
            P(None, ("dp", "tensor"), None),
            P(None, ("dp", "tensor"), None),
            P(None, "dp", None),
            P("section", None),
            P("section", "dp", None, "tensor"),
            P("section", "dp", None),
            P("section", "dp", "tensor"),
            P("section", None, None),
            P("section", None),
            P("section", None),
            P("section", None),
            P("section", None),
            P("section", None),
            P("section", "tensor", "dp"),
        ),
        out_specs=(
            P("section", None, ("dp", "tensor"), None),
            P("section", None, ("dp", "tensor"), None),
            P("section", None),
            P("section", "dp", None, "tensor"),
            P("section", ("dp", "tensor"), None),
            P("section", "dp", "tensor"),
            P("section", None, None),
            P("section", None),
            P("section", None),
            P("section", None),
            P("section", None),
            P("section", None),
            P("section", "tensor", "dp"),
        ),
        check_vma=False,
    )
```

```python
import functools

import jax
import jax.numpy as jnp
from jax import lax
from jax.experimental import pallas as pl
from jax.experimental.pallas import tpu as pltpu
from jax.sharding import PartitionSpec as P

D = 1024
DI = 2048
H = 32
N = 128
CONV = 4
T = 512
ROWS = 128
CH = 512
HL = 8
WZX = 1024
WP = 1408
WALL = 1920
NDP = 16
EPSILON = 1e-05
LOG2E = 1.4426950408889634
NEG = -1e30
F32 = jnp.float32
BF16 = jnp.bfloat16
MESH = pl.DeviceIdType.MESH
VM = pltpu.VMEM
FWD_VMEM = 12 << 20
BWD_VMEM = 16 << 20


def dot_nn(a, b):
    return lax.dot_general(a, b, (((1,), (0,)), ((), ())), preferred_element_type=F32)


def dot_nt(a, b):
    return lax.dot_general(a, b, (((1,), (1,)), ((), ())), preferred_element_type=F32)


def dot_tn(a, b):
    return lax.dot_general(a, b, (((0,), (0,)), ((), ())), preferred_element_type=F32)


def pieces(v, count):
    parts = []
    for _ in range(count):
        part = v.astype(BF16)
        parts.append(part)
        v = v - part.astype(F32)
    return parts


def sum_rows_nt(selector, v, count):
    return sum(dot_nt(selector, part) for part in pieces(v, count))


def rows_times(v, matrix):
    a, b, c = pieces(v, 3)
    stacked = jnp.concatenate([a.astype(F32), b.astype(F32), c.astype(F32), jnp.zeros_like(v)], 0)
    out = dot_nn(stacked.astype(BF16), matrix)
    return out[0:8] + out[8:16] + out[16:24]


def iota(shape, dim):
    return lax.broadcasted_iota(jnp.int32, shape, dim)


def segment_of(position, e0, e1):
    return (position >= e0).astype(jnp.int32) + (position >= e1).astype(jnp.int32)


def conv_masks(e0, e1):
    p = iota((T, 128), 0)
    seg = segment_of(p, e0, e1)
    return [
        jnp.where((p >= k) & (segment_of(p - k, e0, e1) == seg), 1.0, 0.0).astype(F32)
        for k in range(1, CONV)
    ]


def conv_pre(v, masks, cw, lanes):
    pre = cw[CONV : CONV + 1, lanes] + cw[CONV - 1 : CONV, lanes] * v
    for k in range(1, CONV):
        pre = pre + cw[CONV - 1 - k : CONV - k, lanes] * (masks[k - 1] * pltpu.roll(v, k, 0))
    return pre


def sigmoid(v):
    return 0.5 * jnp.tanh(0.5 * v) + 0.5


def steps_of(dt_tile, hp_ref):
    raw = jnp.transpose(dt_tile)[0:HL] + hp_ref[:, 0:1]
    step = jnp.maximum(raw, 0.0) + jnp.log1p(jnp.exp(-jnp.abs(raw)))
    rate = hp_ref[:, 1:2]
    upper = jnp.where(iota((T, T), 0) <= iota((T, T), 1), 1.0, 0.0).astype(BF16)
    cum = rows_times(step * rate, upper) * LOG2E
    columns = jnp.transpose(
        jnp.concatenate([cum, step, jnp.zeros((112, T), F32)], axis=0)
    )
    return raw, step, cum, columns


def pair_columns(columns, first, j, rows=T):
    low = iota((rows, 128), 1) < 64
    return jnp.where(
        low,
        jnp.broadcast_to(columns[:, first + 2 * j : first + 2 * j + 1], (rows, 128)),
        jnp.broadcast_to(columns[:, first + 2 * j + 1 : first + 2 * j + 2], (rows, 128)),
    )


def tile(j):
    return slice(128 * j, 128 * j + 128)


def layer_params(par, layer):
    return (
        par.at[layer, :, pl.ds(0, 768)],
        par.at[layer, :, pl.ds(768, 128)],
        par.at[layer, :, pl.ds(896, 512)],
    )


def skip_row(hp, j):
    low = iota((1, 128), 1) < 64
    first = jnp.broadcast_to(hp[2 * j : 2 * j + 1, 2:3], (1, 128))
    second = jnp.broadcast_to(hp[2 * j + 1 : 2 * j + 2, 2:3], (1, 128))
    return jnp.where(low, first, second)


def segment_ends(lengths):
    c = lax.axis_index("section")
    first = lengths[c, 0, 0]
    return first, first + lengths[c, 0, 1]


def project(hid, w, proj):
    tokens = hid[...].reshape(T, D)
    for first, width in ((0, 512), (512, 512), (1024, 384)):
        at = slice(first, first + width)
        proj[:, at] = dot_nn(tokens, w[:, :, :, at].reshape(D, width))


def scale_back(db, w, d_scaled):
    d_scaled[...] = dot_nn(db[...].reshape(T, D), w[:, :, :, WP:WALL].reshape(D, CH))


def mixer_fwd_kernel(layer, lens, par, hid, w, *rest, early=None):
    with_grad = layer == 1
    if with_grad:
        db, proj, kept, part, yssd, coef, d_scaled, gg, inn, xb, bb, cb, cumr, colr, *rest = rest
        st, buf, send_sems, recv_sems = rest
        me = Peers()
        barrier_start(me.ts)
        scale_back(db, w, d_scaled)
    else:
        proj, kept, part, yssd, st, gg, inn, xb, bb, cb, cumr, colr = rest
    cw, hp, rows = layer_params(par, layer)
    project(hid, w, proj)
    if early is not None:
        early()
    e0, e1 = segment_ends(lens)
    masks = conv_masks(e0, e1)
    _, _, cum, columns = steps_of(proj[:, 1280:1408], hp)
    cumr[...] = cum
    colr[...] = columns
    for j in range(4):
        v = proj[:, 512 + 128 * j : 640 + 128 * j]
        pre = conv_pre(v, masks, cw, tile(j))
        kept[:, tile(j)] = pre
        act = pre * sigmoid(pre)
        inn[:, tile(j)] = act
        xb[:, tile(j)] = (act * pair_columns(columns, HL, j)).astype(BF16)
    for j, ref in ((0, bb), (1, cb)):
        lanes = slice(512 + 128 * j, 640 + 128 * j)
        pre = conv_pre(proj[:, 1024 + 128 * j : 1152 + 128 * j], masks, cw, lanes)
        kept[:, lanes] = pre
        ref[...] = (pre * sigmoid(pre)).astype(BF16)
    low = iota((128, 128), 1) < 64
    for i in range(4):
        n = 128 * (i + 1)
        here = slice(128 * i, n)
        scores = dot_nt(cb[here, :], bb[0:n, :])
        p = iota((128, n), 0) + 128 * i
        q = iota((128, n), 1)
        bias = jnp.where((p >= q) & (segment_of(p, e0, e1) == segment_of(q, e0, e1)), 0.0, NEG).astype(F32)
        for j in range(4):
            mixing = []
            for h in (2 * j, 2 * j + 1):
                decay = jnp.exp2(colr[here, h : h + 1] - cumr[h : h + 1, 0:n] + bias)
                mixing.append((scores * decay).astype(BF16))
            both = dot_nn(jnp.concatenate(mixing, axis=0), xb[0:n, tile(j)])
            yssd[here, tile(j)] = jnp.where(low, both[0:128], both[128:256])
    squares = jnp.zeros((8, T), F32)
    dots = jnp.zeros((8, T), F32)
    ones = jnp.ones((8, 128), BF16)
    for j in range(4):
        z = proj[:, tile(j)]
        gated = (yssd[:, tile(j)] + skip_row(hp, j) * inn[:, tile(j)]) * (z * sigmoid(z))
        gained = gated * rows[0:1, tile(j)]
        gg[:, tile(j)] = gained.astype(BF16)
        squares = squares + sum_rows_nt(ones, gated * gated, 1)
        if with_grad:
            dots = dots + sum_rows_nt(ones, gained * d_scaled[:, tile(j)], 2)
    row = iota((8, T), 0)
    both = jnp.where(row == 0, squares, jnp.where(row == 1, dots, 0.0))
    for i in range(4):
        st[i] = both[:, tile(i)]
    if with_grad:
        exchange = stats_exchange(Link(send_sems, recv_sems), st, buf, coef, me)
        next(exchange)
    for x in range(4):
        columns_out = slice(256 * x, 256 * x + 256)
        branch = dot_nt(gg[...], w[x, :, :, WP:WALL].reshape(256, CH)).astype(BF16)
        part[:, :, columns_out] = branch.reshape(4, ROWS, 256)
    if with_grad:
        run(exchange)


def vmem_specs(count):
    return [pl.BlockSpec(memory_space=VM)] * count


def fwd_scratch():
    return [
        VM((T, CH), BF16),
        VM((T, CH), F32),
        VM((T, CH), BF16),
        VM((T, N), BF16),
        VM((T, N), BF16),
        VM((8, T), F32),
        VM((T, 128), F32),
    ]


def mixer_fwd(layer, lens, par, hid, w, *db):
    out_shape = [
        jax.ShapeDtypeStruct((T, WP), F32),
        jax.ShapeDtypeStruct((T, 768), F32),
        jax.ShapeDtypeStruct((4, ROWS, D), BF16),
        jax.ShapeDtypeStruct((T, CH), F32),
        jax.ShapeDtypeStruct((4, 8, 128), F32),
    ] + [jax.ShapeDtypeStruct((T, CH), F32)] * layer
    shared = {"collective_id": 2, "has_side_effects": True} if layer else {}
    return pl.pallas_call(
        functools.partial(mixer_fwd_kernel, layer),
        out_shape=tuple(out_shape),
        in_specs=[pl.BlockSpec(memory_space=pltpu.SMEM)] + vmem_specs(3 + len(db)),
        out_specs=tuple(vmem_specs(len(out_shape))),
        scratch_shapes=fwd_scratch() + ([VM((4, 8, 128), F32), VM((4, 4, 8, 128), F32)] + link_scratch(3)) * layer,
        compiler_params=pltpu.CompilerParams(vmem_limit_bytes=FWD_VMEM, **shared),
        name="mixer_fwd",
    )(lens, par, hid, w, *db)


def head_selector(j):
    head = 2 * j + (iota((8, 128), 1) >= 64).astype(jnp.int32)
    return jnp.where(iota((8, 128), 0) == head, 1.0, 0.0).astype(BF16)


def back_roll(v, k):
    return pltpu.roll(v, T - k, 0)


def conv_back(d_pre, v, masks, cw, lanes, sums, column0):
    d_v = cw[CONV - 1 : CONV, lanes] * d_pre
    out = slice(column0, column0 + 128)
    sums[CONV : CONV + 1, out] = jnp.sum(d_pre, axis=0, keepdims=True)
    sums[CONV - 1 : CONV, out] = jnp.sum(d_pre * v, axis=0, keepdims=True)
    for k in range(1, CONV):
        masked = masks[k - 1] * d_pre
        d_v = d_v + cw[CONV - 1 - k : CONV - k, lanes] * back_roll(masked, k)
        sums[CONV - 1 - k : CONV - k, out] = jnp.sum(masked * pltpu.roll(v, k, 0), axis=0, keepdims=True)
    return d_v


def mixer_bwd_kernel(layer, lens, par, w, proj, kept, yssd, coef, *rest, early=None, later=None):
    given, *rest = rest
    dh, d_proj, scaled, sums, heads, inn, xb, dyb, dyf, dx, bb, cb, d_c, cumr, colr, *rest = rest
    if layer == 1:
        d_scaled = given
    else:
        db, d_scaled = given, rest[0]
        scale_back(db, w, d_scaled)
    cw, hp, rows = layer_params(par, layer)
    e0, e1 = segment_ends(lens)
    masks = conv_masks(e0, e1)
    raw, step, cum, columns = steps_of(proj[:, 1280:1408], hp)
    cumr[...] = cum
    colr[...] = columns
    norm_cols = jnp.transpose(jnp.concatenate(
        [jnp.concatenate([coef[i] for i in range(4)], axis=1), jnp.zeros((120, T), F32)], axis=0
    ))
    s_col = jnp.broadcast_to(norm_cols[:, 0:1], (T, 128))
    k_col = jnp.broadcast_to(norm_cols[:, 1:2], (T, 128))
    sums[...] = jnp.zeros_like(sums)
    d_skip = jnp.zeros((8, T), F32)
    for j in range(4):
        selector = head_selector(j)
        pre = kept[:, tile(j)]
        act = pre * sigmoid(pre)
        inn[:, tile(j)] = act
        xb[:, tile(j)] = (act * pair_columns(columns, HL, j)).astype(BF16)
        z = proj[:, tile(j)]
        sig = sigmoid(z)
        gate = z * sig
        y = yssd[:, tile(j)] + skip_row(hp, j) * act
        gated = y * gate
        gs = gated * s_col
        gain = rows[0:1, tile(j)]
        dsc = d_scaled[:, tile(j)]
        scaled[:, tile(j)] = (gs * gain).astype(BF16)
        sums[5:6, tile(j)] = jnp.sum(gs * dsc, axis=0, keepdims=True)
        d_gated = s_col * gain * dsc - gated * k_col
        d_proj[:, tile(j)] = (d_gated * y * (sig * (1.0 + z * (1.0 - sig)))).astype(BF16)
        dy = d_gated * gate
        dyf[:, tile(j)] = dy
        dyb[:, tile(j)] = dy.astype(BF16)
        d_skip = d_skip + sum_rows_nt(selector, dy * act, 2)
    for j, ref in ((0, bb), (1, cb)):
        pre = kept[:, 512 + 128 * j : 640 + 128 * j]
        ref[...] = (pre * sigmoid(pre)).astype(BF16)
    if early is not None:
        early()
    d_c[...] = jnp.zeros_like(d_c)
    low = iota((128, 128), 1) < 64
    zero = jnp.zeros((128, 128), BF16)
    d_b_blocks = []
    for i in range(4):
        first = 128 * i
        n = T - first
        here = slice(first, first + 128)
        scores = dot_nt(bb[here, :], cb[first:T, :])
        q = iota((128, n), 0) + first
        p = iota((128, n), 1) + first
        bias = jnp.where((p >= q) & (segment_of(p, e0, e1) == segment_of(q, e0, e1)), 0.0, NEG).astype(F32)
        d_scores = jnp.zeros((128, n), F32)
        for j in range(4):
            x_tile = xb[here, tile(j)]
            dy_tile = dyb[first:T, tile(j)]
            heads_of = jnp.concatenate([jnp.where(low, x_tile, zero), jnp.where(low, zero, x_tile)], axis=0)
            d_mixing = dot_nt(heads_of, dy_tile)
            mixing = []
            for k in (0, 1):
                h = 2 * j + k
                decay = jnp.exp2(cumr[h : h + 1, first:T] - colr[here, h : h + 1] + bias)
                mixing.append((scores * decay).astype(BF16))
                d_scores = d_scores + d_mixing[128 * k : 128 * k + 128] * decay
            both = dot_nn(jnp.concatenate(mixing, axis=0), dy_tile)
            dx[here, tile(j)] = jnp.where(low, both[0:128], both[128:256])
        d_scores = d_scores.astype(BF16)
        d_b_blocks.append(dot_nn(d_scores, cb[first:T, :]))
        d_c[first:T, :] = d_c[first:T, :] + dot_tn(d_scores, bb[here, :])
    if later is not None:
        later()
    d_cum = jnp.zeros((8, T), F32)
    d_step = jnp.zeros((8, T), F32)
    for j in range(4):
        selector = head_selector(j)
        dxt = dx[:, tile(j)]
        act = inn[:, tile(j)]
        change = dyb[:, tile(j)].astype(F32) * yssd[:, tile(j)] - xb[:, tile(j)].astype(F32) * dxt
        d_cum = d_cum + sum_rows_nt(selector, change, 3)
        d_step = d_step + sum_rows_nt(selector, act * dxt, 2)
        d_act = pair_columns(columns, HL, j) * dxt + skip_row(hp, j) * dyf[:, tile(j)]
        v = proj[:, 512 + 128 * j : 640 + 128 * j]
        pre = kept[:, tile(j)]
        sig = sigmoid(pre)
        d_pre = d_act * (sig * (1.0 + pre * (1.0 - sig)))
        d_proj[:, 512 + 128 * j : 640 + 128 * j] = conv_back(d_pre, v, masks, cw, tile(j), sums, 128 * j).astype(BF16)
    for j in (0, 1):
        lanes = slice(512 + 128 * j, 640 + 128 * j)
        at = slice(1024 + 128 * j, 1152 + 128 * j)
        v = proj[:, at]
        pre = kept[:, lanes]
        sig = sigmoid(pre)
        d_act = jnp.concatenate(d_b_blocks, axis=0) if j == 0 else d_c[...]
        d_pre = d_act * (sig * (1.0 + pre * (1.0 - sig)))
        d_proj[:, at] = conv_back(d_pre, v, masks, cw, lanes, sums, 512 + 128 * j).astype(BF16)
    lower = jnp.where(iota((T, T), 0) >= iota((T, T), 1), 1.0, 0.0).astype(BF16)
    d_a = rows_times(d_cum, lower)
    rate = hp[:, 1:2]
    d_raw = (d_step + rate * d_a) * sigmoid(raw)
    d_proj[:, 1280:1408] = jnp.transpose(
        jnp.concatenate([d_raw, jnp.zeros((120, T), F32)], axis=0)
    ).astype(BF16)
    bias_grad = jnp.broadcast_to(jnp.sum(d_raw, axis=1, keepdims=True), (8, 128))
    rate_grad = jnp.broadcast_to(jnp.sum(d_a * step, axis=1, keepdims=True) * rate, (8, 128))
    skip_grad = jnp.broadcast_to(jnp.sum(d_skip, axis=1, keepdims=True), (8, 128))
    lane = iota((8, 128), 1)
    by_head = jnp.where(
        lane == 0, bias_grad, jnp.where(lane == 1, rate_grad, jnp.where(lane == 2, skip_grad, 0.0))
    )
    heads[...] = jnp.transpose(jnp.concatenate([by_head, jnp.zeros((120, 128), F32)], axis=0))[0:8]
    for x in range(4):
        back = dot_nt(d_proj[...], w[x, :, :, 0:WP].reshape(256, WP)).astype(BF16)
        dh[:, :, 256 * x : 256 * x + 256] = back.reshape(4, ROWS, 256)


def bwd_scratch():
    return [
        VM((4, ROWS, D), BF16),
        VM((T, WP), BF16),
        VM((T, CH), BF16),
    ], [
        VM((T, CH), F32),
        VM((T, CH), BF16),
        VM((T, CH), BF16),
        VM((T, CH), F32),
        VM((T, CH), F32),
        VM((T, N), BF16),
        VM((T, N), BF16),
        VM((T, N), F32),
        VM((8, T), F32),
        VM((T, 128), F32),
    ]


def places():
    section = lax.axis_index("section")
    dp = lax.axis_index("dp")
    return section, dp // 4, dp % 4, lax.axis_index("tensor")


class Peers:
    def __init__(self):
        self.c, self.x, self.z, self.t = places()
        self.core = {"section": 1 - self.c}
        self.xs = [{"dp": ((self.x + o) % 4) * 4 + self.z} for o in (1, 2, 3)]
        self.zs = [{"dp": self.x * 4 + (self.z + o) % 4} for o in (1, 2, 3)]
        self.ts = [{"tensor": (self.t + o) % 4} for o in (1, 2, 3)]
        self.far_ts = [{"section": 1 - self.c, "tensor": (self.t + o) % 4} for o in (1, 2, 3)]

    def near_dp(self):
        return [self.core] + self.xs + self.zs + self.ts

    def everyone(self):
        return [self.core] + self.xs + self.zs + self.ts + self.far_ts


def barrier_start(peers):
    barrier = pltpu.get_barrier_semaphore()
    for peer in peers:
        pl.semaphore_signal(barrier, inc=1, device_id=peer, device_id_type=MESH)


def barrier_end(peers):
    pl.semaphore_wait(pltpu.get_barrier_semaphore(), len(peers))


def greet(peers):
    barrier_start(peers)
    barrier_end(peers)


class Link:
    def __init__(self, send_sems, recv_sems):
        self.send_sems, self.recv_sems, self.sent = send_sems, recv_sems, []

    def send(self, src, dst, peer):
        k = len(self.sent)
        copy = pltpu.make_async_remote_copy(
            src_ref=src, dst_ref=dst, send_sem=self.send_sems.at[k], recv_sem=self.recv_sems.at[k],
            device_id=peer, device_id_type=MESH,
        )
        copy.start()
        self.sent.append(copy)
        return copy

    def drain(self):
        for copy in self.sent:
            copy.wait_send()


def spread(link, block, r, peers):
    plus, minus = peers[0], peers[2]

    def go(k, half, peer):
        return link.send(block(k, half), block(k, half), peer)

    from_left = [go(r, 0, plus)]
    from_right = [go(r, 1, minus)]
    from_left.append(go(r, 1, plus))
    from_right.append(go(r, 0, minus))
    yield
    from_left[0].wait_recv()
    far = [go((r + 3) % 4, 0, plus)]
    from_right[0].wait_recv()
    far.append(go((r + 1) % 4, 1, minus))
    yield
    for copy in (from_left[1], from_right[1]):
        copy.wait_recv()
    yield
    for copy in far:
        copy.wait_recv()
    yield


def collect(link, part, relay, sums, inbox, r, peers):
    plus, minus = peers[0], peers[2]
    left, right, far = (r + 3) % 4, (r + 1) % 4, (r + 2) % 4
    up = link.send(part(far, 0), relay.at[0], plus)
    down = link.send(part(far, 1), relay.at[1], minus)
    last = [
        link.send(part(right, 1), inbox(0, 1), plus),
        link.send(part(left, 0), inbox(1, 0), minus),
    ]
    yield
    up.wait_recv()
    sums[0] = (part(right, 0)[...].astype(F32) + relay[0].astype(F32)).astype(BF16)
    last.append(link.send(sums.at[0], inbox(0, 0), plus))
    down.wait_recv()
    sums[1] = (part(left, 1)[...].astype(F32) + relay[1].astype(F32)).astype(BF16)
    last.append(link.send(sums.at[1], inbox(1, 1), minus))
    yield
    for copy in last:
        copy.wait_recv()
    yield


def run(steps):
    for _ in steps:
        pass


def token_halves(ref):
    return lambda k, half: ref.at[k, pl.ds(64 * half, 64)]


def collect_tokens(link, ref, relay, sums, inbox, me):
    return collect(link, token_halves(ref), relay, sums, token_halves(inbox), me.t, me.ts)


def spread_tokens(link, ref, me):
    return spread(link, token_halves(ref), me.t, me.ts)


def core_rows(c):
    first = pl.multiple_of(32 * c, 32)
    return pl.ds(first, 32), pl.ds(first, 16), pl.ds(pl.multiple_of(32 * c + 16, 16), 16)


def gather_layer(link, own_sem, shard, w, me):
    c, x, z = me.c, me.x, me.z
    whole, a, b = core_rows(c)
    own = pltpu.make_async_copy(shard, w.at[x, z, whole], own_sem)
    own.start()
    first = []
    for o in range(3):
        first.append(link.send(shard.at[pl.ds(0, 16)], w.at[x, z, a], me.zs[o]))
        first.append(link.send(shard.at[pl.ds(16, 16)], w.at[x, z, b], me.xs[o]))
    yield
    own.wait()
    for copy in first:
        copy.wait_recv()
    along_x = spread(link, lambda k, half: w.at[k, pl.ds(2 * half, 2), a], x, me.xs)
    along_z = spread(link, lambda k, half: w.at[pl.ds(2 * half, 2), k, b], z, me.zs)
    next(along_x)
    next(along_z)
    core = []

    def to_core(o):
        block_a = w.at[(x + o) % 4, :, a]
        block_b = w.at[:, (z + o) % 4, b]
        core.append(link.send(block_a, block_a, me.core))
        core.append(link.send(block_b, block_b, me.core))

    to_core(0)
    yield
    next(along_x)
    next(along_z)
    yield
    next(along_x)
    next(along_z)
    to_core(1)
    to_core(3)
    yield
    next(along_x)
    next(along_z)
    to_core(2)
    yield
    for copy in core:
        copy.wait_recv()
    yield


GATHER_COPIES = 6 + 12 + 8


def reduce_rings(link, factors, grads, out_a, out_b, core_in, acc, relay, sums, inbox, me):
    c, x, z = me.c, me.x, me.z
    hid, d_proj, db, scaled = factors
    a, b = pl.ds(0, 16), pl.ds(16, 16)
    arrive = []
    for xx in range(4):
        at = slice(256 * xx, 256 * xx + 256)
        rows_in = dot_tn(hid[:, :, at].reshape(T, 256), d_proj[...]).astype(BF16)
        rows_out = dot_tn(db[:, :, at].reshape(T, 256), scaled[...]).astype(BF16)
        for k in range(8):
            block = slice(32 * k, 32 * k + 32)
            grads[k % 2, xx, k // 2, :, 0:WP] = rows_in[block]
            grads[k % 2, xx, k // 2, :, WP:WALL] = rows_out[block]
        arrive.append(link.send(grads.at[1 - c, xx], core_in.at[xx], me.core))
        if xx % 2 == 1:
            yield
    for xx in range(4):
        arrive[xx].wait_recv()
        acc[xx] = grads[c, xx] + core_in[xx]
    along_x = collect(
        link, lambda k, half: acc.at[k, pl.ds(2 * half, 2), a], relay.at[0], sums.at[0],
        lambda d, half: inbox.at[0, d, pl.ds(2 * half, 2)], x, me.xs,
    )
    next(along_x)
    along_z = collect(
        link, lambda k, half: acc.at[pl.ds(2 * half, 2), k, b], relay.at[1], sums.at[1],
        lambda d, half: inbox.at[1, d, pl.ds(2 * half, 2)], z, me.zs,
    )
    next(along_z)
    yield
    next(along_x)
    next(along_z)
    yield
    next(along_x)
    out_a[...] = (
        acc[x, :, a].astype(F32) + inbox[0, 0].astype(F32) + inbox[0, 1].astype(F32)
    ).astype(BF16)
    next(along_z)
    out_b[...] = (
        acc[:, z, b].astype(F32) + inbox[1, 0].astype(F32) + inbox[1, 1].astype(F32)
    ).astype(BF16)
    yield


RING_COPIES = 4 + 12


def reduce_last(link, sum_a, sum_b, out, bc_all, last_in, me):
    c, x, z = me.c, me.x, me.z
    last_a = [link.send(sum_a.at[(z + o + 1) % 4], last_in.at[0, o], me.zs[o]) for o in range(3)]
    last_b = [link.send(sum_b.at[(x + o + 1) % 4], last_in.at[1, o], me.xs[o]) for o in range(3)]
    yield
    rows, rows_a, rows_b = core_rows(c)
    for k, (copies, at, mine) in enumerate(((last_a, rows_a, sum_a.at[z]), (last_b, rows_b, sum_b.at[x]))):
        for copy in copies:
            copy.wait_recv()
        out[at, :] = (
            mine[...].astype(F32)
            + last_in[k, 0].astype(F32) + last_in[k, 1].astype(F32) + last_in[k, 2].astype(F32)
        )
    swap = [link.send(out.at[rows], out.at[rows], me.core)]

    def wanted(t):
        return pl.ds(pl.multiple_of(32 * c + 16 * (t % 2), 16), 16)

    bc_all[me.t, c] = out[wanted(me.t), 1024:1280]
    slot = bc_all.at[me.t, c]
    swap.append(link.send(slot, slot, me.core))
    for o in range(3):
        block = out.at[wanted(me.t + o + 1), pl.ds(1024, 256)]
        swap.append(link.send(block, slot, me.ts[o]))
        swap.append(link.send(block, slot, me.far_ts[o]))
    yield
    for copy in swap:
        copy.wait_recv()
    yield


LAST_COPIES = 6 + 8


def ring_scratch():
    return [
        VM((2, 4, 4, 32, WALL), BF16),
        VM((4, 4, 32, WALL), BF16), VM((4, 4, 32, WALL), BF16),
        VM((2, 2, 2, 16, WALL), BF16), VM((2, 2, 2, 16, WALL), BF16),
        VM((2, 2, 4, 16, WALL), BF16),
    ]


def last_scratch():
    return [VM((64, WALL), F32), VM((4, 2, 16, 2 * N), F32), VM((2, 3, 16, WALL), BF16)]


def token_scratch():
    return [VM((2, 64, D), BF16), VM((2, 64, D), BF16), VM((2, ROWS, D), BF16)]


def dma_sems(n):
    return pltpu.SemaphoreType.DMA((n,))


def link_scratch(*counts):
    return [pltpu.SemaphoreType.DMA((n,)) for n in counts for _ in range(2)]


def input_norm(u, gain):
    return u * lax.rsqrt(jnp.mean(u * u, axis=-1, keepdims=True) + EPSILON) * gain


def gain_of(par, layer):
    return par[layer, 0:1, 1408:2432]


def gather_kernel(
    lengths, w_in, w_bc, w_dt, w_out, conv_w, flat, u0, cot,
    w0, shard1, par, hid, db, valid,
    wsh, shards, turned, own_sem, g_s, g_r, e_s, e_r, h_s, h_r, d_s, d_r,
):
    me = Peers()
    c, t = me.c, me.t
    barrier_start(me.near_dp())
    wsh[:, 0:WZX] = w_in[...]
    wsh[:, 1024:1280] = w_bc[...]
    dt_rows = jnp.concatenate([w_dt[...].astype(F32), jnp.zeros((HL, 64), F32)], axis=1)
    dt_rows = jnp.concatenate([dt_rows, jnp.zeros((120, 128), F32)], axis=0)
    wsh[:, 1280:1408] = jnp.transpose(dt_rows)[0:64].astype(BF16)
    wsh[:, WP:WALL] = w_out[...]
    shards[c] = wsh[core_rows(c)[0], :]
    own = pl.ds(pl.multiple_of(CH * t, CH), CH)
    par[c] = jnp.zeros((8, 2432), F32)
    par[c, 0:4, 0:512] = conv_w[:, own]
    par[c, 0:4, 512:768] = conv_w[:, DI : DI + 2 * N]
    par[c, 4:5, 0:512] = flat[:, own]
    par[c, 4:5, 512:768] = flat[:, DI : DI + 2 * N]
    by_row = jnp.broadcast_to(flat[:, 5376:5504], (8, 128))
    row = iota((8, 128), 0)
    by_row = jnp.where(
        row == 0, by_row,
        jnp.where(row == 1, pltpu.roll(by_row, 128 - H, 1), pltpu.roll(by_row, 128 - 2 * H, 1)),
    )
    turned[...] = jnp.transpose(jnp.concatenate([by_row, jnp.zeros((120, 128), F32)], axis=0))
    heads = turned[pl.ds(pl.multiple_of(HL * t, HL), HL), :]
    par[c, :, 768:896] = jnp.where(iota((8, 128), 1) == 1, -jnp.exp(heads), heads)
    par[c, 0:1, 896:1408] = flat[:, pl.ds(pl.multiple_of(2304 + CH * t, 256), CH)]
    par[c, 0:1, 1408:2432] = flat[:, 4352:5376]
    end = lengths[c, 0, 0] + lengths[c, 0, 1]
    valid[...] = jnp.where(iota((ROWS, 128), 0) + ROWS * t < end, 1.0, 0.0).astype(F32)
    barrier_end(me.near_dp())
    early, weights = Link(e_s, e_r), Link(g_s, g_r)
    theirs = early.send(wsh.at[core_rows(1 - c)[0]], shards.at[c], me.core)
    par_copy = early.send(par.at[c], par.at[c], me.core)
    for j in range(8):
        db[t, :, tile(j)] = (cot[:, tile(j)] * valid[...]).astype(BF16)
    theirs.wait_recv()
    layer0 = gather_layer(weights, own_sem.at[0], shards.at[0], w0, me)
    next(layer0)
    par_copy.wait_recv()
    hid[t] = input_norm(u0[...], gain_of(par, 0)).astype(BF16)
    tokens, branch = Link(h_s, h_r), Link(d_s, d_r)
    hid_steps = spread_tokens(tokens, hid, me)
    db_steps = spread_tokens(branch, db, me)
    next(hid_steps)
    next(layer0)
    next(db_steps)
    next(layer0)
    next(hid_steps)
    shard1[...] = shards[1]
    next(layer0)
    next(db_steps)
    run(layer0)
    run(hid_steps)
    run(db_steps)
    for link in (early, weights, tokens, branch):
        link.drain()


def gather(*arrays):
    return pl.pallas_call(
        gather_kernel,
        out_shape=(
            jax.ShapeDtypeStruct((4, 4, 64, WALL), BF16),
            jax.ShapeDtypeStruct((32, WALL), BF16),
            jax.ShapeDtypeStruct((2, 8, 2432), F32),
            jax.ShapeDtypeStruct((4, ROWS, D), BF16),
            jax.ShapeDtypeStruct((4, ROWS, D), BF16),
            jax.ShapeDtypeStruct((ROWS, 128), F32),
        ),
        in_specs=[pl.BlockSpec(memory_space=pltpu.SMEM)] + vmem_specs(8),
        out_specs=tuple(vmem_specs(6)),
        scratch_shapes=[
            VM((64, WALL), BF16), VM((2, 32, WALL), BF16), VM((128, 128), F32),
            dma_sems(1),
        ]
        + link_scratch(GATHER_COPIES, 2, 6, 6),
        compiler_params=pltpu.CompilerParams(
            collective_id=0, has_side_effects=True, vmem_limit_bytes=6 << 20
        ),
        name="gather_weights",
    )(*arrays)


def column_of(row):
    return jnp.transpose(jnp.broadcast_to(row, (128, 128)))


def middle_kernel(
    lens, par, hid0, w0, u0, valid, shard1,
    proj, kept, yssd, total, u_next, s_out, hid, w1,
    part, st, gg, inn, xb, bb, cb, cumr, colr,
    relay, sums, inbox, sbuf, own_sem, g_s, g_r, p_s, p_r, b_s, b_r, h_s, h_r,
):
    me = Peers()
    t = me.t
    barrier_start(me.near_dp())
    weights, tokens, small, spreading = Link(g_s, g_r), Link(p_s, p_r), Link(b_s, b_r), Link(h_s, h_r)
    started = []

    def early():
        barrier_end(me.near_dp())
        started.append(gather_layer(weights, own_sem.at[0], shard1, w1, me))
        next(started[0])

    mixer_fwd_kernel(
        0, lens, par, hid0, w0, proj, kept, part, yssd, st, gg, inn, xb, bb, cb, cumr, colr, early=early
    )
    layer1 = started[0]
    sum_steps = collect_tokens(tokens, part, relay, sums, inbox, me)
    next(sum_steps)
    stats = [small.send(st.at[(t + o + 1) % 4], sbuf.at[o], me.ts[o]) for o in range(3)]
    next(layer1)
    next(sum_steps)
    for copy in stats:
        copy.wait_recv()
    s_row = lax.rsqrt((st[t] + sbuf[0] + sbuf[1] + sbuf[2]) / DI + EPSILON)
    s_out[...] = s_row
    scale = column_of(s_row[0:1]) * valid[...]
    next(layer1)
    run(sum_steps)
    total[...] = part[t].astype(F32) + inbox[0].astype(F32) + inbox[1].astype(F32)
    for j in range(8):
        u_next[:, tile(j)] = u0[:, tile(j)] + scale * total[:, tile(j)]
    hid[t] = input_norm(u_next[...], gain_of(par, 1)).astype(BF16)
    hid_steps = spread_tokens(spreading, hid, me)
    next(hid_steps)
    next(layer1)
    next(hid_steps)
    run(layer1)
    run(hid_steps)
    for link in (weights, tokens, small, spreading):
        link.drain()


def middle(*arrays):
    return pl.pallas_call(
        middle_kernel,
        out_shape=(
            jax.ShapeDtypeStruct((T, WP), F32),
            jax.ShapeDtypeStruct((T, 768), F32),
            jax.ShapeDtypeStruct((T, CH), F32),
            jax.ShapeDtypeStruct((ROWS, D), F32),
            jax.ShapeDtypeStruct((ROWS, D), F32),
            jax.ShapeDtypeStruct((8, 128), F32),
            jax.ShapeDtypeStruct((4, ROWS, D), BF16),
            jax.ShapeDtypeStruct((4, 4, 64, WALL), BF16),
        ),
        in_specs=[pl.BlockSpec(memory_space=pltpu.SMEM)] + vmem_specs(6),
        out_specs=tuple(vmem_specs(8)),
        scratch_shapes=[VM((4, ROWS, D), BF16), VM((4, 8, 128), F32)] + fwd_scratch() + token_scratch()
        + [VM((3, 8, 128), F32), pltpu.SemaphoreType.DMA((1,))]
        + link_scratch(GATHER_COPIES, 6, 3, 6),
        compiler_params=pltpu.CompilerParams(
            collective_id=1, has_side_effects=True, vmem_limit_bytes=16 << 20
        ),
        name="forward_0_and_tokens",
    )(*arrays)


def stats_exchange(link, st, buf, coef, me):
    barrier_end(me.ts)
    copies = [link.send(st, buf.at[me.t], peer) for peer in me.ts]
    buf[me.t] = st[...]
    yield
    for copy in copies:
        copy.wait_recv()
    for i in range(4):
        both = buf[0, i] + buf[1, i] + buf[2, i] + buf[3, i]
        s = lax.rsqrt(both[0:1] / DI + EPSILON)
        k = s * s * s * (both[1:2] / DI)
        row = iota((8, 128), 0)
        coef[i] = jnp.where(row == 0, s, jnp.where(row == 1, k, 0.0))
    link.drain()
    yield


def norm_back(u, gain, g, d_hidden):
    r = lax.rsqrt(jnp.mean(u * u, axis=-1, keepdims=True) + EPSILON)
    mean = jnp.mean(u * gain * d_hidden, axis=-1, keepdims=True)
    d_u = g + r * gain * d_hidden - u * (r * r * r) * mean
    return d_u, jnp.sum(u * r * d_hidden, axis=0, keepdims=True)


def back_middle_kernel(
    lens, par, w1, proj1, kept1, yssd1, coef1, d_scaled1, u, cot, valid, total0, s0, hid1, db1,
    sums1, heads1, g1, ng, db, coef, sum_a, sum_b,
    dh, d_proj1, scaled1, inn, xb, dyb, dyf, dx, bb, cb, d_c, cumr, colr,
    relay, sums, inbox, grads, core_in, acc, g_relay, g_sums, g_inbox,
    g_s, g_r, p_s, p_r, b_s, b_r, h_s, h_r,
):
    me = Peers()
    t = me.t
    barrier_start(me.near_dp())
    mixer_bwd_kernel(
        1, lens, par, w1, proj1, kept1, yssd1, coef1, d_scaled1, dh, d_proj1, scaled1, sums1, heads1,
        inn, xb, dyb, dyf, dx, bb, cb, d_c, cumr, colr,
        early=lambda: barrier_end(me.near_dp()),
    )
    weights, tokens, small, spreading = Link(g_s, g_r), Link(p_s, p_r), Link(b_s, b_r), Link(h_s, h_r)
    sum_steps = collect_tokens(tokens, dh, relay, sums, inbox, me)
    next(sum_steps)
    layer1 = reduce_rings(
        weights, (hid1, d_proj1, db1, scaled1), grads, sum_a, sum_b, core_in, acc,
        g_relay, g_sums, g_inbox, me,
    )
    next(layer1)
    next(sum_steps)
    next(layer1)
    next(layer1)
    run(sum_steps)
    total = dh[t].astype(F32) + inbox[0].astype(F32) + inbox[1].astype(F32)
    d_u, gain_term = norm_back(u[...], gain_of(par, 1), cot[...], total)
    g1[...] = d_u
    ng[...] = gain_term
    mean = jnp.zeros((ROWS, 128), F32)
    for j in range(8):
        d_branch = (g1[:, tile(j)] * valid[...]).astype(BF16)
        db[t, :, tile(j)] = d_branch
        mean = mean + d_branch.astype(F32) * total0[:, tile(j)]
    db_steps = spread_tokens(spreading, db, me)
    next(db_steps)
    mean = jnp.broadcast_to(jnp.sum(mean, axis=-1, keepdims=True), (128, 128))
    mean_row = jnp.transpose(mean)[0:8] / DI
    s = s0[0:1, :]
    row = iota((8, 128), 0)
    coef[t] = jnp.where(row == 0, s, jnp.where(row == 1, s * s * s * mean_row, 0.0))
    coef_copies = [small.send(coef.at[t], coef.at[t], peer) for peer in me.ts]
    next(layer1)
    next(db_steps)
    next(layer1)
    run(db_steps)
    for copy in coef_copies:
        copy.wait_recv()
    for link in (weights, tokens, small, spreading):
        link.drain()


def back_middle(*arrays):
    return pl.pallas_call(
        back_middle_kernel,
        out_shape=(
            jax.ShapeDtypeStruct((8, 768), F32),
            jax.ShapeDtypeStruct((8, 128), F32),
            jax.ShapeDtypeStruct((ROWS, D), F32),
            jax.ShapeDtypeStruct((1, D), F32),
            jax.ShapeDtypeStruct((4, ROWS, D), BF16),
            jax.ShapeDtypeStruct((4, 8, 128), F32),
            jax.ShapeDtypeStruct((4, 16, WALL), BF16),
            jax.ShapeDtypeStruct((4, 16, WALL), BF16),
        ),
        in_specs=[pl.BlockSpec(memory_space=pltpu.SMEM)] + vmem_specs(14),
        out_specs=tuple(vmem_specs(8)),
        scratch_shapes=bwd_scratch()[0] + bwd_scratch()[1] + token_scratch() + ring_scratch() + link_scratch(RING_COPIES, 6, 3, 6),
        compiler_params=pltpu.CompilerParams(
            collective_id=3, has_side_effects=True, vmem_limit_bytes=26 << 20
        ),
        name="backward_1_and_tokens",
    )(*arrays)


def small_sum(link, own, arrived, by_z, by_x, by_t, me):
    c, x, z, t = me.c, me.x, me.z, me.t
    swap = link.send(own.at[1 - c], arrived, me.core)
    yield
    swap.wait_recv()
    by_z[z] = own[c] + arrived[...]
    copies = [link.send(by_z.at[z], by_z.at[z], peer) for peer in me.zs]
    yield
    for copy in copies:
        copy.wait_recv()
    by_x[x] = by_z[0] + by_z[1] + by_z[2] + by_z[3]
    copies = [link.send(by_x.at[x], by_x.at[x], peer) for peer in me.xs]
    yield
    for copy in copies:
        copy.wait_recv()
    by_t[t] = by_x[0] + by_x[1] + by_x[2] + by_x[3]
    copies = [link.send(by_t.at[t], by_t.at[t], peer) for peer in me.ts]
    yield
    for copy in copies:
        copy.wait_recv()
    yield


def finish_kernel(
    lens, w0, proj0, kept0, yssd0, coef0, db0,
    part, u0, u1, g1, valid, par, coef1, ng1, sums1, heads1, sum_a1, sum_b1, hid0,
    lo, lg, smt, nmt, picked, o_bc,
    dh, d_proj0, scaled0, inn, xb, dyb, dyf, dx, bb, cb, d_c, cumr, colr, d_scaled0, sums0, heads0,
    relay, sums, inbox, relay2, sums2, inbox2, los, lgs, sms, smr, smz, smx, nms, nmr, nmz, nmx, sum_a0, sum_b0,
    grads, core_in, acc, g_relay, g_sums, g_inbox, w_grad0, bc_all0, last_in0, w_grad1, bc_all1, last_in1,
    g_s, g_r, f_s, f_r, l_s, l_r, p_s, p_r, q_s, q_r, b_s, b_r,
):
    me = Peers()
    c, x, z, t = me.c, me.x, me.z, me.t
    barrier_start(me.everyone())
    weights, final0, final1 = Link(g_s, g_r), Link(f_s, f_r), Link(l_s, l_r)
    tokens, tokens2, small = Link(p_s, p_r), Link(q_s, q_r), Link(b_s, b_r)
    last1 = reduce_last(final1, sum_a1, sum_b1, w_grad1, bc_all1, last_in1, me)
    out_steps = collect_tokens(tokens2, part, relay2, sums2, inbox2, me)

    def early():
        barrier_end(me.everyone())
        next(last1)
        next(out_steps)

    def later():
        next(last1)
        next(out_steps)

    mixer_bwd_kernel(
        0, lens, par, w0, proj0, kept0, yssd0, coef0, db0, dh, d_proj0, scaled0, sums0, heads0,
        inn, xb, dyb, dyf, dx, bb, cb, d_c, cumr, colr, d_scaled0, early=early, later=later,
    )
    for layer, (by_channel, heads) in enumerate(((sums0, heads0), (sums1, heads1))):
        sms[layer, 0:8, :] = by_channel[:, 0:512]
        sms[layer, 8:16, 0:256] = by_channel[:, 512:768]
        sms[layer, 8:16, 256:384] = heads[...]
        sms[layer, 8:16, 384:512] = jnp.zeros((8, 128), F32)
    chain = small_sum(small, sms, smr, smz, smx, smt, me)
    next(chain)
    back_steps = collect_tokens(tokens, dh, relay, sums, inbox, me)
    next(back_steps)
    layer0 = reduce_rings(
        weights, (hid0, d_proj0, db0, scaled0), grads, sum_a0, sum_b0, core_in, acc,
        g_relay, g_sums, g_inbox, me,
    )
    next(layer0)
    next(chain)
    next(back_steps)
    next(layer0)
    next(layer0)
    next(chain)
    los[0] = u1[...]
    lgs[1] = g1[...]
    next(layer0)
    run(back_steps)
    total = dh[t].astype(F32) + inbox[0].astype(F32) + inbox[1].astype(F32)
    d_u, gain_term = norm_back(u0[...], gain_of(par, 0), g1[...], total)
    lgs[0] = d_u
    lg_copy = small.send(lgs.at[1 - c], lg.at[c], me.core)
    lg[c] = lgs[c]
    for layer, term in enumerate((gain_term, ng1[...])):
        for j in range(8):
            nms[layer, j : j + 1, :] = term[:, tile(j)]
    norm_chain = small_sum(small, nms, nmr, nmz, nmx, nmt, me)
    next(norm_chain)
    next(chain)
    run(last1)
    next(norm_chain)
    next(layer0)
    last0 = reduce_last(final0, sum_a0, sum_b0, w_grad0, bc_all0, last_in0, me)
    next(last0)
    next(norm_chain)
    run(out_steps)
    los[1] = part[t].astype(F32) + inbox2[0].astype(F32) + inbox2[1].astype(F32)
    scale = column_of(coef1[t][0:1]) * valid[...]
    for j in range(8):
        los[1, :, tile(j)] = u1[:, tile(j)] + scale * los[1, :, tile(j)]
    lo_copy = small.send(los.at[1 - c], lo.at[c], me.core)
    lo[c] = los[c]
    next(norm_chain)
    next(last0)
    run(last0)
    picked[...] = jnp.where(c == 0, w_grad0[...], w_grad1[...])
    half = t // 2
    bc0 = bc_all0[0, half] + bc_all0[1, half] + bc_all0[2, half] + bc_all0[3, half]
    bc1 = bc_all1[0, half] + bc_all1[1, half] + bc_all1[2, half] + bc_all1[3, half]
    o_bc[...] = jnp.where(c == 0, bc0, bc1)
    run(chain)
    run(norm_chain)
    lo_copy.wait_recv()
    lg_copy.wait_recv()
    for link in (weights, final0, final1, tokens, tokens2, small):
        link.drain()


def finish(*arrays):
    return pl.pallas_call(
        finish_kernel,
        out_shape=(
            jax.ShapeDtypeStruct((2, ROWS, D), F32),
            jax.ShapeDtypeStruct((2, ROWS, D), F32),
            jax.ShapeDtypeStruct((4, 16, 512), F32),
            jax.ShapeDtypeStruct((4, 8, 128), F32),
            jax.ShapeDtypeStruct((64, WALL), F32),
            jax.ShapeDtypeStruct((16, 2 * N), F32),
        ),
        in_specs=[pl.BlockSpec(memory_space=pltpu.SMEM)] + vmem_specs(19),
        out_specs=tuple(vmem_specs(6)),
        scratch_shapes=bwd_scratch()[0] + bwd_scratch()[1]
        + [VM((T, CH), F32), VM((8, 768), F32), VM((8, 128), F32)]
        + token_scratch() + token_scratch()
        + [
            VM((2, ROWS, D), F32), VM((2, ROWS, D), F32),
            VM((2, 16, 512), F32), VM((16, 512), F32), VM((4, 16, 512), F32), VM((4, 16, 512), F32),
            VM((2, 8, 128), F32), VM((8, 128), F32), VM((4, 8, 128), F32), VM((4, 8, 128), F32),
            VM((4, 16, WALL), BF16), VM((4, 16, WALL), BF16),
        ]
        + ring_scratch() + last_scratch() + last_scratch()
        + link_scratch(RING_COPIES, LAST_COPIES, LAST_COPIES, 6, 6, 22),
        compiler_params=pltpu.CompilerParams(
            collective_id=4, has_side_effects=True, vmem_limit_bytes=34 << 20
        ),
        name="backward_0_and_gradients",
    )(*arrays)


def write_kernel(lo, lg, smt, nmt, picked, bc, *rest):
    outs, (in_part, dt, conv_w, conv_b, gain, norm, heads, sem) = rest[:13], rest[13:]
    (o_lo, o_lg, o_norm, o_in, o_bc, o_dt, o_cw, o_cb, o_dtb, o_alog, o_skip, o_gain, o_out) = outs
    copies = []

    def write(src, dst):
        copy = pltpu.make_async_copy(src, dst, sem.at[len(copies)])
        copy.start()
        copies.append(copy)

    write(lo, o_lo)
    write(lg, o_lg)
    write(bc, o_bc)
    in_part[:, 0, :] = picked[:, 0:512]
    in_part[:, 1, :] = picked[:, 512:1024]
    write(in_part, o_in)
    write(picked.at[:, pl.ds(WP, CH)], o_out)
    dt_rows = jnp.concatenate([picked[:, 1280:1408], jnp.zeros((64, 128), F32)], axis=0)
    dt[...] = jnp.transpose(dt_rows)[0:HL, 0:64]
    write(dt, o_dt)
    shared = smt[0, 8:16] + smt[1, 8:16] + smt[2, 8:16] + smt[3, 8:16]
    norms = nmt[0] + nmt[1] + nmt[2] + nmt[3]
    for j in range(8):
        norm[:, tile(j)] = norms[j : j + 1]
    write(norm, o_norm)
    conv_w[:, DI : DI + 2 * N] = shared[0:4, 0:256]
    conv_b[:, DI : DI + 2 * N] = shared[4:5, 0:256]
    for k in range(4):
        at = slice(512 * k, 512 * k + 512)
        conv_w[:, at] = smt[k, 0:4, :]
        conv_b[:, at] = smt[k, 4:5, :]
        gain[:, at] = smt[k, 5:6, :]
    write(conv_w, o_cw)
    write(conv_b, o_cb)
    write(gain, o_gain)
    all_heads = smt[0, 8:16, 256:384]
    for k in range(1, 4):
        all_heads = all_heads + pltpu.roll(smt[k, 8:16, 256:384], HL * k, 1)
    for k, out in ((0, o_dtb), (1, o_alog), (2, o_skip)):
        heads[k] = all_heads[k : k + 1, 0:H]
        write(heads.at[k], out)
    for copy in copies:
        copy.wait()


def write_outputs(*arrays):
    hbm_spec = pl.BlockSpec(memory_space=pltpu.HBM)
    shapes = [
        (2, ROWS, D), (2, ROWS, D), (1, D), (64, 2, CH), (16, 2 * N), (HL, 64), (CONV, DI + 2 * N),
        (1, DI + 2 * N), (1, H), (1, H), (1, H), (1, DI), (64, CH),
    ]
    return pl.pallas_call(
        write_kernel,
        out_shape=tuple(jax.ShapeDtypeStruct(shape, F32) for shape in shapes),
        in_specs=vmem_specs(6),
        out_specs=(hbm_spec,) * 13,
        scratch_shapes=[
            VM((64, 2, CH), F32), VM((HL, 64), F32), VM((CONV, DI + 2 * N), F32),
            VM((1, DI + 2 * N), F32), VM((1, DI), F32), VM((1, D), F32), VM((3, 1, H), F32),
            pltpu.SemaphoreType.DMA((13,)),
        ],
        compiler_params=pltpu.CompilerParams(vmem_limit_bytes=6 << 20),
        name="write_outputs",
    )(*arrays)


def body(
    activations, cotangent, lengths, norm_gain, in_weight, bc_weight, dt_weight, conv_weight,
    conv_bias, dt_bias, a_log, d_skip, gated_gain, out_weight,
):
    section = lax.axis_index("section")
    u0 = lax.dynamic_index_in_dim(activations, section, 0, keepdims=False)
    cot = lax.dynamic_index_in_dim(cotangent, section, 0, keepdims=False)
    flat = jnp.concatenate(
        [conv_bias, gated_gain, norm_gain, dt_bias, a_log, d_skip, jnp.zeros((1, 32), F32)], axis=1
    )
    w0, shard1, par, hid0, db1, valid = gather(
        lengths, in_weight[0].reshape(64, WZX), bc_weight[0], dt_weight[0].T, out_weight[0].T,
        conv_weight[0], flat, u0, cot,
    )
    proj0, kept0, y0, total0, u1, s0, hid1, w1 = middle(lengths, par, hid0, w0, u0, valid, shard1)
    proj1, kept1, part1, y1, coef1, d_scaled1 = mixer_fwd(1, lengths, par, hid1, w1, db1)
    sums1, heads1, g1, ng1, db0, coef0, sum_a1, sum_b1 = back_middle(
        lengths, par, w1, proj1, kept1, y1, coef1, d_scaled1, u1, cot, valid, total0, s0, hid1, db1
    )
    outs = write_outputs(
        *finish(
            lengths, w0, proj0, kept0, y0, coef0, db0, part1, u0, u1, g1, valid, par, coef1, ng1,
            sums1, heads1, sum_a1, sum_b1, hid0,
        )
    )
    outs = [out.T if k in (5, 12) else out for k, out in enumerate(outs)]
    plain = (2, 8, 9, 10, 7, 11)
    return tuple(out if k in plain else out[None] for k, out in enumerate(outs))


def solution(mesh):
    return jax.shard_map(
        body,
        mesh=mesh,
        in_specs=(
            P(None, ("dp", "tensor"), None),
            P(None, ("dp", "tensor"), None),
            P(None, "dp", None),
            P("section", None),
            P("section", "dp", None, "tensor"),
            P("section", "dp", None),
            P("section", "dp", "tensor"),
            P("section", None, None),
            P("section", None),
            P("section", None),
            P("section", None),
            P("section", None),
            P("section", None),
            P("section", "tensor", "dp"),
        ),
        out_specs=(
            P("section", None, ("dp", "tensor"), None),
            P("section", None, ("dp", "tensor"), None),
            P("section", None),
            P("section", "dp", None, "tensor"),
            P("section", ("dp", "tensor"), None),
            P("section", "dp", "tensor"),
            P("section", None, None),
            P("section", None),
            P("section", None),
            P("section", None),
            P("section", None),
            P("section", None),
            P("section", "tensor", "dp"),
        ),
        check_vma=False,
    )
```

```python
import functools

import jax
import jax.numpy as jnp
from jax import lax
from jax.experimental import pallas as pl
from jax.experimental.pallas import tpu as pltpu
from jax.sharding import PartitionSpec as P

D = 1024
DI = 2048
H = 32
N = 128
CONV = 4
T = 512
ROWS = 128
CH = 512
HL = 8
WZX = 1024
WP = 1408
WALL = 1920
NDP = 16
EPSILON = 1e-05
LOG2E = 1.4426950408889634
NEG = -1e30
F32 = jnp.float32
BF16 = jnp.bfloat16
MESH = pl.DeviceIdType.MESH
VM = pltpu.VMEM
FWD_VMEM = 12 << 20
BWD_VMEM = 16 << 20


def dot_nn(a, b):
    return lax.dot_general(a, b, (((1,), (0,)), ((), ())), preferred_element_type=F32)


def dot_nt(a, b):
    return lax.dot_general(a, b, (((1,), (1,)), ((), ())), preferred_element_type=F32)


def dot_tn(a, b):
    return lax.dot_general(a, b, (((0,), (0,)), ((), ())), preferred_element_type=F32)


def pieces(v, count):
    parts = []
    for _ in range(count):
        part = v.astype(BF16)
        parts.append(part)
        v = v - part.astype(F32)
    return parts


def sum_rows_nt(selector, v, count):
    return sum(dot_nt(selector, part) for part in pieces(v, count))


def rows_times(v, matrix):
    a, b, c = pieces(v, 3)
    stacked = jnp.concatenate([a.astype(F32), b.astype(F32), c.astype(F32), jnp.zeros_like(v)], 0)
    out = dot_nn(stacked.astype(BF16), matrix)
    return out[0:8] + out[8:16] + out[16:24]


def iota(shape, dim):
    return lax.broadcasted_iota(jnp.int32, shape, dim)


def segment_of(position, e0, e1):
    return (position >= e0).astype(jnp.int32) + (position >= e1).astype(jnp.int32)


def conv_masks(e0, e1):
    p = iota((T, 128), 0)
    seg = segment_of(p, e0, e1)
    return [
        jnp.where((p >= k) & (segment_of(p - k, e0, e1) == seg), 1.0, 0.0).astype(F32)
        for k in range(1, CONV)
    ]


def conv_pre(v, masks, cw, lanes):
    pre = cw[CONV : CONV + 1, lanes] + cw[CONV - 1 : CONV, lanes] * v
    for k in range(1, CONV):
        pre = pre + cw[CONV - 1 - k : CONV - k, lanes] * (masks[k - 1] * pltpu.roll(v, k, 0))
    return pre


def sigmoid(v):
    return 0.5 * jnp.tanh(0.5 * v) + 0.5


def steps_of(dt_tile, hp_ref):
    raw = jnp.transpose(dt_tile)[0:HL] + hp_ref[:, 0:1]
    step = jnp.maximum(raw, 0.0) + jnp.log1p(jnp.exp(-jnp.abs(raw)))
    rate = hp_ref[:, 1:2]
    upper = jnp.where(iota((T, T), 0) <= iota((T, T), 1), 1.0, 0.0).astype(BF16)
    cum = rows_times(step * rate, upper) * LOG2E
    columns = jnp.transpose(
        jnp.concatenate([cum, step, jnp.zeros((112, T), F32)], axis=0)
    )
    return raw, step, cum, columns


def pair_columns(columns, first, j, rows=T):
    low = iota((rows, 128), 1) < 64
    return jnp.where(
        low,
        jnp.broadcast_to(columns[:, first + 2 * j : first + 2 * j + 1], (rows, 128)),
        jnp.broadcast_to(columns[:, first + 2 * j + 1 : first + 2 * j + 2], (rows, 128)),
    )


def tile(j):
    return slice(128 * j, 128 * j + 128)


def layer_params(par, layer):
    return (
        par.at[layer, :, pl.ds(0, 768)],
        par.at[layer, :, pl.ds(768, 128)],
        par.at[layer, :, pl.ds(896, 512)],
    )


def skip_row(hp, j):
    low = iota((1, 128), 1) < 64
    first = jnp.broadcast_to(hp[2 * j : 2 * j + 1, 2:3], (1, 128))
    second = jnp.broadcast_to(hp[2 * j + 1 : 2 * j + 2, 2:3], (1, 128))
    return jnp.where(low, first, second)


def segment_ends(lengths):
    c = lax.axis_index("section")
    first = lengths[c, 0, 0]
    return first, first + lengths[c, 0, 1]


def project(hid, w, proj):
    tokens = hid[...].reshape(T, D)
    for first, width in ((0, 512), (512, 512), (1024, 384)):
        at = slice(first, first + width)
        proj[:, at] = dot_nn(tokens, w[:, :, :, at].reshape(D, width))


def scale_back(db, w, d_scaled):
    d_scaled[...] = dot_nn(db[...].reshape(T, D), w[:, :, :, WP:WALL].reshape(D, CH))


def mixer_fwd_kernel(layer, lens, par, hid, w, *rest, early=None):
    with_grad = layer == 1
    if with_grad:
        db, proj, kept, part, yssd, coef, d_scaled, gg, inn, xb, bb, cb, cumr, colr, *rest = rest
        st, buf, send_sems, recv_sems = rest
        me = Peers()
        barrier_start(me.ts)
        scale_back(db, w, d_scaled)
    else:
        proj, kept, part, yssd, st, gg, inn, xb, bb, cb, cumr, colr = rest
    cw, hp, rows = layer_params(par, layer)
    project(hid, w, proj)
    if early is not None:
        early()
    e0, e1 = segment_ends(lens)
    masks = conv_masks(e0, e1)
    _, _, cum, columns = steps_of(proj[:, 1280:1408], hp)
    cumr[...] = cum
    colr[...] = columns
    for j in range(4):
        v = proj[:, 512 + 128 * j : 640 + 128 * j]
        pre = conv_pre(v, masks, cw, tile(j))
        kept[:, tile(j)] = pre
        act = pre * sigmoid(pre)
        inn[:, tile(j)] = act
        xb[:, tile(j)] = (act * pair_columns(columns, HL, j)).astype(BF16)
    for j, ref in ((0, bb), (1, cb)):
        lanes = slice(512 + 128 * j, 640 + 128 * j)
        pre = conv_pre(proj[:, 1024 + 128 * j : 1152 + 128 * j], masks, cw, lanes)
        kept[:, lanes] = pre
        ref[...] = (pre * sigmoid(pre)).astype(BF16)
    low = iota((128, 128), 1) < 64
    for i in range(4):
        n = 128 * (i + 1)
        here = slice(128 * i, n)
        scores = dot_nt(cb[here, :], bb[0:n, :])
        p = iota((128, n), 0) + 128 * i
        q = iota((128, n), 1)
        bias = jnp.where((p >= q) & (segment_of(p, e0, e1) == segment_of(q, e0, e1)), 0.0, NEG).astype(F32)
        for j in range(4):
            mixing = []
            for h in (2 * j, 2 * j + 1):
                decay = jnp.exp2(colr[here, h : h + 1] - cumr[h : h + 1, 0:n] + bias)
                mixing.append((scores * decay).astype(BF16))
            both = dot_nn(jnp.concatenate(mixing, axis=0), xb[0:n, tile(j)])
            yssd[here, tile(j)] = jnp.where(low, both[0:128], both[128:256])
    squares = jnp.zeros((8, T), F32)
    dots = jnp.zeros((8, T), F32)
    ones = jnp.ones((8, 128), BF16)
    for j in range(4):
        z = proj[:, tile(j)]
        gated = (yssd[:, tile(j)] + skip_row(hp, j) * inn[:, tile(j)]) * (z * sigmoid(z))
        gained = gated * rows[0:1, tile(j)]
        gg[:, tile(j)] = gained.astype(BF16)
        squares = squares + sum_rows_nt(ones, gated * gated, 1)
        if with_grad:
            dots = dots + sum_rows_nt(ones, gained * d_scaled[:, tile(j)], 2)
    row = iota((8, T), 0)
    both = jnp.where(row == 0, squares, jnp.where(row == 1, dots, 0.0))
    for i in range(4):
        st[i] = both[:, tile(i)]
    if with_grad:
        exchange = stats_exchange(Link(send_sems, recv_sems), st, buf, coef, me)
        next(exchange)
    for x in range(4):
        columns_out = slice(256 * x, 256 * x + 256)
        branch = dot_nt(gg[...], w[x, :, :, WP:WALL].reshape(256, CH)).astype(BF16)
        part[:, :, columns_out] = branch.reshape(4, ROWS, 256)
    if with_grad:
        run(exchange)


def vmem_specs(count):
    return [pl.BlockSpec(memory_space=VM)] * count


def fwd_scratch():
    return [
        VM((T, CH), BF16),
        VM((T, CH), F32),
        VM((T, CH), BF16),
        VM((T, N), BF16),
        VM((T, N), BF16),
        VM((8, T), F32),
        VM((T, 128), F32),
    ]


def mixer_fwd(layer, lens, par, hid, w, *db):
    out_shape = [
        jax.ShapeDtypeStruct((T, WP), F32),
        jax.ShapeDtypeStruct((T, 768), F32),
        jax.ShapeDtypeStruct((4, ROWS, D), BF16),
        jax.ShapeDtypeStruct((T, CH), F32),
        jax.ShapeDtypeStruct((4, 8, 128), F32),
    ] + [jax.ShapeDtypeStruct((T, CH), F32)] * layer
    shared = {"collective_id": 2, "has_side_effects": True} if layer else {}
    return pl.pallas_call(
        functools.partial(mixer_fwd_kernel, layer),
        out_shape=tuple(out_shape),
        in_specs=[pl.BlockSpec(memory_space=pltpu.SMEM)] + vmem_specs(3 + len(db)),
        out_specs=tuple(vmem_specs(len(out_shape))),
        scratch_shapes=fwd_scratch() + ([VM((4, 8, 128), F32), VM((4, 4, 8, 128), F32)] + link_scratch(3)) * layer,
        compiler_params=pltpu.CompilerParams(vmem_limit_bytes=FWD_VMEM, **shared),
        name="mixer_fwd",
    )(lens, par, hid, w, *db)


def head_selector(j):
    head = 2 * j + (iota((8, 128), 1) >= 64).astype(jnp.int32)
    return jnp.where(iota((8, 128), 0) == head, 1.0, 0.0).astype(BF16)


def back_roll(v, k):
    return pltpu.roll(v, T - k, 0)


def conv_back(d_pre, v, masks, cw, lanes, sums, column0):
    d_v = cw[CONV - 1 : CONV, lanes] * d_pre
    out = slice(column0, column0 + 128)
    sums[CONV : CONV + 1, out] = jnp.sum(d_pre, axis=0, keepdims=True)
    sums[CONV - 1 : CONV, out] = jnp.sum(d_pre * v, axis=0, keepdims=True)
    for k in range(1, CONV):
        masked = masks[k - 1] * d_pre
        d_v = d_v + cw[CONV - 1 - k : CONV - k, lanes] * back_roll(masked, k)
        sums[CONV - 1 - k : CONV - k, out] = jnp.sum(masked * pltpu.roll(v, k, 0), axis=0, keepdims=True)
    return d_v


def mixer_bwd_kernel(layer, lens, par, w, proj, kept, yssd, coef, *rest, early=None, later=None):
    given, *rest = rest
    dh, d_proj, scaled, sums, heads, inn, xb, dyb, dyf, dx, bb, cb, d_c, cumr, colr, *rest = rest
    if layer == 1:
        d_scaled = given
    else:
        db, d_scaled = given, rest[0]
        scale_back(db, w, d_scaled)
    cw, hp, rows = layer_params(par, layer)
    e0, e1 = segment_ends(lens)
    masks = conv_masks(e0, e1)
    raw, step, cum, columns = steps_of(proj[:, 1280:1408], hp)
    cumr[...] = cum
    colr[...] = columns
    norm_cols = jnp.transpose(jnp.concatenate(
        [jnp.concatenate([coef[i] for i in range(4)], axis=1), jnp.zeros((120, T), F32)], axis=0
    ))
    s_col = jnp.broadcast_to(norm_cols[:, 0:1], (T, 128))
    k_col = jnp.broadcast_to(norm_cols[:, 1:2], (T, 128))
    sums[...] = jnp.zeros_like(sums)
    d_skip = jnp.zeros((8, T), F32)
    for j in range(4):
        selector = head_selector(j)
        pre = kept[:, tile(j)]
        act = pre * sigmoid(pre)
        inn[:, tile(j)] = act
        xb[:, tile(j)] = (act * pair_columns(columns, HL, j)).astype(BF16)
        z = proj[:, tile(j)]
        sig = sigmoid(z)
        gate = z * sig
        y = yssd[:, tile(j)] + skip_row(hp, j) * act
        gated = y * gate
        gs = gated * s_col
        gain = rows[0:1, tile(j)]
        dsc = d_scaled[:, tile(j)]
        scaled[:, tile(j)] = (gs * gain).astype(BF16)
        sums[5:6, tile(j)] = jnp.sum(gs * dsc, axis=0, keepdims=True)
        d_gated = s_col * gain * dsc - gated * k_col
        d_proj[:, tile(j)] = (d_gated * y * (sig * (1.0 + z * (1.0 - sig)))).astype(BF16)
        dy = d_gated * gate
        dyf[:, tile(j)] = dy
        dyb[:, tile(j)] = dy.astype(BF16)
        d_skip = d_skip + sum_rows_nt(selector, dy * act, 2)
    for j, ref in ((0, bb), (1, cb)):
        pre = kept[:, 512 + 128 * j : 640 + 128 * j]
        ref[...] = (pre * sigmoid(pre)).astype(BF16)
    if early is not None:
        early()
    d_c[...] = jnp.zeros_like(d_c)
    low = iota((128, 128), 1) < 64
    zero = jnp.zeros((128, 128), BF16)
    d_b_blocks = []
    for i in range(4):
        first = 128 * i
        n = T - first
        here = slice(first, first + 128)
        scores = dot_nt(bb[here, :], cb[first:T, :])
        q = iota((128, n), 0) + first
        p = iota((128, n), 1) + first
        bias = jnp.where((p >= q) & (segment_of(p, e0, e1) == segment_of(q, e0, e1)), 0.0, NEG).astype(F32)
        d_scores = jnp.zeros((128, n), F32)
        for j in range(4):
            x_tile = xb[here, tile(j)]
            dy_tile = dyb[first:T, tile(j)]
            heads_of = jnp.concatenate([jnp.where(low, x_tile, zero), jnp.where(low, zero, x_tile)], axis=0)
            d_mixing = dot_nt(heads_of, dy_tile)
            mixing = []
            for k in (0, 1):
                h = 2 * j + k
                decay = jnp.exp2(cumr[h : h + 1, first:T] - colr[here, h : h + 1] + bias)
                mixing.append((scores * decay).astype(BF16))
                d_scores = d_scores + d_mixing[128 * k : 128 * k + 128] * decay
            both = dot_nn(jnp.concatenate(mixing, axis=0), dy_tile)
            dx[here, tile(j)] = jnp.where(low, both[0:128], both[128:256])
        d_scores = d_scores.astype(BF16)
        d_b_blocks.append(dot_nn(d_scores, cb[first:T, :]))
        d_c[first:T, :] = d_c[first:T, :] + dot_tn(d_scores, bb[here, :])
    if later is not None:
        later()
    d_cum = jnp.zeros((8, T), F32)
    d_step = jnp.zeros((8, T), F32)
    for j in range(4):
        selector = head_selector(j)
        dxt = dx[:, tile(j)]
        act = inn[:, tile(j)]
        change = dyb[:, tile(j)].astype(F32) * yssd[:, tile(j)] - xb[:, tile(j)].astype(F32) * dxt
        d_cum = d_cum + sum_rows_nt(selector, change, 3)
        d_step = d_step + sum_rows_nt(selector, act * dxt, 2)
        d_act = pair_columns(columns, HL, j) * dxt + skip_row(hp, j) * dyf[:, tile(j)]
        v = proj[:, 512 + 128 * j : 640 + 128 * j]
        pre = kept[:, tile(j)]
        sig = sigmoid(pre)
        d_pre = d_act * (sig * (1.0 + pre * (1.0 - sig)))
        d_proj[:, 512 + 128 * j : 640 + 128 * j] = conv_back(d_pre, v, masks, cw, tile(j), sums, 128 * j).astype(BF16)
    for j in (0, 1):
        lanes = slice(512 + 128 * j, 640 + 128 * j)
        at = slice(1024 + 128 * j, 1152 + 128 * j)
        v = proj[:, at]
        pre = kept[:, lanes]
        sig = sigmoid(pre)
        d_act = jnp.concatenate(d_b_blocks, axis=0) if j == 0 else d_c[...]
        d_pre = d_act * (sig * (1.0 + pre * (1.0 - sig)))
        d_proj[:, at] = conv_back(d_pre, v, masks, cw, lanes, sums, 512 + 128 * j).astype(BF16)
    lower = jnp.where(iota((T, T), 0) >= iota((T, T), 1), 1.0, 0.0).astype(BF16)
    d_a = rows_times(d_cum, lower)
    rate = hp[:, 1:2]
    d_raw = (d_step + rate * d_a) * sigmoid(raw)
    d_proj[:, 1280:1408] = jnp.transpose(
        jnp.concatenate([d_raw, jnp.zeros((120, T), F32)], axis=0)
    ).astype(BF16)
    bias_grad = jnp.broadcast_to(jnp.sum(d_raw, axis=1, keepdims=True), (8, 128))
    rate_grad = jnp.broadcast_to(jnp.sum(d_a * step, axis=1, keepdims=True) * rate, (8, 128))
    skip_grad = jnp.broadcast_to(jnp.sum(d_skip, axis=1, keepdims=True), (8, 128))
    lane = iota((8, 128), 1)
    by_head = jnp.where(
        lane == 0, bias_grad, jnp.where(lane == 1, rate_grad, jnp.where(lane == 2, skip_grad, 0.0))
    )
    heads[...] = jnp.transpose(jnp.concatenate([by_head, jnp.zeros((120, 128), F32)], axis=0))[0:8]
    for x in range(4):
        back = dot_nt(d_proj[...], w[x, :, :, 0:WP].reshape(256, WP)).astype(BF16)
        dh[:, :, 256 * x : 256 * x + 256] = back.reshape(4, ROWS, 256)


def bwd_scratch():
    return [
        VM((4, ROWS, D), BF16),
        VM((T, WP), BF16),
        VM((T, CH), BF16),
    ], [
        VM((T, CH), F32),
        VM((T, CH), BF16),
        VM((T, CH), BF16),
        VM((T, CH), F32),
        VM((T, CH), F32),
        VM((T, N), BF16),
        VM((T, N), BF16),
        VM((T, N), F32),
        VM((8, T), F32),
        VM((T, 128), F32),
    ]


def places():
    section = lax.axis_index("section")
    dp = lax.axis_index("dp")
    return section, dp // 4, dp % 4, lax.axis_index("tensor")


class Peers:
    def __init__(self):
        self.c, self.x, self.z, self.t = places()
        self.core = {"section": 1 - self.c}
        self.xs = [{"dp": ((self.x + o) % 4) * 4 + self.z} for o in (1, 2, 3)]
        self.zs = [{"dp": self.x * 4 + (self.z + o) % 4} for o in (1, 2, 3)]
        self.ts = [{"tensor": (self.t + o) % 4} for o in (1, 2, 3)]
        self.far_ts = [{"section": 1 - self.c, "tensor": (self.t + o) % 4} for o in (1, 2, 3)]

    def near_dp(self):
        return [self.core] + self.xs + self.zs + self.ts

    def everyone(self):
        return [self.core] + self.xs + self.zs + self.ts + self.far_ts


def barrier_start(peers):
    barrier = pltpu.get_barrier_semaphore()
    for peer in peers:
        pl.semaphore_signal(barrier, inc=1, device_id=peer, device_id_type=MESH)


def barrier_end(peers):
    pl.semaphore_wait(pltpu.get_barrier_semaphore(), len(peers))


def greet(peers):
    barrier_start(peers)
    barrier_end(peers)


class Link:
    def __init__(self, send_sems, recv_sems):
        self.send_sems, self.recv_sems, self.sent = send_sems, recv_sems, []

    def send(self, src, dst, peer):
        k = len(self.sent)
        copy = pltpu.make_async_remote_copy(
            src_ref=src, dst_ref=dst, send_sem=self.send_sems.at[k], recv_sem=self.recv_sems.at[k],
            device_id=peer, device_id_type=MESH,
        )
        copy.start()
        self.sent.append(copy)
        return copy

    def drain(self):
        for copy in self.sent:
            copy.wait_send()


def spread(link, block, r, peers):
    plus, minus = peers[0], peers[2]

    def go(k, half, peer):
        return link.send(block(k, half), block(k, half), peer)

    from_left = [go(r, 0, plus)]
    from_right = [go(r, 1, minus)]
    from_left.append(go(r, 1, plus))
    from_right.append(go(r, 0, minus))
    yield
    from_left[0].wait_recv()
    far = [go((r + 3) % 4, 0, plus)]
    from_right[0].wait_recv()
    far.append(go((r + 1) % 4, 1, minus))
    yield
    for copy in (from_left[1], from_right[1]):
        copy.wait_recv()
    yield
    for copy in far:
        copy.wait_recv()
    yield


def collect(link, part, relay, sums, inbox, r, peers):
    plus, minus = peers[0], peers[2]
    left, right, far = (r + 3) % 4, (r + 1) % 4, (r + 2) % 4
    up = link.send(part(far, 0), relay.at[0], plus)
    down = link.send(part(far, 1), relay.at[1], minus)
    last = [
        link.send(part(right, 1), inbox(0, 1), plus),
        link.send(part(left, 0), inbox(1, 0), minus),
    ]
    yield
    up.wait_recv()
    sums[0] = (part(right, 0)[...].astype(F32) + relay[0].astype(F32)).astype(BF16)
    last.append(link.send(sums.at[0], inbox(0, 0), plus))
    down.wait_recv()
    sums[1] = (part(left, 1)[...].astype(F32) + relay[1].astype(F32)).astype(BF16)
    last.append(link.send(sums.at[1], inbox(1, 1), minus))
    yield
    for copy in last:
        copy.wait_recv()
    yield


def run(steps):
    for _ in steps:
        pass


def token_halves(ref):
    return lambda k, half: ref.at[k, pl.ds(64 * half, 64)]


def collect_tokens(link, ref, relay, sums, inbox, me):
    return collect(link, token_halves(ref), relay, sums, token_halves(inbox), me.t, me.ts)


def spread_tokens(link, ref, me):
    return spread(link, token_halves(ref), me.t, me.ts)


def core_rows(c):
    first = pl.multiple_of(32 * c, 32)
    return pl.ds(first, 32), pl.ds(first, 16), pl.ds(pl.multiple_of(32 * c + 16, 16), 16)


def gather_layer(link, own_sem, shard, w, me):
    c, x, z = me.c, me.x, me.z
    whole, a, b = core_rows(c)
    own = pltpu.make_async_copy(shard, w.at[x, z, whole], own_sem)
    own.start()
    first = []
    for o in range(3):
        first.append(link.send(shard.at[pl.ds(0, 16)], w.at[x, z, a], me.zs[o]))
        first.append(link.send(shard.at[pl.ds(16, 16)], w.at[x, z, b], me.xs[o]))
    yield
    own.wait()
    for copy in first:
        copy.wait_recv()
    along_x = spread(link, lambda k, half: w.at[k, pl.ds(2 * half, 2), a], x, me.xs)
    along_z = spread(link, lambda k, half: w.at[pl.ds(2 * half, 2), k, b], z, me.zs)
    next(along_x)
    next(along_z)
    core = []

    def to_core(o):
        block_a = w.at[(x + o) % 4, :, a]
        block_b = w.at[:, (z + o) % 4, b]
        core.append(link.send(block_a, block_a, me.core))
        core.append(link.send(block_b, block_b, me.core))

    to_core(0)
    yield
    next(along_x)
    next(along_z)
    yield
    next(along_x)
    next(along_z)
    to_core(1)
    to_core(3)
    yield
    next(along_x)
    next(along_z)
    to_core(2)
    yield
    for copy in core:
        copy.wait_recv()
    yield


GATHER_COPIES = 6 + 12 + 8


def reduce_rings(link, factors, grads, out_a, out_b, core_in, acc, relay, sums, inbox, me):
    c, x, z = me.c, me.x, me.z
    hid, d_proj, db, scaled = factors
    a, b = pl.ds(0, 16), pl.ds(16, 16)
    arrive = []
    for xx in range(4):
        at = slice(256 * xx, 256 * xx + 256)
        rows_in = dot_tn(hid[:, :, at].reshape(T, 256), d_proj[...]).astype(BF16)
        rows_out = dot_tn(db[:, :, at].reshape(T, 256), scaled[...]).astype(BF16)
        for k in range(8):
            block = slice(32 * k, 32 * k + 32)
            grads[k % 2, xx, k // 2, :, 0:WP] = rows_in[block]
            grads[k % 2, xx, k // 2, :, WP:WALL] = rows_out[block]
        arrive.append(link.send(grads.at[1 - c, xx], core_in.at[xx], me.core))
        if xx % 2 == 1:
            yield
    for xx in range(4):
        arrive[xx].wait_recv()
        acc[xx] = grads[c, xx] + core_in[xx]
    along_x = collect(
        link, lambda k, half: acc.at[k, pl.ds(2 * half, 2), a], relay.at[0], sums.at[0],
        lambda d, half: inbox.at[0, d, pl.ds(2 * half, 2)], x, me.xs,
    )
    next(along_x)
    along_z = collect(
        link, lambda k, half: acc.at[pl.ds(2 * half, 2), k, b], relay.at[1], sums.at[1],
        lambda d, half: inbox.at[1, d, pl.ds(2 * half, 2)], z, me.zs,
    )
    next(along_z)
    yield
    next(along_x)
    next(along_z)
    yield
    next(along_x)
    out_a[...] = (
        acc[x, :, a].astype(F32) + inbox[0, 0].astype(F32) + inbox[0, 1].astype(F32)
    ).astype(BF16)
    next(along_z)
    out_b[...] = (
        acc[:, z, b].astype(F32) + inbox[1, 0].astype(F32) + inbox[1, 1].astype(F32)
    ).astype(BF16)
    yield


RING_COPIES = 4 + 12


def reduce_last(link, sum_a, sum_b, out, bc_all, last_in, me):
    c, x, z = me.c, me.x, me.z
    last_a = [link.send(sum_a.at[(z + o + 1) % 4], last_in.at[0, o], me.zs[o]) for o in range(3)]
    last_b = [link.send(sum_b.at[(x + o + 1) % 4], last_in.at[1, o], me.xs[o]) for o in range(3)]
    yield
    rows, rows_a, rows_b = core_rows(c)
    for k, (copies, at, mine) in enumerate(((last_a, rows_a, sum_a.at[z]), (last_b, rows_b, sum_b.at[x]))):
        for copy in copies:
            copy.wait_recv()
        out[at, :] = (
            mine[...].astype(F32)
            + last_in[k, 0].astype(F32) + last_in[k, 1].astype(F32) + last_in[k, 2].astype(F32)
        )
    swap = [link.send(out.at[rows], out.at[rows], me.core)]

    def wanted(t):
        return pl.ds(pl.multiple_of(32 * c + 16 * (t % 2), 16), 16)

    bc_all[me.t, c] = out[wanted(me.t), 1024:1280]
    slot = bc_all.at[me.t, c]
    swap.append(link.send(slot, slot, me.core))
    for o in range(3):
        block = out.at[wanted(me.t + o + 1), pl.ds(1024, 256)]
        swap.append(link.send(block, slot, me.ts[o]))
        swap.append(link.send(block, slot, me.far_ts[o]))
    yield
    for copy in swap:
        copy.wait_recv()
    yield


LAST_COPIES = 6 + 8


def ring_scratch():
    return [
        VM((2, 4, 4, 32, WALL), BF16),
        VM((4, 4, 32, WALL), BF16), VM((4, 4, 32, WALL), BF16),
        VM((2, 2, 2, 16, WALL), BF16), VM((2, 2, 2, 16, WALL), BF16),
        VM((2, 2, 4, 16, WALL), BF16),
    ]


def last_scratch():
    return [VM((64, WALL), F32), VM((4, 2, 16, 2 * N), F32), VM((2, 3, 16, WALL), BF16)]


def token_scratch():
    return [VM((2, 64, D), BF16), VM((2, 64, D), BF16), VM((2, ROWS, D), BF16)]


def dma_sems(n):
    return pltpu.SemaphoreType.DMA((n,))


def link_scratch(*counts):
    return [pltpu.SemaphoreType.DMA((n,)) for n in counts for _ in range(2)]


def input_norm(u, gain):
    return u * lax.rsqrt(jnp.mean(u * u, axis=-1, keepdims=True) + EPSILON) * gain


def gain_of(par, layer):
    return par[layer, 0:1, 1408:2432]


def gather_kernel(
    lengths, w_in, w_bc, w_dt, w_out, conv_w, flat, u0, cot,
    w0, shard1, par, hid, db, valid,
    wsh, shards, turned, own_sem, g_s, g_r, e_s, e_r, h_s, h_r, d_s, d_r,
):
    me = Peers()
    c, t = me.c, me.t
    barrier_start(me.near_dp())
    wsh[:, 0:WZX] = w_in[...]
    wsh[:, 1024:1280] = w_bc[...]
    dt_rows = jnp.concatenate([w_dt[...].astype(F32), jnp.zeros((HL, 64), F32)], axis=1)
    dt_rows = jnp.concatenate([dt_rows, jnp.zeros((120, 128), F32)], axis=0)
    wsh[:, 1280:1408] = jnp.transpose(dt_rows)[0:64].astype(BF16)
    wsh[:, WP:WALL] = w_out[...]
    shards[c] = wsh[core_rows(c)[0], :]
    own = pl.ds(pl.multiple_of(CH * t, CH), CH)
    par[c] = jnp.zeros((8, 2432), F32)
    par[c, 0:4, 0:512] = conv_w[:, own]
    par[c, 0:4, 512:768] = conv_w[:, DI : DI + 2 * N]
    par[c, 4:5, 0:512] = flat[:, own]
    par[c, 4:5, 512:768] = flat[:, DI : DI + 2 * N]
    by_row = jnp.broadcast_to(flat[:, 5376:5504], (8, 128))
    row = iota((8, 128), 0)
    by_row = jnp.where(
        row == 0, by_row,
        jnp.where(row == 1, pltpu.roll(by_row, 128 - H, 1), pltpu.roll(by_row, 128 - 2 * H, 1)),
    )
    turned[...] = jnp.transpose(jnp.concatenate([by_row, jnp.zeros((120, 128), F32)], axis=0))
    heads = turned[pl.ds(pl.multiple_of(HL * t, HL), HL), :]
    par[c, :, 768:896] = jnp.where(iota((8, 128), 1) == 1, -jnp.exp(heads), heads)
    par[c, 0:1, 896:1408] = flat[:, pl.ds(pl.multiple_of(2304 + CH * t, 256), CH)]
    par[c, 0:1, 1408:2432] = flat[:, 4352:5376]
    end = lengths[c, 0, 0] + lengths[c, 0, 1]
    valid[...] = jnp.where(iota((ROWS, 128), 0) + ROWS * t < end, 1.0, 0.0).astype(F32)
    barrier_end(me.near_dp())
    early, weights = Link(e_s, e_r), Link(g_s, g_r)
    theirs = early.send(wsh.at[core_rows(1 - c)[0]], shards.at[c], me.core)
    par_copy = early.send(par.at[c], par.at[c], me.core)
    for j in range(8):
        db[t, :, tile(j)] = (cot[:, tile(j)] * valid[...]).astype(BF16)
    theirs.wait_recv()
    layer0 = gather_layer(weights, own_sem.at[0], shards.at[0], w0, me)
    next(layer0)
    par_copy.wait_recv()
    hid[t] = input_norm(u0[...], gain_of(par, 0)).astype(BF16)
    tokens, branch = Link(h_s, h_r), Link(d_s, d_r)
    hid_steps = spread_tokens(tokens, hid, me)
    db_steps = spread_tokens(branch, db, me)
    next(hid_steps)
    next(layer0)
    next(db_steps)
    next(layer0)
    next(hid_steps)
    shard1[...] = shards[1]
    next(layer0)
    next(db_steps)
    run(layer0)
    run(hid_steps)
    run(db_steps)
    for link in (early, weights, tokens, branch):
        link.drain()


def gather(*arrays):
    return pl.pallas_call(
        gather_kernel,
        out_shape=(
            jax.ShapeDtypeStruct((4, 4, 64, WALL), BF16),
            jax.ShapeDtypeStruct((32, WALL), BF16),
            jax.ShapeDtypeStruct((2, 8, 2432), F32),
            jax.ShapeDtypeStruct((4, ROWS, D), BF16),
            jax.ShapeDtypeStruct((4, ROWS, D), BF16),
            jax.ShapeDtypeStruct((ROWS, 128), F32),
        ),
        in_specs=[pl.BlockSpec(memory_space=pltpu.SMEM)] + vmem_specs(8),
        out_specs=tuple(vmem_specs(6)),
        scratch_shapes=[
            VM((64, WALL), BF16), VM((2, 32, WALL), BF16), VM((128, 128), F32),
            dma_sems(1),
        ]
        + link_scratch(GATHER_COPIES, 2, 6, 6),
        compiler_params=pltpu.CompilerParams(
            collective_id=0, has_side_effects=True, vmem_limit_bytes=6 << 20
        ),
        name="gather_weights",
    )(*arrays)


def column_of(row):
    return jnp.transpose(jnp.broadcast_to(row, (128, 128)))


def middle_kernel(
    lens, par, hid0, w0, u0, valid, shard1,
    proj, kept, yssd, total, u_next, s_out, hid, w1,
    part, st, gg, inn, xb, bb, cb, cumr, colr,
    relay, sums, inbox, sbuf, own_sem, g_s, g_r, p_s, p_r, b_s, b_r, h_s, h_r,
):
    me = Peers()
    t = me.t
    barrier_start(me.near_dp())
    weights, tokens, small, spreading = Link(g_s, g_r), Link(p_s, p_r), Link(b_s, b_r), Link(h_s, h_r)
    started = []

    def early():
        barrier_end(me.near_dp())
        started.append(gather_layer(weights, own_sem.at[0], shard1, w1, me))
        next(started[0])

    mixer_fwd_kernel(
        0, lens, par, hid0, w0, proj, kept, part, yssd, st, gg, inn, xb, bb, cb, cumr, colr, early=early
    )
    layer1 = started[0]
    sum_steps = collect_tokens(tokens, part, relay, sums, inbox, me)
    next(sum_steps)
    stats = [small.send(st.at[(t + o + 1) % 4], sbuf.at[o], me.ts[o]) for o in range(3)]
    next(layer1)
    next(sum_steps)
    for copy in stats:
        copy.wait_recv()
    s_row = lax.rsqrt((st[t] + sbuf[0] + sbuf[1] + sbuf[2]) / DI + EPSILON)
    s_out[...] = s_row
    scale = column_of(s_row[0:1]) * valid[...]
    next(layer1)
    run(sum_steps)
    total[...] = part[t].astype(F32) + inbox[0].astype(F32) + inbox[1].astype(F32)
    for j in range(8):
        u_next[:, tile(j)] = u0[:, tile(j)] + scale * total[:, tile(j)]
    hid[t] = input_norm(u_next[...], gain_of(par, 1)).astype(BF16)
    hid_steps = spread_tokens(spreading, hid, me)
    next(hid_steps)
    next(layer1)
    next(hid_steps)
    run(layer1)
    run(hid_steps)
    for link in (weights, tokens, small, spreading):
        link.drain()


def middle(*arrays):
    return pl.pallas_call(
        middle_kernel,
        out_shape=(
            jax.ShapeDtypeStruct((T, WP), F32),
            jax.ShapeDtypeStruct((T, 768), F32),
            jax.ShapeDtypeStruct((T, CH), F32),
            jax.ShapeDtypeStruct((ROWS, D), F32),
            jax.ShapeDtypeStruct((ROWS, D), F32),
            jax.ShapeDtypeStruct((8, 128), F32),
            jax.ShapeDtypeStruct((4, ROWS, D), BF16),
            jax.ShapeDtypeStruct((4, 4, 64, WALL), BF16),
        ),
        in_specs=[pl.BlockSpec(memory_space=pltpu.SMEM)] + vmem_specs(6),
        out_specs=tuple(vmem_specs(8)),
        scratch_shapes=[VM((4, ROWS, D), BF16), VM((4, 8, 128), F32)] + fwd_scratch() + token_scratch()
        + [VM((3, 8, 128), F32), pltpu.SemaphoreType.DMA((1,))]
        + link_scratch(GATHER_COPIES, 6, 3, 6),
        compiler_params=pltpu.CompilerParams(
            collective_id=1, has_side_effects=True, vmem_limit_bytes=16 << 20
        ),
        name="forward_0_and_tokens",
    )(*arrays)


def stats_exchange(link, st, buf, coef, me):
    barrier_end(me.ts)
    copies = [link.send(st, buf.at[me.t], peer) for peer in me.ts]
    buf[me.t] = st[...]
    yield
    for copy in copies:
        copy.wait_recv()
    for i in range(4):
        both = buf[0, i] + buf[1, i] + buf[2, i] + buf[3, i]
        s = lax.rsqrt(both[0:1] / DI + EPSILON)
        k = s * s * s * (both[1:2] / DI)
        row = iota((8, 128), 0)
        coef[i] = jnp.where(row == 0, s, jnp.where(row == 1, k, 0.0))
    link.drain()
    yield


def norm_back(u, gain, g, d_hidden):
    r = lax.rsqrt(jnp.mean(u * u, axis=-1, keepdims=True) + EPSILON)
    mean = jnp.mean(u * gain * d_hidden, axis=-1, keepdims=True)
    d_u = g + r * gain * d_hidden - u * (r * r * r) * mean
    return d_u, jnp.sum(u * r * d_hidden, axis=0, keepdims=True)


def back_middle_kernel(
    lens, par, w1, proj1, kept1, yssd1, coef1, d_scaled1, u, cot, valid, total0, s0, hid1, db1,
    sums1, heads1, g1, ng, db, coef, sum_a, sum_b,
    dh, d_proj1, scaled1, inn, xb, dyb, dyf, dx, bb, cb, d_c, cumr, colr,
    relay, sums, inbox, grads, core_in, acc, g_relay, g_sums, g_inbox,
    g_s, g_r, p_s, p_r, b_s, b_r, h_s, h_r,
):
    me = Peers()
    t = me.t
    barrier_start(me.near_dp())
    mixer_bwd_kernel(
        1, lens, par, w1, proj1, kept1, yssd1, coef1, d_scaled1, dh, d_proj1, scaled1, sums1, heads1,
        inn, xb, dyb, dyf, dx, bb, cb, d_c, cumr, colr,
        early=lambda: barrier_end(me.near_dp()),
    )
    weights, tokens, small, spreading = Link(g_s, g_r), Link(p_s, p_r), Link(b_s, b_r), Link(h_s, h_r)
    sum_steps = collect_tokens(tokens, dh, relay, sums, inbox, me)
    next(sum_steps)
    layer1 = reduce_rings(
        weights, (hid1, d_proj1, db1, scaled1), grads, sum_a, sum_b, core_in, acc,
        g_relay, g_sums, g_inbox, me,
    )
    next(layer1)
    next(sum_steps)
    next(layer1)
    next(layer1)
    run(sum_steps)
    total = dh[t].astype(F32) + inbox[0].astype(F32) + inbox[1].astype(F32)
    d_u, gain_term = norm_back(u[...], gain_of(par, 1), cot[...], total)
    g1[...] = d_u
    ng[...] = gain_term
    mean = jnp.zeros((ROWS, 128), F32)
    for j in range(8):
        d_branch = (g1[:, tile(j)] * valid[...]).astype(BF16)
        db[t, :, tile(j)] = d_branch
        mean = mean + d_branch.astype(F32) * total0[:, tile(j)]
    db_steps = spread_tokens(spreading, db, me)
    next(db_steps)
    mean = jnp.broadcast_to(jnp.sum(mean, axis=-1, keepdims=True), (128, 128))
    mean_row = jnp.transpose(mean)[0:8] / DI
    s = s0[0:1, :]
    row = iota((8, 128), 0)
    coef[t] = jnp.where(row == 0, s, jnp.where(row == 1, s * s * s * mean_row, 0.0))
    coef_copies = [small.send(coef.at[t], coef.at[t], peer) for peer in me.ts]
    next(layer1)
    next(db_steps)
    next(layer1)
    run(db_steps)
    for copy in coef_copies:
        copy.wait_recv()
    for link in (weights, tokens, small, spreading):
        link.drain()


def back_middle(*arrays):
    return pl.pallas_call(
        back_middle_kernel,
        out_shape=(
            jax.ShapeDtypeStruct((8, 768), F32),
            jax.ShapeDtypeStruct((8, 128), F32),
            jax.ShapeDtypeStruct((ROWS, D), F32),
            jax.ShapeDtypeStruct((1, D), F32),
            jax.ShapeDtypeStruct((4, ROWS, D), BF16),
            jax.ShapeDtypeStruct((4, 8, 128), F32),
            jax.ShapeDtypeStruct((4, 16, WALL), BF16),
            jax.ShapeDtypeStruct((4, 16, WALL), BF16),
        ),
        in_specs=[pl.BlockSpec(memory_space=pltpu.SMEM)] + vmem_specs(14),
        out_specs=tuple(vmem_specs(8)),
        scratch_shapes=bwd_scratch()[0] + bwd_scratch()[1] + token_scratch() + ring_scratch() + link_scratch(RING_COPIES, 6, 3, 6),
        compiler_params=pltpu.CompilerParams(
            collective_id=3, has_side_effects=True, vmem_limit_bytes=26 << 20
        ),
        name="backward_1_and_tokens",
    )(*arrays)


def small_sum(link, own, arrived, by_z, by_x, by_t, me):
    c, x, z, t = me.c, me.x, me.z, me.t
    swap = link.send(own.at[1 - c], arrived, me.core)
    yield
    swap.wait_recv()
    by_z[z] = own[c] + arrived[...]
    copies = [link.send(by_z.at[z], by_z.at[z], peer) for peer in me.zs]
    yield
    for copy in copies:
        copy.wait_recv()
    by_x[x] = by_z[0] + by_z[1] + by_z[2] + by_z[3]
    copies = [link.send(by_x.at[x], by_x.at[x], peer) for peer in me.xs]
    yield
    for copy in copies:
        copy.wait_recv()
    by_t[t] = by_x[0] + by_x[1] + by_x[2] + by_x[3]
    copies = [link.send(by_t.at[t], by_t.at[t], peer) for peer in me.ts]
    yield
    for copy in copies:
        copy.wait_recv()
    yield


def finish_kernel(
    lens, w0, proj0, kept0, yssd0, coef0, db0,
    part, u0, u1, g1, valid, par, coef1, ng1, sums1, heads1, sum_a1, sum_b1, hid0,
    lo, lg, smt, nmt, picked, o_bc,
    dh, d_proj0, scaled0, inn, xb, dyb, dyf, dx, bb, cb, d_c, cumr, colr, d_scaled0, sums0, heads0,
    relay, sums, inbox, relay2, sums2, inbox2, los, lgs, sms, smr, smz, smx, nms, nmr, nmz, nmx, sum_a0, sum_b0,
    grads, core_in, acc, g_relay, g_sums, g_inbox, w_grad0, bc_all0, last_in0, w_grad1, bc_all1, last_in1,
    g_s, g_r, f_s, f_r, l_s, l_r, p_s, p_r, q_s, q_r, b_s, b_r,
):
    me = Peers()
    c, x, z, t = me.c, me.x, me.z, me.t
    barrier_start(me.everyone())
    weights, final0, final1 = Link(g_s, g_r), Link(f_s, f_r), Link(l_s, l_r)
    tokens, tokens2, small = Link(p_s, p_r), Link(q_s, q_r), Link(b_s, b_r)
    last1 = reduce_last(final1, sum_a1, sum_b1, w_grad1, bc_all1, last_in1, me)
    out_steps = collect_tokens(tokens2, part, relay2, sums2, inbox2, me)

    def early():
        barrier_end(me.everyone())
        next(last1)
        next(out_steps)

    def later():
        next(last1)
        next(out_steps)

    mixer_bwd_kernel(
        0, lens, par, w0, proj0, kept0, yssd0, coef0, db0, dh, d_proj0, scaled0, sums0, heads0,
        inn, xb, dyb, dyf, dx, bb, cb, d_c, cumr, colr, d_scaled0, early=early, later=later,
    )
    for layer, (by_channel, heads) in enumerate(((sums0, heads0), (sums1, heads1))):
        sms[layer, 0:8, :] = by_channel[:, 0:512]
        sms[layer, 8:16, 0:256] = by_channel[:, 512:768]
        sms[layer, 8:16, 256:384] = heads[...]
        sms[layer, 8:16, 384:512] = jnp.zeros((8, 128), F32)
    chain = small_sum(small, sms, smr, smz, smx, smt, me)
    next(chain)
    back_steps = collect_tokens(tokens, dh, relay, sums, inbox, me)
    next(back_steps)
    layer0 = reduce_rings(
        weights, (hid0, d_proj0, db0, scaled0), grads, sum_a0, sum_b0, core_in, acc,
        g_relay, g_sums, g_inbox, me,
    )
    next(layer0)
    next(chain)
    next(back_steps)
    next(layer0)
    next(layer0)
    next(chain)
    los[0] = u1[...]
    lgs[1] = g1[...]
    next(layer0)
    run(back_steps)
    total = dh[t].astype(F32) + inbox[0].astype(F32) + inbox[1].astype(F32)
    d_u, gain_term = norm_back(u0[...], gain_of(par, 0), g1[...], total)
    lgs[0] = d_u
    lg_copy = small.send(lgs.at[1 - c], lg.at[c], me.core)
    lg[c] = lgs[c]
    for layer, term in enumerate((gain_term, ng1[...])):
        for j in range(8):
            nms[layer, j : j + 1, :] = term[:, tile(j)]
    norm_chain = small_sum(small, nms, nmr, nmz, nmx, nmt, me)
    next(norm_chain)
    next(layer0)
    last0 = reduce_last(final0, sum_a0, sum_b0, w_grad0, bc_all0, last_in0, me)
    next(last0)
    next(chain)
    run(last1)
    next(norm_chain)
    next(norm_chain)
    run(out_steps)
    los[1] = part[t].astype(F32) + inbox2[0].astype(F32) + inbox2[1].astype(F32)
    scale = column_of(coef1[t][0:1]) * valid[...]
    for j in range(8):
        los[1, :, tile(j)] = u1[:, tile(j)] + scale * los[1, :, tile(j)]
    lo_copy = small.send(los.at[1 - c], lo.at[c], me.core)
    lo[c] = los[c]
    next(last0)
    next(norm_chain)
    run(last0)
    picked[...] = jnp.where(c == 0, w_grad0[...], w_grad1[...])
    half = t // 2
    bc0 = bc_all0[0, half] + bc_all0[1, half] + bc_all0[2, half] + bc_all0[3, half]
    bc1 = bc_all1[0, half] + bc_all1[1, half] + bc_all1[2, half] + bc_all1[3, half]
    o_bc[...] = jnp.where(c == 0, bc0, bc1)
    run(chain)
    run(norm_chain)
    lo_copy.wait_recv()
    lg_copy.wait_recv()
    for link in (weights, final0, final1, tokens, tokens2, small):
        link.drain()


def finish(*arrays):
    return pl.pallas_call(
        finish_kernel,
        out_shape=(
            jax.ShapeDtypeStruct((2, ROWS, D), F32),
            jax.ShapeDtypeStruct((2, ROWS, D), F32),
            jax.ShapeDtypeStruct((4, 16, 512), F32),
            jax.ShapeDtypeStruct((4, 8, 128), F32),
            jax.ShapeDtypeStruct((64, WALL), F32),
            jax.ShapeDtypeStruct((16, 2 * N), F32),
        ),
        in_specs=[pl.BlockSpec(memory_space=pltpu.SMEM)] + vmem_specs(19),
        out_specs=tuple(vmem_specs(6)),
        scratch_shapes=bwd_scratch()[0] + bwd_scratch()[1]
        + [VM((T, CH), F32), VM((8, 768), F32), VM((8, 128), F32)]
        + token_scratch() + token_scratch()
        + [
            VM((2, ROWS, D), F32), VM((2, ROWS, D), F32),
            VM((2, 16, 512), F32), VM((16, 512), F32), VM((4, 16, 512), F32), VM((4, 16, 512), F32),
            VM((2, 8, 128), F32), VM((8, 128), F32), VM((4, 8, 128), F32), VM((4, 8, 128), F32),
            VM((4, 16, WALL), BF16), VM((4, 16, WALL), BF16),
        ]
        + ring_scratch() + last_scratch() + last_scratch()
        + link_scratch(RING_COPIES, LAST_COPIES, LAST_COPIES, 6, 6, 22),
        compiler_params=pltpu.CompilerParams(
            collective_id=4, has_side_effects=True, vmem_limit_bytes=34 << 20
        ),
        name="backward_0_and_gradients",
    )(*arrays)


def write_kernel(lo, lg, smt, nmt, picked, bc, *rest):
    outs, (in_part, dt, conv_w, conv_b, gain, norm, heads, sem) = rest[:13], rest[13:]
    (o_lo, o_lg, o_norm, o_in, o_bc, o_dt, o_cw, o_cb, o_dtb, o_alog, o_skip, o_gain, o_out) = outs
    copies = []

    def write(src, dst):
        copy = pltpu.make_async_copy(src, dst, sem.at[len(copies)])
        copy.start()
        copies.append(copy)

    write(lo, o_lo)
    write(lg, o_lg)
    write(bc, o_bc)
    in_part[:, 0, :] = picked[:, 0:512]
    in_part[:, 1, :] = picked[:, 512:1024]
    write(in_part, o_in)
    write(picked.at[:, pl.ds(WP, CH)], o_out)
    dt_rows = jnp.concatenate([picked[:, 1280:1408], jnp.zeros((64, 128), F32)], axis=0)
    dt[...] = jnp.transpose(dt_rows)[0:HL, 0:64]
    write(dt, o_dt)
    shared = smt[0, 8:16] + smt[1, 8:16] + smt[2, 8:16] + smt[3, 8:16]
    norms = nmt[0] + nmt[1] + nmt[2] + nmt[3]
    for j in range(8):
        norm[:, tile(j)] = norms[j : j + 1]
    write(norm, o_norm)
    conv_w[:, DI : DI + 2 * N] = shared[0:4, 0:256]
    conv_b[:, DI : DI + 2 * N] = shared[4:5, 0:256]
    for k in range(4):
        at = slice(512 * k, 512 * k + 512)
        conv_w[:, at] = smt[k, 0:4, :]
        conv_b[:, at] = smt[k, 4:5, :]
        gain[:, at] = smt[k, 5:6, :]
    write(conv_w, o_cw)
    write(conv_b, o_cb)
    write(gain, o_gain)
    all_heads = smt[0, 8:16, 256:384]
    for k in range(1, 4):
        all_heads = all_heads + pltpu.roll(smt[k, 8:16, 256:384], HL * k, 1)
    for k, out in ((0, o_dtb), (1, o_alog), (2, o_skip)):
        heads[k] = all_heads[k : k + 1, 0:H]
        write(heads.at[k], out)
    for copy in copies:
        copy.wait()


def write_outputs(*arrays):
    hbm_spec = pl.BlockSpec(memory_space=pltpu.HBM)
    shapes = [
        (2, ROWS, D), (2, ROWS, D), (1, D), (64, 2, CH), (16, 2 * N), (HL, 64), (CONV, DI + 2 * N),
        (1, DI + 2 * N), (1, H), (1, H), (1, H), (1, DI), (64, CH),
    ]
    return pl.pallas_call(
        write_kernel,
        out_shape=tuple(jax.ShapeDtypeStruct(shape, F32) for shape in shapes),
        in_specs=vmem_specs(6),
        out_specs=(hbm_spec,) * 13,
        scratch_shapes=[
            VM((64, 2, CH), F32), VM((HL, 64), F32), VM((CONV, DI + 2 * N), F32),
            VM((1, DI + 2 * N), F32), VM((1, DI), F32), VM((1, D), F32), VM((3, 1, H), F32),
            pltpu.SemaphoreType.DMA((13,)),
        ],
        compiler_params=pltpu.CompilerParams(vmem_limit_bytes=6 << 20),
        name="write_outputs",
    )(*arrays)


def body(
    activations, cotangent, lengths, norm_gain, in_weight, bc_weight, dt_weight, conv_weight,
    conv_bias, dt_bias, a_log, d_skip, gated_gain, out_weight,
):
    section = lax.axis_index("section")
    u0 = lax.dynamic_index_in_dim(activations, section, 0, keepdims=False)
    cot = lax.dynamic_index_in_dim(cotangent, section, 0, keepdims=False)
    flat = jnp.concatenate(
        [conv_bias, gated_gain, norm_gain, dt_bias, a_log, d_skip, jnp.zeros((1, 32), F32)], axis=1
    )
    w0, shard1, par, hid0, db1, valid = gather(
        lengths, in_weight[0].reshape(64, WZX), bc_weight[0], dt_weight[0].T, out_weight[0].T,
        conv_weight[0], flat, u0, cot,
    )
    proj0, kept0, y0, total0, u1, s0, hid1, w1 = middle(lengths, par, hid0, w0, u0, valid, shard1)
    proj1, kept1, part1, y1, coef1, d_scaled1 = mixer_fwd(1, lengths, par, hid1, w1, db1)
    sums1, heads1, g1, ng1, db0, coef0, sum_a1, sum_b1 = back_middle(
        lengths, par, w1, proj1, kept1, y1, coef1, d_scaled1, u1, cot, valid, total0, s0, hid1, db1
    )
    outs = write_outputs(
        *finish(
            lengths, w0, proj0, kept0, y0, coef0, db0, part1, u0, u1, g1, valid, par, coef1, ng1,
            sums1, heads1, sum_a1, sum_b1, hid0,
        )
    )
    outs = [out.T if k in (5, 12) else out for k, out in enumerate(outs)]
    plain = (2, 8, 9, 10, 7, 11)
    return tuple(out if k in plain else out[None] for k, out in enumerate(outs))


def solution(mesh):
    return jax.shard_map(
        body,
        mesh=mesh,
        in_specs=(
            P(None, ("dp", "tensor"), None),
            P(None, ("dp", "tensor"), None),
            P(None, "dp", None),
            P("section", None),
            P("section", "dp", None, "tensor"),
            P("section", "dp", None),
            P("section", "dp", "tensor"),
            P("section", None, None),
            P("section", None),
            P("section", None),
            P("section", None),
            P("section", None),
            P("section", None),
            P("section", "tensor", "dp"),
        ),
        out_specs=(
            P("section", None, ("dp", "tensor"), None),
            P("section", None, ("dp", "tensor"), None),
            P("section", None),
            P("section", "dp", None, "tensor"),
            P("section", ("dp", "tensor"), None),
            P("section", "dp", "tensor"),
            P("section", None, None),
            P("section", None),
            P("section", None),
            P("section", None),
            P("section", None),
            P("section", None),
            P("section", "tensor", "dp"),
        ),
        check_vma=False,
    )
```
